32 devices in a mesh: ctx: 4 (over y, core), exp: 8 (over z, x).
Axes of the slice: x: 2, y: 2, z: 4, core: 2. Of those that a mesh axis runs over, the one named last changes fastest.
Arguments:
- queries: bfloat16 [4, 8, 64, 4096], P('ctx', 'exp'), may hold values from -90 to 90
- new_keys_values: bfloat16 [4, 8, 64, 512], P('ctx', 'exp'), may hold values from -4.5 to 4.5
- cached_keys_values: bfloat16 [4, 8, 64, 512], P('ctx', 'exp'), may hold values from -4.5 to 4.5
- residual: bfloat16 [4, 8, 64, 4096], P(None, 'exp', None, 'ctx'), may hold values from -17 to 17
- out_weight: bfloat16 [4096, 4096], P('exp', 'ctx'), may hold values from -0.125 to 0.125
- norm_gain: float32 [4096], P('ctx'), may hold values from 0.1 to 1.9
- routes: int32 [4, 8, 64, 8], P(None, 'exp'), may hold values from 0 to 127, as said below
- gates: float32 [4, 8, 64, 8], P(None, 'exp'), may hold values from 0.3 to 1
- w_gate_up: bfloat16 [8, 4096, 3072], P('exp', 'ctx'), may hold values from -0.125 to 0.125
- w_down: bfloat16 [8, 1536, 4096], P('exp', None, 'ctx'), may hold values from -0.15625 to 0.15625
Outputs:
- layer_out: bfloat16 [4, 8, 64, 4096], P(None, 'exp', None, 'ctx')
The draws below stay inside these ranges and needn't reach their ends.
Inputs may be any that keep to these rules, and one draw needn't show every extreme that they name: `routes`: each row names 8 different experts, at most one of them below 8. Among the rows that share the second index, an expert below 8 is named by at most 16 of them, and some expert by exactly 16.
All inputs are finite; a program needn't handle non-finite values.
Results may differ from the reference program's by a relative error of at most 0.02.
Values may be sent and summed in bfloat16 or wider, within the bound.
No kernel may reach another device: no remote copies, remote signals or barrier semaphores. Data moves between devices by JAX's collectives and lax.ppermute only.
A program may use at most 64 MiB of HBM per device.

```python
import math
import jax
import jax.numpy as jnp
from jax import lax

D = 4096
QUERY_HEADS = 32
KEY_VALUE_HEADS = 2
HEAD_SIZE = 128
FF = 1536
EXPERTS = 128
TOP = 8
TOK_DEV = 64
PAST_PER_BLOCK = 64
GROUP_TOTAL = 4
HELD_COUNT = 8
NEW_TOKENS = 256
PAST_PER_SEQ = 256
TOKENS = 2048
CAP = 16


def token_major(values):
    shaped = values.reshape(HELD_COUNT, GROUP_TOTAL, TOK_DEV, values.shape[2])
    return jnp.transpose(shaped, (1, 0, 2, 3))


def shared_rows(key, strength):
    root_random_key = jax.random.fold_in(key, 0)
    token_rows = jnp.clip(jax.random.normal(root_random_key, (HELD_COUNT, NEW_TOKENS, 2 * KEY_VALUE_HEADS * HEAD_SIZE), jnp.float32), -4.0, 4.0)
    places = jnp.arange(NEW_TOKENS)
    paired = (places % 32 == 5).astype(jnp.float32)[None, :, None] * strength
    key_portion = token_rows[:, :, :KEY_VALUE_HEADS * HEAD_SIZE]
    key_portion = (1.0 - paired) * key_portion
    return jnp.concatenate([key_portion, token_rows[:, :, KEY_VALUE_HEADS * HEAD_SIZE:]], axis=2)


def draw_new_keys_values(key, part):
    strength = 0.0
    token_rows = shared_rows(key, strength)
    return token_major(token_rows).astype(jnp.bfloat16)


def draw_queries(key, part):
    key = jax.random.fold_in(key, 2)
    query = 2.0 * jnp.clip(jax.random.normal(key, (HELD_COUNT, NEW_TOKENS, QUERY_HEADS * HEAD_SIZE), jnp.float32), -4.0, 4.0)
    return token_major(query).astype(jnp.bfloat16)


def draw_residual(key, part):
    key = jax.random.fold_in(key, 3)
    first, second, third = jax.random.split(key, 3)
    random_noise = jnp.clip(jax.random.normal(first, (TOKENS, D), jnp.float32), -4.0, 4.0)
    row_level = jax.random.uniform(second, (TOKENS, 1), jnp.float32)
    column_level = jax.random.uniform(third, (1, D), jnp.float32)
    rising = jnp.arange(D, dtype=jnp.float32)[None, :] / D
    row_scale = jnp.exp(math.log(10.0) * row_level) / 3.16
    column_scale = jnp.exp(math.log(3.0) * rising + math.log(3.3) * column_level) / 15.0
    values = random_noise * row_scale * column_scale
    return values.reshape(GROUP_TOTAL, HELD_COUNT, TOK_DEV, D).astype(jnp.bfloat16)


def route_block(key):
    first, second, third, fourth, fifth = jax.random.split(key, 5)
    order = jax.random.permutation(first, HELD_COUNT)
    second_load = jax.random.randint(second, (), 1, CAP + 1)
    slots = jnp.arange(NEW_TOKENS)
    spread = 2 + (slots - CAP - second_load) % (HELD_COUNT - 2)
    picked = jnp.where(slots < CAP, 0, jnp.where(slots < CAP + second_load, 1, spread))
    resident_pick = order[picked]
    others_span = EXPERTS - HELD_COUNT
    stride = others_span // TOP
    offset = jax.random.randint(fourth, (NEW_TOKENS, 1), 0, others_span)
    leading = jnp.where(slots < NEW_TOKENS // 4, resident_pick, HELD_COUNT + offset[:, 0])
    others = HELD_COUNT + (offset + stride * jnp.arange(1, TOP)[None, :]) % others_span
    listed = jnp.concatenate([leading[:, None], others], axis=1)
    listed = listed[jax.random.permutation(third, NEW_TOKENS)]
    turn = jax.random.randint(fifth, (NEW_TOKENS, 1), 0, TOP)
    where_from = (jnp.arange(TOP)[None, :] - turn) % TOP
    return jnp.take_along_axis(listed, where_from, axis=1).astype(jnp.int32)


def draw_routes(key, part):
    key = jax.random.fold_in(key, 4)
    blocks = jax.vmap(lambda index: route_block(jax.random.fold_in(key, index)))(jnp.arange(HELD_COUNT))
    blocks = blocks.reshape(HELD_COUNT, GROUP_TOTAL, TOK_DEV, TOP)
    return jnp.transpose(blocks, (1, 0, 2, 3)).astype(jnp.int32)


def raised(values, stream_key, source, target, parts, factor):
    def block_of(dim):
        return (jnp.arange(values.shape[dim]) // (values.shape[dim] // parts)).reshape((-1,) + (1,) * (values.ndim - 1 - dim))

    near = jax.random.permutation(stream_key, parts)[block_of(target)]
    far = (block_of(target) + parts // 2) % parts
    return jnp.where((block_of(source) == near) | (block_of(source) == far), factor * values, values)


def levels(key, dims, shards, smallest, high):
    def one(position, blocks):
        steps = jax.random.uniform(jax.random.fold_in(jax.random.fold_in(key, 6), position), (blocks,), jnp.float32, smallest / len(shards), high / len(shards))
        return jnp.repeat(jnp.exp(steps), dims[position] // blocks).reshape((-1,) + (1,) * (len(dims) - position - 1))

    gain = one(*shards[0])
    for cut in shards[1:]:
        gain = gain * one(*cut)
    return gain


def centred(key, dims, scale, limit, pieces=(), kind=jnp.bfloat16):
    level = levels(key, dims, pieces, -0.22, 0.18) if pieces else 1.0
    values = jax.random.normal(key, dims, jnp.float32) * scale * level
    return jnp.minimum(jnp.maximum(values, -limit), limit).astype(kind)


def gaussian_with(rng, shape, width, bound, cuts, heavy, kind=jnp.bfloat16):
    values = width * jax.random.normal(rng, shape, jnp.float32)
    if cuts:
        values = values * levels(rng, shape, cuts, -0.22, 0.18)
    return jnp.clip(raised(values, jax.random.fold_in(rng, 3), *heavy), -bound, bound).astype(kind)


def setup_inputs(seed: int = 0) -> dict:
    splits = jax.random.split(jax.random.key(seed), 11)
    return {
        "queries": draw_queries(jax.random.fold_in(splits[10], 71), 0),
        "new_keys_values": draw_new_keys_values(jax.random.fold_in(splits[10], 71), 0),
        "cached_keys_values": centred(splits[2], (GROUP_TOTAL, HELD_COUNT, PAST_PER_BLOCK, 2 * KEY_VALUE_HEADS * HEAD_SIZE), 1.0, 4.5, ((0, 4), (1, 8))),
        "residual": draw_residual(jax.random.fold_in(splits[10], 71), 0),
        "out_weight": gaussian_with(splits[4], (QUERY_HEADS * HEAD_SIZE, D), (QUERY_HEADS * HEAD_SIZE) ** -0.5, 0.125, ((0, 8), (1, 4)), (0, 1, 8, 2.0)),
        "norm_gain": jnp.clip(1.0 + 0.18 * jax.random.normal(splits[5], (D,), jnp.float32), 0.1, 1.9),
        "routes": draw_routes(jax.random.fold_in(splits[10], 71), 0),
        "gates": jnp.clip(0.3 + 0.7 * jax.random.uniform(splits[7], (GROUP_TOTAL, HELD_COUNT, TOK_DEV, TOP), jnp.float32) ** levels(splits[7], (GROUP_TOTAL, HELD_COUNT, TOK_DEV, TOP), ((1, 8),), -0.2, 0.2), 0.3, 1.0),
        "w_gate_up": gaussian_with(splits[8], (HELD_COUNT, D, 2 * FF), D ** -0.5, 0.125, ((0, 8), (1, 4)), (1, 2, 4, 2.0)),
        "w_down": centred(splits[9], (HELD_COUNT, FF, D), FF ** -0.5, 0.15625, ((0, 8), (2, 4))),
    }


NEG_FILL = -1e+30

def head_attention(query_head, key_head, value_head, visible):
    scores = jnp.dot(query_head.astype(jnp.float32), key_head.astype(jnp.float32).T, precision=lax.Precision.HIGHEST) * HEAD_SIZE ** (-0.5)
    row_max = lax.optimization_barrier(jnp.max(jnp.where(visible, scores, NEG_FILL), axis=1, keepdims=True))
    weights = jnp.where(visible, jnp.exp(scores - row_max), 0.0)
    rounded = lax.optimization_barrier(weights.astype(jnp.bfloat16)).astype(jnp.float32)
    numerator = jnp.dot(rounded, value_head.astype(jnp.float32), precision=lax.Precision.HIGHEST)
    return (numerator / lax.optimization_barrier(jnp.sum(weights, axis=1, keepdims=True))).astype(jnp.bfloat16)

def sequence_major(array):
    return jnp.transpose(array, (1, 0, 2, 3)).reshape(HELD_COUNT * NEW_TOKENS, array.shape[3])

def reference(queries, new_keys_values, cached_keys_values, residual, out_weight, norm_gain, routes, gates, w_gate_up, w_down):
    seq_query = jnp.transpose(queries, (1, 0, 2, 3)).reshape(HELD_COUNT, NEW_TOKENS, QUERY_HEADS, HEAD_SIZE)
    sequence_keys_values = jnp.transpose(new_keys_values, (1, 0, 2, 3)).reshape(HELD_COUNT, NEW_TOKENS, 2, KEY_VALUE_HEADS, HEAD_SIZE)
    sequence_cached = jnp.transpose(cached_keys_values, (1, 0, 2, 3)).reshape(HELD_COUNT, PAST_PER_SEQ, 2, KEY_VALUE_HEADS, HEAD_SIZE)
    seq_all = jnp.concatenate([sequence_cached, sequence_keys_values], axis=1)
    row_places = jnp.arange(NEW_TOKENS, dtype=jnp.int32)
    key_places = jnp.arange(PAST_PER_SEQ + NEW_TOKENS, dtype=jnp.int32) - PAST_PER_SEQ
    visible = row_places[:, None] >= key_places[None, :]
    group_extent = QUERY_HEADS // KEY_VALUE_HEADS

    def one_sequence(operands):
        query_rows, key_rows = operands

        def one_head(head):
            query_head = lax.dynamic_index_in_dim(query_rows, head, 1, keepdims=False)
            common_key_head = head // group_extent
            key_head = lax.dynamic_index_in_dim(key_rows[:, 0], common_key_head, 1, keepdims=False)
            value_head = lax.dynamic_index_in_dim(key_rows[:, 1], common_key_head, 1, keepdims=False)
            return head_attention(query_head, key_head, value_head, visible)
        heads_out = lax.map(one_head, jnp.arange(QUERY_HEADS, dtype=jnp.int32))
        return jnp.transpose(heads_out, (1, 0, 2)).reshape(NEW_TOKENS, QUERY_HEADS * HEAD_SIZE)
    attended = lax.map(one_sequence, (seq_query, seq_all)).reshape(TOKENS, QUERY_HEADS * HEAD_SIZE)
    projected = jnp.dot(attended.astype(jnp.float32), out_weight.astype(jnp.float32), precision=lax.Precision.HIGHEST)
    mixed = sequence_major(residual).astype(jnp.float32) + projected
    normed = (mixed * lax.rsqrt(lax.optimization_barrier(jnp.mean(mixed * mixed, axis=1, keepdims=True)) + 1e-06) * norm_gain[None, :]).astype(jnp.bfloat16)
    route_rows = sequence_major(routes)
    gate_rows = sequence_major(gates)
    resident = route_rows < HELD_COUNT
    has_expert = jnp.any(resident, axis=1)
    target = lax.optimization_barrier(jnp.sum(jnp.where(resident, route_rows, 0), axis=1)).astype(jnp.int32)
    target = jnp.where(has_expert, target, HELD_COUNT).astype(jnp.int32)
    gate_share = lax.optimization_barrier(jnp.sum(jnp.where(resident, gate_rows, 0.0), axis=1))
    padded = jnp.concatenate([normed, jnp.zeros((1, D), jnp.bfloat16)], axis=0)
    width_block = D // GROUP_TOTAL
    most_rows = HELD_COUNT * CAP

    def one_expert(operands):
        expert, gate_up, down_proj = operands
        chosen = jnp.nonzero(target == expert, size=most_rows, fill_value=TOKENS)[0].astype(jnp.int32)
        row_block = padded[chosen].astype(jnp.float32)
        gate_up_wide = gate_up.astype(jnp.float32)
        summed = jnp.zeros((most_rows, 2 * FF), jnp.float32)
        for piece_index in range(GROUP_TOTAL):
            partial_term = jnp.dot(row_block[:, piece_index * width_block:(piece_index + 1) * width_block], gate_up_wide[piece_index * width_block:(piece_index + 1) * width_block], precision=lax.Precision.HIGHEST)
            summed = summed + lax.optimization_barrier(partial_term.astype(jnp.bfloat16)).astype(jnp.float32)
        activated = (jax.nn.silu(summed[:, :FF]) * summed[:, FF:]).astype(jnp.bfloat16)
        out_rows = jnp.dot(activated.astype(jnp.float32), down_proj.astype(jnp.float32), precision=lax.Precision.HIGHEST).astype(jnp.bfloat16)
        return (chosen, out_rows)
    chosen, out_rows = lax.map(one_expert, (jnp.arange(HELD_COUNT, dtype=jnp.int32), w_gate_up, w_down))
    collected = jnp.zeros((TOKENS + 1, D), jnp.float32).at[chosen.reshape(-1)].set(out_rows.reshape(-1, D).astype(jnp.float32))[:TOKENS]
    result = (mixed + gate_share[:, None] * collected).astype(jnp.bfloat16)
    return jnp.transpose(result.reshape(HELD_COUNT, GROUP_TOTAL, TOK_DEV, D), (1, 0, 2, 3))
```

```python
import functools

import jax
import jax.numpy as jnp
from jax import lax
from jax.experimental import pallas as pl
from jax.experimental.pallas import tpu as pltpu
from jax.sharding import PartitionSpec as P

D = 4096
QUERY_HEADS = 32
KEY_VALUE_HEADS = 2
HEAD_SIZE = 128
GROUP_EXTENT = QUERY_HEADS // KEY_VALUE_HEADS
NEG_FILL = -1e30
BF16 = jnp.bfloat16
F32 = jnp.float32
VMEM = pl.BlockSpec(memory_space=pltpu.VMEM)


def call(kernel, out_shape, n_in, scratch=(), cost=(0, 0), limit=32, **kw):
    kw.setdefault("in_specs", [VMEM] * n_in)
    kw.setdefault("out_specs", jax.tree.map(lambda _: VMEM, out_shape))
    return pl.pallas_call(
        kernel,
        out_shape=out_shape,
        scratch_shapes=list(scratch),
        cost_estimate=pl.CostEstimate(flops=cost[0], bytes_accessed=cost[1], transcendentals=0),
        compiler_params=pltpu.CompilerParams(vmem_limit_bytes=limit * 2**20),
        **kw,
    )


def sds(shape, dtype):
    return jax.ShapeDtypeStruct(shape, dtype)


def dot(a, b):
    return jnp.dot(a, b, preferred_element_type=F32)


def pack_kernel(C, q_ref, new_ref, past_ref, *outs):
    c = lax.axis_index("ctx")
    lo = lax.rem(lax.axis_index("exp"), 2)
    heads = QUERY_HEADS // C
    qw = heads // 2 * HEAD_SIZE
    for t in range(2):
        for s in range(C):
            target = jnp.bitwise_xor(c, s)
            out = outs[t * C + s]
            offset = (target * heads + jnp.bitwise_xor(lo, t) * (heads // 2)) * HEAD_SIZE
            out[:, :qw] = q_ref[:, pl.ds(pl.multiple_of(offset, HEAD_SIZE), qw)]
            kv = lax.div(target * heads, GROUP_EXTENT)
            k_at = pl.ds(pl.multiple_of(kv * HEAD_SIZE, HEAD_SIZE), HEAD_SIZE)
            v_at = pl.ds(pl.multiple_of((KEY_VALUE_HEADS + kv) * HEAD_SIZE, HEAD_SIZE), HEAD_SIZE)
            out[:, qw : qw + 128] = new_ref[:, k_at]
            out[:, qw + 128 : qw + 256] = new_ref[:, v_at]
            out[:, qw + 256 : qw + 384] = past_ref[:, k_at]
            out[:, qw + 384 :] = past_ref[:, v_at]


def attend_kernel(C, tok, *refs):
    msgs, out, q_s, kv_s = refs[: 2 * C], refs[2 * C], refs[2 * C + 1], refs[2 * C + 2]
    c = lax.axis_index("ctx")
    qw = q_s.shape[2]
    rows = C * tok
    for t in range(2):
        for s in range(C):
            msg = msgs[t * C + s]
            at = pl.multiple_of(jnp.bitwise_xor(c, s) * tok, tok)
            q_s[t, pl.ds(at, tok), :] = msg[:, :qw]
            kv_s[t, pl.ds(rows + at, tok), :] = msg[:, qw : qw + 256]
            kv_s[t, pl.ds(at, tok), :] = msg[:, qw + 256 :]
    block = 128
    for t in range(2):
        for b in range(rows // block):
            seen = rows + (b + 1) * block
            k = kv_s[t, :seen, :HEAD_SIZE]
            v = kv_s[t, :seen, HEAD_SIZE:]
            row = lax.broadcasted_iota(jnp.int32, (block, seen), 0) + (rows + b * block)
            visible = lax.broadcasted_iota(jnp.int32, (block, seen), 1) <= row
            for h in range(qw // HEAD_SIZE):
                q = q_s[t, b * block : (b + 1) * block, h * HEAD_SIZE : (h + 1) * HEAD_SIZE]
                scores = lax.dot_general(q, k, (((1,), (1,)), ((), ())), preferred_element_type=F32)
                scores = jnp.where(visible, scores * HEAD_SIZE ** (-0.5), NEG_FILL)
                weights = jnp.exp(scores - jnp.max(scores, axis=1, keepdims=True))
                total = jnp.sum(weights, axis=1, keepdims=True)
                numerator = dot(weights.astype(BF16), v)
                out[
                    t * rows + b * block : t * rows + (b + 1) * block,
                    h * HEAD_SIZE : (h + 1) * HEAD_SIZE,
                ] = (numerator / total).astype(BF16)


def route_kernel(E, cap, routes_ref, gates_ref, place_ref, gate_ref):
    e = lax.axis_index("exp")
    rows = routes_ref.shape[0]
    routes = routes_ref[...]
    resident = routes < E
    target = jnp.sum(jnp.where(resident, routes, 0), axis=1, keepdims=True)
    has = jnp.sum(resident.astype(jnp.int32), axis=1, keepdims=True) > 0
    gate = jnp.sum(jnp.where(resident, gates_ref[...], 0.0), axis=1, keepdims=True)
    gate_ref[...] = jnp.broadcast_to(gate, gate_ref.shape)
    lanes = lax.broadcasted_iota(jnp.int32, (rows, 128), 1)
    one_hot = jnp.where((target == lanes) & has, 1.0, 0.0)
    earlier = (
        lax.broadcasted_iota(jnp.int32, (rows, rows), 1)
        < lax.broadcasted_iota(jnp.int32, (rows, rows), 0)
    ).astype(F32).astype(BF16)
    rank = jnp.sum(dot(earlier, one_hot.astype(BF16)) * one_hot, axis=1, keepdims=True)
    slot = jnp.bitwise_xor(target, e) * cap + rank.astype(jnp.int32)
    slot = jnp.where(has, slot, -1)
    places = lax.broadcasted_iota(jnp.int32, (rows, E * cap), 1)
    place_ref[...] = jnp.where(slot == places, 1.0, 0.0).astype(BF16)


def project_kernel(C, *refs):
    atts, ws = refs[:C], refs[C : C + 2 * (C - 1)]
    acc, last, stacked = refs[-3:]
    c = lax.axis_index("ctx")
    hi = lax.div(lax.axis_index("exp"), 2)
    for s in range(C):
        stacked[jnp.bitwise_xor(c, s)] = atts[s][...]
    half = ws[0].shape[1]
    for j in range(2):
        total = None
        for k in range(C - 1):
            term = dot(stacked[lax.rem(hi - k + C, C)], ws[2 * k + j][...])
            total = term if total is None else total + term
        acc[:, j * half : (j + 1) * half] = total
    last[...] = stacked[lax.rem(hi + 1, C)]


def last_kernel(j, acc_ref, last_ref, w_ref, own_ref, send_ref):
    half = w_ref.shape[1]
    rows = own_ref.shape[0]
    total = acc_ref[:, j * half : (j + 1) * half] + dot(last_ref[...], w_ref[...])
    own_ref[...] = total[:rows]
    send_ref[...] = total[rows:].astype(BF16)


def mix_kernel(E, cap, own0, own1, got0, got1, res_ref, gain_ref, place_ref, mixed_ref, *outs):
    half = own0.shape[1]
    for j, (own, got) in enumerate(((own0, got0), (own1, got1))):
        at = slice(j * half, (j + 1) * half)
        mixed = res_ref[:, at].astype(F32) + (own[...] + got[...].astype(F32))
        mixed_ref[:, at] = mixed
        scaled = (mixed * gain_ref[:, at]).astype(BF16)
        picked = lax.dot_general(
            place_ref[...], scaled, (((0,), (0,)), ((), ())), preferred_element_type=F32
        ).astype(BF16)
        for s in range(E):
            outs[s][:, at] = picked[s * cap : (s + 1) * cap]


def gate_up_kernel(C, E, cap, *refs):
    xs, gain_ref, w_ref = refs[:E], refs[E], refs[E + 1]
    outs, x_s, part_s, sq_s = refs[E + 2 : E + 2 + C], refs[-3], refs[-2], refs[-1]
    c = lax.axis_index("ctx")
    j = pl.program_id(0)
    own_rows = E * cap // C
    width = w_ref.shape[1]
    wide = outs[0].shape[1] - 128

    @pl.when(j == 0)
    def _():
        e = lax.axis_index("exp")
        for s in range(E):
            at = pl.multiple_of(jnp.bitwise_xor(e, s) * cap, cap)
            x_s[pl.ds(at, cap), :] = xs[s][...]
        plain = x_s[...].astype(F32) / gain_ref[...]
        square = jnp.sum(plain * plain, axis=1, keepdims=True)
        high = square.astype(BF16).astype(F32)
        lane = lax.broadcasted_iota(jnp.int32, sq_s.shape, 1)
        parts = jnp.where(lane == 0, high, jnp.where(lane == 1, square - high, 0.0))
        sq_s[...] = parts.astype(BF16)
        for s in range(C):
            at = pl.multiple_of(jnp.bitwise_xor(c, s) * own_rows, own_rows)
            outs[s][:, wide:] = sq_s[pl.ds(at, own_rows), :]

    part_s[...] = dot(x_s[...], w_ref[...]).astype(BF16)
    col = pl.multiple_of(j * width, 128)
    for s in range(C):
        at = pl.multiple_of(jnp.bitwise_xor(c, s) * own_rows, own_rows)
        outs[s][:, pl.ds(col, width)] = part_s[pl.ds(at, own_rows), :]


def activate_kernel(hidden, *refs):
    xs, out = refs[:-1], refs[-1]

    def summed(at):
        total = xs[0][:, at].astype(F32)
        for x in xs[1:]:
            total = total + x[:, at].astype(F32)
        return total

    square = jnp.sum(summed(slice(2 * hidden, 2 * hidden + 128)), axis=1, keepdims=True)
    scale = lax.rsqrt(square / D + 1e-6)
    gate = summed(slice(0, hidden)) * scale
    up = summed(slice(hidden, 2 * hidden)) * scale
    out[...] = (gate / (1.0 + jnp.exp(-gate)) * up).astype(BF16)


def down_kernel(C, E, cap, *refs):
    acts, w_ref, outs, x_s, part_s = refs[:C], refs[C], refs[C + 1 : C + 1 + E], refs[-2], refs[-1]
    c = lax.axis_index("ctx")
    e = lax.axis_index("exp")
    j = pl.program_id(0)
    own_rows = E * cap // C
    width = w_ref.shape[1]

    @pl.when(j == 0)
    def _():
        for s in range(C):
            at = pl.multiple_of(jnp.bitwise_xor(c, s) * own_rows, own_rows)
            x_s[pl.ds(at, own_rows), :] = acts[s][...]

    part_s[...] = dot(x_s[...], w_ref[...]).astype(BF16)
    col = pl.multiple_of(j * width, 128)
    for s in range(E):
        at = pl.multiple_of(jnp.bitwise_xor(e, s) * cap, cap)
        outs[s][:, pl.ds(col, width)] = part_s[pl.ds(at, cap), :]


def combine_kernel(E, cap, mixed_ref, place_ref, gate_ref, *refs):
    xs, out, x_s = refs[:E], refs[E], refs[E + 1]
    for s in range(E):
        x_s[s * cap : (s + 1) * cap, :] = xs[s][...]
    collected = dot(place_ref[...], x_s[...])
    out[...] = (mixed_ref[...] + gate_ref[:, :1] * collected).astype(BF16)


def body(
    queries,
    new_keys_values,
    cached_keys_values,
    residual,
    out_weight,
    norm_gain,
    routes,
    gates,
    w_gate_up,
    w_down,
):
    C = lax.axis_size("ctx")
    E = lax.axis_size("exp")
    tok = queries.shape[2]
    rows = C * tok
    width = residual.shape[3]
    hidden = w_down.shape[1]
    cap = rows // (2 * E)
    qw = QUERY_HEADS // C // 2 * HEAD_SIZE

    def permute(x, target):
        pairs = []
        for c in range(C):
            for e in range(E):
                c2, e2 = target(c, e)
                pairs.append((c * E + e, c2 * E + e2))
        return lax.ppermute(x, ("ctx", "exp"), pairs)

    def along_ctx(s):
        return lambda c, e: (c ^ s, e)

    def along_exp(s):
        return lambda c, e: (c, e ^ s)

    half = width // 2
    ring = lambda c, e: (c, (e + 2) % E)
    pieces = [[out_weight[:, j * half : (j + 1) * half] for j in range(2)]]

    msgs = call(
        functools.partial(pack_kernel, C),
        [sds((tok, qw + 512), BF16)] * (2 * C),
        3,
        cost=(0, 4 * 2**20),
    )(
        queries.reshape(tok, queries.shape[3]),
        new_keys_values.reshape(tok, new_keys_values.shape[3]),
        cached_keys_values.reshape(tok, cached_keys_values.shape[3]),
    )
    got = [msgs[0]]
    for i in range(1, 2 * C):
        t, s = divmod(i, C)
        got.append(permute(msgs[i], lambda c, e, s=s, t=t: (c ^ s, e ^ t)))
    for k in range(1, C):
        pieces.append([permute(p, ring) for p in pieces[-1]])

    place, gate = call(
        functools.partial(route_kernel, E, cap),
        [sds((rows, E * cap), BF16), sds((rows, 128), F32)],
        2,
        cost=(0, 2**20),
    )(routes.reshape(rows, routes.shape[3]), gates.reshape(rows, gates.shape[3]))

    attended = call(
        functools.partial(attend_kernel, C, tok),
        sds((2 * rows, qw), BF16),
        2 * C,
        scratch=[pltpu.VMEM((2, rows, qw), BF16), pltpu.VMEM((2, 2 * rows, 2 * HEAD_SIZE), BF16)],
        cost=(4 * 2 * rows * 2 * rows * qw, 16 * 2**20),
    )(*got)
    atts = [attended] + [permute(attended, along_ctx(s)) for s in range(1, C)]

    early = [p for pair in pieces[: C - 1] for p in pair]
    acc, last = call(
        functools.partial(project_kernel, C),
        [sds((2 * rows, width), F32), sds((2 * rows, qw), BF16)],
        C + len(early),
        scratch=[pltpu.VMEM((C, 2 * rows, qw), BF16)],
        cost=(4 * rows * qw * width * (C - 1), 8 * 2**20),
    )(*atts, *early)
    own, arrived = [], []
    for j in range(2):
        mine, send = call(
            functools.partial(last_kernel, j),
            [sds((rows, half), F32), sds((rows, half), BF16)],
            3,
            cost=(4 * rows * qw * half, 2**20),
        )(acc, last, pieces[C - 1][j])
        own.append(mine)
        arrived.append(permute(send, along_exp(1)))

    gain = norm_gain.reshape(1, width)
    mixed, *outgoing = call(
        functools.partial(mix_kernel, E, cap),
        [sds((rows, width), F32)] + [sds((cap, width), BF16)] * E,
        7,
        cost=(0, 4 * 2**20),
    )(*own, *arrived, residual.reshape(rows, width), gain, place)
    incoming = [outgoing[0]] + [permute(outgoing[s], along_exp(s)) for s in range(1, E)]

    slots = E * cap
    own_rows = slots // C
    steps = 4
    wide = 2 * hidden
    whole = lambda shape: pl.BlockSpec(shape, lambda j: (0,) * len(shape))
    partials = call(
        functools.partial(gate_up_kernel, C, E, cap),
        [sds((own_rows, wide + 128), BF16)] * C,
        E + 2,
        scratch=[
            pltpu.VMEM((slots, width), BF16),
            pltpu.VMEM((slots, wide // steps), BF16),
            pltpu.VMEM((slots, 128), BF16),
        ],
        cost=(2 * slots * width * wide, 2 * width * wide),
        grid=(steps,),
        in_specs=[whole((cap, width))] * E
        + [whole((1, width)), pl.BlockSpec((width, wide // steps), lambda j: (0, j))],
        out_specs=[whole((own_rows, wide + 128))] * C,
    )(*incoming, gain, w_gate_up.reshape(width, wide))
    terms = [partials[0]] + [permute(partials[s], along_ctx(s)) for s in range(1, C)]
    activated = call(
        functools.partial(activate_kernel, hidden),
        sds((own_rows, hidden), BF16),
        C,
        cost=(0, 2**20),
    )(*terms)
    acts = [activated] + [permute(activated, along_ctx(s)) for s in range(1, C)]
    steps = 2
    expert_out = call(
        functools.partial(down_kernel, C, E, cap),
        [sds((cap, width), BF16)] * E,
        C + 1,
        scratch=[pltpu.VMEM((slots, hidden), BF16), pltpu.VMEM((slots, width // steps), BF16)],
        cost=(2 * slots * width * hidden, 2 * width * hidden),
        grid=(steps,),
        in_specs=[whole((own_rows, hidden))] * C
        + [pl.BlockSpec((hidden, width // steps), lambda j: (0, j))],
        out_specs=[whole((cap, width))] * E,
    )(*acts, w_down.reshape(hidden, width))
    returned = [expert_out[0]] + [permute(expert_out[s], along_exp(s)) for s in range(1, E)]
    result = call(
        functools.partial(combine_kernel, E, cap),
        sds((rows, width), BF16),
        3 + E,
        scratch=[pltpu.VMEM((slots, width), BF16)],
        cost=(0, 2 * 2**20),
    )(mixed, place, gate, *returned)
    return result.reshape(C, 1, tok, width)


def solution(mesh):
    in_specs = (
        P("ctx", "exp", None, None),
        P("ctx", "exp", None, None),
        P("ctx", "exp", None, None),
        P(None, "exp", None, "ctx"),
        P("exp", "ctx"),
        P("ctx"),
        P(None, "exp", None, None),
        P(None, "exp", None, None),
        P("exp", "ctx", None),
        P("exp", None, "ctx"),
    )
    out_specs = P(None, "exp", None, "ctx")
    return jax.shard_map(body, mesh=mesh, in_specs=in_specs, out_specs=out_specs, check_vma=False)
```

```python
import functools

import jax
import jax.numpy as jnp
from jax import lax
from jax.experimental import pallas as pl
from jax.experimental.pallas import tpu as pltpu
from jax.sharding import PartitionSpec as P

D = 4096
QUERY_HEADS = 32
KEY_VALUE_HEADS = 2
HEAD_SIZE = 128
GROUP_EXTENT = QUERY_HEADS // KEY_VALUE_HEADS
NEG_FILL = -1e30
BF16 = jnp.bfloat16
F32 = jnp.float32
VMEM = pl.BlockSpec(memory_space=pltpu.VMEM)
HBM = pl.BlockSpec(memory_space=pltpu.HBM)


def call(kernel, out_shape, n_in, scratch=(), cost=(0, 0), limit=32, **kw):
    kw.setdefault("in_specs", [VMEM] * n_in)
    kw.setdefault("out_specs", jax.tree.map(lambda _: VMEM, out_shape))
    return pl.pallas_call(
        kernel,
        out_shape=out_shape,
        scratch_shapes=list(scratch),
        cost_estimate=pl.CostEstimate(flops=cost[0], bytes_accessed=cost[1], transcendentals=0),
        compiler_params=pltpu.CompilerParams(vmem_limit_bytes=limit * 2**20),
        **kw,
    )


def sds(shape, dtype):
    return jax.ShapeDtypeStruct(shape, dtype)


def dot(a, b):
    return jnp.dot(a, b, preferred_element_type=F32)


def spread(d):
    return (d >> 1) * 4 + (d & 1)


def own_hi_lo():
    e = lax.axis_index("exp")
    return lax.div(e, 4) * 2 + lax.rem(e, 2), lax.rem(lax.div(e, 2), 2)


def aligned(x, n):
    return pl.multiple_of(x, n)


def pack_kernel(C, qw, q_ref, new_ref, past_ref, *refs):
    outs, sems = refs[:-1], refs[-1]
    c = lax.axis_index("ctx")
    _, lo = own_hi_lo()
    copies = []

    def copy(src, dst):
        copies.append(pltpu.make_async_copy(src, dst, sems.at[len(copies)]))
        copies[-1].start()

    for s in reversed(range(C)):
        target = jnp.bitwise_xor(c, s)
        out = outs[s]
        first = lax.div(target, 2) * 4 + lax.rem(target, 2)
        for t in range(2):
            offset = (first + 2 * jnp.bitwise_xor(lo, t)) * qw
            copy(q_ref.at[:, pl.ds(aligned(offset, 128), qw)], out.at[:, t * qw : (t + 1) * qw])
        kv = lax.div(target * (2 * qw // HEAD_SIZE), GROUP_EXTENT)
        at = 2 * qw
        for ref in (new_ref, past_ref):
            for part in (0, KEY_VALUE_HEADS):
                offset = (part + kv) * HEAD_SIZE
                copy(ref.at[:, pl.ds(aligned(offset, 128), 128)], out.at[:, at : at + 128])
                at += 128
    for c in copies:
        c.wait()


def attend_kernel(C, tok, *refs):
    msgs, outs, q_s, kv_s = refs[:C], refs[C : C + 2], refs[C + 2], refs[C + 3]
    c = lax.axis_index("ctx")
    qw = outs[0].shape[1]
    rows = C * tok
    for s in range(C):
        msg = msgs[s]
        at = aligned(jnp.bitwise_xor(c, s) * tok, tok)
        q_s[pl.ds(at, tok), :] = msg[:, : 2 * qw]
        kv_s[pl.ds(rows + at, tok), :] = msg[:, 2 * qw : 2 * qw + 256]
        kv_s[pl.ds(at, tok), :] = msg[:, 2 * qw + 256 :]
    block = 128
    for b in range(rows // block):
        seen = rows + (b + 1) * block
        k = kv_s[:seen, :HEAD_SIZE]
        v = kv_s[:seen, HEAD_SIZE:]
        row = lax.broadcasted_iota(jnp.int32, (block, seen), 0) + (rows + b * block)
        visible = lax.broadcasted_iota(jnp.int32, (block, seen), 1) <= row
        at = slice(b * block, (b + 1) * block)
        for h in range(2 * qw // HEAD_SIZE):
            q = q_s[at, h * HEAD_SIZE : (h + 1) * HEAD_SIZE]
            scores = lax.dot_general(q, k, (((1,), (1,)), ((), ())), preferred_element_type=F32)
            scores = jnp.where(visible, scores * HEAD_SIZE ** (-0.5), NEG_FILL)
            weights = jnp.exp(scores - jnp.max(scores, axis=1, keepdims=True))
            total = jnp.sum(weights, axis=1, keepdims=True)
            numerator = dot(weights.astype(BF16), v)
            t, col = divmod(h * HEAD_SIZE, qw)
            outs[t][at, col : col + HEAD_SIZE] = (numerator / total).astype(BF16)


def route_kernel(E, cap, routes_ref, gates_ref, place_ref, gate_ref):
    e = lax.axis_index("exp")
    rows = routes_ref.shape[0]
    routes = routes_ref[...]
    resident = routes < E
    target = jnp.sum(jnp.where(resident, routes, 0), axis=1, keepdims=True)
    has = jnp.sum(resident.astype(jnp.int32), axis=1, keepdims=True) > 0
    gate = jnp.sum(jnp.where(resident, gates_ref[...], 0.0), axis=1, keepdims=True)
    gate_ref[...] = jnp.broadcast_to(gate, gate_ref.shape)
    lanes = lax.broadcasted_iota(jnp.int32, (rows, 128), 1)
    one_hot = jnp.where((target == lanes) & has, 1.0, 0.0)
    earlier = (
        lax.broadcasted_iota(jnp.int32, (rows, rows), 1)
        < lax.broadcasted_iota(jnp.int32, (rows, rows), 0)
    ).astype(F32).astype(BF16)
    rank = jnp.sum(dot(earlier, one_hot.astype(BF16)) * one_hot, axis=1, keepdims=True)
    slot = jnp.bitwise_xor(target, e) * cap + rank.astype(jnp.int32)
    slot = jnp.where(has, slot, -1)
    places = lax.broadcasted_iota(jnp.int32, (rows, E * cap), 1)
    place_ref[...] = jnp.where(slot == places, 1.0, 0.0).astype(BF16)


def project_kernel(C, spans, *refs):
    atts, res_ref, ws = refs[:C], refs[C], refs[C + 1 : C + 1 + len(spans)]
    acc, last, stacked = refs[-3:]
    c = lax.axis_index("ctx")
    hi, _ = own_hi_lo()
    for s in range(C):
        stacked[jnp.bitwise_xor(c, s)] = atts[s][...]
    rows = res_ref.shape[0]
    width = acc.shape[1]
    half = width // 2
    for j in range(2):
        at = slice(j * half, (j + 1) * half)
        total = None
        for (d, first, count), w in zip(spans, ws):
            term = dot(stacked[jnp.bitwise_xor(hi, d), :, first : first + count], w[:, at])
            total = term if total is None else total + term
        acc[:rows, at] = total[:rows] + res_ref[:, at].astype(F32)
        acc[rows:, at] = total[rows:]
    count = last.shape[1]
    last[...] = stacked[jnp.bitwise_xor(hi, C - 1), :, stacked.shape[2] - count :]


def last_kernel(E, cap, acc_ref, last_ref, w_ref, mine_ref, other_ref, own_ref, full_ref, keep_ref, send_ref):
    rows = own_ref.shape[0]
    total = acc_ref[...] + dot(last_ref[...], w_ref[...])
    own_ref[...] = total[:rows]
    rounded = total.astype(BF16)
    full_ref[...] = rounded[rows:]
    for t, place in enumerate((mine_ref, other_ref)):
        picked = lax.dot_general(
            place[...],
            rounded[t * rows : (t + 1) * rows],
            (((0,), (0,)), ((), ())),
            preferred_element_type=F32,
        )
        for d in range(E // 2):
            near, far = spread(d) ^ (2 * t), spread(d) ^ 2 ^ (2 * t)
            at = (2 * d + t) * cap
            keep_ref[at : at + cap, :] = picked[near * cap : (near + 1) * cap]
            at = (2 * d + 1 - t) * cap
            send_ref[at : at + cap, :] = picked[far * cap : (far + 1) * cap].astype(BF16)


def outgoing_kernel(keep_ref, got_ref, gain_ref, *outs):
    scaled = ((keep_ref[...] + got_ref[...].astype(F32)) * gain_ref[...]).astype(BF16)
    count = outs[0].shape[0]
    for d, out in enumerate(outs):
        out[...] = scaled[d * count : (d + 1) * count]


def gate_up_kernel(C, E, cap, order, *refs):
    xs, gain_ref, w_ref, keep_ref, send_ref, x_s, part_s = refs[: E // 2], *refs[E // 2 :]
    c = lax.axis_index("ctx")
    e = lax.axis_index("exp")
    own_rows = E * cap // C
    wide = w_ref.shape[1]
    for d in range(E // 2):
        for t in range(2):
            at = aligned(jnp.bitwise_xor(e, spread(d) ^ (2 * t)) * cap, cap)
            x_s[pl.ds(at, cap), :] = xs[d][t * cap : (t + 1) * cap, :]
    plain = x_s[...].astype(F32) / gain_ref[...]
    square = jnp.sum(plain * plain, axis=1, keepdims=True)
    lane = lax.broadcasted_iota(jnp.int32, (E * cap, 128), 1)
    part_s[:, wide:] = jnp.where(lane == 0, square, 0.0)
    step = 512
    for j in range(wide // step):
        at = slice(j * step, (j + 1) * step)
        part_s[:, at] = dot(x_s[...], w_ref[:, at])
    for i, r in enumerate(order):
        at = aligned(jnp.bitwise_xor(c, r) * own_rows, own_rows)
        block = part_s[pl.ds(at, own_rows), :]
        if i < C // 2:
            keep_ref[i * own_rows : (i + 1) * own_rows, :] = block
        else:
            to = (i - C // 2) * own_rows
            send_ref[to : to + own_rows, :wide] = block[:, :wide].astype(BF16)
            square = block[:, wide:]
            high = square.astype(BF16).astype(F32)
            lane = lax.broadcasted_iota(jnp.int32, square.shape, 1)
            low = pltpu.roll(square - high, 1, 1)
            pair = jnp.where(lane == 1, low, high)
            send_ref[to : to + own_rows, wide:] = pair.astype(BF16)


def halve_kernel(keep_in, got_ref, keep_ref, send_ref):
    rows = keep_ref.shape[0]
    wide = keep_ref.shape[1] - 128
    total = keep_in[...] + got_ref[...].astype(F32)
    keep_ref[...] = total[:rows]
    send_ref[:, :wide] = total[rows:, :wide].astype(BF16)
    square = jnp.sum(total[rows:, wide:], axis=1, keepdims=True)
    high = square.astype(BF16).astype(F32)
    lane = lax.broadcasted_iota(jnp.int32, (rows, 128), 1)
    pair = jnp.where(lane == 0, high, jnp.where(lane == 1, square - high, 0.0))
    send_ref[:, wide:] = pair.astype(BF16)


def activate_kernel(hidden, keep_ref, got_ref, out):
    def summed(at):
        return keep_ref[:, at] + got_ref[:, at].astype(F32)

    square = jnp.sum(summed(slice(2 * hidden, 2 * hidden + 128)), axis=1, keepdims=True)
    scale = lax.rsqrt(square / D + 1e-6)
    gate = summed(slice(0, hidden)) * scale
    up = summed(slice(hidden, 2 * hidden)) * scale
    out[...] = (gate / (1.0 + jnp.exp(-gate)) * up).astype(BF16)


def down_kernel(C, E, cap, *refs):
    acts, w_ref, outs, x_s, part_s = refs[:C], refs[C], refs[C + 1 : C + 1 + E // 2], refs[-2], refs[-1]
    c = lax.axis_index("ctx")
    e = lax.axis_index("exp")
    own_rows = E * cap // C
    for s in range(C):
        at = aligned(jnp.bitwise_xor(c, s) * own_rows, own_rows)
        x_s[pl.ds(at, own_rows), :] = acts[s][...]
    part_s[...] = dot(x_s[...], w_ref[...]).astype(BF16)
    for d in range(E // 2):
        for t in range(2):
            at = aligned(jnp.bitwise_xor(e, spread(d) ^ (2 * t)) * cap, cap)
            outs[d][t * cap : (t + 1) * cap, :] = part_s[pl.ds(at, cap), :]


def forward_kernel(cap, *refs):
    for d, x in enumerate(refs[:-1]):
        refs[-1][d * cap : (d + 1) * cap, :] = x[cap:, :]


def combine_kernel(E, cap, own_ref, got_ref, place_ref, gate_ref, *refs):
    xs, far, out, x_s = refs[: E // 2], refs[E // 2], refs[E // 2 + 1], refs[E // 2 + 2]
    for d in range(E // 2):
        at = spread(d) * cap
        x_s[at : at + cap, :] = xs[d][:cap, :]
        at = (spread(d) ^ 2) * cap
        x_s[at : at + cap, :] = far[d * cap : (d + 1) * cap, :]
    collected = dot(place_ref[...], x_s[...])
    mixed = own_ref[...] + got_ref[...].astype(F32)
    out[...] = (mixed + gate_ref[:, :1] * collected).astype(BF16)


def body(
    queries,
    new_keys_values,
    cached_keys_values,
    residual,
    out_weight,
    norm_gain,
    routes,
    gates,
    w_gate_up,
    w_down,
):
    C = lax.axis_size("ctx")
    E = lax.axis_size("exp")
    tok = queries.shape[2]
    rows = C * tok
    width = residual.shape[3]
    hidden = w_down.shape[1]
    wide = 2 * hidden
    cap = rows // (2 * E)
    slots = E * cap
    own_rows = slots // C
    qw = QUERY_HEADS // E * HEAD_SIZE

    def permute(x, ctx=0, exp=0):
        pairs = [(c * E + e, (c ^ ctx) * E + (e ^ exp)) for c in range(C) for e in range(E)]
        return lax.ppermute(x, ("ctx", "exp"), pairs)

    def after(x, *others):
        return lax.optimization_barrier((x, *others))[0]

    cuts = [(0, qw // 2), (qw // 2, qw // 4), (qw * 3 // 4, qw // 4)]
    chunks = [out_weight[a : a + n] for a, n in cuts]
    shards = {0: [(0, qw, out_weight)]}
    for d in range(2, C, 2):
        shards[d] = [(0, cuts[0][1], permute(chunks[0], exp=spread(d)))]
    shards[1] = [(0, qw, permute(out_weight, exp=1))]

    msgs = call(
        functools.partial(pack_kernel, C, qw),
        [sds((tok, 2 * qw + 512), BF16)] * C,
        3,
        scratch=[pltpu.SemaphoreType.DMA((6 * C,))],
        in_specs=[HBM] * 3,
        cost=(0, 4 * 2**20),
    )(
        queries.reshape(tok, queries.shape[3]),
        new_keys_values.reshape(tok, new_keys_values.shape[3]),
        cached_keys_values.reshape(tok, cached_keys_values.shape[3]),
    )
    got = [msgs[0]] + [permute(msgs[s], ctx=s) for s in range(1, C)]
    mine, other = call(
        functools.partial(attend_kernel, C, tok),
        [sds((rows, qw), BF16)] * 2,
        C,
        scratch=[pltpu.VMEM((rows, 2 * qw), BF16), pltpu.VMEM((2 * rows, 2 * HEAD_SIZE), BF16)],
        cost=(4 * 2 * rows * 2 * rows * qw, 16 * 2**20),
        limit=16,
    )(*got)
    theirs = permute(other, exp=2)
    for d in range(2, C, 2):
        for (a, n), chunk in zip(cuts[1:], chunks[1:]):
            shards[d].append((a, n, permute(after(chunk, mine), exp=spread(d))))
    place, gate = call(
        functools.partial(route_kernel, E, cap),
        [sds((rows, slots), BF16), sds((rows, 128), F32)],
        2,
        cost=(0, 2**20),
    )(
        after(routes, mine).reshape(rows, routes.shape[3]),
        after(gates, mine).reshape(rows, gates.shape[3]),
    )
    attended = jnp.concatenate([mine, theirs], axis=0)
    atts = {0: attended}
    for s in range(2, C, 2):
        atts[s] = permute(attended, ctx=s)
    atts[1] = permute(attended, ctx=1)
    for d in range(3, C, 2):
        shards[d] = [
            (a, n, permute(after(w, mine), exp=1)) for a, n, w in shards[d - 1]
        ]
    for s in range(3, C, 2):
        atts[s] = permute(after(atts[s - 1], shards[2][1][2]), ctx=1)
    other_place = permute(place, exp=2)

    spans, pieces = [], []
    for d in range(C):
        for a, n, w in shards[d]:
            spans.append((d, a, n))
            pieces.append(w)
    last_rows = spans[-1][2]
    acc, last = call(
        functools.partial(project_kernel, C, spans[:-1]),
        [sds((2 * rows, width), F32), sds((2 * rows, last_rows), BF16)],
        C + len(spans),
        scratch=[pltpu.VMEM((C, 2 * rows, qw), BF16)],
        cost=(4 * rows * qw * width * (C - 1), 8 * 2**20),
    )(*[atts[s] for s in range(C)], residual.reshape(rows, width), *pieces[:-1])
    own, full, keep, send = call(
        functools.partial(last_kernel, E, cap),
        [
            sds((rows, width), F32),
            sds((rows, width), BF16),
            sds((slots, width), F32),
            sds((slots, width), BF16),
        ],
        5,
        cost=(4 * rows * (last_rows + slots) * width, 6 * 2**20),
    )(acc, last, pieces[-1], place, other_place)
    gain = norm_gain.reshape(1, width)
    outgoing = call(
        outgoing_kernel,
        [sds((2 * cap, width), BF16)] * (E // 2),
        3,
        cost=(0, 2**20),
    )(keep, permute(send, exp=2), gain)
    incoming = [outgoing[0]] + [permute(outgoing[d], exp=spread(d)) for d in range(1, E // 2)]

    order = [0]
    bit = C // 2
    while bit:
        order = order + [r | bit for r in order]
        bit //= 2
    keep, send = call(
        functools.partial(gate_up_kernel, C, E, cap, order),
        [sds((slots // 2, wide + 128), F32), sds((slots // 2, wide + 128), BF16)],
        E // 2 + 2,
        scratch=[pltpu.VMEM((slots, width), BF16), pltpu.VMEM((slots, wide + 128), F32)],
        cost=(2 * slots * width * wide, 2 * width * wide),
    )(*incoming, gain, w_gate_up.reshape(width, wide))
    arrived = permute(after(full, *incoming), exp=2)
    bit = 1
    while 2 * bit < C:
        count = keep.shape[0] // 2
        keep, send = call(
            halve_kernel,
            [sds((count, wide + 128), F32), sds((count, wide + 128), BF16)],
            2,
            cost=(0, 2**21),
        )(keep, permute(send, ctx=bit))
        bit *= 2
    activated = call(
        functools.partial(activate_kernel, hidden),
        sds((own_rows, hidden), BF16),
        2,
        cost=(0, 2**20),
    )(keep, permute(send, ctx=bit))
    acts = {0: activated}
    while bit:
        for r in list(acts):
            acts[r ^ bit] = permute(acts[r], ctx=bit)
        bit //= 2
    expert_out = call(
        functools.partial(down_kernel, C, E, cap),
        [sds((2 * cap, width), BF16)] * (E // 2),
        C + 1,
        scratch=[pltpu.VMEM((slots, hidden), BF16), pltpu.VMEM((slots, width), BF16)],
        cost=(2 * slots * width * hidden, 2 * width * hidden),
    )(*[acts[s] for s in range(C)], w_down.reshape(hidden, width))
    returned = [expert_out[0]]
    returned += [permute(expert_out[d], exp=spread(d)) for d in range(1, E // 2)]
    far = call(
        functools.partial(forward_kernel, cap), sds((slots // 2, width), BF16), E // 2, cost=(0, 2**19)
    )(*returned)
    result = call(
        functools.partial(combine_kernel, E, cap),
        sds((rows, width), BF16),
        5 + E // 2,
        scratch=[pltpu.VMEM((slots, width), BF16)],
        cost=(0, 2 * 2**20),
    )(own, arrived, place, gate, *returned, permute(far, exp=2))
    return result.reshape(C, 1, tok, width)


def solution(mesh):
    in_specs = (
        P("ctx", "exp", None, None),
        P("ctx", "exp", None, None),
        P("ctx", "exp", None, None),
        P(None, "exp", None, "ctx"),
        P("exp", "ctx"),
        P("ctx"),
        P(None, "exp", None, None),
        P(None, "exp", None, None),
        P("exp", "ctx", None),
        P("exp", None, "ctx"),
    )
    out_specs = P(None, "exp", None, "ctx")
    return jax.shard_map(body, mesh=mesh, in_specs=in_specs, out_specs=out_specs, check_vma=False)
```

```python
import functools

import jax
import jax.numpy as jnp
from jax import lax
from jax.experimental import pallas as pl
from jax.experimental.pallas import tpu as pltpu
from jax.sharding import PartitionSpec as P

D = 4096
QUERY_HEADS = 32
KEY_VALUE_HEADS = 2
HEAD_SIZE = 128
GROUP_EXTENT = QUERY_HEADS // KEY_VALUE_HEADS
NEG_FILL = -1e30
BF16 = jnp.bfloat16
F32 = jnp.float32
VMEM = pl.BlockSpec(memory_space=pltpu.VMEM)
HBM = pl.BlockSpec(memory_space=pltpu.HBM)


def call(kernel, out_shape, n_in, scratch=(), cost=(0, 0), limit=32, **kw):
    kw.setdefault("in_specs", [VMEM] * n_in)
    kw.setdefault("out_specs", jax.tree.map(lambda _: VMEM, out_shape))
    return pl.pallas_call(
        kernel,
        out_shape=out_shape,
        scratch_shapes=list(scratch),
        cost_estimate=pl.CostEstimate(flops=cost[0], bytes_accessed=cost[1], transcendentals=0),
        compiler_params=pltpu.CompilerParams(vmem_limit_bytes=limit * 2**20),
        **kw,
    )


def sds(shape, dtype):
    return jax.ShapeDtypeStruct(shape, dtype)


def dot(a, b):
    return jnp.dot(a, b, preferred_element_type=F32)


PAIR = 4


def spread(d):
    return (d // PAIR) * 2 * PAIR + d % PAIR


def own_hi_lo():
    e = lax.axis_index("exp")
    return lax.div(e, 2 * PAIR) * PAIR + lax.rem(e, PAIR), lax.rem(lax.div(e, PAIR), 2)


def aligned(x, n):
    return pl.multiple_of(x, n)


def pack_kernel(C, qw, q_ref, new_ref, past_ref, w_ref, *refs):
    outs, halves, sems = refs[:C], refs[C:-1], refs[-1]
    c = lax.axis_index("ctx")
    _, lo = own_hi_lo()
    copies = []

    def copy(src, dst):
        copies.append(pltpu.make_async_copy(src, dst, sems.at[len(copies)]))
        copies[-1].start()

    for s in reversed(range(C)):
        target = jnp.bitwise_xor(c, s)
        out = outs[s]
        for t in range(2):
            shard = lax.div(target, PAIR) * 2 * PAIR + lax.rem(target, PAIR)
            shard = shard + PAIR * jnp.bitwise_xor(lo, t)
            copy(q_ref.at[:, pl.ds(aligned(shard * qw, 128), qw)], out.at[:, t * qw : (t + 1) * qw])
            kv = lax.div(shard * (qw // HEAD_SIZE), GROUP_EXTENT)
            at = 2 * qw + t * 4 * HEAD_SIZE
            for ref in (new_ref, past_ref):
                for part in (0, KEY_VALUE_HEADS):
                    offset = (part + kv) * HEAD_SIZE
                    copy(ref.at[:, pl.ds(aligned(offset, 128), 128)], out.at[:, at : at + 128])
                    at += 128
    half = halves[0].shape[1]
    for j in range(2):
        copy(w_ref.at[:, j * half : (j + 1) * half], halves[j])
    for c in copies:
        c.wait()


def attend_kernel(C, t, *refs):
    msgs, out, kv_s = refs[:C], refs[C], refs[C + 1]
    c = lax.axis_index("ctx")
    tok, qw = msgs[0].shape[0], out.shape[1]
    rows = C * tok
    q_s = refs[C + 2]
    for s in range(C):
        msg = msgs[s]
        at = aligned(jnp.bitwise_xor(c, s) * tok, tok)
        first = 2 * qw + t * 4 * HEAD_SIZE
        q_s[pl.ds(at, tok), :] = msg[:, t * qw : (t + 1) * qw]
        kv_s[pl.ds(rows + at, tok), :] = msg[:, first : first + 2 * HEAD_SIZE]
        kv_s[pl.ds(at, tok), :] = msg[:, first + 2 * HEAD_SIZE : first + 4 * HEAD_SIZE]
    block = 128
    for b in range(rows // block):
        seen = rows + (b + 1) * block
        k = kv_s[:seen, :HEAD_SIZE]
        v = kv_s[:seen, HEAD_SIZE:]
        row = lax.broadcasted_iota(jnp.int32, (block, seen), 0) + (rows + b * block)
        visible = lax.broadcasted_iota(jnp.int32, (block, seen), 1) <= row
        at = slice(b * block, (b + 1) * block)
        for h in range(qw // HEAD_SIZE):
            q = q_s[at, h * HEAD_SIZE : (h + 1) * HEAD_SIZE]
            scores = lax.dot_general(q, k, (((1,), (1,)), ((), ())), preferred_element_type=F32)
            scores = jnp.where(visible, scores * HEAD_SIZE ** (-0.5), NEG_FILL)
            weights = jnp.exp(scores - jnp.max(scores, axis=1, keepdims=True))
            total = jnp.sum(weights, axis=1, keepdims=True)
            numerator = dot(weights.astype(BF16), v)
            out[at, h * HEAD_SIZE : (h + 1) * HEAD_SIZE] = (numerator / total).astype(BF16)


def route_kernel(E, cap, routes_ref, gates_ref, place_ref, gate_ref):
    e = lax.axis_index("exp")
    rows = routes_ref.shape[0]
    routes = routes_ref[...]
    resident = routes < E
    target = jnp.sum(jnp.where(resident, routes, 0), axis=1, keepdims=True)
    has = jnp.sum(resident.astype(jnp.int32), axis=1, keepdims=True) > 0
    gate = jnp.sum(jnp.where(resident, gates_ref[...], 0.0), axis=1, keepdims=True)
    gate_ref[...] = jnp.broadcast_to(gate, gate_ref.shape)
    lanes = lax.broadcasted_iota(jnp.int32, (rows, 128), 1)
    one_hot = jnp.where((target == lanes) & has, 1.0, 0.0)
    earlier = (
        lax.broadcasted_iota(jnp.int32, (rows, rows), 1)
        < lax.broadcasted_iota(jnp.int32, (rows, rows), 0)
    ).astype(F32).astype(BF16)
    rank = jnp.sum(dot(earlier, one_hot.astype(BF16)) * one_hot, axis=1, keepdims=True)
    slot = jnp.bitwise_xor(target, e) * cap + rank.astype(jnp.int32)
    slot = jnp.where(has, slot, -1)
    places = lax.broadcasted_iota(jnp.int32, (rows, E * cap), 1)
    place_ref[...] = jnp.where(slot == places, 1.0, 0.0).astype(BF16)


def project_kernel(C, with_residual, *refs):
    atts, ws, acc, last, stacked = refs[:C], refs[C : C + 2 * (C - 1)], refs[-3], refs[-2], refs[-1]
    hi, _ = own_hi_lo()
    turn = jnp.bitwise_xor(lax.axis_index("ctx"), hi)
    for s in range(C):
        stacked[jnp.bitwise_xor(turn, s)] = atts[s][...]
    half = acc.shape[1] // 2
    for j in range(2):
        at = slice(j * half, (j + 1) * half)
        total = refs[-4][:, at].astype(F32) if with_residual else None
        for d in range(C - 1):
            w = ws[2 * d + j]
            term = dot(stacked[d], w[...] if w.shape[1] == half else w[:, at])
            total = term if total is None else total + term
        acc[:, at] = total
    last[...] = stacked[C - 1]


def last_kernel(E, cap, *refs):
    accs, lasts, ws, places, (own_ref, full_ref, keep_ref, send_ref) = (
        refs[:2],
        refs[2:4],
        refs[4:6],
        refs[6:8],
        refs[8:],
    )
    half = ws[0].shape[1]
    for j in range(2):
        cols = slice(j * half, (j + 1) * half)
        for t in range(2):
            total = accs[t][:, cols] + dot(lasts[t][...], ws[j][...])
            rounded = total.astype(BF16)
            if t == 0:
                own_ref[:, cols] = total
            else:
                full_ref[:, cols] = rounded
            picked = lax.dot_general(
                places[t][...], rounded, (((0,), (0,)), ((), ())), preferred_element_type=F32
            )
            for d in range(E // 2):
                near, far = spread(d) ^ (PAIR * t), spread(d) ^ PAIR ^ (PAIR * t)
                at = (2 * d + t) * cap
                keep_ref[at : at + cap, cols] = picked[near * cap : (near + 1) * cap]
                at = (2 * d + 1 - t) * cap
                send_ref[at : at + cap, cols] = picked[far * cap : (far + 1) * cap].astype(BF16)


def outgoing_kernel(keep_ref, got_ref, gain_ref, *outs):
    scaled = ((keep_ref[...] + got_ref[...].astype(F32)) * gain_ref[...]).astype(BF16)
    count = outs[0].shape[0]
    for d, out in enumerate(outs):
        out[...] = scaled[d * count : (d + 1) * count]


def gate_up_kernel(C, E, cap, order, *refs):
    xs, gain_ref, w_ref, keep_ref, send_ref, x_s, part_s = refs[: E // 2], *refs[E // 2 :]
    c = lax.axis_index("ctx")
    e = lax.axis_index("exp")
    own_rows = E * cap // C
    wide = w_ref.shape[1]
    for d in range(E // 2):
        for t in range(2):
            at = aligned(jnp.bitwise_xor(e, spread(d) ^ (PAIR * t)) * cap, cap)
            x_s[pl.ds(at, cap), :] = xs[d][t * cap : (t + 1) * cap, :]
    plain = x_s[...].astype(F32) / gain_ref[...]
    square = jnp.sum(plain * plain, axis=1, keepdims=True)
    lane = lax.broadcasted_iota(jnp.int32, (E * cap, 128), 1)
    part_s[:, wide:] = jnp.where(lane == 0, square, 0.0)
    step = 512
    for j in range(wide // step):
        at = slice(j * step, (j + 1) * step)
        part_s[:, at] = dot(x_s[...], w_ref[:, at])
    for i, r in enumerate(order):
        at = aligned(jnp.bitwise_xor(c, r) * own_rows, own_rows)
        block = part_s[pl.ds(at, own_rows), :]
        if i < C // 2:
            keep_ref[i * own_rows : (i + 1) * own_rows, :] = block
        else:
            to = (i - C // 2) * own_rows
            send_ref[to : to + own_rows, :wide] = block[:, :wide].astype(BF16)
            square = block[:, wide:]
            high = square.astype(BF16).astype(F32)
            lane = lax.broadcasted_iota(jnp.int32, square.shape, 1)
            low = pltpu.roll(square - high, 1, 1)
            pair = jnp.where(lane == 1, low, high)
            send_ref[to : to + own_rows, wide:] = pair.astype(BF16)


def halve_kernel(keep_in, got_ref, keep_ref, send_ref):
    rows = keep_ref.shape[0]
    wide = keep_ref.shape[1] - 128
    total = keep_in[...] + got_ref[...].astype(F32)
    keep_ref[...] = total[:rows]
    send_ref[:, :wide] = total[rows:, :wide].astype(BF16)
    square = jnp.sum(total[rows:, wide:], axis=1, keepdims=True)
    high = square.astype(BF16).astype(F32)
    lane = lax.broadcasted_iota(jnp.int32, (rows, 128), 1)
    pair = jnp.where(lane == 0, high, jnp.where(lane == 1, square - high, 0.0))
    send_ref[:, wide:] = pair.astype(BF16)


def activate_kernel(hidden, keep_ref, got_ref, out):
    def summed(at):
        return keep_ref[:, at] + got_ref[:, at].astype(F32)

    square = jnp.sum(summed(slice(2 * hidden, 2 * hidden + 128)), axis=1, keepdims=True)
    scale = lax.rsqrt(square / D + 1e-6)
    gate = summed(slice(0, hidden)) * scale
    up = summed(slice(hidden, 2 * hidden)) * scale
    out[...] = (gate / (1.0 + jnp.exp(-gate)) * up).astype(BF16)


def down_kernel(C, E, cap, *refs):
    acts, w_ref, outs, x_s, part_s = refs[:C], refs[C], refs[C + 1 : C + 1 + E // 2], refs[-2], refs[-1]
    c = lax.axis_index("ctx")
    e = lax.axis_index("exp")
    own_rows = E * cap // C
    for s in range(C):
        at = aligned(jnp.bitwise_xor(c, s) * own_rows, own_rows)
        x_s[pl.ds(at, own_rows), :] = acts[s][...]
    part_s[...] = dot(x_s[...], w_ref[...]).astype(BF16)
    for d in range(E // 2):
        for t in range(2):
            at = aligned(jnp.bitwise_xor(e, spread(d) ^ (PAIR * t)) * cap, cap)
            outs[d][t * cap : (t + 1) * cap, :] = part_s[pl.ds(at, cap), :]


def forward_kernel(cap, *refs):
    for d, x in enumerate(refs[:-1]):
        refs[-1][d * cap : (d + 1) * cap, :] = x[cap:, :]


def combine_kernel(E, cap, own_ref, got_ref, place_ref, gate_ref, *refs):
    xs, far, out, x_s = refs[: E // 2], refs[E // 2], refs[E // 2 + 1], refs[E // 2 + 2]
    for d in range(E // 2):
        at = spread(d) * cap
        x_s[at : at + cap, :] = xs[d][:cap, :]
        at = (spread(d) ^ PAIR) * cap
        x_s[at : at + cap, :] = far[d * cap : (d + 1) * cap, :]
    collected = dot(place_ref[...], x_s[...])
    mixed = own_ref[...] + got_ref[...].astype(F32)
    out[...] = (mixed + gate_ref[:, :1] * collected).astype(BF16)


def body(
    queries,
    new_keys_values,
    cached_keys_values,
    residual,
    out_weight,
    norm_gain,
    routes,
    gates,
    w_gate_up,
    w_down,
):
    C = lax.axis_size("ctx")
    E = lax.axis_size("exp")
    tok = queries.shape[2]
    rows = C * tok
    width = residual.shape[3]
    hidden = w_down.shape[1]
    wide = 2 * hidden
    cap = rows // (2 * E)
    slots = E * cap
    own_rows = slots // C
    qw = QUERY_HEADS // E * HEAD_SIZE

    def permute(x, ctx=0, exp=0):
        pairs = [(c * E + e, (c ^ ctx) * E + (e ^ exp)) for c in range(C) for e in range(E)]
        return lax.ppermute(x, ("ctx", "exp"), pairs)

    def after(x, *others):
        return lax.optimization_barrier((x, *others))[0]

    half = width // 2
    *msgs, half_a, half_b = call(
        functools.partial(pack_kernel, C, qw),
        [sds((tok, 2 * qw + 8 * HEAD_SIZE), BF16)] * C + [sds((qw, half), BF16)] * 2,
        4,
        scratch=[pltpu.SemaphoreType.DMA((10 * C + 2,))],
        in_specs=[HBM] * 4,
        cost=(0, 4 * 2**20),
        limit=57,
    )(
        queries.reshape(tok, queries.shape[3]),
        new_keys_values.reshape(tok, new_keys_values.shape[3]),
        cached_keys_values.reshape(tok, cached_keys_values.shape[3]),
        out_weight,
    )
    got = [msgs[0]] + [permute(msgs[s], ctx=s) for s in range(1, C)]
    shards = {0: [out_weight, out_weight], 1: [None, permute(half_b, exp=1)]}
    for d in range(2, C, 2):
        shards[d] = [permute(half_a, exp=spread(d)), None]
    step = [shards[1][1]] + [shards[d][0] for d in range(2, C, 2)]
    got[0] = after(got[0], *step)
    shards[1][0] = permute(after(half_a, *step), exp=1)
    for d in range(2, C, 2):
        shards[d][1] = permute(after(half_b, *step), exp=spread(d))
    step = [shards[1][0]] + [shards[d][1] for d in range(2, C, 2)]
    for d in range(3, C, 2):
        shards[d] = [
            permute(after(shards[d - 1][0], *step), exp=1),
            permute(after(shards[1][1], *step), exp=spread(d - 1)),
        ]

    def attend(t, msgs):
        return call(
            functools.partial(attend_kernel, C, t),
            sds((rows, qw), BF16),
            C,
            scratch=[pltpu.VMEM((2 * rows, 2 * HEAD_SIZE), BF16), pltpu.VMEM((rows, qw), BF16)],
            cost=(4 * rows * 2 * rows * qw, 8 * 2**20),
            limit=16,
        )(*msgs)

    other = attend(1, got)
    theirs = permute(other, exp=PAIR)
    mine = attend(0, [after(got[0], other)] + got[1:])

    def gather(x, before):
        atts = {0: x, 1: permute(x, ctx=1)}
        for s in range(2, C, 2):
            atts[s] = permute(x, ctx=s)
            atts[s + 1] = permute(after(atts[s], *before), ctx=1)
        return [atts[s] for s in range(C)]

    mine_all = gather(mine, [])
    theirs_all = gather(after(theirs, *step), [])
    place, gate = call(
        functools.partial(route_kernel, E, cap),
        [sds((rows, slots), BF16), sds((rows, 128), F32)],
        2,
        cost=(0, 2**20),
        limit=16,
    )(
        after(routes, mine).reshape(rows, routes.shape[3]),
        after(gates, mine).reshape(rows, gates.shape[3]),
    )
    other_place = permute(place, exp=PAIR)

    def project(atts, *extra):
        return call(
            functools.partial(project_kernel, C, bool(extra)),
            [sds((rows, width), F32), sds((rows, qw), BF16)],
            C + 2 * (C - 1) + len(extra),
            scratch=[pltpu.VMEM((C, rows, qw), BF16)],
            cost=(2 * rows * qw * width * (C - 1), 4 * 2**20),
        )(*atts, *[w for d in range(C - 1) for w in shards[d]], *extra)

    acc, last = project(mine_all, residual.reshape(rows, width))
    acc_far, last_far = project(theirs_all)
    own, full, keep, send = call(
        functools.partial(last_kernel, E, cap),
        [
            sds((rows, width), F32),
            sds((rows, width), BF16),
            sds((slots, width), F32),
            sds((slots, width), BF16),
        ],
        8,
        cost=(4 * rows * (qw + slots) * width, 6 * 2**20),
    )(acc, acc_far, last, last_far, *shards[C - 1], place, other_place)
    gain = norm_gain.reshape(1, width)
    outgoing = call(
        outgoing_kernel,
        [sds((2 * cap, width), BF16)] * (E // 2),
        3,
        cost=(0, 2**20),
    )(keep, permute(send, exp=PAIR), gain)
    incoming = [outgoing[0]] + [permute(outgoing[d], exp=spread(d)) for d in range(1, E // 2)]

    order = [0]
    bit = C // 2
    while bit:
        order = order + [r | bit for r in order]
        bit //= 2
    keep, send = call(
        functools.partial(gate_up_kernel, C, E, cap, order),
        [sds((slots // 2, wide + 128), F32), sds((slots // 2, wide + 128), BF16)],
        E // 2 + 2,
        scratch=[pltpu.VMEM((slots, width), BF16), pltpu.VMEM((slots, wide + 128), F32)],
        cost=(2 * slots * width * wide, 2 * width * wide),
    )(*incoming, gain, w_gate_up.reshape(width, wide))
    arrived = permute(after(full, *incoming), exp=PAIR)
    bit = 1
    while 2 * bit < C:
        count = keep.shape[0] // 2
        keep, send = call(
            halve_kernel,
            [sds((count, wide + 128), F32), sds((count, wide + 128), BF16)],
            2,
            cost=(0, 2**21),
        )(keep, permute(send, ctx=bit))
        bit *= 2
    activated = call(
        functools.partial(activate_kernel, hidden),
        sds((own_rows, hidden), BF16),
        2,
        cost=(0, 2**20),
    )(keep, permute(send, ctx=bit))
    acts = {0: activated}
    while bit:
        for r in list(acts):
            acts[r ^ bit] = permute(acts[r], ctx=bit)
        bit //= 2
    expert_out = call(
        functools.partial(down_kernel, C, E, cap),
        [sds((2 * cap, width), BF16)] * (E // 2),
        C + 1,
        scratch=[pltpu.VMEM((slots, hidden), BF16), pltpu.VMEM((slots, width), BF16)],
        cost=(2 * slots * width * hidden, 2 * width * hidden),
    )(*[acts[s] for s in range(C)], w_down.reshape(hidden, width))
    returned = [expert_out[0]]
    returned += [permute(expert_out[d], exp=spread(d)) for d in range(1, E // 2)]
    far = call(
        functools.partial(forward_kernel, cap), sds((slots // 2, width), BF16), E // 2, cost=(0, 2**19)
    )(*returned)
    result = call(
        functools.partial(combine_kernel, E, cap),
        sds((rows, width), BF16),
        5 + E // 2,
        scratch=[pltpu.VMEM((slots, width), BF16)],
        cost=(0, 2 * 2**20),
    )(own, arrived, place, gate, *returned, permute(far, exp=PAIR))
    return result.reshape(C, 1, tok, width)


def solution(mesh):
    in_specs = (
        P("ctx", "exp", None, None),
        P("ctx", "exp", None, None),
        P("ctx", "exp", None, None),
        P(None, "exp", None, "ctx"),
        P("exp", "ctx"),
        P("ctx"),
        P(None, "exp", None, None),
        P(None, "exp", None, None),
        P("exp", "ctx", None),
        P("exp", None, "ctx"),
    )
    out_specs = P(None, "exp", None, "ctx")
    return jax.shard_map(body, mesh=mesh, in_specs=in_specs, out_specs=out_specs, check_vma=False)
```

```python
import functools

import jax
import jax.numpy as jnp
from jax import lax
from jax.experimental import pallas as pl
from jax.experimental.pallas import tpu as pltpu
from jax.sharding import PartitionSpec as P

D = 4096
QUERY_HEADS = 32
KEY_VALUE_HEADS = 2
HEAD_SIZE = 128
GROUP_EXTENT = QUERY_HEADS // KEY_VALUE_HEADS
NEG_FILL = -1e30
BF16 = jnp.bfloat16
F32 = jnp.float32
VMEM = pl.BlockSpec(memory_space=pltpu.VMEM)
HBM = pl.BlockSpec(memory_space=pltpu.HBM)
ANY = pl.BlockSpec(memory_space=pl.ANY)


def call(kernel, out_shape, n_in, scratch=(), cost=(0, 0), limit=32, **kw):
    kw.setdefault("in_specs", [VMEM] * n_in)
    kw.setdefault("out_specs", jax.tree.map(lambda _: VMEM, out_shape))
    return pl.pallas_call(
        kernel,
        out_shape=out_shape,
        scratch_shapes=list(scratch),
        cost_estimate=pl.CostEstimate(flops=cost[0], bytes_accessed=cost[1], transcendentals=0),
        compiler_params=pltpu.CompilerParams(vmem_limit_bytes=limit * 2**20),
        **kw,
    )


def sds(shape, dtype):
    return jax.ShapeDtypeStruct(shape, dtype)


def dot(a, b):
    return jnp.dot(a, b, preferred_element_type=F32)


PAIR = 4


def spread(d):
    return (d // PAIR) * 2 * PAIR + d % PAIR


def own_hi_lo():
    e = lax.axis_index("exp")
    return lax.div(e, 2 * PAIR) * PAIR + lax.rem(e, PAIR), lax.rem(lax.div(e, PAIR), 2)


def aligned(x, n):
    return pl.multiple_of(x, n)


def pack_kernel(C, qw, q_ref, new_ref, past_ref, w_ref, res_ref, *refs):
    outs, halves, res_out, sems = refs[:C], refs[C : C + 2], refs[C + 2], refs[C + 3]
    c = lax.axis_index("ctx")
    _, lo = own_hi_lo()
    copies = []

    def copy(src, dst):
        copies.append(pltpu.make_async_copy(src, dst, sems.at[len(copies)]))
        copies[-1].start()

    half = halves[0].shape[1]
    kv = new_ref.shape[1]
    for j in (1, 0):
        copy(w_ref.at[:, j * half : (j + 1) * half], halves[j])
    for s in reversed(range(C)):
        target = jnp.bitwise_xor(c, s)
        out = outs[s]
        for t in range(2):
            shard = lax.div(target, PAIR) * 2 * PAIR + lax.rem(target, PAIR)
            shard = shard + PAIR * jnp.bitwise_xor(lo, t)
            copy(q_ref.at[:, pl.ds(aligned(shard * qw, 128), qw)], out.at[:, t * qw : (t + 1) * qw])
        copy(new_ref, out.at[:, 2 * qw : 2 * qw + kv])
        copy(past_ref, out.at[:, 2 * qw + kv :])
    copy(res_ref, res_out)
    for c in copies:
        c.wait()


def attend_kernel(C, t, *refs):
    msgs, out, kv_s = refs[:C], refs[C], refs[C + 1]
    c = lax.axis_index("ctx")
    tok, qw = msgs[0].shape[0], out.shape[1]
    rows = C * tok
    q_s = refs[C + 2]
    _, lo = own_hi_lo()
    shard = lax.div(c, PAIR) * 2 * PAIR + lax.rem(c, PAIR) + PAIR * jnp.bitwise_xor(lo, t)
    head = lax.div(shard * (qw // HEAD_SIZE), GROUP_EXTENT)
    for s in range(C):
        msg = msgs[s]
        at = aligned(jnp.bitwise_xor(c, s) * tok, tok)
        q_s[pl.ds(at, tok), :] = msg[:, t * qw : (t + 1) * qw]
        for i, to in ((0, rows + at), (1, at)):
            for part in range(2):
                first = 2 * qw + (i * 2 + part) * KEY_VALUE_HEADS * HEAD_SIZE
                cols = pl.ds(aligned(first + head * HEAD_SIZE, 128), HEAD_SIZE)
                kv_s[pl.ds(to, tok), part * HEAD_SIZE : (part + 1) * HEAD_SIZE] = msg[:, cols]
    block = 128
    for b in range(rows // block):
        seen = rows + (b + 1) * block
        k = kv_s[:seen, :HEAD_SIZE]
        v = kv_s[:seen, HEAD_SIZE:]
        row = lax.broadcasted_iota(jnp.int32, (block, seen), 0) + (rows + b * block)
        visible = lax.broadcasted_iota(jnp.int32, (block, seen), 1) <= row
        at = slice(b * block, (b + 1) * block)
        for h in range(qw // HEAD_SIZE):
            q = q_s[at, h * HEAD_SIZE : (h + 1) * HEAD_SIZE]
            scores = lax.dot_general(q, k, (((1,), (1,)), ((), ())), preferred_element_type=F32)
            scores = jnp.where(visible, scores * HEAD_SIZE ** (-0.5), NEG_FILL)
            weights = jnp.exp(scores - jnp.max(scores, axis=1, keepdims=True))
            total = jnp.sum(weights, axis=1, keepdims=True)
            numerator = dot(weights.astype(BF16), v)
            out[at, h * HEAD_SIZE : (h + 1) * HEAD_SIZE] = (numerator / total).astype(BF16)


def route_kernel(E, cap, routes_ref, gates_ref, place_ref, gate_ref, line_s, gate_s):
    e = lax.axis_index("exp")
    blocks, _, tok = routes_ref.shape
    rows = blocks * tok
    for i in range(blocks):
        routes = routes_ref[i]
        resident = routes < E
        target = jnp.sum(jnp.where(resident, routes + 1, 0), axis=0, keepdims=True) - 1
        gate = jnp.sum(jnp.where(resident, gates_ref[i], 0.0), axis=0, keepdims=True)
        line_s[:, i * tok : (i + 1) * tok] = jnp.broadcast_to(target, (8, tok))
        gate_s[:, i * tok : (i + 1) * tok] = jnp.broadcast_to(gate, (128, tok))
    target = line_s[:1, :]
    gate_ref[...] = gate_s[...].T
    has = target >= 0
    experts = lax.broadcasted_iota(jnp.int32, (E, rows), 0)
    one_hot = jnp.where(target == experts, 1.0, 0.0)
    earlier = jnp.where(
        lax.broadcasted_iota(jnp.int32, (rows, rows), 0)
        < lax.broadcasted_iota(jnp.int32, (rows, rows), 1),
        1.0,
        0.0,
    ).astype(BF16)
    rank = jnp.sum(dot(one_hot.astype(BF16), earlier) * one_hot, axis=0, keepdims=True)
    slot = jnp.bitwise_xor(target, e) * cap + rank.astype(jnp.int32)
    slot = jnp.where(has, slot, -1)
    places = lax.broadcasted_iota(jnp.int32, (E * cap, rows), 0)
    place_ref[...] = jnp.where(slot == places, 1.0, 0.0).astype(BF16)


def project_kernel(C, with_residual, *refs):
    own_w, refs = refs[:2], refs[2:]
    if with_residual:
        res, refs = refs[0], refs[1:]
    atts, ws, (acc, last, stacked, w_s, res_s, sems) = refs[:C], refs[C : 3 * C - 4], refs[3 * C - 4 :]
    hi, _ = own_hi_lo()
    copies = [pltpu.make_async_copy(own_w[j], w_s.at[j], sems.at[j]) for j in range(2)]
    if with_residual:
        copies.append(pltpu.make_async_copy(res, res_s, sems.at[2]))
    for c in copies:
        c.start()
    turn = jnp.bitwise_xor(lax.axis_index("ctx"), hi)
    for s in range(C):
        stacked[jnp.bitwise_xor(turn, s)] = atts[s][...]
    last[...] = stacked[C - 1]
    half = acc.shape[1] // 2
    for j in range(2):
        at = slice(j * half, (j + 1) * half)
        total = None
        for d in range(1, C - 1):
            term = dot(stacked[d], ws[2 * (d - 1) + j][...])
            total = term if total is None else total + term
        if j == 0:
            for c in copies:
                c.wait()
        total = total + dot(stacked[0], w_s[j])
        if with_residual:
            total = total + res_s[:, at].astype(F32)
        acc[:, at] = total


def last_kernel(E, cap, j, *refs):
    accs, lasts, w_ref, places, (own_ref, full_ref, keep_ref, send_ref) = (
        refs[:2],
        refs[2:4],
        refs[4],
        refs[5:7],
        refs[7:],
    )
    half = w_ref.shape[1]
    cols = slice(j * half, (j + 1) * half)
    for t in (1, 0):
        total = accs[t][:, cols] + dot(lasts[t][...], w_ref[...])
        rounded = total.astype(BF16)
        if t == 0:
            own_ref[...] = total
        else:
            full_ref[...] = rounded
        picked = dot(places[t][...], rounded)
        for d in range(E // 2):
            near, far = spread(d) ^ (PAIR * t), spread(d) ^ PAIR ^ (PAIR * t)
            at = (2 * d + t) * cap
            keep_ref[at : at + cap, :] = picked[near * cap : (near + 1) * cap]
            at = (2 * d + 1 - t) * cap
            send_ref[at : at + cap, :] = picked[far * cap : (far + 1) * cap].astype(BF16)


def outgoing_kernel(j, keep_ref, got_ref, gain_ref, *outs):
    half = keep_ref.shape[1]
    gain = gain_ref[:, j * half : (j + 1) * half]
    scaled = ((keep_ref[...] + got_ref[...].astype(F32)) * gain).astype(BF16)
    count = outs[0].shape[0]
    for d, out in enumerate(outs):
        out[...] = scaled[d * count : (d + 1) * count]


def gate_up_kernel(C, E, cap, order, *refs):
    xs, gain_ref, w_ref, keep_ref, send_ref, x_s, part_s = refs[:E], *refs[E:]
    c = lax.axis_index("ctx")
    e = lax.axis_index("exp")
    own_rows = E * cap // C
    wide = w_ref.shape[1]
    for d in range(E // 2):
        for t in range(2):
            at = aligned(jnp.bitwise_xor(e, spread(d) ^ (PAIR * t)) * cap, cap)
            for j in range(2):
                half = xs[d].shape[1]
                cols = slice(j * half, (j + 1) * half)
                x_s[pl.ds(at, cap), cols] = xs[j * (E // 2) + d][t * cap : (t + 1) * cap, :]
    plain = x_s[...].astype(F32) / gain_ref[...]
    square = jnp.sum(plain * plain, axis=1, keepdims=True)
    lane = lax.broadcasted_iota(jnp.int32, (E * cap, 128), 1)
    part_s[:, wide:] = jnp.where(lane == 0, square, 0.0)
    step = 512
    for j in range(wide // step):
        at = slice(j * step, (j + 1) * step)
        part_s[:, at] = dot(x_s[...], w_ref[:, at])
    for i, r in enumerate(order):
        at = aligned(jnp.bitwise_xor(c, r) * own_rows, own_rows)
        block = part_s[pl.ds(at, own_rows), :]
        if i < C // 2:
            keep_ref[i * own_rows : (i + 1) * own_rows, :] = block
        else:
            to = (i - C // 2) * own_rows
            send_ref[to : to + own_rows, :wide] = block[:, :wide].astype(BF16)
            square = block[:, wide:]
            high = square.astype(BF16).astype(F32)
            lane = lax.broadcasted_iota(jnp.int32, square.shape, 1)
            low = pltpu.roll(square - high, 1, 1)
            pair = jnp.where(lane == 1, low, high)
            send_ref[to : to + own_rows, wide:] = pair.astype(BF16)


def halve_kernel(keep_in, got_ref, keep_ref, send_ref):
    rows = keep_ref.shape[0]
    wide = keep_ref.shape[1] - 128
    total = keep_in[...] + got_ref[...].astype(F32)
    keep_ref[...] = total[:rows]
    send_ref[:, :wide] = total[rows:, :wide].astype(BF16)
    square = jnp.sum(total[rows:, wide:], axis=1, keepdims=True)
    high = square.astype(BF16).astype(F32)
    lane = lax.broadcasted_iota(jnp.int32, (rows, 128), 1)
    pair = jnp.where(lane == 0, high, jnp.where(lane == 1, square - high, 0.0))
    send_ref[:, wide:] = pair.astype(BF16)


def activate_kernel(hidden, keep_ref, got_ref, out):
    def summed(at):
        return keep_ref[:, at] + got_ref[:, at].astype(F32)

    square = jnp.sum(summed(slice(2 * hidden, 2 * hidden + 128)), axis=1, keepdims=True)
    scale = lax.rsqrt(square / D + 1e-6)
    gate = summed(slice(0, hidden)) * scale
    up = summed(slice(hidden, 2 * hidden)) * scale
    out[...] = (gate / (1.0 + jnp.exp(-gate)) * up).astype(BF16)


def down_kernel(C, E, cap, *refs):
    acts, w_ref, outs, x_s, part_s = refs[:C], refs[C], refs[C + 1 : C + 1 + E // 2], refs[-2], refs[-1]
    c = lax.axis_index("ctx")
    e = lax.axis_index("exp")
    own_rows = E * cap // C
    for s in range(C):
        at = aligned(jnp.bitwise_xor(c, s) * own_rows, own_rows)
        x_s[pl.ds(at, own_rows), :] = acts[s][...]
    part_s[...] = dot(x_s[...], w_ref[...]).astype(BF16)
    for d in range(E // 2):
        for t in range(2):
            at = aligned(jnp.bitwise_xor(e, spread(d) ^ (PAIR * t)) * cap, cap)
            outs[d][t * cap : (t + 1) * cap, :] = part_s[pl.ds(at, cap), :]


def forward_kernel(cap, *refs):
    for d, x in enumerate(refs[:-1]):
        refs[-1][d * cap : (d + 1) * cap, :] = x[cap:, :]


def combine_kernel(E, cap, own0, own1, got0, got1, place_ref, gate_ref, *refs):
    xs, far, out, x_s = refs[: E // 2], refs[E // 2], refs[E // 2 + 1], refs[E // 2 + 2]
    for d in range(E // 2):
        at = spread(d) * cap
        x_s[at : at + cap, :] = xs[d][:cap, :]
        at = (spread(d) ^ PAIR) * cap
        x_s[at : at + cap, :] = far[d * cap : (d + 1) * cap, :]
    half = own0.shape[1]
    for j, (own, got) in enumerate(((own0, got0), (own1, got1))):
        cols = slice(j * half, (j + 1) * half)
        collected = lax.dot_general(
            place_ref[...], x_s[:, cols], (((0,), (0,)), ((), ())), preferred_element_type=F32
        )
        mixed = own[...] + got[...].astype(F32)
        out[:, cols] = (mixed + gate_ref[:, :1] * collected).astype(BF16)


def body(
    queries,
    new_keys_values,
    cached_keys_values,
    residual,
    out_weight,
    norm_gain,
    routes,
    gates,
    w_gate_up,
    w_down,
):
    C = lax.axis_size("ctx")
    E = lax.axis_size("exp")
    tok = queries.shape[2]
    rows = C * tok
    width = residual.shape[3]
    hidden = w_down.shape[1]
    wide = 2 * hidden
    cap = rows // (2 * E)
    slots = E * cap
    own_rows = slots // C
    qw = QUERY_HEADS // E * HEAD_SIZE

    def permute(x, ctx=0, exp=0):
        pairs = [(c * E + e, (c ^ ctx) * E + (e ^ exp)) for c in range(C) for e in range(E)]
        return lax.ppermute(x, ("ctx", "exp"), pairs)

    def after(x, *others):
        return lax.optimization_barrier((x, *others))[0]

    half = width // 2
    kv = new_keys_values.shape[3]
    *msgs, half_a, half_b, res = call(
        functools.partial(pack_kernel, C, qw),
        [sds((tok, 2 * qw + 2 * kv), BF16)] * C
        + [sds((qw, half), BF16)] * 2
        + [sds((rows, width), BF16)],
        5,
        scratch=[pltpu.SemaphoreType.DMA((4 * C + 3,))],
        in_specs=[HBM] * 5,
        cost=(0, 4 * 2**20),
        limit=57,
    )(
        queries.reshape(tok, queries.shape[3]),
        new_keys_values.reshape(tok, new_keys_values.shape[3]),
        cached_keys_values.reshape(tok, cached_keys_values.shape[3]),
        out_weight,
        residual.reshape(rows, width),
    )
    got = [msgs[0]] + [permute(msgs[s], ctx=s) for s in range(1, C)]
    shards = {0: [half_a, half_b], 1: [None, permute(half_b, exp=1)]}
    for d in range(2, C, 2):
        shards[d] = [permute(half_a, exp=spread(d)), None]
    step = [shards[1][1]] + [shards[d][0] for d in range(2, C, 2)]
    tokens_last = lambda x: jnp.transpose(x.reshape(C, tok, x.shape[3]), (0, 2, 1))
    place, gate = call(
        functools.partial(route_kernel, E, cap),
        [sds((slots, rows), BF16), sds((rows, 128), F32)],
        2,
        scratch=[pltpu.VMEM((8, rows), jnp.int32), pltpu.VMEM((128, rows), F32)],
        cost=(0, 2**20),
        limit=16,
    )(tokens_last(after(routes, msgs[0])), tokens_last(after(gates, msgs[0])))
    other_place = permute(place, exp=PAIR)
    got[1] = after(got[1], other_place, *step)
    shards[1][0] = permute(after(half_a, *step), exp=1)
    for d in range(2, C, 2):
        shards[d][1] = permute(after(half_b, *step), exp=spread(d))
    step = [shards[1][0]] + [shards[d][1] for d in range(2, C, 2)]
    for d in range(3, C, 2):
        shards[d] = [
            permute(after(shards[d - 1][0], *step), exp=1),
            permute(after(shards[1][1], *step), exp=spread(d - 1)),
        ]

    def attend(t, msgs):
        return call(
            functools.partial(attend_kernel, C, t),
            sds((rows, qw), BF16),
            C,
            scratch=[pltpu.VMEM((2 * rows, 2 * HEAD_SIZE), BF16), pltpu.VMEM((rows, qw), BF16)],
            cost=(4 * rows * 2 * rows * qw, 8 * 2**20),
            limit=16,
        )(*msgs)

    other = attend(1, got)
    theirs = permute(other, exp=PAIR)
    mine = attend(0, [got[0], after(got[1], other)] + got[2:])

    def gather(x, before):
        atts = {0: x, 1: permute(x, ctx=1)}
        for s in range(2, C, 2):
            atts[s] = permute(x, ctx=s)
            atts[s + 1] = permute(after(atts[s], *before), ctx=1)
        return [atts[s] for s in range(C)]

    mine_all = gather(after(mine, *step), [])
    theirs_all = gather(after(theirs, mine), [])

    def project(atts, *extra):
        operands = [*shards[0], *extra, *atts]
        operands += [w for d in range(1, C - 1) for w in shards[d]]
        return call(
            functools.partial(project_kernel, C, bool(extra)),
            [sds((rows, width), F32), sds((rows, qw), BF16)],
            len(operands),
            scratch=[
                pltpu.VMEM((C, rows, qw), BF16),
                pltpu.VMEM((2, qw, half), BF16),
                pltpu.VMEM((rows, width), BF16),
                pltpu.SemaphoreType.DMA((3,)),
            ],
            in_specs=[ANY] * (2 + len(extra)) + [VMEM] * (len(operands) - 2 - len(extra)),
            cost=(2 * rows * qw * width * (C - 1), 4 * 2**20),
        )(*operands)

    acc, last = project(mine_all, res)
    acc_far, last_far = project(theirs_all)
    gain = norm_gain.reshape(1, width)
    own, full, outgoing, incoming = [], [], [], []
    for j in range(2):
        mine_j, full_j, keep, send = call(
            functools.partial(last_kernel, E, cap, j),
            [
                sds((rows, half), F32),
                sds((rows, half), BF16),
                sds((slots, half), F32),
                sds((slots, half), BF16),
            ],
            7,
            cost=(4 * rows * (qw + slots) * half, 3 * 2**20),
        )(acc, acc_far, last, last_far, shards[C - 1][j], place, other_place)
        own.append(mine_j)
        full.append(full_j)
        rows_out = call(
            functools.partial(outgoing_kernel, j),
            [sds((2 * cap, half), BF16)] * (E // 2),
            3,
            cost=(0, 2**20),
        )(keep, after(permute(send, exp=PAIR), *incoming), gain)
        came = {0: rows_out[0]}
        for d in reversed(range(1, E // 2)):
            came[d] = permute(rows_out[d], exp=spread(d))
        incoming += [came[d] for d in range(E // 2)]
    arrived = [permute(after(full[0], incoming[E // 2 + 1]), exp=PAIR)]

    order = [0]
    bit = C // 2
    while bit:
        order = order + [r | bit for r in order]
        bit //= 2
    keep, send = call(
        functools.partial(gate_up_kernel, C, E, cap, order),
        [sds((slots // 2, wide + 128), F32), sds((slots // 2, wide + 128), BF16)],
        E + 2,
        scratch=[pltpu.VMEM((slots, width), BF16), pltpu.VMEM((slots, wide + 128), F32)],
        cost=(2 * slots * width * wide, 2 * width * wide),
    )(*incoming, gain, w_gate_up.reshape(width, wide))
    arrived.append(permute(after(full[1], keep), exp=PAIR))
    bit = 1
    while 2 * bit < C:
        count = keep.shape[0] // 2
        keep, send = call(
            halve_kernel,
            [sds((count, wide + 128), F32), sds((count, wide + 128), BF16)],
            2,
            cost=(0, 2**21),
        )(keep, permute(send, ctx=bit))
        bit *= 2
    activated = call(
        functools.partial(activate_kernel, hidden),
        sds((own_rows, hidden), BF16),
        2,
        cost=(0, 2**20),
    )(after(keep, arrived[0]), permute(send, ctx=bit))
    acts = {0: activated}
    while bit:
        for r in list(acts):
            acts[r ^ bit] = permute(acts[r], ctx=bit)
        bit //= 2
    expert_out = call(
        functools.partial(down_kernel, C, E, cap),
        [sds((2 * cap, width), BF16)] * (E // 2),
        C + 1,
        scratch=[pltpu.VMEM((slots, hidden), BF16), pltpu.VMEM((slots, width), BF16)],
        cost=(2 * slots * width * hidden, 2 * width * hidden),
    )(after(acts[0], arrived[1]), *[acts[s] for s in range(1, C)], w_down.reshape(hidden, width))
    returned = [expert_out[0]]
    returned += [permute(expert_out[d], exp=spread(d)) for d in reversed(range(1, E // 2))][::-1]
    far = call(
        functools.partial(forward_kernel, cap), sds((slots // 2, width), BF16), E // 2, cost=(0, 2**19)
    )(*returned)
    result = call(
        functools.partial(combine_kernel, E, cap),
        sds((rows, width), BF16),
        7 + E // 2,
        scratch=[pltpu.VMEM((slots, width), BF16)],
        cost=(0, 2 * 2**20),
    )(*own, *arrived, place, gate, *returned, permute(far, exp=PAIR))
    return result.reshape(C, 1, tok, width)


def solution(mesh):
    in_specs = (
        P("ctx", "exp", None, None),
        P("ctx", "exp", None, None),
        P("ctx", "exp", None, None),
        P(None, "exp", None, "ctx"),
        P("exp", "ctx"),
        P("ctx"),
        P(None, "exp", None, None),
        P(None, "exp", None, None),
        P("exp", "ctx", None),
        P("exp", None, "ctx"),
    )
    out_specs = P(None, "exp", None, "ctx")
    return jax.shard_map(body, mesh=mesh, in_specs=in_specs, out_specs=out_specs, check_vma=False)
```

```python
import functools

import jax
import jax.numpy as jnp
from jax import lax
from jax.experimental import pallas as pl
from jax.experimental.pallas import tpu as pltpu
from jax.sharding import PartitionSpec as P

D = 4096
QUERY_HEADS = 32
KEY_VALUE_HEADS = 2
HEAD_SIZE = 128
GROUP_EXTENT = QUERY_HEADS // KEY_VALUE_HEADS
NEG_FILL = -1e30
BF16 = jnp.bfloat16
F32 = jnp.float32
VMEM = pl.BlockSpec(memory_space=pltpu.VMEM)
HBM = pl.BlockSpec(memory_space=pltpu.HBM)
ANY = pl.BlockSpec(memory_space=pl.ANY)


def call(kernel, out_shape, n_in, scratch=(), cost=(0, 0), limit=32, **kw):
    kw.setdefault("in_specs", [VMEM] * n_in)
    kw.setdefault("out_specs", jax.tree.map(lambda _: VMEM, out_shape))
    return pl.pallas_call(
        kernel,
        out_shape=out_shape,
        scratch_shapes=list(scratch),
        cost_estimate=pl.CostEstimate(flops=cost[0], bytes_accessed=cost[1], transcendentals=0),
        compiler_params=pltpu.CompilerParams(vmem_limit_bytes=limit * 2**20),
        **kw,
    )


def sds(shape, dtype):
    return jax.ShapeDtypeStruct(shape, dtype)


def dot(a, b):
    return jnp.dot(a, b, preferred_element_type=F32)


PAIR = 4


def spread(d):
    return (d // PAIR) * 2 * PAIR + d % PAIR


def own_hi_lo():
    e = lax.axis_index("exp")
    return lax.div(e, 2 * PAIR) * PAIR + lax.rem(e, PAIR), lax.rem(lax.div(e, PAIR), 2)


def aligned(x, n):
    return pl.multiple_of(x, n)


def pack_kernel(C, qw, q_ref, new_ref, past_ref, w_ref, res_ref, *refs):
    outs, halves, res_out, sems = refs[:C], refs[C : C + 2], refs[C + 2], refs[C + 3]
    c = lax.axis_index("ctx")
    _, lo = own_hi_lo()
    copies = []

    def copy(src, dst):
        copies.append(pltpu.make_async_copy(src, dst, sems.at[len(copies)]))
        copies[-1].start()

    half = halves[0].shape[1]
    kv = new_ref.shape[1]
    for j in (1, 0):
        copy(w_ref.at[:, j * half : (j + 1) * half], halves[j])
    for s in reversed(range(C)):
        target = jnp.bitwise_xor(c, s)
        out = outs[s]
        for t in range(2):
            shard = lax.div(target, PAIR) * 2 * PAIR + lax.rem(target, PAIR)
            shard = shard + PAIR * jnp.bitwise_xor(lo, t)
            copy(q_ref.at[:, pl.ds(aligned(shard * qw, 128), qw)], out.at[:, t * qw : (t + 1) * qw])
        copy(new_ref, out.at[:, 2 * qw : 2 * qw + kv])
        copy(past_ref, out.at[:, 2 * qw + kv :])
    copy(res_ref, res_out)
    for c in copies:
        c.wait()


def attend_kernel(C, t, *refs):
    msgs, out, kv_s = refs[:C], refs[C], refs[C + 1]
    c = lax.axis_index("ctx")
    tok, qw = msgs[0].shape[0], out.shape[1]
    rows = C * tok
    q_s = refs[C + 2]
    _, lo = own_hi_lo()
    shard = lax.div(c, PAIR) * 2 * PAIR + lax.rem(c, PAIR) + PAIR * jnp.bitwise_xor(lo, t)
    head = lax.div(shard * (qw // HEAD_SIZE), GROUP_EXTENT)
    for s in range(C):
        msg = msgs[s]
        at = aligned(jnp.bitwise_xor(c, s) * tok, tok)
        q_s[pl.ds(at, tok), :] = msg[:, t * qw : (t + 1) * qw]
        for i, to in ((0, rows + at), (1, at)):
            for part in range(2):
                first = 2 * qw + (i * 2 + part) * KEY_VALUE_HEADS * HEAD_SIZE
                cols = pl.ds(aligned(first + head * HEAD_SIZE, 128), HEAD_SIZE)
                kv_s[pl.ds(to, tok), part * HEAD_SIZE : (part + 1) * HEAD_SIZE] = msg[:, cols]
    block = 128
    for b in range(rows // block):
        seen = rows + (b + 1) * block
        k = kv_s[:seen, :HEAD_SIZE]
        v = kv_s[:seen, HEAD_SIZE:]
        row = lax.broadcasted_iota(jnp.int32, (block, seen), 0) + (rows + b * block)
        visible = lax.broadcasted_iota(jnp.int32, (block, seen), 1) <= row
        at = slice(b * block, (b + 1) * block)
        for h in range(qw // HEAD_SIZE):
            q = q_s[at, h * HEAD_SIZE : (h + 1) * HEAD_SIZE]
            scores = lax.dot_general(q, k, (((1,), (1,)), ((), ())), preferred_element_type=F32)
            scores = jnp.where(visible, scores * HEAD_SIZE ** (-0.5), NEG_FILL)
            weights = jnp.exp(scores - jnp.max(scores, axis=1, keepdims=True))
            total = jnp.sum(weights, axis=1, keepdims=True)
            numerator = dot(weights.astype(BF16), v)
            out[at, h * HEAD_SIZE : (h + 1) * HEAD_SIZE] = (numerator / total).astype(BF16)


def route_kernel(E, cap, routes_ref, gates_ref, place_ref, gate_ref, line_s, gate_s):
    e = lax.axis_index("exp")
    blocks, _, tok = routes_ref.shape
    rows = blocks * tok
    for i in range(blocks):
        routes = routes_ref[i]
        resident = routes < E
        target = jnp.sum(jnp.where(resident, routes + 1, 0), axis=0, keepdims=True) - 1
        gate = jnp.sum(jnp.where(resident, gates_ref[i], 0.0), axis=0, keepdims=True)
        line_s[:, i * tok : (i + 1) * tok] = jnp.broadcast_to(target, (8, tok))
        gate_s[:, i * tok : (i + 1) * tok] = jnp.broadcast_to(gate, (128, tok))
    target = line_s[:1, :]
    gate_ref[...] = gate_s[...].T
    has = target >= 0
    experts = lax.broadcasted_iota(jnp.int32, (E, rows), 0)
    one_hot = jnp.where(target == experts, 1.0, 0.0)
    earlier = jnp.where(
        lax.broadcasted_iota(jnp.int32, (rows, rows), 0)
        < lax.broadcasted_iota(jnp.int32, (rows, rows), 1),
        1.0,
        0.0,
    ).astype(BF16)
    rank = jnp.sum(dot(one_hot.astype(BF16), earlier) * one_hot, axis=0, keepdims=True)
    slot = jnp.bitwise_xor(target, e) * cap + rank.astype(jnp.int32)
    slot = jnp.where(has, slot, -1)
    places = lax.broadcasted_iota(jnp.int32, (E * cap, rows), 0)
    place_ref[...] = jnp.where(slot == places, 1.0, 0.0).astype(BF16)


def project_kernel(C, with_residual, *refs):
    own_w, refs = refs[:2], refs[2:]
    if with_residual:
        res, refs = refs[0], refs[1:]
    atts, ws, (acc, last, stacked, w_s, res_s, sems) = refs[:C], refs[C : 3 * C - 4], refs[3 * C - 4 :]
    hi, _ = own_hi_lo()
    copies = [pltpu.make_async_copy(own_w[j], w_s.at[j], sems.at[j]) for j in range(2)]
    if with_residual:
        copies.append(pltpu.make_async_copy(res, res_s, sems.at[2]))
    for c in copies:
        c.start()
    turn = jnp.bitwise_xor(lax.axis_index("ctx"), hi)
    for s in range(C):
        stacked[jnp.bitwise_xor(turn, s)] = atts[s][...]
    last[...] = stacked[C - 1]
    half = acc.shape[1] // 2
    for j in range(2):
        at = slice(j * half, (j + 1) * half)
        total = None
        for d in range(1, C - 1):
            term = dot(stacked[d], ws[2 * (d - 1) + j][...])
            total = term if total is None else total + term
        if j == 0:
            for c in copies:
                c.wait()
        total = total + dot(stacked[0], w_s[j])
        if with_residual:
            total = total + res_s[:, at].astype(F32)
        acc[:, at] = total


def last_kernel(E, cap, *refs):
    accs, lasts, ws, places = refs[:2], refs[2:4], refs[4:6], refs[6:8]
    own_ref, *full_refs, keep_ref, send_ref = refs[8:]
    half = ws[0].shape[1]
    for j in range(2):
        cols = slice(j * half, (j + 1) * half)
        for t in (1, 0):
            total = accs[t][:, cols] + dot(lasts[t][...], ws[j][...])
            rounded = total.astype(BF16)
            if t == 0:
                own_ref[:, cols] = total
            else:
                first = 0
                for full in full_refs:
                    full[:, cols] = rounded[first : first + full.shape[0]]
                    first += full.shape[0]
            picked = dot(places[t][...], rounded)
            for d in range(E // 2):
                near, far = spread(d) ^ (PAIR * t), spread(d) ^ PAIR ^ (PAIR * t)
                at = (2 * d + t) * cap
                keep_ref[at : at + cap, cols] = picked[near * cap : (near + 1) * cap]
                at = (2 * d + 1 - t) * cap
                send_ref[at : at + cap, cols] = picked[far * cap : (far + 1) * cap].astype(BF16)


def outgoing_kernel(keep_ref, got_ref, gain_ref, *outs):
    scaled = ((keep_ref[...] + got_ref[...].astype(F32)) * gain_ref[...]).astype(BF16)
    count = outs[0].shape[0]
    for d, out in enumerate(outs):
        out[...] = scaled[d * count : (d + 1) * count]


def gate_up_kernel(C, E, cap, order, *refs):
    xs, gain_ref, w_ref, keep_ref, send_ref, x_s, part_s = refs[: E // 2], *refs[E // 2 :]
    c = lax.axis_index("ctx")
    e = lax.axis_index("exp")
    own_rows = E * cap // C
    wide = w_ref.shape[1]
    for d in range(E // 2):
        for t in range(2):
            at = aligned(jnp.bitwise_xor(e, spread(d) ^ (PAIR * t)) * cap, cap)
            x_s[pl.ds(at, cap), :] = xs[d][t * cap : (t + 1) * cap, :]
    plain = x_s[...].astype(F32) / gain_ref[...]
    square = jnp.sum(plain * plain, axis=1, keepdims=True)
    lane = lax.broadcasted_iota(jnp.int32, (E * cap, 128), 1)
    part_s[:, wide:] = jnp.where(lane == 0, square, 0.0)
    step = 512
    for j in range(wide // step):
        at = slice(j * step, (j + 1) * step)
        part_s[:, at] = dot(x_s[...], w_ref[:, at])
    for i, r in enumerate(order):
        at = aligned(jnp.bitwise_xor(c, r) * own_rows, own_rows)
        block = part_s[pl.ds(at, own_rows), :]
        if i < C // 2:
            keep_ref[i * own_rows : (i + 1) * own_rows, :] = block
        else:
            to = (i - C // 2) * own_rows
            send_ref[to : to + own_rows, :wide] = block[:, :wide].astype(BF16)
            square = block[:, wide:]
            high = square.astype(BF16).astype(F32)
            lane = lax.broadcasted_iota(jnp.int32, square.shape, 1)
            low = pltpu.roll(square - high, 1, 1)
            pair = jnp.where(lane == 1, low, high)
            send_ref[to : to + own_rows, wide:] = pair.astype(BF16)


def halve_kernel(keep_in, got_ref, keep_ref, send_ref):
    rows = keep_ref.shape[0]
    wide = keep_ref.shape[1] - 128
    total = keep_in[...] + got_ref[...].astype(F32)
    keep_ref[...] = total[:rows]
    send_ref[:, :wide] = total[rows:, :wide].astype(BF16)
    square = jnp.sum(total[rows:, wide:], axis=1, keepdims=True)
    high = square.astype(BF16).astype(F32)
    lane = lax.broadcasted_iota(jnp.int32, (rows, 128), 1)
    pair = jnp.where(lane == 0, high, jnp.where(lane == 1, square - high, 0.0))
    send_ref[:, wide:] = pair.astype(BF16)


def activate_kernel(hidden, keep_ref, got_ref, out):
    def summed(at):
        return keep_ref[:, at] + got_ref[:, at].astype(F32)

    square = jnp.sum(summed(slice(2 * hidden, 2 * hidden + 128)), axis=1, keepdims=True)
    scale = lax.rsqrt(square / D + 1e-6)
    gate = summed(slice(0, hidden)) * scale
    up = summed(slice(hidden, 2 * hidden)) * scale
    out[...] = (gate / (1.0 + jnp.exp(-gate)) * up).astype(BF16)


def down_kernel(C, E, cap, *refs):
    acts, w_ref, outs, x_s, part_s = refs[:C], refs[C], refs[C + 1 : C + 1 + E // 2], refs[-2], refs[-1]
    c = lax.axis_index("ctx")
    e = lax.axis_index("exp")
    own_rows = E * cap // C
    for s in range(C):
        at = aligned(jnp.bitwise_xor(c, s) * own_rows, own_rows)
        x_s[pl.ds(at, own_rows), :] = acts[s][...]
    part_s[...] = dot(x_s[...], w_ref[...]).astype(BF16)
    for d in range(E // 2):
        for t in range(2):
            at = aligned(jnp.bitwise_xor(e, spread(d) ^ (PAIR * t)) * cap, cap)
            outs[d][t * cap : (t + 1) * cap, :] = part_s[pl.ds(at, cap), :]


def forward_kernel(cap, *refs):
    for d, x in enumerate(refs[:-1]):
        refs[-1][d * cap : (d + 1) * cap, :] = x[cap:, :]


def combine_kernel(E, cap, own, got0, got1, got2, place_ref, gate_ref, *refs):
    xs, far, out, x_s = refs[: E // 2], refs[E // 2], refs[E // 2 + 1], refs[E // 2 + 2]
    for d in range(E // 2):
        at = spread(d) * cap
        x_s[at : at + cap, :] = xs[d][:cap, :]
        at = (spread(d) ^ PAIR) * cap
        x_s[at : at + cap, :] = far[d * cap : (d + 1) * cap, :]
    half = own.shape[1] // 2
    for j in range(2):
        cols = slice(j * half, (j + 1) * half)
        collected = lax.dot_general(
            place_ref[...], x_s[:, cols], (((0,), (0,)), ((), ())), preferred_element_type=F32
        )
        first = 0
        for got in (got0, got1, got2):
            at = slice(first, first + got.shape[0])
            first += got.shape[0]
            mixed = own[at, cols] + got[:, cols].astype(F32)
            out[at, cols] = (mixed + gate_ref[at, :1] * collected[at]).astype(BF16)


def body(
    queries,
    new_keys_values,
    cached_keys_values,
    residual,
    out_weight,
    norm_gain,
    routes,
    gates,
    w_gate_up,
    w_down,
):
    C = lax.axis_size("ctx")
    E = lax.axis_size("exp")
    tok = queries.shape[2]
    rows = C * tok
    width = residual.shape[3]
    hidden = w_down.shape[1]
    wide = 2 * hidden
    cap = rows // (2 * E)
    slots = E * cap
    own_rows = slots // C
    qw = QUERY_HEADS // E * HEAD_SIZE

    def permute(x, ctx=0, exp=0):
        pairs = [(c * E + e, (c ^ ctx) * E + (e ^ exp)) for c in range(C) for e in range(E)]
        return lax.ppermute(x, ("ctx", "exp"), pairs)

    def after(x, *others):
        return lax.optimization_barrier((x, *others))[0]

    half = width // 2
    kv = new_keys_values.shape[3]
    *msgs, half_a, half_b, res = call(
        functools.partial(pack_kernel, C, qw),
        [sds((tok, 2 * qw + 2 * kv), BF16)] * C
        + [sds((qw, half), BF16)] * 2
        + [sds((rows, width), BF16)],
        5,
        scratch=[pltpu.SemaphoreType.DMA((4 * C + 3,))],
        in_specs=[HBM] * 5,
        cost=(0, 4 * 2**20),
        limit=57,
    )(
        queries.reshape(tok, queries.shape[3]),
        new_keys_values.reshape(tok, new_keys_values.shape[3]),
        cached_keys_values.reshape(tok, cached_keys_values.shape[3]),
        out_weight,
        residual.reshape(rows, width),
    )
    got = [msgs[0]] + [permute(msgs[s], ctx=s) for s in range(1, C)]
    shards = {0: [half_a, half_b], 1: [None, permute(half_b, exp=1)]}
    for d in range(2, C, 2):
        shards[d] = [permute(half_a, exp=spread(d)), None]
    step = [shards[1][1]] + [shards[d][0] for d in range(2, C, 2)]
    got[1] = after(got[1], *step)
    shards[1][0] = permute(after(half_a, *step), exp=1)
    for d in range(2, C, 2):
        shards[d][1] = permute(after(half_b, *step), exp=spread(d))
    step = [shards[1][0]] + [shards[d][1] for d in range(2, C, 2)]
    for d in range(3, C, 2):
        shards[d] = [
            permute(after(shards[d - 1][0], *step), exp=1),
            permute(after(shards[1][1], *step), exp=spread(d - 1)),
        ]

    def attend(t, msgs):
        return call(
            functools.partial(attend_kernel, C, t),
            sds((rows, qw), BF16),
            C,
            scratch=[pltpu.VMEM((2 * rows, 2 * HEAD_SIZE), BF16), pltpu.VMEM((rows, qw), BF16)],
            cost=(0, 2**14),
            limit=16,
        )(*msgs)

    other = attend(1, got)
    theirs = permute(other, exp=PAIR)
    mine = attend(0, [got[0], after(got[1], other)] + got[2:])

    def gather(x, before):
        atts = {0: x, 1: permute(x, ctx=1)}
        for s in range(2, C, 2):
            atts[s] = permute(x, ctx=s)
            atts[s + 1] = permute(after(atts[s], *before), ctx=1)
        return [atts[s] for s in range(C)]

    tokens_last = lambda x: jnp.transpose(x.reshape(C, tok, x.shape[3]), (0, 2, 1))
    place, gate = call(
        functools.partial(route_kernel, E, cap),
        [sds((slots, rows), BF16), sds((rows, 128), F32)],
        2,
        scratch=[pltpu.VMEM((8, rows), jnp.int32), pltpu.VMEM((128, rows), F32)],
        cost=(0, 2**20),
        limit=16,
    )(tokens_last(after(routes, other)), tokens_last(after(gates, other)))
    other_place = permute(after(place, theirs), exp=PAIR)
    mine_all = gather(mine, [])
    theirs_all = gather(after(theirs, mine, *step), [])

    def project(atts, *extra):
        operands = [*shards[0], *extra, *atts]
        operands += [w for d in range(1, C - 1) for w in shards[d]]
        return call(
            functools.partial(project_kernel, C, bool(extra)),
            [sds((rows, width), F32), sds((rows, qw), BF16)],
            len(operands),
            scratch=[
                pltpu.VMEM((C, rows, qw), BF16),
                pltpu.VMEM((2, qw, half), BF16),
                pltpu.VMEM((rows, width), BF16),
                pltpu.SemaphoreType.DMA((3,)),
            ],
            in_specs=[ANY] * (2 + len(extra)) + [VMEM] * (len(operands) - 2 - len(extra)),
            cost=(0, 2**14),
        )(*operands)

    acc, last = project(mine_all, res)
    acc_far, last_far = project(theirs_all)
    gain = norm_gain.reshape(1, width)
    parts = (rows // 4, rows // 8, rows * 5 // 8)
    own, *full, keep, send = call(
        functools.partial(last_kernel, E, cap),
        [
            sds((rows, width), F32),
            *[sds((n, width), BF16) for n in parts],
            sds((slots, width), F32),
            sds((slots, width), BF16),
        ],
        8,
        cost=(4 * rows * (qw + slots) * width, 2**20),
    )(acc, acc_far, last, last_far, *shards[C - 1], place, other_place)
    received = permute(send, exp=PAIR)
    outgoing = call(
        outgoing_kernel, [sds((2 * cap, width), BF16)] * (E // 2), 3, cost=(0, 2**20)
    )(keep, received, gain)
    incoming = {0: outgoing[0]}
    for d in reversed(range(1, E // 2)):
        incoming[d] = permute(outgoing[d], exp=spread(d))
    incoming = [incoming[d] for d in range(E // 2)]
    arrived = [permute(after(full[0], received), exp=PAIR)]
    incoming[0] = after(incoming[0], arrived[0])
    arrived.append(permute(after(full[1], arrived[0]), exp=PAIR))
    arrived.append(permute(after(full[2], arrived[1]), exp=PAIR))

    order = [0]
    bit = C // 2
    while bit:
        order = order + [r | bit for r in order]
        bit //= 2
    keep, send = call(
        functools.partial(gate_up_kernel, C, E, cap, order),
        [sds((slots // 2, wide + 128), F32), sds((slots // 2, wide + 128), BF16)],
        E // 2 + 2,
        scratch=[pltpu.VMEM((slots, width), BF16), pltpu.VMEM((slots, wide + 128), F32)],
        cost=(2 * slots * width * wide, 2 * width * wide),
    )(*incoming, gain, w_gate_up.reshape(width, wide))
    keep = after(keep, arrived[1])
    bit = 1
    while 2 * bit < C:
        count = keep.shape[0] // 2
        keep, send = call(
            halve_kernel,
            [sds((count, wide + 128), F32), sds((count, wide + 128), BF16)],
            2,
            cost=(0, 2**21),
        )(keep, permute(send, ctx=bit))
        bit *= 2
    activated = call(
        functools.partial(activate_kernel, hidden),
        sds((own_rows, hidden), BF16),
        2,
        cost=(0, 2**20),
    )(keep, permute(send, ctx=bit))
    acts = {0: activated}
    while bit:
        for r in list(acts):
            acts[r ^ bit] = permute(acts[r], ctx=bit)
        bit //= 2
    expert_out = call(
        functools.partial(down_kernel, C, E, cap),
        [sds((2 * cap, width), BF16)] * (E // 2),
        C + 1,
        scratch=[pltpu.VMEM((slots, hidden), BF16), pltpu.VMEM((slots, width), BF16)],
        cost=(2 * slots * width * hidden, 2 * width * hidden),
    )(after(acts[0], arrived[2]), *[acts[s] for s in range(1, C)], w_down.reshape(hidden, width))
    returned = [expert_out[0]]
    returned += [permute(expert_out[d], exp=spread(d)) for d in reversed(range(1, E // 2))][::-1]
    far = call(
        functools.partial(forward_kernel, cap), sds((slots // 2, width), BF16), E // 2, cost=(0, 2**19)
    )(*returned)
    result = call(
        functools.partial(combine_kernel, E, cap),
        sds((rows, width), BF16),
        7 + E // 2,
        scratch=[pltpu.VMEM((slots, width), BF16)],
        cost=(0, 2 * 2**20),
    )(own, *arrived, place, gate, *returned, permute(far, exp=PAIR))
    return result.reshape(C, 1, tok, width)


def solution(mesh):
    in_specs = (
        P("ctx", "exp", None, None),
        P("ctx", "exp", None, None),
        P("ctx", "exp", None, None),
        P(None, "exp", None, "ctx"),
        P("exp", "ctx"),
        P("ctx"),
        P(None, "exp", None, None),
        P(None, "exp", None, None),
        P("exp", "ctx", None),
        P("exp", None, "ctx"),
    )
    out_specs = P(None, "exp", None, "ctx")
    return jax.shard_map(body, mesh=mesh, in_specs=in_specs, out_specs=out_specs, check_vma=False)
```

```python
import functools

import jax
import jax.numpy as jnp
from jax import lax
from jax.experimental import pallas as pl
from jax.experimental.pallas import tpu as pltpu
from jax.sharding import PartitionSpec as P

D = 4096
QUERY_HEADS = 32
KEY_VALUE_HEADS = 2
HEAD_SIZE = 128
GROUP_EXTENT = QUERY_HEADS // KEY_VALUE_HEADS
NEG_FILL = -1e30
BF16 = jnp.bfloat16
F32 = jnp.float32
VMEM = pl.BlockSpec(memory_space=pltpu.VMEM)
HBM = pl.BlockSpec(memory_space=pltpu.HBM)
ANY = pl.BlockSpec(memory_space=pl.ANY)


def call(kernel, out_shape, n_in, scratch=(), cost=(0, 0), limit=32, **kw):
    kw.setdefault("in_specs", [VMEM] * n_in)
    kw.setdefault("out_specs", jax.tree.map(lambda _: VMEM, out_shape))
    return pl.pallas_call(
        kernel,
        out_shape=out_shape,
        scratch_shapes=list(scratch),
        cost_estimate=pl.CostEstimate(flops=cost[0], bytes_accessed=cost[1], transcendentals=0),
        compiler_params=pltpu.CompilerParams(vmem_limit_bytes=limit * 2**20),
        **kw,
    )


def sds(shape, dtype):
    return jax.ShapeDtypeStruct(shape, dtype)


def dot(a, b):
    return jnp.dot(a, b, preferred_element_type=F32)


PAIR = 4
PACK_LIMIT = 57


def spread(d):
    return (d // PAIR) * 2 * PAIR + d % PAIR


def own_hi_lo():
    e = lax.axis_index("exp")
    return lax.div(e, 2 * PAIR) * PAIR + lax.rem(e, PAIR), lax.rem(lax.div(e, PAIR), 2)


def aligned(x, n):
    return pl.multiple_of(x, n)


def run_copies(pairs, sems):
    copies = [pltpu.make_async_copy(src, dst, sems.at[i]) for i, (src, dst) in enumerate(pairs)]
    for c in copies:
        c.start()
    for c in copies:
        c.wait()


def pack_kernel(C, qw, q_ref, new_ref, past_ref, *refs):
    outs, sems = refs[:C], refs[C]
    c = lax.axis_index("ctx")
    _, lo = own_hi_lo()
    kv = new_ref.shape[1]
    pairs = []
    for s in reversed(range(C)):
        target = jnp.bitwise_xor(c, s)
        out = outs[s]
        for t in range(2):
            shard = lax.div(target, PAIR) * 2 * PAIR + lax.rem(target, PAIR)
            shard = shard + PAIR * jnp.bitwise_xor(lo, t)
            at = pl.ds(aligned(shard * qw, 128), qw)
            pairs.append((q_ref.at[:, at], out.at[:, t * qw : (t + 1) * qw]))
        pairs.append((new_ref, out.at[:, 2 * qw : 2 * qw + kv]))
        pairs.append((past_ref, out.at[:, 2 * qw + kv :]))
    run_copies(pairs, sems)


def halve_weight_kernel(w_ref, a_ref, b_ref, sems):
    half = a_ref.shape[1]
    run_copies([(w_ref.at[:, half:], b_ref), (w_ref.at[:, :half], a_ref)], sems)


def attend_kernel(C, t, *refs):
    msgs, out, kv_s, q_s = refs[:C], refs[C], refs[-2], refs[-1]
    if t == 1:
        refs[C + 1][...] = msgs[0][...]
    c = lax.axis_index("ctx")
    tok, qw = msgs[0].shape[0], out.shape[1]
    rows = C * tok
    _, lo = own_hi_lo()
    shard = lax.div(c, PAIR) * 2 * PAIR + lax.rem(c, PAIR) + PAIR * jnp.bitwise_xor(lo, t)
    head = lax.div(shard * (qw // HEAD_SIZE), GROUP_EXTENT)
    for s in range(C):
        msg = msgs[s]
        at = aligned(jnp.bitwise_xor(c, s) * tok, tok)
        q_s[pl.ds(at, tok), :] = msg[:, t * qw : (t + 1) * qw]
        for i, to in ((0, rows + at), (1, at)):
            for part in range(2):
                first = 2 * qw + (i * 2 + part) * KEY_VALUE_HEADS * HEAD_SIZE
                cols = pl.ds(aligned(first + head * HEAD_SIZE, 128), HEAD_SIZE)
                kv_s[pl.ds(to, tok), part * HEAD_SIZE : (part + 1) * HEAD_SIZE] = msg[:, cols]
    block = 128
    for b in range(rows // block):
        seen = rows + (b + 1) * block
        k = kv_s[:seen, :HEAD_SIZE]
        v = kv_s[:seen, HEAD_SIZE:]
        row = lax.broadcasted_iota(jnp.int32, (block, seen), 0) + (rows + b * block)
        visible = lax.broadcasted_iota(jnp.int32, (block, seen), 1) <= row
        at = slice(b * block, (b + 1) * block)
        for h in range(qw // HEAD_SIZE):
            q = q_s[at, h * HEAD_SIZE : (h + 1) * HEAD_SIZE]
            scores = lax.dot_general(q, k, (((1,), (1,)), ((), ())), preferred_element_type=F32)
            scores = jnp.where(visible, scores * HEAD_SIZE ** (-0.5), NEG_FILL)
            weights = jnp.exp(scores - jnp.max(scores, axis=1, keepdims=True))
            total = jnp.sum(weights, axis=1, keepdims=True)
            numerator = dot(weights.astype(BF16), v)
            out[at, h * HEAD_SIZE : (h + 1) * HEAD_SIZE] = (numerator / total).astype(BF16)


def route_kernel(E, cap, routes_ref, gates_ref, *refs):
    place_ref, gate_ref, line_s, gate_s = refs[3], refs[4], refs[-2], refs[-1]
    for src, dst in zip(refs[:3], refs[5:8]):
        dst[...] = src[...]
    e = lax.axis_index("exp")
    blocks, _, tok = routes_ref.shape
    rows = blocks * tok
    for i in range(blocks):
        routes = routes_ref[i]
        resident = routes < E
        target = jnp.sum(jnp.where(resident, routes + 1, 0), axis=0, keepdims=True) - 1
        gate = jnp.sum(jnp.where(resident, gates_ref[i], 0.0), axis=0, keepdims=True)
        line_s[:, i * tok : (i + 1) * tok] = jnp.broadcast_to(target, (8, tok))
        gate_s[:, i * tok : (i + 1) * tok] = jnp.broadcast_to(gate, (128, tok))
    target = line_s[:1, :]
    gate_ref[...] = gate_s[...].T
    has = target >= 0
    experts = lax.broadcasted_iota(jnp.int32, (E, rows), 0)
    one_hot = jnp.where(target == experts, 1.0, 0.0)
    earlier = jnp.where(
        lax.broadcasted_iota(jnp.int32, (rows, rows), 0)
        < lax.broadcasted_iota(jnp.int32, (rows, rows), 1),
        1.0,
        0.0,
    ).astype(BF16)
    rank = jnp.sum(dot(one_hot.astype(BF16), earlier) * one_hot, axis=0, keepdims=True)
    slot = jnp.bitwise_xor(target, e) * cap + rank.astype(jnp.int32)
    slot = jnp.where(has, slot, -1)
    places = lax.broadcasted_iota(jnp.int32, (E * cap, rows), 0)
    place_ref[...] = jnp.where(slot == places, 1.0, 0.0).astype(BF16)


def project_kernel(C, with_residual, *refs):
    own_w, refs = refs[:2], refs[2:]
    if with_residual:
        res, refs = refs[0], refs[1:]
    atts, ws, (acc, last, stacked) = refs[:C], refs[C : 3 * C - 4], refs[3 * C - 4 :]
    hi, _ = own_hi_lo()
    turn = jnp.bitwise_xor(lax.axis_index("ctx"), hi)
    for s in range(C):
        stacked[jnp.bitwise_xor(turn, s)] = atts[s][...]
    last[...] = stacked[C - 1]
    half = acc.shape[1] // 2
    for j in range(2):
        at = slice(j * half, (j + 1) * half)
        total = None
        for d in range(C - 1):
            w = own_w[j] if d == 0 else ws[2 * (d - 1) + j]
            term = dot(stacked[d], w[...])
            total = term if total is None else total + term
        if with_residual:
            total = total + res[:, at].astype(F32)
        acc[:, at] = total


def last_kernel(E, cap, *refs):
    accs, lasts, ws, places = refs[:2], refs[2:4], refs[4:6], refs[6:8]
    own_ref, *full_refs, keep_ref, send_ref = refs[8:]
    half = ws[0].shape[1]
    for j in range(2):
        cols = slice(j * half, (j + 1) * half)
        for t in (1, 0):
            total = accs[t][:, cols] + dot(lasts[t][...], ws[j][...])
            rounded = total.astype(BF16)
            if t == 0:
                own_ref[:, cols] = total
            else:
                first = 0
                for full in full_refs:
                    full[:, cols] = rounded[first : first + full.shape[0]]
                    first += full.shape[0]
            picked = dot(places[t][...], rounded)
            for d in range(E // 2):
                near, far = spread(d) ^ (PAIR * t), spread(d) ^ PAIR ^ (PAIR * t)
                at = (2 * d + t) * cap
                keep_ref[at : at + cap, cols] = picked[near * cap : (near + 1) * cap]
                at = (2 * d + 1 - t) * cap
                send_ref[at : at + cap, cols] = picked[far * cap : (far + 1) * cap].astype(BF16)


def outgoing_kernel(keep_ref, got_ref, gain_ref, *outs):
    scaled = ((keep_ref[...] + got_ref[...].astype(F32)) * gain_ref[...]).astype(BF16)
    count = outs[0].shape[0]
    for d, out in enumerate(outs):
        out[...] = scaled[d * count : (d + 1) * count]


def gate_up_kernel(C, E, cap, order, *refs):
    xs, gain_ref, w_ref, keep_ref, send_ref, x_s, part_s = refs[: E // 2], *refs[E // 2 :]
    c = lax.axis_index("ctx")
    e = lax.axis_index("exp")
    own_rows = E * cap // C
    wide = w_ref.shape[1]
    for d in range(E // 2):
        for t in range(2):
            at = aligned(jnp.bitwise_xor(e, spread(d) ^ (PAIR * t)) * cap, cap)
            x_s[pl.ds(at, cap), :] = xs[d][t * cap : (t + 1) * cap, :]
    plain = x_s[...].astype(F32) / gain_ref[...]
    square = jnp.sum(plain * plain, axis=1, keepdims=True)
    lane = lax.broadcasted_iota(jnp.int32, (E * cap, 128), 1)
    part_s[:, wide:] = jnp.where(lane == 0, square, 0.0)
    step = 512
    for j in range(wide // step):
        at = slice(j * step, (j + 1) * step)
        part_s[:, at] = dot(x_s[...], w_ref[:, at])
    for i, r in enumerate(order):
        at = aligned(jnp.bitwise_xor(c, r) * own_rows, own_rows)
        block = part_s[pl.ds(at, own_rows), :]
        if i < C // 2:
            keep_ref[i * own_rows : (i + 1) * own_rows, :] = block
        else:
            to = (i - C // 2) * own_rows
            send_ref[to : to + own_rows, :wide] = block[:, :wide].astype(BF16)
            square = block[:, wide:]
            high = square.astype(BF16).astype(F32)
            lane = lax.broadcasted_iota(jnp.int32, square.shape, 1)
            low = pltpu.roll(square - high, 1, 1)
            pair = jnp.where(lane == 1, low, high)
            send_ref[to : to + own_rows, wide:] = pair.astype(BF16)


def halve_kernel(keep_in, got_ref, keep_ref, send_ref):
    rows = keep_ref.shape[0]
    wide = keep_ref.shape[1] - 128
    total = keep_in[...] + got_ref[...].astype(F32)
    keep_ref[...] = total[:rows]
    send_ref[:, :wide] = total[rows:, :wide].astype(BF16)
    square = jnp.sum(total[rows:, wide:], axis=1, keepdims=True)
    high = square.astype(BF16).astype(F32)
    lane = lax.broadcasted_iota(jnp.int32, (rows, 128), 1)
    pair = jnp.where(lane == 0, high, jnp.where(lane == 1, square - high, 0.0))
    send_ref[:, wide:] = pair.astype(BF16)


def activate_kernel(hidden, keep_ref, got_ref, out):
    def summed(at):
        return keep_ref[:, at] + got_ref[:, at].astype(F32)

    square = jnp.sum(summed(slice(2 * hidden, 2 * hidden + 128)), axis=1, keepdims=True)
    scale = lax.rsqrt(square / D + 1e-6)
    gate = summed(slice(0, hidden)) * scale
    up = summed(slice(hidden, 2 * hidden)) * scale
    out[...] = (gate / (1.0 + jnp.exp(-gate)) * up).astype(BF16)


def down_kernel(C, E, cap, *refs):
    acts, w_ref, outs, x_s, part_s = refs[:C], refs[C], refs[C + 1 : C + 1 + E // 2], refs[-2], refs[-1]
    c = lax.axis_index("ctx")
    e = lax.axis_index("exp")
    own_rows = E * cap // C
    for s in range(C):
        at = aligned(jnp.bitwise_xor(c, s) * own_rows, own_rows)
        x_s[pl.ds(at, own_rows), :] = acts[s][...]
    part_s[...] = dot(x_s[...], w_ref[...]).astype(BF16)
    for d in range(E // 2):
        for t in range(2):
            at = aligned(jnp.bitwise_xor(e, spread(d) ^ (PAIR * t)) * cap, cap)
            outs[d][t * cap : (t + 1) * cap, :] = part_s[pl.ds(at, cap), :]


def forward_kernel(cap, *refs):
    for d, x in enumerate(refs[:-1]):
        refs[-1][d * cap : (d + 1) * cap, :] = x[cap:, :]


def combine_kernel(E, cap, own, got0, got1, place_ref, gate_ref, *refs):
    xs, far, out, x_s = refs[: E // 2], refs[E // 2], refs[E // 2 + 1], refs[E // 2 + 2]
    for d in range(E // 2):
        at = spread(d) * cap
        x_s[at : at + cap, :] = xs[d][:cap, :]
        at = (spread(d) ^ PAIR) * cap
        x_s[at : at + cap, :] = far[d * cap : (d + 1) * cap, :]
    half = own.shape[1] // 2
    for j in range(2):
        cols = slice(j * half, (j + 1) * half)
        collected = lax.dot_general(
            place_ref[...], x_s[:, cols], (((0,), (0,)), ((), ())), preferred_element_type=F32
        )
        few = got0.shape[0]
        for got, at in ((got0, slice(0, few)), (got1, slice(few, own.shape[0]))):
            mixed = own[at, cols] + got[:, cols].astype(F32)
            out[at, cols] = (mixed + gate_ref[at, :1] * collected[at]).astype(BF16)


def body(
    queries,
    new_keys_values,
    cached_keys_values,
    residual,
    out_weight,
    norm_gain,
    routes,
    gates,
    w_gate_up,
    w_down,
):
    C = lax.axis_size("ctx")
    E = lax.axis_size("exp")
    tok = queries.shape[2]
    rows = C * tok
    width = residual.shape[3]
    hidden = w_down.shape[1]
    wide = 2 * hidden
    cap = rows // (2 * E)
    slots = E * cap
    own_rows = slots // C
    qw = QUERY_HEADS // E * HEAD_SIZE

    def permute(x, ctx=0, exp=0):
        pairs = [(c * E + e, (c ^ ctx) * E + (e ^ exp)) for c in range(C) for e in range(E)]
        return lax.ppermute(x, ("ctx", "exp"), pairs)

    def after(x, *others):
        return lax.optimization_barrier((x, *others))[0]

    half = width // 2
    kv = new_keys_values.shape[3]
    msgs = call(
        functools.partial(pack_kernel, C, qw),
        [sds((tok, 2 * qw + 2 * kv), BF16)] * C,
        3,
        scratch=[pltpu.SemaphoreType.DMA((4 * C,))],
        in_specs=[HBM] * 3,
        out_specs=[ANY] * C,
        cost=(0, 2**20),
        limit=PACK_LIMIT,
    )(
        queries.reshape(tok, queries.shape[3]),
        new_keys_values.reshape(tok, kv),
        cached_keys_values.reshape(tok, kv),
    )
    half_a, half_b = call(
        halve_weight_kernel,
        [sds((qw, half), BF16)] * 2,
        1,
        scratch=[pltpu.SemaphoreType.DMA((2,))],
        in_specs=[HBM],
        out_specs=[ANY] * 2,
        cost=(0, 2**20),
        limit=PACK_LIMIT,
    )(after(out_weight, msgs[0]))
    res = residual.reshape(rows, width)
    got = [msgs[0]] + [permute(msgs[s], ctx=s) for s in range(1, C)]
    shards = {0: [half_a, half_b], 1: [None, permute(half_b, exp=1)]}
    for d in range(2, C, 2):
        shards[d] = [permute(half_a, exp=spread(d)), None]
    step = [shards[1][1]] + [shards[d][0] for d in range(2, C, 2)]
    got[1] = after(got[1], *step)
    step += got[1:]
    shards[1][0] = permute(after(half_a, *step), exp=1)
    for d in range(2, C, 2):
        shards[d][1] = permute(after(half_b, *step), exp=spread(d))
    step = [shards[1][0]] + [shards[d][1] for d in range(2, C, 2)]
    for d in range(3, C, 2):
        shards[d] = [
            permute(after(shards[d - 1][0], *step), exp=1),
            permute(after(shards[1][1], *step), exp=spread(d - 1)),
        ]

    step2 = step

    def attend(t, msgs):
        return call(
            functools.partial(attend_kernel, C, t),
            [sds((rows, qw), BF16)] + [sds(msgs[0].shape, BF16)] * t,
            C,
            scratch=[pltpu.VMEM((2 * rows, 2 * HEAD_SIZE), BF16), pltpu.VMEM((rows, qw), BF16)],
            cost=(0, 2**14),
            limit=16,
        )(*msgs)

    other, own_msg = attend(1, got)
    theirs = permute(other, exp=PAIR)
    (mine,) = attend(0, [own_msg, after(got[1], other)] + got[2:])
    tokens_last = lambda x: jnp.transpose(x.reshape(C, tok, x.shape[3]), (0, 2, 1))
    place, gate, *staged = call(
        functools.partial(route_kernel, E, cap),
        [sds((slots, rows), BF16), sds((rows, 128), F32)]
        + [sds((qw, half), BF16)] * 2
        + [sds((rows, width), BF16)],
        5,
        scratch=[pltpu.VMEM((8, rows), jnp.int32), pltpu.VMEM((128, rows), F32)],
        cost=(0, 2**14),
        limit=16,
    )(tokens_last(after(routes, mine)), tokens_last(after(gates, mine)), half_a, half_b, res)
    shards[0], res = staged[:2], staged[2]

    def gather(x, before):
        atts = {0: x, 1: permute(x, ctx=1)}
        for s in range(2, C, 2):
            atts[s] = permute(x, ctx=s)
            atts[s + 1] = permute(after(atts[s], *before), ctx=1)
        return [atts[s] for s in range(C)]

    other_place = permute(after(place, theirs), exp=PAIR)
    step = shards[C - 1]
    mine_all = gather(mine, [])
    theirs_all = gather(after(theirs, place, *step2), [])
    mine_all[1] = after(mine_all[1], other_place, *step)

    def project(atts, *extra):
        operands = [*shards[0], *extra, *atts]
        operands += [w for d in range(1, C - 1) for w in shards[d]]
        return call(
            functools.partial(project_kernel, C, bool(extra)),
            [sds((rows, width), F32), sds((rows, qw), BF16)],
            len(operands),
            scratch=[
                pltpu.VMEM((C, rows, qw), BF16),
            ],
            cost=(0, 2**14),
        )(*operands)

    acc, last = project(mine_all, res)
    acc_far, last_far = project(theirs_all)
    gain = norm_gain.reshape(1, width)
    parts = (rows * 3 // 8, rows * 5 // 8)
    own, *full, keep, send = call(
        functools.partial(last_kernel, E, cap),
        [
            sds((rows, width), F32),
            *[sds((n, width), BF16) for n in parts],
            sds((slots, width), F32),
            sds((slots, width), BF16),
        ],
        8,
        cost=(4 * rows * (qw + slots) * width, 2**20),
    )(acc, acc_far, last, last_far, *shards[C - 1], place, other_place)
    received = permute(send, exp=PAIR)
    outgoing = call(
        outgoing_kernel, [sds((2 * cap, width), BF16)] * (E // 2), 3, cost=(0, 2**20)
    )(keep, received, gain)
    incoming = {0: outgoing[0]}
    for d in reversed(range(1, E // 2)):
        incoming[d] = permute(outgoing[d], exp=spread(d))
    incoming = [incoming[d] for d in range(E // 2)]
    arrived = [permute(after(full[0], received), exp=PAIR)]
    incoming[0] = after(incoming[0], arrived[0])
    arrived.append(permute(after(full[1], arrived[0]), exp=PAIR))

    order = [0]
    bit = C // 2
    while bit:
        order = order + [r | bit for r in order]
        bit //= 2
    keep, send = call(
        functools.partial(gate_up_kernel, C, E, cap, order),
        [sds((slots // 2, wide + 128), F32), sds((slots // 2, wide + 128), BF16)],
        E // 2 + 2,
        scratch=[pltpu.VMEM((slots, width), BF16), pltpu.VMEM((slots, wide + 128), F32)],
        cost=(2 * slots * width * wide, 2 * width * wide),
    )(*incoming, gain, w_gate_up.reshape(width, wide))
    bit = 1
    while 2 * bit < C:
        count = keep.shape[0] // 2
        keep, send = call(
            halve_kernel,
            [sds((count, wide + 128), F32), sds((count, wide + 128), BF16)],
            2,
            cost=(0, 2**21),
        )(keep, permute(send, ctx=bit))
        bit *= 2
    activated = call(
        functools.partial(activate_kernel, hidden),
        sds((own_rows, hidden), BF16),
        2,
        cost=(0, 2**20),
    )(keep, permute(send, ctx=bit))
    acts = {0: activated}
    acts[bit] = after(permute(activated, ctx=bit), arrived[1])
    bit //= 2
    while bit:
        for r in list(acts):
            acts[r ^ bit] = permute(acts[r], ctx=bit)
        bit //= 2
    expert_out = call(
        functools.partial(down_kernel, C, E, cap),
        [sds((2 * cap, width), BF16)] * (E // 2),
        C + 1,
        scratch=[pltpu.VMEM((slots, hidden), BF16), pltpu.VMEM((slots, width), BF16)],
        cost=(2 * slots * width * hidden, 2 * width * hidden),
    )(acts[0], *[acts[s] for s in range(1, C)], w_down.reshape(hidden, width))
    returned = [expert_out[0]]
    returned += [permute(expert_out[d], exp=spread(d)) for d in reversed(range(1, E // 2))][::-1]
    far = call(
        functools.partial(forward_kernel, cap), sds((slots // 2, width), BF16), E // 2, cost=(0, 2**19)
    )(*returned)
    result = call(
        functools.partial(combine_kernel, E, cap),
        sds((rows, width), BF16),
        6 + E // 2,
        scratch=[pltpu.VMEM((slots, width), BF16)],
        cost=(0, 2 * 2**20),
    )(own, *arrived, place, gate, *returned, permute(far, exp=PAIR))
    return result.reshape(C, 1, tok, width)


def solution(mesh):
    in_specs = (
        P("ctx", "exp", None, None),
        P("ctx", "exp", None, None),
        P("ctx", "exp", None, None),
        P(None, "exp", None, "ctx"),
        P("exp", "ctx"),
        P("ctx"),
        P(None, "exp", None, None),
        P(None, "exp", None, None),
        P("exp", "ctx", None),
        P("exp", None, "ctx"),
    )
    out_specs = P(None, "exp", None, "ctx")
    return jax.shard_map(body, mesh=mesh, in_specs=in_specs, out_specs=out_specs, check_vma=False)
```

```python
import functools

import jax
import jax.numpy as jnp
from jax import lax
from jax.experimental import pallas as pl
from jax.experimental.pallas import tpu as pltpu
from jax.sharding import PartitionSpec as P

D = 4096
QUERY_HEADS = 32
KEY_VALUE_HEADS = 2
HEAD_SIZE = 128
GROUP_EXTENT = QUERY_HEADS // KEY_VALUE_HEADS
NEG_FILL = -1e30
BF16 = jnp.bfloat16
F32 = jnp.float32
VMEM = pl.BlockSpec(memory_space=pltpu.VMEM)
HBM = pl.BlockSpec(memory_space=pltpu.HBM)
ANY = pl.BlockSpec(memory_space=pl.ANY)


def call(kernel, out_shape, n_in, scratch=(), cost=(0, 0), limit=32, **kw):
    kw.setdefault("in_specs", [VMEM] * n_in)
    kw.setdefault("out_specs", jax.tree.map(lambda _: VMEM, out_shape))
    return pl.pallas_call(
        kernel,
        out_shape=out_shape,
        scratch_shapes=list(scratch),
        cost_estimate=pl.CostEstimate(flops=cost[0], bytes_accessed=cost[1], transcendentals=0),
        compiler_params=pltpu.CompilerParams(vmem_limit_bytes=limit * 2**20),
        **kw,
    )


def sds(shape, dtype):
    return jax.ShapeDtypeStruct(shape, dtype)


def dot(a, b):
    return jnp.dot(a, b, preferred_element_type=F32)


PAIR = 4
PACK_LIMIT = 16


def spread(d):
    return (d // PAIR) * 2 * PAIR + d % PAIR


def own_hi_lo():
    e = lax.axis_index("exp")
    return lax.div(e, 2 * PAIR) * PAIR + lax.rem(e, PAIR), lax.rem(lax.div(e, PAIR), 2)


def aligned(x, n):
    return pl.multiple_of(x, n)


def run_copies(pairs, sems):
    copies = [pltpu.make_async_copy(src, dst, sems.at[i]) for i, (src, dst) in enumerate(pairs)]
    for c in copies:
        c.start()
    for c in copies:
        c.wait()


def pack_kernel(C, qw, q_ref, new_ref, past_ref, *refs):
    outs, sems = refs[:C], refs[C]
    c = lax.axis_index("ctx")
    _, lo = own_hi_lo()
    kv = new_ref.shape[1]
    pairs = []
    for s in reversed(range(C)):
        target = jnp.bitwise_xor(c, s)
        out = outs[s]
        for t in range(2):
            shard = lax.div(target, PAIR) * 2 * PAIR + lax.rem(target, PAIR)
            shard = shard + PAIR * jnp.bitwise_xor(lo, t)
            at = pl.ds(aligned(shard * qw, 128), qw)
            pairs.append((q_ref.at[:, at], out.at[:, t * qw : (t + 1) * qw]))
        pairs.append((new_ref, out.at[:, 2 * qw : 2 * qw + kv]))
        pairs.append((past_ref, out.at[:, 2 * qw + kv :]))
    run_copies(pairs, sems)


def attend_kernel(C, t, *refs):
    msgs, out, kv_s, q_s = refs[:C], refs[C], refs[-2], refs[-1]
    if t == 1:
        refs[C + 1][...] = msgs[0][...]
    c = lax.axis_index("ctx")
    tok, qw = msgs[0].shape[0], out.shape[1]
    rows = C * tok
    _, lo = own_hi_lo()
    shard = lax.div(c, PAIR) * 2 * PAIR + lax.rem(c, PAIR) + PAIR * jnp.bitwise_xor(lo, t)
    head = lax.div(shard * (qw // HEAD_SIZE), GROUP_EXTENT)
    for s in range(C):
        msg = msgs[s]
        at = aligned(jnp.bitwise_xor(c, s) * tok, tok)
        q_s[pl.ds(at, tok), :] = msg[:, t * qw : (t + 1) * qw]
        for i, to in ((0, rows + at), (1, at)):
            for part in range(2):
                first = 2 * qw + (i * 2 + part) * KEY_VALUE_HEADS * HEAD_SIZE
                cols = pl.ds(aligned(first + head * HEAD_SIZE, 128), HEAD_SIZE)
                kv_s[pl.ds(to, tok), part * HEAD_SIZE : (part + 1) * HEAD_SIZE] = msg[:, cols]
    block = 128
    for b in range(rows // block):
        seen = rows + (b + 1) * block
        k = kv_s[:seen, :HEAD_SIZE]
        v = kv_s[:seen, HEAD_SIZE:]
        row = lax.broadcasted_iota(jnp.int32, (block, seen), 0) + (rows + b * block)
        visible = lax.broadcasted_iota(jnp.int32, (block, seen), 1) <= row
        at = slice(b * block, (b + 1) * block)
        for h in range(qw // HEAD_SIZE):
            q = q_s[at, h * HEAD_SIZE : (h + 1) * HEAD_SIZE]
            scores = lax.dot_general(q, k, (((1,), (1,)), ((), ())), preferred_element_type=F32)
            scores = jnp.where(visible, scores * HEAD_SIZE ** (-0.5), NEG_FILL)
            weights = jnp.exp(scores - jnp.max(scores, axis=1, keepdims=True))
            total = jnp.sum(weights, axis=1, keepdims=True)
            numerator = dot(weights.astype(BF16), v)
            out[at, h * HEAD_SIZE : (h + 1) * HEAD_SIZE] = (numerator / total).astype(BF16)


def route_kernel(E, cap, routes_ref, gates_ref, *refs):
    place_ref, gate_ref, line_s, gate_s = refs[2], refs[3], refs[-2], refs[-1]
    for src, dst in zip(refs[:2], refs[4:6]):
        dst[...] = src[...]
    e = lax.axis_index("exp")
    blocks, _, tok = routes_ref.shape
    rows = blocks * tok
    for i in range(blocks):
        routes = routes_ref[i]
        resident = routes < E
        target = jnp.sum(jnp.where(resident, routes + 1, 0), axis=0, keepdims=True) - 1
        gate = jnp.sum(jnp.where(resident, gates_ref[i], 0.0), axis=0, keepdims=True)
        line_s[:, i * tok : (i + 1) * tok] = jnp.broadcast_to(target, (8, tok))
        gate_s[:, i * tok : (i + 1) * tok] = jnp.broadcast_to(gate, (128, tok))
    target = line_s[:1, :]
    gate_ref[...] = gate_s[...].T
    has = target >= 0
    experts = lax.broadcasted_iota(jnp.int32, (E, rows), 0)
    one_hot = jnp.where(target == experts, 1.0, 0.0)
    earlier = jnp.where(
        lax.broadcasted_iota(jnp.int32, (rows, rows), 0)
        < lax.broadcasted_iota(jnp.int32, (rows, rows), 1),
        1.0,
        0.0,
    ).astype(BF16)
    rank = jnp.sum(dot(one_hot.astype(BF16), earlier) * one_hot, axis=0, keepdims=True)
    slot = jnp.bitwise_xor(target, e) * cap + rank.astype(jnp.int32)
    slot = jnp.where(has, slot, -1)
    places = lax.broadcasted_iota(jnp.int32, (E * cap, rows), 0)
    place_ref[...] = jnp.where(slot == places, 1.0, 0.0).astype(BF16)


def project_kernel(C, cut, with_residual, *refs):
    refs, (acc, last, stacked) = list(refs[:-3]), refs[-3:]
    res = refs.pop(0) if with_residual else None
    atts, ws = refs[:C], refs[C:]
    hi, _ = own_hi_lo()
    turn = jnp.bitwise_xor(lax.axis_index("ctx"), hi)
    for s in range(C):
        stacked[jnp.bitwise_xor(turn, s)] = atts[s][...]
    last[...] = stacked[C - 1]
    width = acc.shape[1]
    for j, at in enumerate((slice(0, cut), slice(cut, width))):
        total = res[:, at].astype(F32) if with_residual else None
        for d in range(C - 1):
            if d < 2:
                w = ws[d][:, at]
            else:
                w = ws[2 * d - 2 + j][...]
            term = dot(stacked[d], w)
            total = term if total is None else total + term
        acc[:, at] = total


def last_kernel(E, cap, *refs):
    accs, lasts, ws, places = refs[:2], refs[2:4], refs[4:6], refs[6:8]
    own_ref, *full_refs, keep_ref, send_ref = refs[8:]
    cut = ws[0].shape[1]
    for j, cols in enumerate((slice(0, cut), slice(cut, own_ref.shape[1]))):
        for t in (1, 0):
            total = accs[t][:, cols] + dot(lasts[t][...], ws[j][...])
            rounded = total.astype(BF16)
            if t == 0:
                own_ref[:, cols] = total
            else:
                first = 0
                for full in full_refs:
                    full[:, cols] = rounded[first : first + full.shape[0]]
                    first += full.shape[0]
            picked = dot(places[t][...], rounded)
            for d in range(E // 2):
                near, far = spread(d) ^ (PAIR * t), spread(d) ^ PAIR ^ (PAIR * t)
                at = (2 * d + t) * cap
                keep_ref[at : at + cap, cols] = picked[near * cap : (near + 1) * cap]
                at = (2 * d + 1 - t) * cap
                send_ref[at : at + cap, cols] = picked[far * cap : (far + 1) * cap].astype(BF16)


def outgoing_kernel(keep_ref, got_ref, gain_ref, *outs):
    scaled = ((keep_ref[...] + got_ref[...].astype(F32)) * gain_ref[...]).astype(BF16)
    count = outs[0].shape[0]
    for d, out in enumerate(outs):
        out[...] = scaled[d * count : (d + 1) * count]


def gate_up_kernel(C, E, cap, order, *refs):
    xs, gain_ref, w_ref, keep_ref, send_ref, x_s, part_s = refs[: E // 2], *refs[E // 2 :]
    c = lax.axis_index("ctx")
    e = lax.axis_index("exp")
    own_rows = E * cap // C
    wide = w_ref.shape[1]
    for d in range(E // 2):
        for t in range(2):
            at = aligned(jnp.bitwise_xor(e, spread(d) ^ (PAIR * t)) * cap, cap)
            x_s[pl.ds(at, cap), :] = xs[d][t * cap : (t + 1) * cap, :]
    plain = x_s[...].astype(F32) / gain_ref[...]
    square = jnp.sum(plain * plain, axis=1, keepdims=True)
    lane = lax.broadcasted_iota(jnp.int32, (E * cap, 128), 1)
    part_s[:, wide:] = jnp.where(lane == 0, square, 0.0)
    step = 512
    for j in range(wide // step):
        at = slice(j * step, (j + 1) * step)
        part_s[:, at] = dot(x_s[...], w_ref[:, at])
    for i, r in enumerate(order):
        at = aligned(jnp.bitwise_xor(c, r) * own_rows, own_rows)
        block = part_s[pl.ds(at, own_rows), :]
        if i < C // 2:
            keep_ref[i * own_rows : (i + 1) * own_rows, :] = block
        else:
            to = (i - C // 2) * own_rows
            send_ref[to : to + own_rows, :wide] = block[:, :wide].astype(BF16)
            square = block[:, wide:]
            high = square.astype(BF16).astype(F32)
            lane = lax.broadcasted_iota(jnp.int32, square.shape, 1)
            low = pltpu.roll(square - high, 1, 1)
            pair = jnp.where(lane == 1, low, high)
            send_ref[to : to + own_rows, wide:] = pair.astype(BF16)


def halve_kernel(keep_in, got_ref, keep_ref, send_ref):
    rows = keep_ref.shape[0]
    wide = keep_ref.shape[1] - 128
    total = keep_in[...] + got_ref[...].astype(F32)
    keep_ref[...] = total[:rows]
    send_ref[:, :wide] = total[rows:, :wide].astype(BF16)
    square = jnp.sum(total[rows:, wide:], axis=1, keepdims=True)
    high = square.astype(BF16).astype(F32)
    lane = lax.broadcasted_iota(jnp.int32, (rows, 128), 1)
    pair = jnp.where(lane == 0, high, jnp.where(lane == 1, square - high, 0.0))
    send_ref[:, wide:] = pair.astype(BF16)


def activate_kernel(hidden, keep_ref, got_ref, out):
    def summed(at):
        return keep_ref[:, at] + got_ref[:, at].astype(F32)

    square = jnp.sum(summed(slice(2 * hidden, 2 * hidden + 128)), axis=1, keepdims=True)
    scale = lax.rsqrt(square / D + 1e-6)
    gate = summed(slice(0, hidden)) * scale
    up = summed(slice(hidden, 2 * hidden)) * scale
    out[...] = (gate / (1.0 + jnp.exp(-gate)) * up).astype(BF16)


def down_kernel(C, E, cap, *refs):
    acts, w_ref, outs, x_s, part_s = refs[:C], refs[C], refs[C + 1 : C + 1 + E // 2], refs[-2], refs[-1]
    c = lax.axis_index("ctx")
    e = lax.axis_index("exp")
    own_rows = E * cap // C
    for s in range(C):
        at = aligned(jnp.bitwise_xor(c, s) * own_rows, own_rows)
        x_s[pl.ds(at, own_rows), :] = acts[s][...]
    part_s[...] = dot(x_s[...], w_ref[...]).astype(BF16)
    for d in range(E // 2):
        for t in range(2):
            at = aligned(jnp.bitwise_xor(e, spread(d) ^ (PAIR * t)) * cap, cap)
            outs[d][t * cap : (t + 1) * cap, :] = part_s[pl.ds(at, cap), :]


def forward_kernel(cap, *refs):
    for d, x in enumerate(refs[:-1]):
        refs[-1][d * cap : (d + 1) * cap, :] = x[cap:, :]


def combine_kernel(E, cap, own, got0, got1, place_ref, gate_ref, *refs):
    xs, far, out, x_s = refs[: E // 2], refs[E // 2], refs[E // 2 + 1], refs[E // 2 + 2]
    for d in range(E // 2):
        at = spread(d) * cap
        x_s[at : at + cap, :] = xs[d][:cap, :]
        at = (spread(d) ^ PAIR) * cap
        x_s[at : at + cap, :] = far[d * cap : (d + 1) * cap, :]
    half = own.shape[1] // 2
    for j in range(2):
        cols = slice(j * half, (j + 1) * half)
        collected = lax.dot_general(
            place_ref[...], x_s[:, cols], (((0,), (0,)), ((), ())), preferred_element_type=F32
        )
        few = got0.shape[0]
        for got, at in ((got0, slice(0, few)), (got1, slice(few, own.shape[0]))):
            mixed = own[at, cols] + got[:, cols].astype(F32)
            out[at, cols] = (mixed + gate_ref[at, :1] * collected[at]).astype(BF16)


def body(
    queries,
    new_keys_values,
    cached_keys_values,
    residual,
    out_weight,
    norm_gain,
    routes,
    gates,
    w_gate_up,
    w_down,
):
    C = lax.axis_size("ctx")
    E = lax.axis_size("exp")
    tok = queries.shape[2]
    rows = C * tok
    width = residual.shape[3]
    hidden = w_down.shape[1]
    wide = 2 * hidden
    cap = rows // (2 * E)
    slots = E * cap
    own_rows = slots // C
    qw = QUERY_HEADS // E * HEAD_SIZE

    def permute(x, ctx=0, exp=0):
        pairs = [(c * E + e, (c ^ ctx) * E + (e ^ exp)) for c in range(C) for e in range(E)]
        return lax.ppermute(x, ("ctx", "exp"), pairs)

    def after(x, *others):
        return lax.optimization_barrier((x, *others))[0]

    cut = width - max(width * 3 // 8, 128)
    kv = new_keys_values.shape[3]
    msgs = call(
        functools.partial(pack_kernel, C, qw),
        [sds((tok, 2 * qw + 2 * kv), BF16)] * C,
        3,
        scratch=[pltpu.SemaphoreType.DMA((4 * C,))],
        in_specs=[HBM] * 3,
        cost=(0, 2**20),
        limit=PACK_LIMIT,
    )(
        queries.reshape(tok, queries.shape[3]),
        new_keys_values.reshape(tok, kv),
        cached_keys_values.reshape(tok, kv),
    )
    res = residual.reshape(rows, width)
    got = [msgs[0]] + [permute(msgs[s], ctx=s) for s in range(1, C)]
    shards = {0: [out_weight], 1: [permute(out_weight, exp=1)]}
    for d in range(2, C, 2):
        shards[d] = [permute(out_weight[:, :cut], exp=spread(d))]
    step = [shards[d][0] for d in range(2, C, 2)]
    got[1] = after(got[1], *step)
    for d in range(2, C, 2):
        shards[d].append(permute(after(out_weight[:, cut:], *got), exp=spread(d)))
        shards[d + 1] = [permute(after(shards[d][0], *got), exp=1)]
    step = shards[1] + [shards[d][1] for d in range(2, C, 2)]
    for d in range(2, C, 2):
        shards[d + 1].append(permute(after(shards[1][0], *step)[:, cut:], exp=spread(d)))

    step2 = step

    def attend(t, msgs):
        return call(
            functools.partial(attend_kernel, C, t),
            [sds((rows, qw), BF16)] + [sds(msgs[0].shape, BF16)] * t,
            C,
            scratch=[pltpu.VMEM((2 * rows, 2 * HEAD_SIZE), BF16), pltpu.VMEM((rows, qw), BF16)],
            cost=(0, 2**14),
            limit=16,
        )(*msgs)

    other, own_msg = attend(1, got)
    theirs = permute(other, exp=PAIR)
    (mine,) = attend(0, [own_msg, after(got[1], other)] + got[2:])
    tokens_last = lambda x: jnp.transpose(x.reshape(C, tok, x.shape[3]), (0, 2, 1))
    place, gate, *staged = call(
        functools.partial(route_kernel, E, cap),
        [sds((slots, rows), BF16), sds((rows, 128), F32)]
        + [sds((qw, width), BF16), sds((rows, width), BF16)],
        4,
        scratch=[pltpu.VMEM((8, rows), jnp.int32), pltpu.VMEM((128, rows), F32)],
        cost=(0, 2**14),
        limit=16,
    )(tokens_last(after(routes, mine)), tokens_last(after(gates, mine)), out_weight, res)
    shards[0], res = staged[:1], staged[1]

    def gather(x, before):
        atts = {0: x, 1: permute(x, ctx=1)}
        for s in range(2, C, 2):
            atts[s] = permute(x, ctx=s)
            atts[s + 1] = permute(after(atts[s], *before), ctx=1)
        return [atts[s] for s in range(C)]

    other_place = permute(after(place, theirs), exp=PAIR)
    step = shards[C - 1]
    mine_all = gather(mine, [])
    theirs_all = gather(after(theirs, place, *step2), [])
    mine_all[1] = after(mine_all[1], other_place, *step)

    def project(atts, *extra):
        operands = [*extra, *atts, *[w for d in range(C - 1) for w in shards[d]]]
        return call(
            functools.partial(project_kernel, C, cut, bool(extra)),
            [sds((rows, width), F32), sds((rows, qw), BF16)],
            len(operands),
            scratch=[
                pltpu.VMEM((C, rows, qw), BF16),
            ],
            cost=(0, 2**14),
        )(*operands)

    acc, last = project(mine_all, res)
    acc_far, last_far = project(theirs_all)
    gain = norm_gain.reshape(1, width)
    parts = (rows * 3 // 8, rows * 5 // 8)
    own, *full, keep, send = call(
        functools.partial(last_kernel, E, cap),
        [
            sds((rows, width), F32),
            *[sds((n, width), BF16) for n in parts],
            sds((slots, width), F32),
            sds((slots, width), BF16),
        ],
        8,
        cost=(4 * rows * (qw + slots) * width, 2**20),
    )(acc, acc_far, last, last_far, *shards[C - 1], place, other_place)
    received = permute(send, exp=PAIR)
    outgoing = call(
        outgoing_kernel, [sds((2 * cap, width), BF16)] * (E // 2), 3, cost=(0, 2**20)
    )(keep, received, gain)
    incoming = {0: outgoing[0]}
    for d in reversed(range(1, E // 2)):
        incoming[d] = permute(outgoing[d], exp=spread(d))
    incoming = [incoming[d] for d in range(E // 2)]
    arrived = [permute(after(full[0], received), exp=PAIR)]
    incoming[0] = after(incoming[0], arrived[0])
    arrived.append(permute(after(full[1], arrived[0]), exp=PAIR))

    order = [0]
    bit = C // 2
    while bit:
        order = order + [r | bit for r in order]
        bit //= 2
    keep, send = call(
        functools.partial(gate_up_kernel, C, E, cap, order),
        [sds((slots // 2, wide + 128), F32), sds((slots // 2, wide + 128), BF16)],
        E // 2 + 2,
        scratch=[pltpu.VMEM((slots, width), BF16), pltpu.VMEM((slots, wide + 128), F32)],
        cost=(2 * slots * width * wide, 2 * width * wide),
    )(*incoming, gain, w_gate_up.reshape(width, wide))
    bit = 1
    while 2 * bit < C:
        count = keep.shape[0] // 2
        keep, send = call(
            halve_kernel,
            [sds((count, wide + 128), F32), sds((count, wide + 128), BF16)],
            2,
            cost=(0, 2**21),
        )(keep, permute(send, ctx=bit))
        bit *= 2
    activated = call(
        functools.partial(activate_kernel, hidden),
        sds((own_rows, hidden), BF16),
        2,
        cost=(0, 2**20),
    )(keep, permute(send, ctx=bit))
    acts = {0: activated}
    acts[bit] = after(permute(activated, ctx=bit), arrived[1])
    bit //= 2
    while bit:
        for r in list(acts):
            acts[r ^ bit] = permute(acts[r], ctx=bit)
        bit //= 2
    expert_out = call(
        functools.partial(down_kernel, C, E, cap),
        [sds((2 * cap, width), BF16)] * (E // 2),
        C + 1,
        scratch=[pltpu.VMEM((slots, hidden), BF16), pltpu.VMEM((slots, width), BF16)],
        cost=(2 * slots * width * hidden, 2 * width * hidden),
    )(acts[0], *[acts[s] for s in range(1, C)], w_down.reshape(hidden, width))
    returned = [expert_out[0]]
    returned += [permute(expert_out[d], exp=spread(d)) for d in reversed(range(1, E // 2))][::-1]
    far = call(
        functools.partial(forward_kernel, cap), sds((slots // 2, width), BF16), E // 2, cost=(0, 2**19)
    )(*returned)
    result = call(
        functools.partial(combine_kernel, E, cap),
        sds((rows, width), BF16),
        6 + E // 2,
        scratch=[pltpu.VMEM((slots, width), BF16)],
        cost=(0, 2 * 2**20),
    )(own, *arrived, place, gate, *returned, permute(far, exp=PAIR))
    return result.reshape(C, 1, tok, width)


def solution(mesh):
    in_specs = (
        P("ctx", "exp", None, None),
        P("ctx", "exp", None, None),
        P("ctx", "exp", None, None),
        P(None, "exp", None, "ctx"),
        P("exp", "ctx"),
        P("ctx"),
        P(None, "exp", None, None),
        P(None, "exp", None, None),
        P("exp", "ctx", None),
        P("exp", None, "ctx"),
    )
    out_specs = P(None, "exp", None, "ctx")
    return jax.shard_map(body, mesh=mesh, in_specs=in_specs, out_specs=out_specs, check_vma=False)
```

```python
import functools

import jax
import jax.numpy as jnp
from jax import lax
from jax.experimental import pallas as pl
from jax.experimental.pallas import tpu as pltpu
from jax.sharding import PartitionSpec as P

D = 4096
QUERY_HEADS = 32
KEY_VALUE_HEADS = 2
HEAD_SIZE = 128
GROUP_EXTENT = QUERY_HEADS // KEY_VALUE_HEADS
NEG_FILL = -1e30
BF16 = jnp.bfloat16
F32 = jnp.float32
VMEM = pl.BlockSpec(memory_space=pltpu.VMEM)
HBM = pl.BlockSpec(memory_space=pltpu.HBM)
ANY = pl.BlockSpec(memory_space=pl.ANY)


def call(kernel, out_shape, n_in, scratch=(), cost=(0, 0), limit=32, **kw):
    kw.setdefault("in_specs", [VMEM] * n_in)
    kw.setdefault("out_specs", jax.tree.map(lambda _: VMEM, out_shape))
    return pl.pallas_call(
        kernel,
        out_shape=out_shape,
        scratch_shapes=list(scratch),
        cost_estimate=pl.CostEstimate(flops=cost[0], bytes_accessed=cost[1], transcendentals=0),
        compiler_params=pltpu.CompilerParams(vmem_limit_bytes=limit * 2**20),
        **kw,
    )


def sds(shape, dtype):
    return jax.ShapeDtypeStruct(shape, dtype)


def dot(a, b):
    return jnp.dot(a, b, preferred_element_type=F32)


PAIR = 4
PACK_LIMIT = 16


def spread(d):
    return (d // PAIR) * 2 * PAIR + d % PAIR


def own_hi_lo():
    e = lax.axis_index("exp")
    return lax.div(e, 2 * PAIR) * PAIR + lax.rem(e, PAIR), lax.rem(lax.div(e, PAIR), 2)


def aligned(x, n):
    return pl.multiple_of(x, n)


def run_copies(pairs, sems):
    copies = [pltpu.make_async_copy(src, dst, sems.at[i]) for i, (src, dst) in enumerate(pairs)]
    for c in copies:
        c.start()
    for c in copies:
        c.wait()


def pack_kernel(C, qw, q_ref, new_ref, past_ref, *refs):
    outs, sems = refs[:C], refs[C]
    c = lax.axis_index("ctx")
    _, lo = own_hi_lo()
    kv = new_ref.shape[1]
    pairs = []
    for s in reversed(range(C)):
        target = jnp.bitwise_xor(c, s)
        out = outs[s]
        for t in range(2):
            shard = lax.div(target, PAIR) * 2 * PAIR + lax.rem(target, PAIR)
            shard = shard + PAIR * jnp.bitwise_xor(lo, t)
            at = pl.ds(aligned(shard * qw, 128), qw)
            pairs.append((q_ref.at[:, at], out.at[:, t * qw : (t + 1) * qw]))
        pairs.append((new_ref, out.at[:, 2 * qw : 2 * qw + kv]))
        pairs.append((past_ref, out.at[:, 2 * qw + kv :]))
    run_copies(pairs, sems)


def attend_kernel(C, t, *refs):
    msgs, out, kv_s, q_s = refs[:C], refs[C], refs[-2], refs[-1]
    if t == 1:
        refs[C + 1][...] = msgs[0][...]
    c = lax.axis_index("ctx")
    tok, qw = msgs[0].shape[0], out.shape[1]
    rows = C * tok
    _, lo = own_hi_lo()
    shard = lax.div(c, PAIR) * 2 * PAIR + lax.rem(c, PAIR) + PAIR * jnp.bitwise_xor(lo, t)
    head = lax.div(shard * (qw // HEAD_SIZE), GROUP_EXTENT)
    for s in range(C):
        msg = msgs[s]
        at = aligned(jnp.bitwise_xor(c, s) * tok, tok)
        q_s[pl.ds(at, tok), :] = msg[:, t * qw : (t + 1) * qw]
        for i, to in ((0, rows + at), (1, at)):
            for part in range(2):
                first = 2 * qw + (i * 2 + part) * KEY_VALUE_HEADS * HEAD_SIZE
                cols = pl.ds(aligned(first + head * HEAD_SIZE, 128), HEAD_SIZE)
                kv_s[pl.ds(to, tok), part * HEAD_SIZE : (part + 1) * HEAD_SIZE] = msg[:, cols]
    block = 128
    for b in range(rows // block):
        seen = rows + (b + 1) * block
        k = kv_s[:seen, :HEAD_SIZE]
        v = kv_s[:seen, HEAD_SIZE:]
        row = lax.broadcasted_iota(jnp.int32, (block, seen), 0) + (rows + b * block)
        visible = lax.broadcasted_iota(jnp.int32, (block, seen), 1) <= row
        at = slice(b * block, (b + 1) * block)
        for h in range(qw // HEAD_SIZE):
            q = q_s[at, h * HEAD_SIZE : (h + 1) * HEAD_SIZE]
            scores = lax.dot_general(q, k, (((1,), (1,)), ((), ())), preferred_element_type=F32)
            scores = jnp.where(visible, scores * HEAD_SIZE ** (-0.5), NEG_FILL)
            weights = jnp.exp(scores - jnp.max(scores, axis=1, keepdims=True))
            total = jnp.sum(weights, axis=1, keepdims=True)
            numerator = dot(weights.astype(BF16), v)
            out[at, h * HEAD_SIZE : (h + 1) * HEAD_SIZE] = (numerator / total).astype(BF16)


def route_kernel(E, cap, routes_ref, gates_ref, *refs):
    place_ref, gate_ref, line_s, gate_s = refs[2], refs[3], refs[-2], refs[-1]
    for src, dst in zip(refs[:2], refs[4:6]):
        dst[...] = src[...]
    e = lax.axis_index("exp")
    blocks, _, tok = routes_ref.shape
    rows = blocks * tok
    for i in range(blocks):
        routes = routes_ref[i]
        resident = routes < E
        target = jnp.sum(jnp.where(resident, routes + 1, 0), axis=0, keepdims=True) - 1
        gate = jnp.sum(jnp.where(resident, gates_ref[i], 0.0), axis=0, keepdims=True)
        line_s[:, i * tok : (i + 1) * tok] = jnp.broadcast_to(target, (8, tok))
        gate_s[:, i * tok : (i + 1) * tok] = jnp.broadcast_to(gate, (128, tok))
    target = line_s[:1, :]
    gate_ref[...] = gate_s[...].T
    has = target >= 0
    experts = lax.broadcasted_iota(jnp.int32, (E, rows), 0)
    one_hot = jnp.where(target == experts, 1.0, 0.0)
    earlier = jnp.where(
        lax.broadcasted_iota(jnp.int32, (rows, rows), 0)
        < lax.broadcasted_iota(jnp.int32, (rows, rows), 1),
        1.0,
        0.0,
    ).astype(BF16)
    rank = jnp.sum(dot(one_hot.astype(BF16), earlier) * one_hot, axis=0, keepdims=True)
    slot = jnp.bitwise_xor(target, e) * cap + rank.astype(jnp.int32)
    slot = jnp.where(has, slot, -1)
    places = lax.broadcasted_iota(jnp.int32, (E * cap, rows), 0)
    place_ref[...] = jnp.where(slot == places, 1.0, 0.0).astype(BF16)


def project_kernel(C, cut, with_residual, *refs):
    refs, (acc, last, stacked) = list(refs[:-3]), refs[-3:]
    res = refs.pop(0) if with_residual else None
    atts, ws = refs[:C], refs[C:]
    hi, _ = own_hi_lo()
    turn = jnp.bitwise_xor(lax.axis_index("ctx"), hi)
    for s in range(C):
        stacked[jnp.bitwise_xor(turn, s)] = atts[s][...]
    last[...] = stacked[C - 1]
    width = acc.shape[1]
    for j, at in enumerate((slice(0, cut), slice(cut, width))):
        total = res[:, at].astype(F32) if with_residual else None
        for d in range(C - 1):
            if d < 2:
                w = ws[d][:, at]
            else:
                w = ws[2 * d - 2 + j][...]
            term = dot(stacked[d], w)
            total = term if total is None else total + term
        acc[:, at] = total


def last_kernel(E, cap, *refs):
    accs, lasts, ws, places = refs[:2], refs[2:4], refs[4:6], refs[6:8]
    own_ref, *full_refs, keep_ref, send_ref = refs[8:]
    cut = ws[0].shape[1]
    for j, cols in enumerate((slice(0, cut), slice(cut, own_ref.shape[1]))):
        for t in (1, 0):
            total = accs[t][:, cols] + dot(lasts[t][...], ws[j][...])
            rounded = total.astype(BF16)
            if t == 0:
                own_ref[:, cols] = total
            else:
                first = 0
                for full in full_refs:
                    full[:, cols] = rounded[first : first + full.shape[0]]
                    first += full.shape[0]
            picked = dot(places[t][...], rounded)
            for d in range(E // 2):
                near, far = spread(d) ^ (PAIR * t), spread(d) ^ PAIR ^ (PAIR * t)
                at = (2 * d + t) * cap
                keep_ref[at : at + cap, cols] = picked[near * cap : (near + 1) * cap]
                at = (2 * d + 1 - t) * cap
                send_ref[at : at + cap, cols] = picked[far * cap : (far + 1) * cap].astype(BF16)


def outgoing_kernel(keep_ref, got_ref, gain_ref, *outs):
    scaled = ((keep_ref[...] + got_ref[...].astype(F32)) * gain_ref[...]).astype(BF16)
    count = outs[0].shape[0]
    for d, out in enumerate(outs):
        out[...] = scaled[d * count : (d + 1) * count]


def gate_up_kernel(C, E, cap, order, *refs):
    xs, gain_ref, w_ref, keep_ref, send_ref, x_s, part_s = refs[: E // 2], *refs[E // 2 :]
    c = lax.axis_index("ctx")
    e = lax.axis_index("exp")
    own_rows = E * cap // C
    wide = w_ref.shape[1]
    for d in range(E // 2):
        for t in range(2):
            at = aligned(jnp.bitwise_xor(e, spread(d) ^ (PAIR * t)) * cap, cap)
            x_s[pl.ds(at, cap), :] = xs[d][t * cap : (t + 1) * cap, :]
    plain = x_s[...].astype(F32) / gain_ref[...]
    square = jnp.sum(plain * plain, axis=1, keepdims=True)
    lane = lax.broadcasted_iota(jnp.int32, (E * cap, 128), 1)
    part_s[:, wide:] = jnp.where(lane == 0, square, 0.0)
    step = 512
    for j in range(wide // step):
        at = slice(j * step, (j + 1) * step)
        part_s[:, at] = dot(x_s[...], w_ref[:, at])
    for i, r in enumerate(order):
        at = aligned(jnp.bitwise_xor(c, r) * own_rows, own_rows)
        block = part_s[pl.ds(at, own_rows), :]
        if i < C // 2:
            keep_ref[i * own_rows : (i + 1) * own_rows, :] = block
        else:
            to = (i - C // 2) * own_rows
            send_ref[to : to + own_rows, :wide] = block[:, :wide].astype(BF16)
            square = block[:, wide:]
            high = square.astype(BF16).astype(F32)
            lane = lax.broadcasted_iota(jnp.int32, square.shape, 1)
            low = pltpu.roll(square - high, 1, 1)
            pair = jnp.where(lane == 1, low, high)
            send_ref[to : to + own_rows, wide:] = pair.astype(BF16)


def halve_kernel(keep_in, got_ref, keep_ref, send_ref):
    rows = keep_ref.shape[0]
    wide = keep_ref.shape[1] - 128
    total = keep_in[...] + got_ref[...].astype(F32)
    keep_ref[...] = total[:rows]
    send_ref[:, :wide] = total[rows:, :wide].astype(BF16)
    square = jnp.sum(total[rows:, wide:], axis=1, keepdims=True)
    high = square.astype(BF16).astype(F32)
    lane = lax.broadcasted_iota(jnp.int32, (rows, 128), 1)
    pair = jnp.where(lane == 0, high, jnp.where(lane == 1, square - high, 0.0))
    send_ref[:, wide:] = pair.astype(BF16)


def activate_kernel(hidden, keep_ref, got_ref, out):
    def summed(at):
        return keep_ref[:, at] + got_ref[:, at].astype(F32)

    square = jnp.sum(summed(slice(2 * hidden, 2 * hidden + 128)), axis=1, keepdims=True)
    scale = lax.rsqrt(square / D + 1e-6)
    gate = summed(slice(0, hidden)) * scale
    up = summed(slice(hidden, 2 * hidden)) * scale
    out[...] = (gate / (1.0 + jnp.exp(-gate)) * up).astype(BF16)


def down_kernel(C, E, cap, *refs):
    acts, w_ref, outs, x_s, part_s = refs[:C], refs[C], refs[C + 1 : C + 1 + E // 2], refs[-2], refs[-1]
    c = lax.axis_index("ctx")
    e = lax.axis_index("exp")
    own_rows = E * cap // C
    for s in range(C):
        at = aligned(jnp.bitwise_xor(c, s) * own_rows, own_rows)
        x_s[pl.ds(at, own_rows), :] = acts[s][...]
    part_s[...] = dot(x_s[...], w_ref[...]).astype(BF16)
    for d in range(E // 2):
        for t in range(2):
            at = aligned(jnp.bitwise_xor(e, spread(d) ^ (PAIR * t)) * cap, cap)
            outs[d][t * cap : (t + 1) * cap, :] = part_s[pl.ds(at, cap), :]


def forward_kernel(cap, *refs):
    for d, x in enumerate(refs[:-1]):
        refs[-1][d * cap : (d + 1) * cap, :] = x[cap:, :]


def combine_kernel(E, cap, own, got0, got1, place_ref, gate_ref, *refs):
    xs, far, out, x_s = refs[: E // 2], refs[E // 2], refs[E // 2 + 1], refs[E // 2 + 2]
    for d in range(E // 2):
        at = spread(d) * cap
        x_s[at : at + cap, :] = xs[d][:cap, :]
        at = (spread(d) ^ PAIR) * cap
        x_s[at : at + cap, :] = far[d * cap : (d + 1) * cap, :]
    half = own.shape[1] // 2
    for j in range(2):
        cols = slice(j * half, (j + 1) * half)
        collected = lax.dot_general(
            place_ref[...], x_s[:, cols], (((0,), (0,)), ((), ())), preferred_element_type=F32
        )
        few = got0.shape[0]
        for got, at in ((got0, slice(0, few)), (got1, slice(few, own.shape[0]))):
            mixed = own[at, cols] + got[:, cols].astype(F32)
            out[at, cols] = (mixed + gate_ref[at, :1] * collected[at]).astype(BF16)


def body(
    queries,
    new_keys_values,
    cached_keys_values,
    residual,
    out_weight,
    norm_gain,
    routes,
    gates,
    w_gate_up,
    w_down,
):
    C = lax.axis_size("ctx")
    E = lax.axis_size("exp")
    tok = queries.shape[2]
    rows = C * tok
    width = residual.shape[3]
    hidden = w_down.shape[1]
    wide = 2 * hidden
    cap = rows // (2 * E)
    slots = E * cap
    own_rows = slots // C
    qw = QUERY_HEADS // E * HEAD_SIZE

    def permute(x, ctx=0, exp=0):
        pairs = [(c * E + e, (c ^ ctx) * E + (e ^ exp)) for c in range(C) for e in range(E)]
        return lax.ppermute(x, ("ctx", "exp"), pairs)

    def after(x, *others):
        return lax.optimization_barrier((x, *others))[0]

    cut = width // 2
    kv = new_keys_values.shape[3]
    msgs = call(
        functools.partial(pack_kernel, C, qw),
        [sds((tok, 2 * qw + 2 * kv), BF16)] * C,
        3,
        scratch=[pltpu.SemaphoreType.DMA((4 * C,))],
        in_specs=[HBM] * 3,
        cost=(0, 2**20),
        limit=PACK_LIMIT,
    )(
        queries.reshape(tok, queries.shape[3]),
        new_keys_values.reshape(tok, kv),
        cached_keys_values.reshape(tok, kv),
    )
    res = residual.reshape(rows, width)
    got = [msgs[0]] + [permute(msgs[s], ctx=s) for s in range(1, C)]
    shards = {0: [out_weight], 1: [permute(out_weight, exp=1)]}
    for d in range(2, C, 2):
        shards[d] = [permute(out_weight[:, :cut], exp=spread(d))]
    step = [shards[d][0] for d in range(2, C, 2)]
    got[1] = after(got[1], *step)
    for d in range(2, C, 2):
        shards[d].append(permute(after(out_weight[:, cut:], *step), exp=spread(d)))
        shards[d + 1] = [permute(after(w, *got), exp=1) for w in shards[d]]
    step = shards[1] + [shards[d][1] for d in range(2, C, 2)]

    step2 = step

    def attend(t, msgs):
        return call(
            functools.partial(attend_kernel, C, t),
            [sds((rows, qw), BF16)] + [sds(msgs[0].shape, BF16)] * t,
            C,
            scratch=[pltpu.VMEM((2 * rows, 2 * HEAD_SIZE), BF16), pltpu.VMEM((rows, qw), BF16)],
            cost=(0, 2**14),
            limit=16,
        )(*msgs)

    other, own_msg = attend(1, got)
    theirs = permute(other, exp=PAIR)
    (mine,) = attend(0, [own_msg, after(got[1], other)] + got[2:])
    tokens_last = lambda x: jnp.transpose(x.reshape(C, tok, x.shape[3]), (0, 2, 1))
    place, gate, *staged = call(
        functools.partial(route_kernel, E, cap),
        [sds((slots, rows), BF16), sds((rows, 128), F32)]
        + [sds((qw, width), BF16), sds((rows, width), BF16)],
        4,
        scratch=[pltpu.VMEM((8, rows), jnp.int32), pltpu.VMEM((128, rows), F32)],
        cost=(0, 2**14),
        limit=16,
    )(tokens_last(after(routes, mine)), tokens_last(after(gates, mine)), out_weight, res)
    shards[0], res = staged[:1], staged[1]

    def gather(x, before):
        atts = {0: x, 1: permute(x, ctx=1)}
        for s in range(2, C, 2):
            atts[s] = permute(x, ctx=s)
            atts[s + 1] = permute(after(atts[s], *before), ctx=1)
        return [atts[s] for s in range(C)]

    other_place = permute(after(place, theirs), exp=PAIR)
    step = shards[C - 1]
    mine_all = gather(mine, [])
    theirs_all = gather(after(theirs, place, *step2), [])
    mine_all[1] = after(mine_all[1], other_place, *step)

    def project(atts, *extra):
        operands = [*extra, *atts, *[w for d in range(C - 1) for w in shards[d]]]
        return call(
            functools.partial(project_kernel, C, cut, bool(extra)),
            [sds((rows, width), F32), sds((rows, qw), BF16)],
            len(operands),
            scratch=[
                pltpu.VMEM((C, rows, qw), BF16),
            ],
            cost=(0, 2**14),
        )(*operands)

    acc, last = project(mine_all, res)
    acc_far, last_far = project(theirs_all)
    gain = norm_gain.reshape(1, width)
    parts = (rows // 4, rows * 3 // 4)
    own, *full, keep, send = call(
        functools.partial(last_kernel, E, cap),
        [
            sds((rows, width), F32),
            *[sds((n, width), BF16) for n in parts],
            sds((slots, width), F32),
            sds((slots, width), BF16),
        ],
        8,
        cost=(4 * rows * (qw + slots) * width, 2**20),
    )(acc, acc_far, last, last_far, *shards[C - 1], place, other_place)
    received = permute(send, exp=PAIR)
    outgoing = call(
        outgoing_kernel, [sds((2 * cap, width), BF16)] * (E // 2), 3, cost=(0, 2**20)
    )(keep, received, gain)
    incoming = {0: outgoing[0]}
    for d in reversed(range(1, E // 2)):
        incoming[d] = permute(outgoing[d], exp=spread(d))
    incoming = [incoming[d] for d in range(E // 2)]
    arrived = [permute(after(full[0], received), exp=PAIR)]
    incoming[0] = after(incoming[0], arrived[0])
    arrived.append(permute(after(full[1], arrived[0]), exp=PAIR))

    order = [0]
    bit = C // 2
    while bit:
        order = order + [r | bit for r in order]
        bit //= 2
    keep, send = call(
        functools.partial(gate_up_kernel, C, E, cap, order),
        [sds((slots // 2, wide + 128), F32), sds((slots // 2, wide + 128), BF16)],
        E // 2 + 2,
        scratch=[pltpu.VMEM((slots, width), BF16), pltpu.VMEM((slots, wide + 128), F32)],
        cost=(2 * slots * width * wide, 2 * width * wide),
    )(*incoming, gain, w_gate_up.reshape(width, wide))
    bit = 1
    while 2 * bit < C:
        count = keep.shape[0] // 2
        keep, send = call(
            halve_kernel,
            [sds((count, wide + 128), F32), sds((count, wide + 128), BF16)],
            2,
            cost=(0, 2**10),
        )(keep, permute(send, ctx=bit))
        bit *= 2
    activated = call(
        functools.partial(activate_kernel, hidden),
        sds((own_rows, hidden), BF16),
        2,
        cost=(0, 2**10),
    )(keep, permute(send, ctx=bit))
    acts = {0: activated}
    acts[bit] = after(permute(activated, ctx=bit), arrived[1])
    bit //= 2
    while bit:
        for r in list(acts):
            acts[r ^ bit] = permute(acts[r], ctx=bit)
        bit //= 2
    expert_out = call(
        functools.partial(down_kernel, C, E, cap),
        [sds((2 * cap, width), BF16)] * (E // 2),
        C + 1,
        scratch=[pltpu.VMEM((slots, hidden), BF16), pltpu.VMEM((slots, width), BF16)],
        cost=(2 * slots * width * hidden, 2 * width * hidden),
    )(acts[0], *[acts[s] for s in range(1, C)], w_down.reshape(hidden, width))
    returned = [expert_out[0]]
    returned += [permute(expert_out[d], exp=spread(d)) for d in reversed(range(1, E // 2))][::-1]
    far = call(
        functools.partial(forward_kernel, cap), sds((slots // 2, width), BF16), E // 2, cost=(0, 2**19)
    )(*returned)
    result = call(
        functools.partial(combine_kernel, E, cap),
        sds((rows, width), BF16),
        6 + E // 2,
        scratch=[pltpu.VMEM((slots, width), BF16)],
        cost=(0, 2 * 2**20),
    )(own, *arrived, place, gate, *returned, permute(far, exp=PAIR))
    return result.reshape(C, 1, tok, width)


def solution(mesh):
    in_specs = (
        P("ctx", "exp", None, None),
        P("ctx", "exp", None, None),
        P("ctx", "exp", None, None),
        P(None, "exp", None, "ctx"),
        P("exp", "ctx"),
        P("ctx"),
        P(None, "exp", None, None),
        P(None, "exp", None, None),
        P("exp", "ctx", None),
        P("exp", None, "ctx"),
    )
    out_specs = P(None, "exp", None, "ctx")
    return jax.shard_map(body, mesh=mesh, in_specs=in_specs, out_specs=out_specs, check_vma=False)
```

```python
import functools

import jax
import jax.numpy as jnp
from jax import lax
from jax.experimental import pallas as pl
from jax.experimental.pallas import tpu as pltpu
from jax.sharding import PartitionSpec as P

D = 4096
QUERY_HEADS = 32
KEY_VALUE_HEADS = 2
HEAD_SIZE = 128
GROUP_EXTENT = QUERY_HEADS // KEY_VALUE_HEADS
NEG_FILL = -1e30
BF16 = jnp.bfloat16
F32 = jnp.float32
VMEM = pl.BlockSpec(memory_space=pltpu.VMEM)
HBM = pl.BlockSpec(memory_space=pltpu.HBM)
ANY = pl.BlockSpec(memory_space=pl.ANY)


def call(kernel, out_shape, n_in, scratch=(), cost=(0, 0), limit=32, **kw):
    kw.setdefault("in_specs", [VMEM] * n_in)
    kw.setdefault("out_specs", jax.tree.map(lambda _: VMEM, out_shape))
    return pl.pallas_call(
        kernel,
        out_shape=out_shape,
        scratch_shapes=list(scratch),
        cost_estimate=pl.CostEstimate(flops=cost[0], bytes_accessed=cost[1], transcendentals=0),
        compiler_params=pltpu.CompilerParams(vmem_limit_bytes=limit * 2**20),
        **kw,
    )


def sds(shape, dtype):
    return jax.ShapeDtypeStruct(shape, dtype)


def dot(a, b):
    return jnp.dot(a, b, preferred_element_type=F32)


PAIR = 4
PACK_LIMIT = 16


def spread(d):
    return (d // PAIR) * 2 * PAIR + d % PAIR


def own_hi_lo():
    e = lax.axis_index("exp")
    return lax.div(e, 2 * PAIR) * PAIR + lax.rem(e, PAIR), lax.rem(lax.div(e, PAIR), 2)


def aligned(x, n):
    return pl.multiple_of(x, n)


def run_copies(pairs, sems):
    copies = [pltpu.make_async_copy(src, dst, sems.at[i]) for i, (src, dst) in enumerate(pairs)]
    for c in copies:
        c.start()
    for c in copies:
        c.wait()


def pack_kernel(C, qw, q_ref, new_ref, past_ref, *refs):
    outs, sems = refs[:C], refs[C]
    c = lax.axis_index("ctx")
    _, lo = own_hi_lo()
    kv = new_ref.shape[1]
    pairs = []
    for s in reversed(range(C)):
        target = jnp.bitwise_xor(c, s)
        out = outs[s]
        for t in range(2):
            shard = lax.div(target, PAIR) * 2 * PAIR + lax.rem(target, PAIR)
            shard = shard + PAIR * jnp.bitwise_xor(lo, t)
            at = pl.ds(aligned(shard * qw, 128), qw)
            pairs.append((q_ref.at[:, at], out.at[:, t * qw : (t + 1) * qw]))
        pairs.append((new_ref, out.at[:, 2 * qw : 2 * qw + kv]))
        pairs.append((past_ref, out.at[:, 2 * qw + kv :]))
    run_copies(pairs, sems)


def attend_kernel(C, t, *refs):
    msgs, out, kv_s, q_s = refs[:C], refs[C], refs[-2], refs[-1]
    if t == 1:
        refs[C + 1][...] = msgs[0][...]
    c = lax.axis_index("ctx")
    tok, qw = msgs[0].shape[0], out.shape[1]
    rows = C * tok
    _, lo = own_hi_lo()
    shard = lax.div(c, PAIR) * 2 * PAIR + lax.rem(c, PAIR) + PAIR * jnp.bitwise_xor(lo, t)
    head = lax.div(shard * (qw // HEAD_SIZE), GROUP_EXTENT)
    for s in range(C):
        msg = msgs[s]
        at = aligned(jnp.bitwise_xor(c, s) * tok, tok)
        q_s[pl.ds(at, tok), :] = msg[:, t * qw : (t + 1) * qw]
        for i, to in ((0, rows + at), (1, at)):
            for part in range(2):
                first = 2 * qw + (i * 2 + part) * KEY_VALUE_HEADS * HEAD_SIZE
                cols = pl.ds(aligned(first + head * HEAD_SIZE, 128), HEAD_SIZE)
                kv_s[pl.ds(to, tok), part * HEAD_SIZE : (part + 1) * HEAD_SIZE] = msg[:, cols]
    block = 128
    for b in range(rows // block):
        seen = rows + (b + 1) * block
        k = kv_s[:seen, :HEAD_SIZE]
        v = kv_s[:seen, HEAD_SIZE:]
        row = lax.broadcasted_iota(jnp.int32, (block, seen), 0) + (rows + b * block)
        visible = lax.broadcasted_iota(jnp.int32, (block, seen), 1) <= row
        at = slice(b * block, (b + 1) * block)
        for h in range(qw // HEAD_SIZE):
            q = q_s[at, h * HEAD_SIZE : (h + 1) * HEAD_SIZE]
            scores = lax.dot_general(q, k, (((1,), (1,)), ((), ())), preferred_element_type=F32)
            scores = jnp.where(visible, scores * HEAD_SIZE ** (-0.5), NEG_FILL)
            weights = jnp.exp(scores - jnp.max(scores, axis=1, keepdims=True))
            total = jnp.sum(weights, axis=1, keepdims=True)
            numerator = dot(weights.astype(BF16), v)
            out[at, h * HEAD_SIZE : (h + 1) * HEAD_SIZE] = (numerator / total).astype(BF16)


def route_kernel(E, cap, routes_ref, gates_ref, *refs):
    place_ref, gate_ref, line_s, gate_s = refs[2], refs[3], refs[-2], refs[-1]
    for src, dst in zip(refs[:2], refs[4:6]):
        dst[...] = src[...]
    e = lax.axis_index("exp")
    blocks, _, tok = routes_ref.shape
    rows = blocks * tok
    for i in range(blocks):
        routes = routes_ref[i]
        resident = routes < E
        target = jnp.sum(jnp.where(resident, routes + 1, 0), axis=0, keepdims=True) - 1
        gate = jnp.sum(jnp.where(resident, gates_ref[i], 0.0), axis=0, keepdims=True)
        line_s[:, i * tok : (i + 1) * tok] = jnp.broadcast_to(target, (8, tok))
        gate_s[:, i * tok : (i + 1) * tok] = jnp.broadcast_to(gate, (128, tok))
    target = line_s[:1, :]
    gate_ref[...] = gate_s[...].T
    has = target >= 0
    experts = lax.broadcasted_iota(jnp.int32, (E, rows), 0)
    one_hot = jnp.where(target == experts, 1.0, 0.0)
    earlier = jnp.where(
        lax.broadcasted_iota(jnp.int32, (rows, rows), 0)
        < lax.broadcasted_iota(jnp.int32, (rows, rows), 1),
        1.0,
        0.0,
    ).astype(BF16)
    rank = jnp.sum(dot(one_hot.astype(BF16), earlier) * one_hot, axis=0, keepdims=True)
    slot = jnp.bitwise_xor(target, e) * cap + rank.astype(jnp.int32)
    slot = jnp.where(has, slot, -1)
    places = lax.broadcasted_iota(jnp.int32, (E * cap, rows), 0)
    place_ref[...] = jnp.where(slot == places, 1.0, 0.0).astype(BF16)


def project_kernel(C, with_residual, *refs):
    refs, (acc, last, stacked) = list(refs[:-3]), refs[-3:]
    res = refs.pop(0) if with_residual else None
    atts, ws = refs[:C], refs[C:]
    hi, _ = own_hi_lo()
    turn = jnp.bitwise_xor(lax.axis_index("ctx"), hi)
    for s in range(C):
        stacked[jnp.bitwise_xor(turn, s)] = atts[s][...]
    last[...] = stacked[C - 1]
    half = acc.shape[1] // 2
    for j in range(2):
        at = slice(j * half, (j + 1) * half)
        total = res[:, at].astype(F32) if with_residual else None
        for d in range(C - 1):
            term = dot(stacked[d], ws[d][:, at])
            total = term if total is None else total + term
        acc[:, at] = total


def last_kernel(E, cap, *refs):
    accs, lasts, w_ref, places = refs[:2], refs[2:4], refs[4], refs[5:7]
    own_ref, full_ref, keep_ref, send_ref = refs[7:]
    half = w_ref.shape[1] // 2
    for j in range(2):
        cols = slice(j * half, (j + 1) * half)
        for t in (1, 0):
            total = accs[t][:, cols] + dot(lasts[t][...], w_ref[:, cols])
            rounded = total.astype(BF16)
            if t == 0:
                own_ref[:, cols] = total
            else:
                full_ref[:, cols] = rounded
            picked = dot(places[t][...], rounded)
            for d in range(E // 2):
                near, far = spread(d) ^ (PAIR * t), spread(d) ^ PAIR ^ (PAIR * t)
                at = (2 * d + t) * cap
                keep_ref[at : at + cap, cols] = picked[near * cap : (near + 1) * cap]
                at = (2 * d + 1 - t) * cap
                send_ref[at : at + cap, cols] = picked[far * cap : (far + 1) * cap].astype(BF16)


def outgoing_kernel(keep_ref, got_ref, gain_ref, *outs):
    scaled = ((keep_ref[...] + got_ref[...].astype(F32)) * gain_ref[...]).astype(BF16)
    count = outs[0].shape[0]
    for d, out in enumerate(outs):
        out[...] = scaled[d * count : (d + 1) * count]


def gate_up_kernel(C, E, cap, order, *refs):
    xs, gain_ref, w_ref, keep_ref, *sends, x_s, part_s = refs[: E // 2], *refs[E // 2 :]
    c = lax.axis_index("ctx")
    e = lax.axis_index("exp")
    own_rows = E * cap // C
    wide = w_ref.shape[1]
    for d in range(E // 2):
        for t in range(2):
            at = aligned(jnp.bitwise_xor(e, spread(d) ^ (PAIR * t)) * cap, cap)
            x_s[pl.ds(at, cap), :] = xs[d][t * cap : (t + 1) * cap, :]
    plain = x_s[...].astype(F32) / gain_ref[...]
    square = jnp.sum(plain * plain, axis=1, keepdims=True)
    lane = lax.broadcasted_iota(jnp.int32, (E * cap, 128), 1)
    part_s[:, wide:] = jnp.where(lane == 0, square, 0.0)
    step = 512
    for j in range(wide // step):
        at = slice(j * step, (j + 1) * step)
        part_s[:, at] = dot(x_s[...], w_ref[:, at])
    for i, r in enumerate(order):
        at = aligned(jnp.bitwise_xor(c, r) * own_rows, own_rows)
        block = part_s[pl.ds(at, own_rows), :]
        if i < C // 2:
            keep_ref[i * own_rows : (i + 1) * own_rows, :] = block
        else:
            first = (i - C // 2) * own_rows
            send_ref = sends[first // sends[0].shape[0]]
            to = first % sends[0].shape[0]
            send_ref[to : to + own_rows, :wide] = block[:, :wide].astype(BF16)
            square = block[:, wide:]
            high = square.astype(BF16).astype(F32)
            lane = lax.broadcasted_iota(jnp.int32, square.shape, 1)
            low = pltpu.roll(square - high, 1, 1)
            pair = jnp.where(lane == 1, low, high)
            send_ref[to : to + own_rows, wide:] = pair.astype(BF16)


def halve_kernel(keep_in, got0, got1, keep_ref, send_ref):
    rows = keep_ref.shape[0]
    wide = keep_ref.shape[1] - 128
    keep_ref[...] = keep_in[:rows, :] + got0[...].astype(F32)
    total = keep_in[rows:, :] + got1[...].astype(F32)
    send_ref[:, :wide] = total[:, :wide].astype(BF16)
    square = jnp.sum(total[:, wide:], axis=1, keepdims=True)
    high = square.astype(BF16).astype(F32)
    lane = lax.broadcasted_iota(jnp.int32, (rows, 128), 1)
    pair = jnp.where(lane == 0, high, jnp.where(lane == 1, square - high, 0.0))
    send_ref[:, wide:] = pair.astype(BF16)


def activate_kernel(hidden, keep_ref, got_ref, out):
    def summed(at):
        return keep_ref[:, at] + got_ref[:, at].astype(F32)

    square = jnp.sum(summed(slice(2 * hidden, 2 * hidden + 128)), axis=1, keepdims=True)
    scale = lax.rsqrt(square / D + 1e-6)
    gate = summed(slice(0, hidden)) * scale
    up = summed(slice(hidden, 2 * hidden)) * scale
    out[...] = (gate / (1.0 + jnp.exp(-gate)) * up).astype(BF16)


def down_kernel(C, E, cap, *refs):
    acts, w_ref, outs, x_s, part_s = refs[:C], refs[C], refs[C + 1 : C + 1 + E // 2], refs[-2], refs[-1]
    c = lax.axis_index("ctx")
    e = lax.axis_index("exp")
    own_rows = E * cap // C
    for s in range(C):
        at = aligned(jnp.bitwise_xor(c, s) * own_rows, own_rows)
        x_s[pl.ds(at, own_rows), :] = acts[s][...]
    part_s[...] = dot(x_s[...], w_ref[...]).astype(BF16)
    for d in range(E // 2):
        for t in range(2):
            at = aligned(jnp.bitwise_xor(e, spread(d) ^ (PAIR * t)) * cap, cap)
            outs[d][t * cap : (t + 1) * cap, :] = part_s[pl.ds(at, cap), :]


def forward_kernel(cap, *refs):
    for d, x in enumerate(refs[:-1]):
        refs[-1][d * cap : (d + 1) * cap, :] = x[cap:, :]


def combine_kernel(E, cap, own, got, place_ref, gate_ref, *refs):
    xs, far, out, x_s = refs[: E // 2], refs[E // 2], refs[E // 2 + 1], refs[E // 2 + 2]
    for d in range(E // 2):
        at = spread(d) * cap
        x_s[at : at + cap, :] = xs[d][:cap, :]
        at = (spread(d) ^ PAIR) * cap
        x_s[at : at + cap, :] = far[d * cap : (d + 1) * cap, :]
    half = own.shape[1] // 2
    for j in range(2):
        cols = slice(j * half, (j + 1) * half)
        collected = lax.dot_general(
            place_ref[...], x_s[:, cols], (((0,), (0,)), ((), ())), preferred_element_type=F32
        )
        mixed = own[:, cols] + got[:, cols].astype(F32)
        out[:, cols] = (mixed + gate_ref[:, :1] * collected).astype(BF16)


def body(
    queries,
    new_keys_values,
    cached_keys_values,
    residual,
    out_weight,
    norm_gain,
    routes,
    gates,
    w_gate_up,
    w_down,
):
    C = lax.axis_size("ctx")
    E = lax.axis_size("exp")
    tok = queries.shape[2]
    rows = C * tok
    width = residual.shape[3]
    hidden = w_down.shape[1]
    wide = 2 * hidden
    cap = rows // (2 * E)
    slots = E * cap
    own_rows = slots // C
    qw = QUERY_HEADS // E * HEAD_SIZE

    def permute(x, ctx=0, exp=0):
        pairs = [(c * E + e, (c ^ ctx) * E + (e ^ exp)) for c in range(C) for e in range(E)]
        return lax.ppermute(x, ("ctx", "exp"), pairs)

    def after(x, *others):
        return lax.optimization_barrier((x, *others))[0]

    kv = new_keys_values.shape[3]
    msgs = call(
        functools.partial(pack_kernel, C, qw),
        [sds((tok, 2 * qw + 2 * kv), BF16)] * C,
        3,
        scratch=[pltpu.SemaphoreType.DMA((4 * C,))],
        in_specs=[HBM] * 3,
        cost=(0, 2**20),
        limit=PACK_LIMIT,
    )(
        queries.reshape(tok, queries.shape[3]),
        new_keys_values.reshape(tok, kv),
        cached_keys_values.reshape(tok, kv),
    )
    res = residual.reshape(rows, width)
    got = [msgs[0]] + [permute(msgs[s], ctx=s) for s in range(1, C)]
    shards = {0: out_weight, 1: permute(out_weight, exp=1)}
    for d in range(2, C, 2):
        shards[d] = permute(out_weight, exp=spread(d))
    step = [shards[d] for d in range(2, C, 2)]

    def attend(t, msgs):
        return call(
            functools.partial(attend_kernel, C, t),
            [sds((rows, qw), BF16)] + [sds(msgs[0].shape, BF16)] * t,
            C,
            scratch=[pltpu.VMEM((2 * rows, 2 * HEAD_SIZE), BF16), pltpu.VMEM((rows, qw), BF16)],
            cost=(0, 2**14),
            limit=16,
        )(*msgs)

    other, own_msg = attend(1, got)
    theirs = permute(other, exp=PAIR)
    for d in range(2, C, 2):
        shards[d + 1] = permute(after(shards[d], other), exp=1)
    (mine,) = attend(0, [own_msg, after(got[1], other, *step)] + got[2:])
    tokens_last = lambda x: jnp.transpose(x.reshape(C, tok, x.shape[3]), (0, 2, 1))
    place, gate, *staged = call(
        functools.partial(route_kernel, E, cap),
        [sds((slots, rows), BF16), sds((rows, 128), F32)]
        + [sds((qw, width), BF16), sds((rows, width), BF16)],
        4,
        scratch=[pltpu.VMEM((8, rows), jnp.int32), pltpu.VMEM((128, rows), F32)],
        cost=(0, 2**14),
        limit=16,
    )(tokens_last(after(routes, mine)), tokens_last(after(gates, mine)), out_weight, res)
    shards[0], res = staged

    def gather(x, before):
        atts = {0: x, 1: permute(x, ctx=1)}
        for s in range(2, C, 2):
            atts[s] = permute(x, ctx=s)
            atts[s + 1] = permute(after(atts[s], *before), ctx=1)
        return [atts[s] for s in range(C)]

    other_place = permute(after(place, theirs), exp=PAIR)
    mine_all = gather(mine, [])
    theirs_all = gather(after(theirs, place, shards[1], *mine_all[2::2]), [])
    mine_all[1] = after(mine_all[1], other_place)

    def project(atts, *extra):
        operands = [*extra, *atts, *[shards[d] for d in range(C - 1)]]
        return call(
            functools.partial(project_kernel, C, bool(extra)),
            [sds((rows, width), F32), sds((rows, qw), BF16)],
            len(operands),
            scratch=[
                pltpu.VMEM((C, rows, qw), BF16),
            ],
            cost=(0, 2**14),
        )(*operands)

    acc, last = project(mine_all, res)
    acc_far, last_far = project(theirs_all)
    gain = norm_gain.reshape(1, width)
    own, full, keep, send = call(
        functools.partial(last_kernel, E, cap),
        [
            sds((rows, width), F32),
            sds((rows, width), BF16),
            sds((slots, width), F32),
            sds((slots, width), BF16),
        ],
        7,
        cost=(4 * rows * (qw + slots) * width, 2**20),
    )(acc, acc_far, last, last_far, shards[C - 1], place, other_place)
    received = permute(send, exp=PAIR)
    outgoing = call(
        outgoing_kernel, [sds((2 * cap, width), BF16)] * (E // 2), 3, cost=(0, 2**20)
    )(keep, received, gain)
    incoming = {0: outgoing[0]}
    for d in reversed(range(1, E // 2)):
        incoming[d] = permute(outgoing[d], exp=spread(d))
    incoming = [incoming[d] for d in range(E // 2)]
    arrived = permute(after(full, received), exp=PAIR)

    order = [0]
    bit = C // 2
    while bit:
        order = order + [r | bit for r in order]
        bit //= 2
    keep, *sends = call(
        functools.partial(gate_up_kernel, C, E, cap, order),
        [sds((slots // 2, wide + 128), F32)] + [sds((slots // 4, wide + 128), BF16)] * 2,
        E // 2 + 2,
        scratch=[pltpu.VMEM((slots, width), BF16), pltpu.VMEM((slots, wide + 128), F32)],
        cost=(2 * slots * width * wide, 2 * width * wide),
    )(*incoming, gain, w_gate_up.reshape(width, wide))
    bit = 1
    while 2 * bit < C:
        count = keep.shape[0] // 2
        keep, send = call(
            halve_kernel,
            [sds((count, wide + 128), F32), sds((count, wide + 128), BF16)],
            3,
            cost=(0, 2**10),
        )(keep, *[permute(x, ctx=bit) for x in sends])
        sends = [send[: count // 2], send[count // 2 :]]
        bit *= 2
    activated = call(
        functools.partial(activate_kernel, hidden),
        sds((own_rows, hidden), BF16),
        2,
        cost=(0, 2**10),
    )(keep, permute(send, ctx=bit))
    acts = {0: activated}
    acts[bit] = after(permute(activated, ctx=bit), arrived)
    bit //= 2
    while bit:
        for r in list(acts):
            acts[r ^ bit] = permute(acts[r], ctx=bit)
        bit //= 2
    expert_out = call(
        functools.partial(down_kernel, C, E, cap),
        [sds((2 * cap, width), BF16)] * (E // 2),
        C + 1,
        scratch=[pltpu.VMEM((slots, hidden), BF16), pltpu.VMEM((slots, width), BF16)],
        cost=(2 * slots * width * hidden, 2 * width * hidden),
    )(acts[0], *[acts[s] for s in range(1, C)], w_down.reshape(hidden, width))
    returned = [expert_out[0]]
    returned += [permute(expert_out[d], exp=spread(d)) for d in reversed(range(1, E // 2))][::-1]
    far = call(
        functools.partial(forward_kernel, cap), sds((slots // 2, width), BF16), E // 2, cost=(0, 2**19)
    )(*returned)
    result = call(
        functools.partial(combine_kernel, E, cap),
        sds((rows, width), BF16),
        5 + E // 2,
        scratch=[pltpu.VMEM((slots, width), BF16)],
        cost=(0, 2 * 2**20),
    )(own, arrived, place, gate, *returned, permute(far, exp=PAIR))
    return result.reshape(C, 1, tok, width)


def solution(mesh):
    in_specs = (
        P("ctx", "exp", None, None),
        P("ctx", "exp", None, None),
        P("ctx", "exp", None, None),
        P(None, "exp", None, "ctx"),
        P("exp", "ctx"),
        P("ctx"),
        P(None, "exp", None, None),
        P(None, "exp", None, None),
        P("exp", "ctx", None),
        P("exp", None, "ctx"),
    )
    out_specs = P(None, "exp", None, "ctx")
    return jax.shard_map(body, mesh=mesh, in_specs=in_specs, out_specs=out_specs, check_vma=False)
```

```python
import functools

import jax
import jax.numpy as jnp
from jax import lax
from jax.experimental import pallas as pl
from jax.experimental.pallas import tpu as pltpu
from jax.sharding import PartitionSpec as P

D = 4096
QUERY_HEADS = 32
KEY_VALUE_HEADS = 2
HEAD_SIZE = 128
GROUP_EXTENT = QUERY_HEADS // KEY_VALUE_HEADS
NEG_FILL = -1e30
BF16 = jnp.bfloat16
F32 = jnp.float32
VMEM = pl.BlockSpec(memory_space=pltpu.VMEM)
HBM = pl.BlockSpec(memory_space=pltpu.HBM)
ANY = pl.BlockSpec(memory_space=pl.ANY)


def call(kernel, out_shape, n_in, scratch=(), cost=(0, 0), limit=32, **kw):
    kw.setdefault("in_specs", [VMEM] * n_in)
    kw.setdefault("out_specs", jax.tree.map(lambda _: VMEM, out_shape))
    return pl.pallas_call(
        kernel,
        out_shape=out_shape,
        scratch_shapes=list(scratch),
        cost_estimate=pl.CostEstimate(flops=cost[0], bytes_accessed=cost[1], transcendentals=0),
        compiler_params=pltpu.CompilerParams(vmem_limit_bytes=limit * 2**20),
        **kw,
    )


def sds(shape, dtype):
    return jax.ShapeDtypeStruct(shape, dtype)


def dot(a, b):
    return jnp.dot(a, b, preferred_element_type=F32)


PAIR = 4
PACK_LIMIT = 16


def spread(d):
    return (d // PAIR) * 2 * PAIR + d % PAIR


def own_hi_lo():
    e = lax.axis_index("exp")
    return lax.div(e, 2 * PAIR) * PAIR + lax.rem(e, PAIR), lax.rem(lax.div(e, PAIR), 2)


def aligned(x, n):
    return pl.multiple_of(x, n)


def run_copies(pairs, sems):
    copies = [pltpu.make_async_copy(src, dst, sems.at[i]) for i, (src, dst) in enumerate(pairs)]
    for c in copies:
        c.start()
    for c in copies:
        c.wait()


def pack_kernel(C, qw, q_ref, new_ref, past_ref, *refs):
    outs, sems = refs[:C], refs[C]
    c = lax.axis_index("ctx")
    _, lo = own_hi_lo()
    kv = new_ref.shape[1]
    pairs = []
    for s in reversed(range(C)):
        target = jnp.bitwise_xor(c, s)
        out = outs[s]
        for t in range(2):
            shard = lax.div(target, PAIR) * 2 * PAIR + lax.rem(target, PAIR)
            shard = shard + PAIR * jnp.bitwise_xor(lo, t)
            at = pl.ds(aligned(shard * qw, 128), qw)
            pairs.append((q_ref.at[:, at], out.at[:, t * qw : (t + 1) * qw]))
        pairs.append((new_ref, out.at[:, 2 * qw : 2 * qw + kv]))
        pairs.append((past_ref, out.at[:, 2 * qw + kv :]))
    run_copies(pairs, sems)


def attend_kernel(C, t, *refs):
    msgs, out, kv_s, q_s = refs[:C], refs[C], refs[-2], refs[-1]
    if t == 1:
        refs[C + 1][...] = msgs[0][...]
    c = lax.axis_index("ctx")
    tok, qw = msgs[0].shape[0], out.shape[1]
    rows = C * tok
    _, lo = own_hi_lo()
    shard = lax.div(c, PAIR) * 2 * PAIR + lax.rem(c, PAIR) + PAIR * jnp.bitwise_xor(lo, t)
    head = lax.div(shard * (qw // HEAD_SIZE), GROUP_EXTENT)
    for s in range(C):
        msg = msgs[s]
        at = aligned(jnp.bitwise_xor(c, s) * tok, tok)
        q_s[pl.ds(at, tok), :] = msg[:, t * qw : (t + 1) * qw]
        for i, to in ((0, rows + at), (1, at)):
            for part in range(2):
                first = 2 * qw + (i * 2 + part) * KEY_VALUE_HEADS * HEAD_SIZE
                cols = pl.ds(aligned(first + head * HEAD_SIZE, 128), HEAD_SIZE)
                kv_s[pl.ds(to, tok), part * HEAD_SIZE : (part + 1) * HEAD_SIZE] = msg[:, cols]
    block = 128
    for b in range(rows // block):
        seen = rows + (b + 1) * block
        k = kv_s[:seen, :HEAD_SIZE]
        v = kv_s[:seen, HEAD_SIZE:]
        row = lax.broadcasted_iota(jnp.int32, (block, seen), 0) + (rows + b * block)
        visible = lax.broadcasted_iota(jnp.int32, (block, seen), 1) <= row
        at = slice(b * block, (b + 1) * block)
        for h in range(qw // HEAD_SIZE):
            q = q_s[at, h * HEAD_SIZE : (h + 1) * HEAD_SIZE]
            scores = lax.dot_general(q, k, (((1,), (1,)), ((), ())), preferred_element_type=F32)
            scores = jnp.where(visible, scores * HEAD_SIZE ** (-0.5), NEG_FILL)
            weights = jnp.exp(scores - jnp.max(scores, axis=1, keepdims=True))
            total = jnp.sum(weights, axis=1, keepdims=True)
            numerator = dot(weights.astype(BF16), v)
            out[at, h * HEAD_SIZE : (h + 1) * HEAD_SIZE] = (numerator / total).astype(BF16)


def route_kernel(E, cap, routes_ref, gates_ref, *refs):
    place_ref, gate_ref, line_s, gate_s = refs[2], refs[3], refs[-2], refs[-1]
    for src, dst in zip(refs[:2], refs[4:6]):
        dst[...] = src[...]
    e = lax.axis_index("exp")
    blocks, _, tok = routes_ref.shape
    rows = blocks * tok
    for i in range(blocks):
        routes = routes_ref[i]
        resident = routes < E
        target = jnp.sum(jnp.where(resident, routes + 1, 0), axis=0, keepdims=True) - 1
        gate = jnp.sum(jnp.where(resident, gates_ref[i], 0.0), axis=0, keepdims=True)
        line_s[:, i * tok : (i + 1) * tok] = jnp.broadcast_to(target, (8, tok))
        gate_s[:, i * tok : (i + 1) * tok] = jnp.broadcast_to(gate, (128, tok))
    target = line_s[:1, :]
    gate_ref[...] = gate_s[...].T
    has = target >= 0
    experts = lax.broadcasted_iota(jnp.int32, (E, rows), 0)
    one_hot = jnp.where(target == experts, 1.0, 0.0)
    earlier = jnp.where(
        lax.broadcasted_iota(jnp.int32, (rows, rows), 0)
        < lax.broadcasted_iota(jnp.int32, (rows, rows), 1),
        1.0,
        0.0,
    ).astype(BF16)
    rank = jnp.sum(dot(one_hot.astype(BF16), earlier) * one_hot, axis=0, keepdims=True)
    slot = jnp.bitwise_xor(target, e) * cap + rank.astype(jnp.int32)
    slot = jnp.where(has, slot, -1)
    places = lax.broadcasted_iota(jnp.int32, (E * cap, rows), 0)
    place_ref[...] = jnp.where(slot == places, 1.0, 0.0).astype(BF16)


def project_kernel(C, with_residual, *refs):
    refs, (acc, last, stacked) = list(refs[:-3]), refs[-3:]
    res = refs.pop(0) if with_residual else None
    atts, ws = refs[:C], refs[C:]
    hi, _ = own_hi_lo()
    turn = jnp.bitwise_xor(lax.axis_index("ctx"), hi)
    for s in range(C):
        stacked[jnp.bitwise_xor(turn, s)] = atts[s][...]
    last[...] = stacked[C - 1]
    half = acc.shape[1] // 2
    acc[...] = res[...].astype(F32) if with_residual else jnp.zeros_like(acc)
    for j in range(2):
        at = slice(j * half, (j + 1) * half)
        total = None
        i = 0
        for d in range(C - 1):
            if d % 2 and d > 1:
                i += 2
                continue
            term = dot(stacked[d], ws[i][:, at])
            total = term if total is None else total + term
            i += 1
        acc[:, at] += total
    i = 0
    for d in range(C - 1):
        if d % 2 and d > 1:
            cut = ws[i].shape[1]
            acc[:, :cut] += dot(stacked[d], ws[i][...])
            acc[:, cut:] += dot(stacked[d], ws[i + 1][...])
            i += 1
        i += 1


def last_kernel(E, cap, *refs):
    accs, lasts, ws, places = refs[:2], refs[2:4], refs[4:6], refs[6:8]
    own_ref, full_ref, keep_ref, send_ref = refs[8:]
    cut = ws[0].shape[1]
    for j, cols in enumerate((slice(0, cut), slice(cut, own_ref.shape[1]))):
        for t in (1, 0):
            total = accs[t][:, cols] + dot(lasts[t][...], ws[j][...])
            rounded = total.astype(BF16)
            if t == 0:
                own_ref[:, cols] = total
            else:
                full_ref[:, cols] = rounded
            picked = dot(places[t][...], rounded)
            for d in range(E // 2):
                near, far = spread(d) ^ (PAIR * t), spread(d) ^ PAIR ^ (PAIR * t)
                at = (2 * d + t) * cap
                keep_ref[at : at + cap, cols] = picked[near * cap : (near + 1) * cap]
                at = (2 * d + 1 - t) * cap
                send_ref[at : at + cap, cols] = picked[far * cap : (far + 1) * cap].astype(BF16)


def outgoing_kernel(keep_ref, got_ref, gain_ref, *outs):
    scaled = ((keep_ref[...] + got_ref[...].astype(F32)) * gain_ref[...]).astype(BF16)
    count = outs[0].shape[0]
    for d, out in enumerate(outs):
        out[...] = scaled[d * count : (d + 1) * count]


def gate_up_kernel(C, E, cap, order, *refs):
    xs, gain_ref, w_ref, keep_ref, *sends, x_s, part_s = refs[: E // 2], *refs[E // 2 :]
    c = lax.axis_index("ctx")
    e = lax.axis_index("exp")
    own_rows = E * cap // C
    wide = w_ref.shape[1]
    for d in range(E // 2):
        for t in range(2):
            at = aligned(jnp.bitwise_xor(e, spread(d) ^ (PAIR * t)) * cap, cap)
            x_s[pl.ds(at, cap), :] = xs[d][t * cap : (t + 1) * cap, :]
    plain = x_s[...].astype(F32) / gain_ref[...]
    square = jnp.sum(plain * plain, axis=1, keepdims=True)
    lane = lax.broadcasted_iota(jnp.int32, (E * cap, 128), 1)
    part_s[:, wide:] = jnp.where(lane == 0, square, 0.0)
    step = 512
    for j in range(wide // step):
        at = slice(j * step, (j + 1) * step)
        part_s[:, at] = dot(x_s[...], w_ref[:, at])
    piece = min(own_rows, sends[0].shape[0])
    for k in range(C * own_rows // piece):
        i, rest = divmod(k * piece, own_rows)
        at = aligned(jnp.bitwise_xor(c, order[i]) * own_rows + rest, piece)
        block = part_s[pl.ds(at, piece), :]
        first = k * piece - C // 2 * own_rows
        if first < 0:
            keep_ref[k * piece : (k + 1) * piece, :] = block
        else:
            send_ref = sends[first // sends[0].shape[0]]
            to = first % sends[0].shape[0]
            send_ref[to : to + piece, :wide] = block[:, :wide].astype(BF16)
            square = block[:, wide:]
            high = square.astype(BF16).astype(F32)
            lane = lax.broadcasted_iota(jnp.int32, square.shape, 1)
            low = pltpu.roll(square - high, 1, 1)
            pair = jnp.where(lane == 1, low, high)
            send_ref[to : to + piece, wide:] = pair.astype(BF16)


def halve_kernel(pieces, keep_in, *refs):
    gots, keep_ref, sends = refs[:pieces], refs[pieces], refs[pieces + 1 :]
    rows = keep_ref.shape[0]
    wide = keep_ref.shape[1] - 128
    count = gots[0].shape[0]
    step = min(count, sends[0].shape[0])
    for at in range(0, 2 * rows, step):
        got = gots[at // count][at % count : at % count + step, :]
        total = keep_in[at : at + step, :] + got.astype(F32)
        if at < rows:
            keep_ref[at : at + step, :] = total
            continue
        send_ref = sends[(at - rows) // sends[0].shape[0]]
        to = (at - rows) % sends[0].shape[0]
        send_ref[to : to + step, :wide] = total[:, :wide].astype(BF16)
        square = jnp.sum(total[:, wide:], axis=1, keepdims=True)
        high = square.astype(BF16).astype(F32)
        lane = lax.broadcasted_iota(jnp.int32, (step, 128), 1)
        pair = jnp.where(lane == 0, high, jnp.where(lane == 1, square - high, 0.0))
        send_ref[to : to + step, wide:] = pair.astype(BF16)


def activate_kernel(hidden, keep_ref, *refs):
    gots, out = refs[:-1], refs[-1]
    count = gots[0].shape[0]
    for i, got in enumerate(gots):
        rows = slice(i * count, (i + 1) * count)

        def summed(at):
            return keep_ref[rows, at] + got[:, at].astype(F32)

        square = jnp.sum(summed(slice(2 * hidden, 2 * hidden + 128)), axis=1, keepdims=True)
        scale = lax.rsqrt(square / D + 1e-6)
        gate = summed(slice(0, hidden)) * scale
        up = summed(slice(hidden, 2 * hidden)) * scale
        out[rows, :] = (gate / (1.0 + jnp.exp(-gate)) * up).astype(BF16)


def down_kernel(C, E, cap, *refs):
    acts, w_ref, outs, x_s, part_s = refs[:C], refs[C], refs[C + 1 : C + 1 + E // 2], refs[-2], refs[-1]
    c = lax.axis_index("ctx")
    e = lax.axis_index("exp")
    own_rows = E * cap // C
    for s in range(C):
        at = aligned(jnp.bitwise_xor(c, s) * own_rows, own_rows)
        x_s[pl.ds(at, own_rows), :] = acts[s][...]
    part_s[...] = dot(x_s[...], w_ref[...]).astype(BF16)
    for d in range(E // 2):
        for t in range(2):
            at = aligned(jnp.bitwise_xor(e, spread(d) ^ (PAIR * t)) * cap, cap)
            outs[d][t * cap : (t + 1) * cap, :] = part_s[pl.ds(at, cap), :]


def forward_kernel(cap, *refs):
    for d, x in enumerate(refs[:-1]):
        refs[-1][d * cap : (d + 1) * cap, :] = x[cap:, :]


def mix_kernel(own, got, out):
    out[...] = own[...] + got[...].astype(F32)


def combine_kernel(E, cap, mixed, place_ref, gate_ref, *refs):
    xs, far, out, x_s = refs[: E // 2], refs[E // 2], refs[E // 2 + 1], refs[E // 2 + 2]
    for d in range(E // 2):
        at = spread(d) * cap
        x_s[at : at + cap, :] = xs[d][:cap, :]
        at = (spread(d) ^ PAIR) * cap
        x_s[at : at + cap, :] = far[d * cap : (d + 1) * cap, :]
    half = mixed.shape[1] // 2
    for j in range(2):
        cols = slice(j * half, (j + 1) * half)
        collected = lax.dot_general(
            place_ref[...], x_s[:, cols], (((0,), (0,)), ((), ())), preferred_element_type=F32
        )
        out[:, cols] = (mixed[:, cols] + gate_ref[:, :1] * collected).astype(BF16)


def body(
    queries,
    new_keys_values,
    cached_keys_values,
    residual,
    out_weight,
    norm_gain,
    routes,
    gates,
    w_gate_up,
    w_down,
):
    C = lax.axis_size("ctx")
    E = lax.axis_size("exp")
    tok = queries.shape[2]
    rows = C * tok
    width = residual.shape[3]
    hidden = w_down.shape[1]
    wide = 2 * hidden
    cap = rows // (2 * E)
    slots = E * cap
    own_rows = slots // C
    qw = QUERY_HEADS // E * HEAD_SIZE

    def permute(x, ctx=0, exp=0):
        pairs = [(c * E + e, (c ^ ctx) * E + (e ^ exp)) for c in range(C) for e in range(E)]
        return lax.ppermute(x, ("ctx", "exp"), pairs)

    def after(x, *others):
        return lax.optimization_barrier((x, *others))[0]

    kv = new_keys_values.shape[3]
    msgs = call(
        functools.partial(pack_kernel, C, qw),
        [sds((tok, 2 * qw + 2 * kv), BF16)] * C,
        3,
        scratch=[pltpu.SemaphoreType.DMA((4 * C,))],
        in_specs=[HBM] * 3,
        cost=(0, 2**20),
        limit=PACK_LIMIT,
    )(
        queries.reshape(tok, queries.shape[3]),
        new_keys_values.reshape(tok, kv),
        cached_keys_values.reshape(tok, kv),
    )
    res = residual.reshape(rows, width)
    got = [msgs[0]] + [permute(msgs[s], ctx=s) for s in range(1, C)]
    shards = {0: out_weight, 1: permute(out_weight, exp=1)}
    for d in range(2, C, 2):
        shards[d] = permute(out_weight, exp=spread(d))
    step = [shards[d] for d in range(2, C, 2)]

    def attend(t, msgs):
        return call(
            functools.partial(attend_kernel, C, t),
            [sds((rows, qw), BF16)] + [sds(msgs[0].shape, BF16)] * t,
            C,
            scratch=[pltpu.VMEM((2 * rows, 2 * HEAD_SIZE), BF16), pltpu.VMEM((rows, qw), BF16)],
            cost=(0, 2**14),
            limit=16,
        )(*msgs)

    other, own_msg = attend(1, got)
    theirs = permute(other, exp=PAIR)
    (mine,) = attend(0, [own_msg, after(got[1], other)] + got[2:])
    cut = width - max(width // 4, 128)
    near = after(shards[1], other)[:, cut:]
    for d in range(2, C, 2):
        shards[d + 1] = (
            permute(after(shards[d], other)[:, :cut], exp=1),
            permute(near, exp=spread(d)),
        )
    tokens_last = lambda x: jnp.transpose(x.reshape(C, tok, x.shape[3]), (0, 2, 1))
    place, gate, *staged = call(
        functools.partial(route_kernel, E, cap),
        [sds((slots, rows), BF16), sds((rows, 128), F32)]
        + [sds((qw, width), BF16), sds((rows, width), BF16)],
        4,
        scratch=[pltpu.VMEM((8, rows), jnp.int32), pltpu.VMEM((128, rows), F32)],
        cost=(0, 2**14),
        limit=16,
    )(tokens_last(after(routes, mine, *step)), tokens_last(after(gates, mine)), out_weight, res)
    shards[0], res = staged

    def gather(x, before):
        atts = {0: x, 1: permute(x, ctx=1)}
        for s in range(2, C, 2):
            atts[s] = permute(x, ctx=s)
            atts[s + 1] = permute(after(atts[s], *before), ctx=1)
        return [atts[s] for s in range(C)]

    other_place = permute(after(place, theirs), exp=PAIR)
    mine_all = gather(mine, [])
    theirs_all = gather(after(theirs, place, *mine_all[2::2], *[shards[d][1] for d in range(3, C, 2)]), [])
    mine_all[1] = after(mine_all[1], other_place)

    def project(atts, *extra):
        operands = [*extra, *atts, shards[0], shards[1], *[w for d in range(2, C - 1) for w in (shards[d] if d % 2 else [shards[d]])]]
        return call(
            functools.partial(project_kernel, C, bool(extra)),
            [sds((rows, width), F32), sds((rows, qw), BF16)],
            len(operands),
            scratch=[
                pltpu.VMEM((C, rows, qw), BF16),
            ],
            cost=(0, 2**14),
        )(*operands)

    acc, last = project(mine_all, res)
    acc_far, last_far = project(theirs_all)
    gain = norm_gain.reshape(1, width)
    own, full, keep, send = call(
        functools.partial(last_kernel, E, cap),
        [
            sds((rows, width), F32),
            sds((rows, width), BF16),
            sds((slots, width), F32),
            sds((slots, width), BF16),
        ],
        8,
        cost=(0, 2**14),
    )(acc, acc_far, last, last_far, *shards[C - 1], place, other_place)
    received = permute(send, exp=PAIR)
    outgoing = call(
        outgoing_kernel, [sds((2 * cap, width), BF16)] * (E // 2), 3, cost=(0, 2**20)
    )(keep, received, gain)
    incoming = {0: outgoing[0]}
    for d in reversed(range(1, E // 2)):
        incoming[d] = permute(outgoing[d], exp=spread(d))
    incoming = [incoming[d] for d in range(E // 2)]
    arrived = permute(after(full, received), exp=PAIR)

    order = [0]
    bit = C // 2
    while bit:
        order = order + [r | bit for r in order]
        bit //= 2
    keep, *sends = call(
        functools.partial(gate_up_kernel, C, E, cap, order),
        [sds((slots // 2, wide + 128), F32)] + [sds((slots // 4, wide + 128), BF16)] * 2,
        E // 2 + 2,
        scratch=[pltpu.VMEM((slots, width), BF16), pltpu.VMEM((slots, wide + 128), F32)],
        cost=(0, 2**10),
    )(*incoming, gain, w_gate_up.reshape(width, wide))
    bit = 1
    while 2 * bit < C:
        count = keep.shape[0] // 2
        keep, *sends = call(
            functools.partial(halve_kernel, len(sends)),
            [sds((count, wide + 128), F32)] + [sds((count // 2, wide + 128), BF16)] * 2,
            1 + len(sends),
            cost=(0, 2**10),
        )(keep, *[permute(x, ctx=bit) for x in sends])
        bit *= 2
    activated = call(
        functools.partial(activate_kernel, hidden),
        sds((own_rows, hidden), BF16),
        1 + len(sends),
        cost=(0, 2**10),
    )(keep, *[permute(x, ctx=bit) for x in sends])
    acts = {0: activated}
    acts[bit] = after(permute(activated, ctx=bit), arrived)
    bit //= 2
    while bit:
        for r in list(acts):
            acts[r ^ bit] = permute(acts[r], ctx=bit)
        bit //= 2
    expert_out = call(
        functools.partial(down_kernel, C, E, cap),
        [sds((2 * cap, width), BF16)] * (E // 2),
        C + 1,
        scratch=[pltpu.VMEM((slots, hidden), BF16), pltpu.VMEM((slots, width), BF16)],
        cost=(2 * slots * width * hidden, 2 * width * hidden),
    )(acts[0], *[acts[s] for s in range(1, C)], w_down.reshape(hidden, width))
    returned = [expert_out[0]]
    returned += [permute(expert_out[d], exp=spread(d)) for d in reversed(range(1, E // 2))][::-1]
    far = call(
        functools.partial(forward_kernel, cap), sds((slots // 2, width), BF16), E // 2, cost=(0, 2**19)
    )(*returned)
    mixed = call(mix_kernel, sds((rows, width), F32), 2, cost=(0, 2**14))(own, arrived)
    result = call(
        functools.partial(combine_kernel, E, cap),
        sds((rows, width), BF16),
        4 + E // 2,
        scratch=[pltpu.VMEM((slots, width), BF16)],
        cost=(0, 2 * 2**20),
    )(mixed, place, gate, *returned, permute(far, exp=PAIR))
    return result.reshape(C, 1, tok, width)


def solution(mesh):
    in_specs = (
        P("ctx", "exp", None, None),
        P("ctx", "exp", None, None),
        P("ctx", "exp", None, None),
        P(None, "exp", None, "ctx"),
        P("exp", "ctx"),
        P("ctx"),
        P(None, "exp", None, None),
        P(None, "exp", None, None),
        P("exp", "ctx", None),
        P("exp", None, "ctx"),
    )
    out_specs = P(None, "exp", None, "ctx")
    return jax.shard_map(body, mesh=mesh, in_specs=in_specs, out_specs=out_specs, check_vma=False)
```

```python
import functools

import jax
import jax.numpy as jnp
from jax import lax
from jax.experimental import pallas as pl
from jax.experimental.pallas import tpu as pltpu
from jax.sharding import PartitionSpec as P

D = 4096
QUERY_HEADS = 32
KEY_VALUE_HEADS = 2
HEAD_SIZE = 128
GROUP_EXTENT = QUERY_HEADS // KEY_VALUE_HEADS
NEG_FILL = -1e30
BF16 = jnp.bfloat16
F32 = jnp.float32
VMEM = pl.BlockSpec(memory_space=pltpu.VMEM)
HBM = pl.BlockSpec(memory_space=pltpu.HBM)
ANY = pl.BlockSpec(memory_space=pl.ANY)


def call(kernel, out_shape, n_in, scratch=(), cost=(0, 0), limit=32, **kw):
    kw.setdefault("in_specs", [VMEM] * n_in)
    kw.setdefault("out_specs", jax.tree.map(lambda _: VMEM, out_shape))
    return pl.pallas_call(
        kernel,
        out_shape=out_shape,
        scratch_shapes=list(scratch),
        cost_estimate=pl.CostEstimate(flops=cost[0], bytes_accessed=cost[1], transcendentals=0),
        compiler_params=pltpu.CompilerParams(vmem_limit_bytes=limit * 2**20),
        **kw,
    )


def in_hbm(x):
    return pltpu.with_memory_space_constraint(x, pltpu.HBM)


def sds(shape, dtype):
    return jax.ShapeDtypeStruct(shape, dtype)


def dot(a, b):
    return jnp.dot(a, b, preferred_element_type=F32)


PAIR = 4
PACK_LIMIT = 16


def spread(d):
    return (d // PAIR) * 2 * PAIR + d % PAIR


def own_hi_lo():
    e = lax.axis_index("exp")
    return lax.div(e, 2 * PAIR) * PAIR + lax.rem(e, PAIR), lax.rem(lax.div(e, PAIR), 2)


def aligned(x, n):
    return pl.multiple_of(x, n)


def run_copies(pairs, sems):
    copies = [pltpu.make_async_copy(src, dst, sems.at[i]) for i, (src, dst) in enumerate(pairs)]
    for c in copies:
        c.start()
    for c in copies:
        c.wait()


def pack_kernel(C, qw, q_ref, new_ref, past_ref, *refs):
    outs, sems = refs[:C], refs[C]
    c = lax.axis_index("ctx")
    _, lo = own_hi_lo()
    kv = new_ref.shape[1]
    pairs = []
    for s in reversed(range(C)):
        target = jnp.bitwise_xor(c, s)
        out = outs[s]
        for t in range(2):
            shard = lax.div(target, PAIR) * 2 * PAIR + lax.rem(target, PAIR)
            shard = shard + PAIR * jnp.bitwise_xor(lo, t)
            at = pl.ds(aligned(shard * qw, 128), qw)
            pairs.append((q_ref.at[:, at], out.at[:, t * qw : (t + 1) * qw]))
        pairs.append((new_ref, out.at[:, 2 * qw : 2 * qw + kv]))
        pairs.append((past_ref, out.at[:, 2 * qw + kv :]))
    run_copies(pairs, sems)


def attend_kernel(C, t, *refs):
    msgs, out, kv_s, q_s = refs[:C], refs[C], refs[-2], refs[-1]
    if t == 1:
        refs[C + 1][...] = msgs[0][...]
    c = lax.axis_index("ctx")
    tok, qw = msgs[0].shape[0], out.shape[1]
    rows = C * tok
    _, lo = own_hi_lo()
    shard = lax.div(c, PAIR) * 2 * PAIR + lax.rem(c, PAIR) + PAIR * jnp.bitwise_xor(lo, t)
    head = lax.div(shard * (qw // HEAD_SIZE), GROUP_EXTENT)
    for s in range(C):
        msg = msgs[s]
        at = aligned(jnp.bitwise_xor(c, s) * tok, tok)
        q_s[pl.ds(at, tok), :] = msg[:, t * qw : (t + 1) * qw]
        for i, to in ((0, rows + at), (1, at)):
            for part in range(2):
                first = 2 * qw + (i * 2 + part) * KEY_VALUE_HEADS * HEAD_SIZE
                cols = pl.ds(aligned(first + head * HEAD_SIZE, 128), HEAD_SIZE)
                kv_s[pl.ds(to, tok), part * HEAD_SIZE : (part + 1) * HEAD_SIZE] = msg[:, cols]
    block = 128
    for b in range(rows // block):
        seen = rows + (b + 1) * block
        k = kv_s[:seen, :HEAD_SIZE]
        v = kv_s[:seen, HEAD_SIZE:]
        row = lax.broadcasted_iota(jnp.int32, (block, seen), 0) + (rows + b * block)
        visible = lax.broadcasted_iota(jnp.int32, (block, seen), 1) <= row
        at = slice(b * block, (b + 1) * block)
        for h in range(qw // HEAD_SIZE):
            q = q_s[at, h * HEAD_SIZE : (h + 1) * HEAD_SIZE]
            scores = lax.dot_general(q, k, (((1,), (1,)), ((), ())), preferred_element_type=F32)
            scores = jnp.where(visible, scores * HEAD_SIZE ** (-0.5), NEG_FILL)
            weights = jnp.exp(scores - jnp.max(scores, axis=1, keepdims=True))
            total = jnp.sum(weights, axis=1, keepdims=True)
            numerator = dot(weights.astype(BF16), v)
            out[at, h * HEAD_SIZE : (h + 1) * HEAD_SIZE] = (numerator / total).astype(BF16)


def route_kernel(E, cap, routes_ref, gates_ref, *refs):
    place_ref, gate_ref, line_s, gate_s = refs[2], refs[3], refs[-2], refs[-1]
    for src, dst in zip(refs[:2], refs[4:6]):
        dst[...] = src[...]
    e = lax.axis_index("exp")
    blocks, _, tok = routes_ref.shape
    rows = blocks * tok
    for i in range(blocks):
        routes = routes_ref[i]
        resident = routes < E
        target = jnp.sum(jnp.where(resident, routes + 1, 0), axis=0, keepdims=True) - 1
        gate = jnp.sum(jnp.where(resident, gates_ref[i], 0.0), axis=0, keepdims=True)
        line_s[:, i * tok : (i + 1) * tok] = jnp.broadcast_to(target, (8, tok))
        gate_s[:, i * tok : (i + 1) * tok] = jnp.broadcast_to(gate, (128, tok))
    target = line_s[:1, :]
    gate_ref[...] = gate_s[...].T
    has = target >= 0
    experts = lax.broadcasted_iota(jnp.int32, (E, rows), 0)
    one_hot = jnp.where(target == experts, 1.0, 0.0)
    earlier = jnp.where(
        lax.broadcasted_iota(jnp.int32, (rows, rows), 0)
        < lax.broadcasted_iota(jnp.int32, (rows, rows), 1),
        1.0,
        0.0,
    ).astype(BF16)
    rank = jnp.sum(dot(one_hot.astype(BF16), earlier) * one_hot, axis=0, keepdims=True)
    slot = jnp.bitwise_xor(target, e) * cap + rank.astype(jnp.int32)
    slot = jnp.where(has, slot, -1)
    places = lax.broadcasted_iota(jnp.int32, (E * cap, rows), 0)
    place_ref[...] = jnp.where(slot == places, 1.0, 0.0).astype(BF16)


def project_kernel(C, with_residual, *refs):
    refs, (acc, last, stacked) = list(refs[:-3]), refs[-3:]
    res = refs.pop(0) if with_residual else None
    atts, ws = refs[:C], refs[C:]
    hi, _ = own_hi_lo()
    turn = jnp.bitwise_xor(lax.axis_index("ctx"), hi)
    for s in range(C):
        stacked[jnp.bitwise_xor(turn, s)] = atts[s][...]
    last[...] = stacked[C - 1]
    half = acc.shape[1] // 2
    for j in range(2):
        at = slice(j * half, (j + 1) * half)
        total = res[:, at].astype(F32) if with_residual else None
        for d in range(C - 1):
            term = dot(stacked[d], ws[d][:, at])
            total = term if total is None else total + term
        acc[:, at] = total


def last_kernel(E, cap, *refs):
    accs, lasts, w_ref, places = refs[:2], refs[2:4], refs[4], refs[5:7]
    own_ref, first_ref, second_ref, keep_ref, send_ref = refs[7:]
    few = first_ref.shape[0]
    half = own_ref.shape[1] // 2
    for j in range(2):
        cols = slice(j * half, (j + 1) * half)
        for t in (1, 0):
            total = accs[t][:, cols] + dot(lasts[t][...], w_ref[:, cols])
            rounded = total.astype(BF16)
            if t == 0:
                own_ref[:, cols] = total
            else:
                first_ref[:, cols] = rounded[:few]
                second_ref[:, cols] = rounded[few:]
            picked = dot(places[t][...], rounded)
            for d in range(E // 2):
                near, far = spread(d) ^ (PAIR * t), spread(d) ^ PAIR ^ (PAIR * t)
                at = (2 * d + t) * cap
                keep_ref[at : at + cap, cols] = picked[near * cap : (near + 1) * cap]
                at = (2 * d + 1 - t) * cap
                send_ref[at : at + cap, cols] = picked[far * cap : (far + 1) * cap].astype(BF16)


def outgoing_kernel(keep_ref, got_ref, gain_ref, *outs):
    scaled = ((keep_ref[...] + got_ref[...].astype(F32)) * gain_ref[...]).astype(BF16)
    count = outs[0].shape[0]
    for d, out in enumerate(outs):
        out[...] = scaled[d * count : (d + 1) * count]


def gate_up_kernel(C, E, cap, order, *refs):
    xs, gain_ref, w_ref, keep_ref, *sends, x_s, part_s = refs[: E // 2], *refs[E // 2 :]
    c = lax.axis_index("ctx")
    e = lax.axis_index("exp")
    own_rows = E * cap // C
    wide = w_ref.shape[1]
    for d in range(E // 2):
        for t in range(2):
            at = aligned(jnp.bitwise_xor(e, spread(d) ^ (PAIR * t)) * cap, cap)
            x_s[pl.ds(at, cap), :] = xs[d][t * cap : (t + 1) * cap, :]
    plain = x_s[...].astype(F32) / gain_ref[...]
    square = jnp.sum(plain * plain, axis=1, keepdims=True)
    lane = lax.broadcasted_iota(jnp.int32, (E * cap, 128), 1)
    part_s[:, wide:] = jnp.where(lane == 0, square, 0.0)
    step = 512
    for j in range(wide // step):
        at = slice(j * step, (j + 1) * step)
        part_s[:, at] = dot(x_s[...], w_ref[:, at])
    piece = min(own_rows, sends[0].shape[0])
    for k in range(C * own_rows // piece):
        i, rest = divmod(k * piece, own_rows)
        at = aligned(jnp.bitwise_xor(c, order[i]) * own_rows + rest, piece)
        block = part_s[pl.ds(at, piece), :]
        first = k * piece - C // 2 * own_rows
        if first < 0:
            keep_ref[k * piece : (k + 1) * piece, :] = block
        else:
            send_ref = sends[first // sends[0].shape[0]]
            to = first % sends[0].shape[0]
            send_ref[to : to + piece, :wide] = block[:, :wide].astype(BF16)
            square = block[:, wide:]
            high = square.astype(BF16).astype(F32)
            lane = lax.broadcasted_iota(jnp.int32, square.shape, 1)
            low = pltpu.roll(square - high, 1, 1)
            pair = jnp.where(lane == 1, low, high)
            send_ref[to : to + piece, wide:] = pair.astype(BF16)


def halve_kernel(pieces, keep_in, *refs):
    gots, keep_ref, sends = refs[:pieces], refs[pieces], refs[pieces + 1 :]
    rows = keep_ref.shape[0]
    wide = keep_ref.shape[1] - 128
    count = gots[0].shape[0]
    step = min(count, sends[0].shape[0])
    for at in range(0, 2 * rows, step):
        got = gots[at // count][at % count : at % count + step, :]
        total = keep_in[at : at + step, :] + got.astype(F32)
        if at < rows:
            keep_ref[at : at + step, :] = total
            continue
        send_ref = sends[(at - rows) // sends[0].shape[0]]
        to = (at - rows) % sends[0].shape[0]
        send_ref[to : to + step, :wide] = total[:, :wide].astype(BF16)
        square = jnp.sum(total[:, wide:], axis=1, keepdims=True)
        high = square.astype(BF16).astype(F32)
        lane = lax.broadcasted_iota(jnp.int32, (step, 128), 1)
        pair = jnp.where(lane == 0, high, jnp.where(lane == 1, square - high, 0.0))
        send_ref[to : to + step, wide:] = pair.astype(BF16)


def activate_kernel(hidden, keep_ref, *refs):
    gots, out = refs[:-1], refs[-1]
    count = gots[0].shape[0]
    for i, got in enumerate(gots):
        rows = slice(i * count, (i + 1) * count)

        def summed(at):
            return keep_ref[rows, at] + got[:, at].astype(F32)

        square = jnp.sum(summed(slice(2 * hidden, 2 * hidden + 128)), axis=1, keepdims=True)
        scale = lax.rsqrt(square / D + 1e-6)
        gate = summed(slice(0, hidden)) * scale
        up = summed(slice(hidden, 2 * hidden)) * scale
        out[rows, :] = (gate / (1.0 + jnp.exp(-gate)) * up).astype(BF16)


def down_kernel(C, E, cap, *refs):
    acts, w_ref, outs, x_s, part_s = refs[:C], refs[C], refs[C + 1 : C + 1 + E // 2], refs[-2], refs[-1]
    c = lax.axis_index("ctx")
    e = lax.axis_index("exp")
    own_rows = E * cap // C
    for s in range(C):
        at = aligned(jnp.bitwise_xor(c, s) * own_rows, own_rows)
        x_s[pl.ds(at, own_rows), :] = acts[s][...]
    part_s[...] = dot(x_s[...], w_ref[...]).astype(BF16)
    for d in range(E // 2):
        for t in range(2):
            at = aligned(jnp.bitwise_xor(e, spread(d) ^ (PAIR * t)) * cap, cap)
            outs[d][t * cap : (t + 1) * cap, :] = part_s[pl.ds(at, cap), :]


def forward_kernel(cap, *refs):
    for d, x in enumerate(refs[:-1]):
        refs[-1][d * cap : (d + 1) * cap, :] = x[cap:, :]


def mix_kernel(own, first, second, out):
    few = first.shape[0]
    out[:few, :] = own[:few, :] + first[...].astype(F32)
    out[few:, :] = own[few:, :] + second[...].astype(F32)


def combine_kernel(E, cap, mixed, place_ref, gate_ref, *refs):
    xs, far, out, x_s = refs[: E // 2], refs[E // 2], refs[E // 2 + 1], refs[E // 2 + 2]
    for d in range(E // 2):
        at = spread(d) * cap
        x_s[at : at + cap, :] = xs[d][:cap, :]
        at = (spread(d) ^ PAIR) * cap
        x_s[at : at + cap, :] = far[d * cap : (d + 1) * cap, :]
    half = mixed.shape[1] // 2
    for j in range(2):
        cols = slice(j * half, (j + 1) * half)
        collected = lax.dot_general(
            place_ref[...], x_s[:, cols], (((0,), (0,)), ((), ())), preferred_element_type=F32
        )
        out[:, cols] = (mixed[:, cols] + gate_ref[:, :1] * collected).astype(BF16)


def body(
    queries,
    new_keys_values,
    cached_keys_values,
    residual,
    out_weight,
    norm_gain,
    routes,
    gates,
    w_gate_up,
    w_down,
):
    C = lax.axis_size("ctx")
    E = lax.axis_size("exp")
    tok = queries.shape[2]
    rows = C * tok
    width = residual.shape[3]
    hidden = w_down.shape[1]
    wide = 2 * hidden
    cap = rows // (2 * E)
    slots = E * cap
    own_rows = slots // C
    qw = QUERY_HEADS // E * HEAD_SIZE

    def permute(x, ctx=0, exp=0):
        pairs = [(c * E + e, (c ^ ctx) * E + (e ^ exp)) for c in range(C) for e in range(E)]
        return lax.ppermute(x, ("ctx", "exp"), pairs)

    def after(x, *others):
        return lax.optimization_barrier((x, *others))[0]

    kv = new_keys_values.shape[3]
    msgs = call(
        functools.partial(pack_kernel, C, qw),
        [sds((tok, 2 * qw + 2 * kv), BF16)] * C,
        3,
        scratch=[pltpu.SemaphoreType.DMA((4 * C,))],
        in_specs=[HBM] * 3,
        cost=(0, 2**20),
        limit=PACK_LIMIT,
    )(
        in_hbm(queries.reshape(tok, queries.shape[3])),
        in_hbm(new_keys_values.reshape(tok, kv)),
        in_hbm(cached_keys_values.reshape(tok, kv)),
    )
    res = residual.reshape(rows, width)
    got = [msgs[0]] + [permute(msgs[s], ctx=s) for s in range(1, C)]
    shards = {0: out_weight, 1: permute(out_weight, exp=1)}
    for d in range(2, C, 2):
        shards[d] = permute(out_weight, exp=spread(d))
    step = [shards[d] for d in range(2, C, 2)]

    def attend(t, msgs):
        return call(
            functools.partial(attend_kernel, C, t),
            [sds((rows, qw), BF16)] + [sds(msgs[0].shape, BF16)] * t,
            C,
            scratch=[pltpu.VMEM((2 * rows, 2 * HEAD_SIZE), BF16), pltpu.VMEM((rows, qw), BF16)],
            cost=(0, 2**14),
            limit=16,
        )(*msgs)

    other, own_msg = attend(1, got)
    theirs = permute(other, exp=PAIR)
    (mine,) = attend(0, [own_msg, after(got[1], other)] + got[2:])
    for d in range(2, C, 2):
        shards[d + 1] = permute(after(shards[d], other), exp=1)
    tokens_last = lambda x: jnp.transpose(x.reshape(C, tok, x.shape[3]), (0, 2, 1))
    place, gate, *staged = call(
        functools.partial(route_kernel, E, cap),
        [sds((slots, rows), BF16), sds((rows, 128), F32)]
        + [sds((qw, width), BF16), sds((rows, width), BF16)],
        4,
        scratch=[pltpu.VMEM((8, rows), jnp.int32), pltpu.VMEM((128, rows), F32)],
        cost=(0, 2**14),
        limit=16,
    )(tokens_last(after(routes, mine, *step)), tokens_last(after(gates, mine)), out_weight, res)
    shards[0], res = staged

    def gather(x, before=lambda: ()):
        atts = {0: x, 1: permute(x, ctx=1)}
        for s in range(2, C, 2):
            atts[s] = permute(x, ctx=s)
        due = before()
        for s in range(2, C, 2):
            atts[s + 1] = permute(after(atts[s], *due), ctx=1)
        return [atts[s] for s in range(C)]

    def project(atts, *extra):
        operands = [*extra, *atts, *[shards[d] for d in range(C - 1)]]
        return call(
            functools.partial(project_kernel, C, bool(extra)),
            [sds((rows, width), F32), sds((rows, qw), BF16)],
            len(operands),
            scratch=[
                pltpu.VMEM((C, rows, qw), BF16),
            ],
            cost=(0, 2**14),
        )(*operands)

    other_place = permute(after(place, theirs), exp=PAIR)
    mine_all = gather(mine)
    acc, last = project(mine_all, res)
    theirs_all = gather(after(theirs, place, shards[1]), lambda: (other_place,))
    acc_far, last_far = project(theirs_all)
    gain = norm_gain.reshape(1, width)
    few = rows * 13 // 16
    own, first, second, keep, send = call(
        functools.partial(last_kernel, E, cap),
        [
            sds((rows, width), F32),
            sds((few, width), BF16),
            sds((rows - few, width), BF16),
            sds((slots, width), F32),
            sds((slots, width), BF16),
        ],
        7,
        cost=(0, 2**14),
    )(acc, acc_far, last, last_far, shards[C - 1], place, other_place)
    received = permute(send, exp=PAIR)
    outgoing = call(
        outgoing_kernel, [sds((2 * cap, width), BF16)] * (E // 2), 3, cost=(0, 2**20)
    )(keep, received, gain)
    incoming = {0: outgoing[0]}
    for d in reversed(range(1, E // 2)):
        incoming[d] = permute(outgoing[d], exp=spread(d))
    incoming = [incoming[d] for d in range(E // 2)]
    first = permute(after(first, received), exp=PAIR)
    second = permute(after(second, first), exp=PAIR)

    order = [0]
    bit = C // 2
    while bit:
        order = order + [r | bit for r in order]
        bit //= 2
    keep, *sends = call(
        functools.partial(gate_up_kernel, C, E, cap, order),
        [sds((slots // 2, wide + 128), F32)] + [sds((slots // 4, wide + 128), BF16)] * 2,
        E // 2 + 2,
        scratch=[pltpu.VMEM((slots, width), BF16), pltpu.VMEM((slots, wide + 128), F32)],
        cost=(0, 2**10),
    )(*incoming, gain, w_gate_up.reshape(width, wide))
    bit = 1
    while 2 * bit < C:
        count = keep.shape[0] // 2
        keep, *sends = call(
            functools.partial(halve_kernel, len(sends)),
            [sds((count, wide + 128), F32)] + [sds((count // 2, wide + 128), BF16)] * 2,
            1 + len(sends),
            cost=(0, 2**10),
        )(keep, *[permute(x, ctx=bit) for x in sends])
        bit *= 2
    activated = call(
        functools.partial(activate_kernel, hidden),
        sds((own_rows, hidden), BF16),
        1 + len(sends),
        cost=(0, 2**10),
    )(keep, *[permute(x, ctx=bit) for x in sends])
    acts = {0: activated}
    acts[bit] = after(permute(activated, ctx=bit), first)
    bit //= 2
    while bit:
        for r in list(acts):
            acts[r ^ bit] = permute(acts[r], ctx=bit)
        bit //= 2
    expert_out = call(
        functools.partial(down_kernel, C, E, cap),
        [sds((2 * cap, width), BF16)] * (E // 2),
        C + 1,
        scratch=[pltpu.VMEM((slots, hidden), BF16), pltpu.VMEM((slots, width), BF16)],
        cost=(2 * slots * width * hidden, 2 * width * hidden),
    )(acts[0], *[acts[s] for s in range(1, C)], w_down.reshape(hidden, width))
    returned = [expert_out[0]]
    returned += [permute(expert_out[d], exp=spread(d)) for d in reversed(range(1, E // 2))][::-1]
    returned[0] = after(returned[0], second)
    far = call(
        functools.partial(forward_kernel, cap), sds((slots // 2, width), BF16), E // 2, cost=(0, 2**19)
    )(*returned)
    mixed = call(mix_kernel, sds((rows, width), F32), 3, cost=(0, 2**14))(own, first, second)
    result = call(
        functools.partial(combine_kernel, E, cap),
        sds((rows, width), BF16),
        4 + E // 2,
        scratch=[pltpu.VMEM((slots, width), BF16)],
        cost=(0, 2 * 2**20),
    )(mixed, place, gate, *returned, permute(far, exp=PAIR))
    return result.reshape(C, 1, tok, width)


def solution(mesh):
    in_specs = (
        P("ctx", "exp", None, None),
        P("ctx", "exp", None, None),
        P("ctx", "exp", None, None),
        P(None, "exp", None, "ctx"),
        P("exp", "ctx"),
        P("ctx"),
        P(None, "exp", None, None),
        P(None, "exp", None, None),
        P("exp", "ctx", None),
        P("exp", None, "ctx"),
    )
    out_specs = P(None, "exp", None, "ctx")
    return jax.shard_map(body, mesh=mesh, in_specs=in_specs, out_specs=out_specs, check_vma=False)
```

```python
import functools
import math

import jax
import jax.numpy as jnp
from jax import lax
from jax.experimental import pallas as pl
from jax.experimental.pallas import tpu as pltpu
from jax.sharding import PartitionSpec as P

D = 4096
QUERY_HEADS = 32
KEY_VALUE_HEADS = 2
HEAD_SIZE = 128
GROUP_EXTENT = QUERY_HEADS // KEY_VALUE_HEADS
NEG_FILL = -1e30
EXPONENT = HEAD_SIZE ** (-0.5) * math.log2(math.e)
BF16 = jnp.bfloat16
F32 = jnp.float32
VMEM = pl.BlockSpec(memory_space=pltpu.VMEM)
HBM = pl.BlockSpec(memory_space=pltpu.HBM)
ANY = pl.BlockSpec(memory_space=pl.ANY)


def call(kernel, out_shape, n_in, scratch=(), cost=(0, 0), limit=32, **kw):
    kw.setdefault("in_specs", [VMEM] * n_in)
    kw.setdefault("out_specs", jax.tree.map(lambda _: VMEM, out_shape))
    return pl.pallas_call(
        kernel,
        out_shape=out_shape,
        scratch_shapes=list(scratch),
        cost_estimate=pl.CostEstimate(flops=cost[0], bytes_accessed=cost[1], transcendentals=0),
        compiler_params=pltpu.CompilerParams(vmem_limit_bytes=limit * 2**20),
        **kw,
    )


def in_hbm(x):
    return pltpu.with_memory_space_constraint(x, pltpu.HBM)


def sds(shape, dtype):
    return jax.ShapeDtypeStruct(shape, dtype)


def dot(a, b):
    return jnp.dot(a, b, preferred_element_type=F32)


PAIR = 4
PACK_LIMIT = 16


def spread(d):
    return (d // PAIR) * 2 * PAIR + d % PAIR


def own_hi_lo():
    e = lax.axis_index("exp")
    return lax.div(e, 2 * PAIR) * PAIR + lax.rem(e, PAIR), lax.rem(lax.div(e, PAIR), 2)


def aligned(x, n):
    return pl.multiple_of(x, n)


def run_copies(pairs, sems):
    copies = [pltpu.make_async_copy(src, dst, sems.at[i]) for i, (src, dst) in enumerate(pairs)]
    for c in copies:
        c.start()
    for c in copies:
        c.wait()


def far_first(C):
    return [*range(2, C), 1, 0]


def hops(E):
    return [*reversed(range(E // 2))]


def pack_kernel(C, qw, q_ref, new_ref, past_ref, *refs):
    outs, sems = refs[:C], refs[C]
    c = lax.axis_index("ctx")
    _, lo = own_hi_lo()
    kv = new_ref.shape[1]
    pairs = []
    for i, s in enumerate(far_first(C)):
        target = jnp.bitwise_xor(c, s)
        out = outs[i]
        for t in range(2):
            shard = lax.div(target, PAIR) * 2 * PAIR + lax.rem(target, PAIR)
            shard = shard + PAIR * jnp.bitwise_xor(lo, t)
            at = pl.ds(aligned(shard * qw, 128), qw)
            pairs.append((q_ref.at[:, at], out.at[:, t * qw : (t + 1) * qw]))
        pairs.append((new_ref, out.at[:, 2 * qw : 2 * qw + kv]))
        pairs.append((past_ref, out.at[:, 2 * qw + kv :]))
    run_copies(pairs, sems)


def attend_kernel(C, t, *refs):
    msgs, out, kv_s, q_s = refs[:C], refs[C], refs[-2], refs[-1]
    if t == 1:
        refs[C + 1][...] = msgs[-1][...]
    c = lax.axis_index("ctx")
    tok, qw = msgs[0].shape[0], out.shape[1]
    rows = C * tok
    _, lo = own_hi_lo()
    shard = lax.div(c, PAIR) * 2 * PAIR + lax.rem(c, PAIR) + PAIR * jnp.bitwise_xor(lo, t)
    head = lax.div(shard * (qw // HEAD_SIZE), GROUP_EXTENT)
    for msg, s in zip(msgs, far_first(C)):
        at = aligned(jnp.bitwise_xor(c, s) * tok, tok)
        q_s[pl.ds(at, tok), :] = msg[:, t * qw : (t + 1) * qw]
        for i, to in ((0, rows + at), (1, at)):
            for part in range(2):
                first = 2 * qw + (i * 2 + part) * KEY_VALUE_HEADS * HEAD_SIZE
                cols = pl.ds(aligned(first + head * HEAD_SIZE, 128), HEAD_SIZE)
                kv_s[pl.ds(to, tok), part * HEAD_SIZE : (part + 1) * HEAD_SIZE] = msg[:, cols]
    block = 128
    visible = lax.broadcasted_iota(jnp.int32, (block, block), 1) <= lax.broadcasted_iota(
        jnp.int32, (block, block), 0
    )
    for b in range(rows // block):
        seen = rows + (b + 1) * block
        k = kv_s[:seen, :HEAD_SIZE]
        v = kv_s[:seen, HEAD_SIZE:]
        at = slice(b * block, (b + 1) * block)
        for h in range(qw // HEAD_SIZE):
            q = q_s[at, h * HEAD_SIZE : (h + 1) * HEAD_SIZE]
            scores = lax.dot_general(q, k, (((1,), (1,)), ((), ())), preferred_element_type=F32)
            parts = (scores[:, : seen - block], jnp.where(visible, scores[:, seen - block :], NEG_FILL))
            top = jnp.maximum(*[jnp.max(x, axis=1, keepdims=True) for x in parts])
            parts = [jnp.exp2((x - top) * EXPONENT) for x in parts]
            total = sum(jnp.sum(x, axis=1, keepdims=True) for x in parts)
            numerator = dot(jnp.concatenate([x.astype(BF16) for x in parts], axis=1), v)
            out[at, h * HEAD_SIZE : (h + 1) * HEAD_SIZE] = (numerator / total).astype(BF16)


def route_kernel(E, cap, routes_ref, gates_ref, *refs):
    place_ref, gate_ref, line_s, gate_s = refs[2], refs[3], refs[-2], refs[-1]
    for src, dst in zip(refs[:2], refs[4:6]):
        dst[...] = src[...]
    e = lax.axis_index("exp")
    blocks, _, tok = routes_ref.shape
    rows = blocks * tok
    for i in range(blocks):
        routes = routes_ref[i]
        resident = routes < E
        target = jnp.sum(jnp.where(resident, routes + 1, 0), axis=0, keepdims=True) - 1
        gate = jnp.sum(jnp.where(resident, gates_ref[i], 0.0), axis=0, keepdims=True)
        line_s[:, i * tok : (i + 1) * tok] = jnp.broadcast_to(target, (8, tok))
        gate_s[:, i * tok : (i + 1) * tok] = jnp.broadcast_to(gate, (128, tok))
    target = line_s[:1, :]
    gate_ref[...] = gate_s[...].T
    has = target >= 0
    experts = lax.broadcasted_iota(jnp.int32, (E, rows), 0)
    one_hot = jnp.where(target == experts, 1.0, 0.0)
    earlier = jnp.where(
        lax.broadcasted_iota(jnp.int32, (rows, rows), 0)
        < lax.broadcasted_iota(jnp.int32, (rows, rows), 1),
        1.0,
        0.0,
    ).astype(BF16)
    rank = jnp.sum(dot(one_hot.astype(BF16), earlier) * one_hot, axis=0, keepdims=True)
    slot = jnp.bitwise_xor(target, e) * cap + rank.astype(jnp.int32)
    slot = jnp.where(has, slot, -1)
    places = lax.broadcasted_iota(jnp.int32, (E * cap, rows), 0)
    place_ref[...] = jnp.where(slot == places, 1.0, 0.0).astype(BF16)


def project_kernel(C, with_residual, *refs):
    refs, (acc, last, stacked) = list(refs[:-3]), refs[-3:]
    res = refs.pop(0) if with_residual else None
    atts, ws = refs[:C], refs[C:]
    hi, _ = own_hi_lo()
    turn = jnp.bitwise_xor(lax.axis_index("ctx"), hi)
    for s in range(C):
        stacked[jnp.bitwise_xor(turn, s)] = atts[s][...]
    last[...] = stacked[C - 1]
    half = acc.shape[1] // 2
    pieces = list(ws)
    shards = [pieces.pop(0) if d < 2 or d % 2 == 0 else (pieces.pop(0), pieces.pop(0)) for d in range(C - 1)]
    for j in range(2):
        at = slice(j * half, (j + 1) * half)
        total = res[:, at].astype(F32) if with_residual else None
        for d, w in enumerate(shards):
            if not isinstance(w, tuple):
                term = dot(stacked[d], w[:, at])
                total = term if total is None else total + term
        acc[:, at] = total
    for d, w in enumerate(shards):
        if isinstance(w, tuple):
            cut = w[0].shape[1]
            acc[:, :cut] += dot(stacked[d], w[0][...])
            acc[:, cut:] += dot(stacked[d], w[1][...])


def last_kernel(E, cap, *refs):
    accs, lasts, ws, places = refs[:2], refs[2:4], refs[4:6], refs[6:8]
    own_ref, first_ref, second_ref, keep_ref, send_ref = refs[8:]
    few = first_ref.shape[0]
    cut = ws[0].shape[1]
    for j, cols in enumerate((slice(0, cut), slice(cut, own_ref.shape[1]))):
        for t in (1, 0):
            total = accs[t][:, cols] + dot(lasts[t][...], ws[j][...])
            rounded = total.astype(BF16)
            if t == 0:
                own_ref[:, cols] = total
            else:
                first_ref[:, cols] = rounded[:few]
                second_ref[:, cols] = rounded[few:]
            picked = dot(places[t][...], rounded)
            for d in range(E // 2):
                near, far = spread(d) ^ (PAIR * t), spread(d) ^ PAIR ^ (PAIR * t)
                at = (2 * d + t) * cap
                keep_ref[at : at + cap, cols] = picked[near * cap : (near + 1) * cap]
                at = (2 * d + 1 - t) * cap
                send_ref[at : at + cap, cols] = picked[far * cap : (far + 1) * cap].astype(BF16)


def outgoing_kernel(keep_ref, got_ref, gain_ref, *outs):
    scaled = ((keep_ref[...] + got_ref[...].astype(F32)) * gain_ref[...]).astype(BF16)
    count = outs[0].shape[0]
    for d, out in enumerate(outs):
        out[...] = scaled[d * count : (d + 1) * count]


def gate_up_kernel(C, E, cap, order, *refs):
    xs, gain_ref, w_ref, keep_ref, *sends, x_s, part_s = refs[: E // 2], *refs[E // 2 :]
    c = lax.axis_index("ctx")
    e = lax.axis_index("exp")
    own_rows = E * cap // C
    wide = w_ref.shape[1]
    for x, d in zip(xs, hops(E)):
        for t in range(2):
            at = aligned(jnp.bitwise_xor(e, spread(d) ^ (PAIR * t)) * cap, cap)
            x_s[pl.ds(at, cap), :] = x[t * cap : (t + 1) * cap, :]
    plain = x_s[...].astype(F32) / gain_ref[...]
    square = jnp.sum(plain * plain, axis=1, keepdims=True)
    lane = lax.broadcasted_iota(jnp.int32, (E * cap, 128), 1)
    part_s[:, wide:] = jnp.where(lane == 0, square, 0.0)
    step = 512
    for j in range(wide // step):
        at = slice(j * step, (j + 1) * step)
        part_s[:, at] = dot(x_s[...], w_ref[:, at])
    piece = min(own_rows, sends[0].shape[0])
    for k in range(C * own_rows // piece):
        i, rest = divmod(k * piece, own_rows)
        at = aligned(jnp.bitwise_xor(c, order[i]) * own_rows + rest, piece)
        block = part_s[pl.ds(at, piece), :]
        first = k * piece - C // 2 * own_rows
        if first < 0:
            keep_ref[k * piece : (k + 1) * piece, :] = block
        else:
            send_ref = sends[first // sends[0].shape[0]]
            to = first % sends[0].shape[0]
            send_ref[to : to + piece, :wide] = block[:, :wide].astype(BF16)
            square = block[:, wide:]
            high = square.astype(BF16).astype(F32)
            lane = lax.broadcasted_iota(jnp.int32, square.shape, 1)
            low = pltpu.roll(square - high, 1, 1)
            pair = jnp.where(lane == 1, low, high)
            send_ref[to : to + piece, wide:] = pair.astype(BF16)


def halve_kernel(pieces, keep_in, *refs):
    gots, keep_ref, sends = refs[:pieces], refs[pieces], refs[pieces + 1 :]
    rows = keep_ref.shape[0]
    wide = keep_ref.shape[1] - 128
    count = gots[0].shape[0]
    step = min(count, sends[0].shape[0])
    for at in range(0, 2 * rows, step):
        got = gots[at // count][at % count : at % count + step, :]
        total = keep_in[at : at + step, :] + got.astype(F32)
        if at < rows:
            keep_ref[at : at + step, :] = total
            continue
        send_ref = sends[(at - rows) // sends[0].shape[0]]
        to = (at - rows) % sends[0].shape[0]
        send_ref[to : to + step, :wide] = total[:, :wide].astype(BF16)
        square = jnp.sum(total[:, wide:], axis=1, keepdims=True)
        high = square.astype(BF16).astype(F32)
        lane = lax.broadcasted_iota(jnp.int32, (step, 128), 1)
        pair = jnp.where(lane == 0, high, jnp.where(lane == 1, square - high, 0.0))
        send_ref[to : to + step, wide:] = pair.astype(BF16)


def activate_kernel(hidden, keep_ref, *refs):
    gots, out = refs[:-1], refs[-1]
    count = gots[0].shape[0]
    for i, got in enumerate(gots):
        rows = slice(i * count, (i + 1) * count)

        def summed(at):
            return keep_ref[rows, at] + got[:, at].astype(F32)

        square = jnp.sum(summed(slice(2 * hidden, 2 * hidden + 128)), axis=1, keepdims=True)
        scale = lax.rsqrt(square / D + 1e-6)
        gate = summed(slice(0, hidden)) * scale
        up = summed(slice(hidden, 2 * hidden)) * scale
        out[rows, :] = (gate / (1.0 + jnp.exp(-gate)) * up).astype(BF16)


def down_kernel(C, E, cap, *refs):
    acts, w_ref, outs, x_s, part_s = refs[:C], refs[C], refs[C + 1 : C + 1 + E // 2], refs[-2], refs[-1]
    c = lax.axis_index("ctx")
    e = lax.axis_index("exp")
    own_rows = E * cap // C
    for s in range(C):
        at = aligned(jnp.bitwise_xor(c, s) * own_rows, own_rows)
        x_s[pl.ds(at, own_rows), :] = acts[s][...]
    part_s[...] = dot(x_s[...], w_ref[...]).astype(BF16)
    for d in range(E // 2):
        for t in range(2):
            at = aligned(jnp.bitwise_xor(e, spread(d) ^ (PAIR * t)) * cap, cap)
            outs[d][t * cap : (t + 1) * cap, :] = part_s[pl.ds(at, cap), :]


def forward_kernel(E, cap, *refs):
    for x, d in zip(refs[:-1], hops(E)):
        refs[-1][d * cap : (d + 1) * cap, :] = x[cap:, :]


def mix_kernel(own, first, second, out):
    few = first.shape[0]
    out[:few, :] = own[:few, :] + first[...].astype(F32)
    out[few:, :] = own[few:, :] + second[...].astype(F32)


def combine_kernel(E, cap, mixed, place_ref, gate_ref, *refs):
    xs, (far, out, x_s, out_s, sems) = refs[: E // 2], refs[E // 2 :]
    for x, d in zip(xs, hops(E)):
        at = spread(d) * cap
        x_s[at : at + cap, :] = x[:cap, :]
        at = (spread(d) ^ PAIR) * cap
        x_s[at : at + cap, :] = far[d * cap : (d + 1) * cap, :]
    count, _, width = out_s.shape
    copies = []
    for j in range(count):
        cols = slice(j * width, (j + 1) * width)
        collected = lax.dot_general(
            place_ref[...], x_s[:, cols], (((0,), (0,)), ((), ())), preferred_element_type=F32
        )
        out_s[j] = (mixed[:, cols] + gate_ref[:, :1] * collected).astype(BF16)
        copies.append(pltpu.make_async_copy(out_s.at[j], out.at[:, cols], sems.at[j]))
        copies[-1].start()
    for c in copies:
        c.wait()


def body(
    queries,
    new_keys_values,
    cached_keys_values,
    residual,
    out_weight,
    norm_gain,
    routes,
    gates,
    w_gate_up,
    w_down,
):
    C = lax.axis_size("ctx")
    E = lax.axis_size("exp")
    tok = queries.shape[2]
    rows = C * tok
    width = residual.shape[3]
    hidden = w_down.shape[1]
    wide = 2 * hidden
    cap = rows // (2 * E)
    slots = E * cap
    own_rows = slots // C
    qw = QUERY_HEADS // E * HEAD_SIZE

    def permute(x, ctx=0, exp=0):
        pairs = [(c * E + e, (c ^ ctx) * E + (e ^ exp)) for c in range(C) for e in range(E)]
        return lax.ppermute(x, ("ctx", "exp"), pairs)

    def after(x, *others):
        return lax.optimization_barrier((x, *others))[0]

    kv = new_keys_values.shape[3]
    msgs = call(
        functools.partial(pack_kernel, C, qw),
        [sds((tok, 2 * qw + 2 * kv), BF16)] * C,
        3,
        scratch=[pltpu.SemaphoreType.DMA((4 * C,))],
        in_specs=[HBM] * 3,
        cost=(0, 2**20),
        limit=PACK_LIMIT,
    )(
        in_hbm(queries.reshape(tok, queries.shape[3])),
        in_hbm(new_keys_values.reshape(tok, kv)),
        in_hbm(cached_keys_values.reshape(tok, kv)),
    )
    res = residual.reshape(rows, width)
    got = [permute(x, ctx=s) if s else x for s, x in zip(far_first(C), msgs)]
    shards = {0: out_weight, 1: permute(out_weight, exp=1)}
    for d in range(2, C, 2):
        shards[d] = permute(out_weight, exp=spread(d))
    step = [shards[d] for d in range(2, C, 2)]

    def attend(t, msgs):
        return call(
            functools.partial(attend_kernel, C, t),
            [sds((rows, qw), BF16)] + [sds(msgs[0].shape, BF16)] * t,
            C,
            scratch=[pltpu.VMEM((2 * rows, 2 * HEAD_SIZE), BF16), pltpu.VMEM((rows, qw), BF16)],
            cost=(0, 2**14),
            limit=16,
        )(*msgs)

    other, own_msg = attend(1, got)
    theirs = permute(other, exp=PAIR)
    (mine,) = attend(0, [after(got[0], other), *got[1:-1], own_msg])
    cut = width - max(width // 4, 128)
    near = after(shards[1], theirs)[:, cut:]
    for d in range(2, C, 2):
        shards[d + 1] = (
            permute(after(shards[d], other)[:, :cut], exp=1),
            permute(near, exp=spread(d)),
        )
    tokens_last = lambda x: jnp.transpose(x.reshape(C, tok, x.shape[3]), (0, 2, 1))
    place, gate, *staged = call(
        functools.partial(route_kernel, E, cap),
        [sds((slots, rows), BF16), sds((rows, 128), F32)]
        + [sds((qw, width), BF16), sds((rows, width), BF16)],
        4,
        scratch=[pltpu.VMEM((8, rows), jnp.int32), pltpu.VMEM((128, rows), F32)],
        cost=(0, 2**14),
        limit=16,
    )(tokens_last(after(routes, mine, *step)), tokens_last(after(gates, mine)), out_weight, res)
    shards[0], res = staged

    def gather(x, before=lambda: ()):
        atts = {0: x, 1: permute(x, ctx=1)}
        for s in range(2, C, 2):
            atts[s] = permute(x, ctx=s)
        due = before()
        for s in range(2, C, 2):
            atts[s + 1] = permute(after(atts[s], *due), ctx=1)
        return [atts[s] for s in range(C)]

    def project(atts, *extra):
        operands = [*extra, *atts, shards[0], shards[1], *[w for d in range(2, C - 1) for w in (shards[d] if d % 2 else [shards[d]])]]
        return call(
            functools.partial(project_kernel, C, bool(extra)),
            [sds((rows, width), F32), sds((rows, qw), BF16)],
            len(operands),
            scratch=[
                pltpu.VMEM((C, rows, qw), BF16),
            ],
            cost=(0, 2**14),
        )(*operands)

    other_place = permute(after(place, theirs), exp=PAIR)
    mine_all = gather(mine)
    acc, last = project(mine_all, res)
    quarter = [shards[d][1] for d in range(3, C, 2)]
    theirs_all = gather(after(theirs, place, shards[1]), lambda: (other_place, *quarter))
    acc_far, last_far = project(theirs_all)
    gain = norm_gain.reshape(1, width)
    few = rows * 13 // 16
    own, first, second, keep, send = call(
        functools.partial(last_kernel, E, cap),
        [
            sds((rows, width), F32),
            sds((few, width), BF16),
            sds((rows - few, width), BF16),
            sds((slots, width), F32),
            sds((slots, width), BF16),
        ],
        8,
        cost=(0, 2**14),
    )(acc, acc_far, last, last_far, *shards[C - 1], place, other_place)
    received = permute(send, exp=PAIR)
    outgoing = call(
        outgoing_kernel, [sds((2 * cap, width), BF16)] * (E // 2), 3, cost=(0, 2**20)
    )(keep, received, gain)
    incoming = [permute(outgoing[d], exp=spread(d)) for d in hops(E)[:-1]] + [outgoing[0]]
    first = permute(after(first, received), exp=PAIR)
    second = permute(after(second, first), exp=PAIR)

    order = [0]
    bit = C // 2
    while bit:
        order = order + [r | bit for r in order]
        bit //= 2
    keep, *sends = call(
        functools.partial(gate_up_kernel, C, E, cap, order),
        [sds((slots // 2, wide + 128), F32)] + [sds((slots // 4, wide + 128), BF16)] * 2,
        E // 2 + 2,
        scratch=[pltpu.VMEM((slots, width), BF16), pltpu.VMEM((slots, wide + 128), F32)],
        cost=(0, 2**10),
    )(*incoming, gain, w_gate_up.reshape(width, wide))
    bit = 1
    while 2 * bit < C:
        count = keep.shape[0] // 2
        keep, *sends = call(
            functools.partial(halve_kernel, len(sends)),
            [sds((count, wide + 128), F32)] + [sds((count // 2, wide + 128), BF16)] * 2,
            1 + len(sends),
            cost=(0, 2**10),
        )(keep, *[permute(x, ctx=bit) for x in sends])
        bit *= 2
    activated = call(
        functools.partial(activate_kernel, hidden),
        sds((own_rows, hidden), BF16),
        1 + len(sends),
        cost=(0, 2**10),
    )(keep, *[permute(x, ctx=bit) for x in sends])
    acts = {0: activated}
    acts[bit] = after(permute(activated, ctx=bit), first)
    bit //= 2
    while bit:
        for r in list(acts):
            acts[r ^ bit] = permute(acts[r], ctx=bit)
        bit //= 2
    expert_out = call(
        functools.partial(down_kernel, C, E, cap),
        [sds((2 * cap, width), BF16)] * (E // 2),
        C + 1,
        scratch=[pltpu.VMEM((slots, hidden), BF16), pltpu.VMEM((slots, width), BF16)],
        cost=(2 * slots * width * hidden, 2 * width * hidden),
    )(acts[0], *[acts[s] for s in range(1, C)], w_down.reshape(hidden, width))
    returned = [permute(expert_out[d], exp=spread(d)) for d in hops(E)[:-1]]
    returned.append(after(expert_out[0], second))
    far = call(
        functools.partial(forward_kernel, E, cap), sds((slots // 2, width), BF16), E // 2, cost=(0, 2**19)
    )(*returned)
    mixed = call(mix_kernel, sds((rows, width), F32), 3, cost=(0, 2**14))(own, first, second)
    columns = min(4, width // 128)
    result = call(
        functools.partial(combine_kernel, E, cap),
        sds((rows, width), BF16),
        4 + E // 2,
        scratch=[
            pltpu.VMEM((slots, width), BF16),
            pltpu.VMEM((columns, rows, width // columns), BF16),
            pltpu.SemaphoreType.DMA((columns,)),
        ],
        out_specs=HBM,
        cost=(0, 2 * 2**20),
    )(mixed, place, gate, *returned, permute(far, exp=PAIR))
    return result.reshape(C, 1, tok, width)


def solution(mesh):
    in_specs = (
        P("ctx", "exp", None, None),
        P("ctx", "exp", None, None),
        P("ctx", "exp", None, None),
        P(None, "exp", None, "ctx"),
        P("exp", "ctx"),
        P("ctx"),
        P(None, "exp", None, None),
        P(None, "exp", None, None),
        P("exp", "ctx", None),
        P("exp", None, "ctx"),
    )
    out_specs = P(None, "exp", None, "ctx")
    return jax.shard_map(body, mesh=mesh, in_specs=in_specs, out_specs=out_specs, check_vma=False)
```

```python
import functools
import math

import jax
import jax.numpy as jnp
from jax import lax
from jax.experimental import pallas as pl
from jax.experimental.pallas import tpu as pltpu
from jax.sharding import PartitionSpec as P

D = 4096
QUERY_HEADS = 32
KEY_VALUE_HEADS = 2
HEAD_SIZE = 128
GROUP_EXTENT = QUERY_HEADS // KEY_VALUE_HEADS
NEG_FILL = -1e30
EXPONENT = HEAD_SIZE ** (-0.5) * math.log2(math.e)
BF16 = jnp.bfloat16
F32 = jnp.float32
VMEM = pl.BlockSpec(memory_space=pltpu.VMEM)
HBM = pl.BlockSpec(memory_space=pltpu.HBM)
ANY = pl.BlockSpec(memory_space=pl.ANY)


def call(kernel, out_shape, n_in, scratch=(), cost=(0, 0), limit=32, **kw):
    kw.setdefault("in_specs", [VMEM] * n_in)
    kw.setdefault("out_specs", jax.tree.map(lambda _: VMEM, out_shape))
    return pl.pallas_call(
        kernel,
        out_shape=out_shape,
        scratch_shapes=list(scratch),
        cost_estimate=pl.CostEstimate(flops=cost[0], bytes_accessed=cost[1], transcendentals=0),
        compiler_params=pltpu.CompilerParams(vmem_limit_bytes=limit * 2**20),
        **kw,
    )


def in_hbm(x):
    return pltpu.with_memory_space_constraint(x, pltpu.HBM)


def sds(shape, dtype):
    return jax.ShapeDtypeStruct(shape, dtype)


def dot(a, b):
    return jnp.dot(a, b, preferred_element_type=F32)


PAIR = 4
PACK_LIMIT = 16


def spread(d):
    return (d // PAIR) * 2 * PAIR + d % PAIR


def own_hi_lo():
    e = lax.axis_index("exp")
    return lax.div(e, 2 * PAIR) * PAIR + lax.rem(e, PAIR), lax.rem(lax.div(e, PAIR), 2)


def aligned(x, n):
    return pl.multiple_of(x, n)


def run_copies(pairs, sems):
    copies = [pltpu.make_async_copy(src, dst, sems.at[i]) for i, (src, dst) in enumerate(pairs)]
    for c in copies:
        c.start()
    for c in copies:
        c.wait()


def far_first(C):
    return [*range(2, C), 1, 0]


def hops(E):
    return [*reversed(range(E // 2))]


def all_hops(E):
    far = [b for b in range(E) if b & PAIR]
    near = [b for b in reversed(range(1, E)) if not b & PAIR]
    order = []
    for i, b in enumerate(far):
        order += [b, *near[i : i + 1]]
    return [*order, 0]


def pack_kernel(C, qw, q_ref, new_ref, past_ref, *refs):
    outs, sems = refs[:C], refs[C]
    c = lax.axis_index("ctx")
    _, lo = own_hi_lo()
    kv = new_ref.shape[1]
    pairs = []
    for i, s in enumerate(far_first(C)):
        target = jnp.bitwise_xor(c, s)
        out = outs[i]
        for t in range(2):
            shard = lax.div(target, PAIR) * 2 * PAIR + lax.rem(target, PAIR)
            shard = shard + PAIR * jnp.bitwise_xor(lo, t)
            at = pl.ds(aligned(shard * qw, 128), qw)
            pairs.append((q_ref.at[:, at], out.at[:, t * qw : (t + 1) * qw]))
        pairs.append((new_ref, out.at[:, 2 * qw : 2 * qw + kv]))
        pairs.append((past_ref, out.at[:, 2 * qw + kv :]))
    run_copies(pairs, sems)


def attend_kernel(C, t, *refs):
    msgs, out, kv_s, q_s = refs[:C], refs[C], refs[-2], refs[-1]
    if t == 1:
        refs[C + 1][...] = msgs[-1][...]
    c = lax.axis_index("ctx")
    tok, qw = msgs[0].shape[0], out.shape[1]
    rows = C * tok
    _, lo = own_hi_lo()
    shard = lax.div(c, PAIR) * 2 * PAIR + lax.rem(c, PAIR) + PAIR * jnp.bitwise_xor(lo, t)
    head = lax.div(shard * (qw // HEAD_SIZE), GROUP_EXTENT)
    for msg, s in zip(msgs, far_first(C)):
        at = aligned(jnp.bitwise_xor(c, s) * tok, tok)
        q_s[pl.ds(at, tok), :] = msg[:, t * qw : (t + 1) * qw]
        for i, to in ((0, rows + at), (1, at)):
            for part in range(2):
                first = 2 * qw + (i * 2 + part) * KEY_VALUE_HEADS * HEAD_SIZE
                cols = pl.ds(aligned(first + head * HEAD_SIZE, 128), HEAD_SIZE)
                kv_s[pl.ds(to, tok), part * HEAD_SIZE : (part + 1) * HEAD_SIZE] = msg[:, cols]
    block = 128
    visible = lax.broadcasted_iota(jnp.int32, (block, block), 1) <= lax.broadcasted_iota(
        jnp.int32, (block, block), 0
    )
    for b in range(rows // block):
        seen = rows + (b + 1) * block
        k = kv_s[:seen, :HEAD_SIZE]
        v = kv_s[:seen, HEAD_SIZE:]
        at = slice(b * block, (b + 1) * block)
        for h in range(qw // HEAD_SIZE):
            q = q_s[at, h * HEAD_SIZE : (h + 1) * HEAD_SIZE]
            scores = lax.dot_general(q, k, (((1,), (1,)), ((), ())), preferred_element_type=F32)
            parts = (scores[:, : seen - block], jnp.where(visible, scores[:, seen - block :], NEG_FILL))
            top = jnp.maximum(*[jnp.max(x, axis=1, keepdims=True) for x in parts])
            parts = [jnp.exp2((x - top) * EXPONENT) for x in parts]
            total = sum(jnp.sum(x, axis=1, keepdims=True) for x in parts)
            numerator = dot(jnp.concatenate([x.astype(BF16) for x in parts], axis=1), v)
            out[at, h * HEAD_SIZE : (h + 1) * HEAD_SIZE] = (numerator / total).astype(BF16)


def route_kernel(E, cap, routes_ref, other_ref, gates_ref, *refs):
    line_s, gate_s = refs[-2:]
    for src, dst in zip(refs[:2], refs[5:7]):
        dst[...] = src[...]
    blocks, _, tok = routes_ref.shape
    rows = blocks * tok
    earlier = jnp.where(
        lax.broadcasted_iota(jnp.int32, (rows, rows), 0)
        < lax.broadcasted_iota(jnp.int32, (rows, rows), 1),
        1.0,
        0.0,
    ).astype(BF16)
    for t, ref in enumerate((routes_ref, other_ref)):
        for i in range(blocks):
            routes = ref[i]
            resident = routes < E
            target = jnp.sum(jnp.where(resident, routes + 1, 0), axis=0, keepdims=True) - 1
            line_s[:, i * tok : (i + 1) * tok] = jnp.broadcast_to(target, (8, tok))
            if t == 0:
                gate = jnp.sum(jnp.where(resident, gates_ref[i], 0.0), axis=0, keepdims=True)
                gate_s[:, i * tok : (i + 1) * tok] = jnp.broadcast_to(gate, (128, tok))
        target = line_s[:1, :]
        experts = lax.broadcasted_iota(jnp.int32, (E, rows), 0)
        one_hot = jnp.where(target == experts, 1.0, 0.0)
        rank = jnp.sum(dot(one_hot.astype(BF16), earlier) * one_hot, axis=0, keepdims=True)
        own = jnp.bitwise_xor(lax.axis_index("exp"), PAIR * t)
        slot = jnp.bitwise_xor(target, own) * cap + rank.astype(jnp.int32)
        slot = jnp.where(target >= 0, slot, -1)
        places = lax.broadcasted_iota(jnp.int32, (E * cap, rows), 0)
        refs[2 + t][...] = jnp.where(slot == places, 1.0, 0.0).astype(BF16)
    refs[4][...] = gate_s[...].T


def project_kernel(C, with_residual, *refs):
    refs, (acc, last, stacked) = list(refs[:-3]), refs[-3:]
    res = refs.pop(0) if with_residual else None
    atts, ws = refs[:C], refs[C:]
    hi, _ = own_hi_lo()
    turn = jnp.bitwise_xor(lax.axis_index("ctx"), hi)
    for s in range(C):
        stacked[jnp.bitwise_xor(turn, s)] = atts[s][...]
    last[...] = stacked[C - 1]
    half = acc.shape[1] // 2
    pieces = list(ws)
    shards = [pieces.pop(0) if d < 2 or d % 2 == 0 else (pieces.pop(0), pieces.pop(0)) for d in range(C - 1)]
    for j in range(2):
        at = slice(j * half, (j + 1) * half)
        total = res[:, at].astype(F32) if with_residual else None
        for d, w in enumerate(shards):
            if not isinstance(w, tuple):
                term = dot(stacked[d], w[:, at])
                total = term if total is None else total + term
        acc[:, at] = total
    for d, w in enumerate(shards):
        if isinstance(w, tuple):
            cut = w[0].shape[1]
            acc[:, :cut] += dot(stacked[d], w[0][...])
            acc[:, cut:] += dot(stacked[d], w[1][...])


def last_kernel(E, cap, *refs):
    accs, lasts, ws, places = refs[:2], refs[2:4], refs[4:6], refs[6:8]
    own_ref, first_ref, second_ref, *outs = refs[8:]
    few = first_ref.shape[0]
    cut = ws[0].shape[1]
    for j, cols in enumerate((slice(0, cut), slice(cut, own_ref.shape[1]))):
        for t in (1, 0):
            total = accs[t][:, cols] + dot(lasts[t][...], ws[j][...])
            rounded = total.astype(BF16)
            if t == 0:
                own_ref[:, cols] = total
            else:
                first_ref[:, cols] = rounded[:few]
                second_ref[:, cols] = rounded[few:]
            picked = dot(places[t][...], rounded).astype(BF16)
            for out, b in zip(outs, all_hops(E)):
                at = (b ^ (PAIR * t)) * cap
                out[t * cap : (t + 1) * cap, cols] = picked[at : at + cap]


def gate_up_kernel(C, E, cap, order, *refs):
    xs, gain_ref, w_ref, keep_ref, *sends, x_s, part_s = refs[:E], *refs[E:]
    c = lax.axis_index("ctx")
    e = lax.axis_index("exp")
    own_rows = E * cap // C
    wide = w_ref.shape[1]
    came = dict(zip(all_hops(E), xs))
    for b in range(E):
        at = aligned(jnp.bitwise_xor(e, b) * cap, cap)
        total = came[b][:cap, :].astype(F32) + came[b ^ PAIR][cap:, :].astype(F32)
        x_s[pl.ds(at, cap), :] = (total * gain_ref[...]).astype(BF16)
        square = jnp.sum(total * total, axis=1, keepdims=True)
        lane = lax.broadcasted_iota(jnp.int32, (cap, 128), 1)
        part_s[pl.ds(at, cap), wide:] = jnp.where(lane == 0, square, 0.0)
    step = 512
    for j in range(wide // step):
        at = slice(j * step, (j + 1) * step)
        part_s[:, at] = dot(x_s[...], w_ref[:, at])
    piece = min(own_rows, sends[0].shape[0])
    for k in range(C * own_rows // piece):
        i, rest = divmod(k * piece, own_rows)
        at = aligned(jnp.bitwise_xor(c, order[i]) * own_rows + rest, piece)
        block = part_s[pl.ds(at, piece), :]
        first = k * piece - C // 2 * own_rows
        if first < 0:
            keep_ref[k * piece : (k + 1) * piece, :] = block
        else:
            send_ref = sends[first // sends[0].shape[0]]
            to = first % sends[0].shape[0]
            send_ref[to : to + piece, :wide] = block[:, :wide].astype(BF16)
            square = block[:, wide:]
            high = square.astype(BF16).astype(F32)
            lane = lax.broadcasted_iota(jnp.int32, square.shape, 1)
            low = pltpu.roll(square - high, 1, 1)
            pair = jnp.where(lane == 1, low, high)
            send_ref[to : to + piece, wide:] = pair.astype(BF16)


def halve_kernel(pieces, keep_in, *refs):
    gots, keep_ref, sends = refs[:pieces], refs[pieces], refs[pieces + 1 :]
    rows = keep_ref.shape[0]
    wide = keep_ref.shape[1] - 128
    count = gots[0].shape[0]
    step = min(count, sends[0].shape[0])
    for at in range(0, 2 * rows, step):
        got = gots[at // count][at % count : at % count + step, :]
        total = keep_in[at : at + step, :] + got.astype(F32)
        if at < rows:
            keep_ref[at : at + step, :] = total
            continue
        send_ref = sends[(at - rows) // sends[0].shape[0]]
        to = (at - rows) % sends[0].shape[0]
        send_ref[to : to + step, :wide] = total[:, :wide].astype(BF16)
        square = jnp.sum(total[:, wide:], axis=1, keepdims=True)
        high = square.astype(BF16).astype(F32)
        lane = lax.broadcasted_iota(jnp.int32, (step, 128), 1)
        pair = jnp.where(lane == 0, high, jnp.where(lane == 1, square - high, 0.0))
        send_ref[to : to + step, wide:] = pair.astype(BF16)


def activate_kernel(hidden, keep_ref, *refs):
    gots, out = refs[:-1], refs[-1]
    count = gots[0].shape[0]
    for i, got in enumerate(gots):
        rows = slice(i * count, (i + 1) * count)

        def summed(at):
            return keep_ref[rows, at] + got[:, at].astype(F32)

        square = jnp.sum(summed(slice(2 * hidden, 2 * hidden + 128)), axis=1, keepdims=True)
        scale = lax.rsqrt(square / D + 1e-6)
        gate = summed(slice(0, hidden)) * scale
        up = summed(slice(hidden, 2 * hidden)) * scale
        out[rows, :] = (gate / (1.0 + jnp.exp(-gate)) * up).astype(BF16)


def down_kernel(C, E, cap, *refs):
    acts, w_ref, outs, x_s, part_s = refs[:C], refs[C], refs[C + 1 : C + 1 + E // 2], refs[-2], refs[-1]
    c = lax.axis_index("ctx")
    e = lax.axis_index("exp")
    own_rows = E * cap // C
    for s in range(C):
        at = aligned(jnp.bitwise_xor(c, s) * own_rows, own_rows)
        x_s[pl.ds(at, own_rows), :] = acts[s][...]
    part_s[...] = dot(x_s[...], w_ref[...]).astype(BF16)
    for d in range(E // 2):
        for t in range(2):
            at = aligned(jnp.bitwise_xor(e, spread(d) ^ (PAIR * t)) * cap, cap)
            outs[d][t * cap : (t + 1) * cap, :] = part_s[pl.ds(at, cap), :]


def forward_kernel(E, cap, *refs):
    for x, d in zip(refs[:-1], hops(E)):
        refs[-1][d * cap : (d + 1) * cap, :] = x[cap:, :]


def mix_kernel(own, first, second, out):
    few = first.shape[0]
    out[:few, :] = own[:few, :] + first[...].astype(F32)
    out[few:, :] = own[few:, :] + second[...].astype(F32)


def combine_kernel(E, cap, mixed, place_ref, gate_ref, *refs):
    xs, (far, out, x_s, out_s, sems) = refs[: E // 2], refs[E // 2 :]
    for x, d in zip(xs, hops(E)):
        at = spread(d) * cap
        x_s[at : at + cap, :] = x[:cap, :]
        at = (spread(d) ^ PAIR) * cap
        x_s[at : at + cap, :] = far[d * cap : (d + 1) * cap, :]
    count, _, width = out_s.shape
    copies = []
    for j in range(count):
        cols = slice(j * width, (j + 1) * width)
        collected = lax.dot_general(
            place_ref[...], x_s[:, cols], (((0,), (0,)), ((), ())), preferred_element_type=F32
        )
        out_s[j] = (mixed[:, cols] + gate_ref[:, :1] * collected).astype(BF16)
        copies.append(pltpu.make_async_copy(out_s.at[j], out.at[:, cols], sems.at[j]))
        copies[-1].start()
    for c in copies:
        c.wait()


def body(
    queries,
    new_keys_values,
    cached_keys_values,
    residual,
    out_weight,
    norm_gain,
    routes,
    gates,
    w_gate_up,
    w_down,
):
    C = lax.axis_size("ctx")
    E = lax.axis_size("exp")
    tok = queries.shape[2]
    rows = C * tok
    width = residual.shape[3]
    hidden = w_down.shape[1]
    wide = 2 * hidden
    cap = rows // (2 * E)
    slots = E * cap
    own_rows = slots // C
    qw = QUERY_HEADS // E * HEAD_SIZE

    def permute(x, ctx=0, exp=0):
        pairs = [(c * E + e, (c ^ ctx) * E + (e ^ exp)) for c in range(C) for e in range(E)]
        return lax.ppermute(x, ("ctx", "exp"), pairs)

    def after(x, *others):
        return lax.optimization_barrier((x, *others))[0]

    kv = new_keys_values.shape[3]
    msgs = call(
        functools.partial(pack_kernel, C, qw),
        [sds((tok, 2 * qw + 2 * kv), BF16)] * C,
        3,
        scratch=[pltpu.SemaphoreType.DMA((4 * C,))],
        in_specs=[HBM] * 3,
        cost=(0, 2**20),
        limit=PACK_LIMIT,
    )(
        in_hbm(queries.reshape(tok, queries.shape[3])),
        in_hbm(new_keys_values.reshape(tok, kv)),
        in_hbm(cached_keys_values.reshape(tok, kv)),
    )
    res = residual.reshape(rows, width)
    got = [permute(x, ctx=s) if s else x for s, x in zip(far_first(C), msgs)]
    shards = {0: out_weight, 1: permute(out_weight, exp=1)}
    for d in range(2, C, 2):
        shards[d] = permute(out_weight, exp=spread(d))
    step = [shards[d] for d in range(2, C, 2)]

    def attend(t, msgs):
        return call(
            functools.partial(attend_kernel, C, t),
            [sds((rows, qw), BF16)] + [sds(msgs[0].shape, BF16)] * t,
            C,
            scratch=[pltpu.VMEM((2 * rows, 2 * HEAD_SIZE), BF16), pltpu.VMEM((rows, qw), BF16)],
            cost=(0, 2**14),
            limit=16,
        )(*msgs)

    tokens_last = lambda x: jnp.transpose(x.reshape(C, tok, x.shape[3]), (0, 2, 1))
    own_routes = tokens_last(routes)
    other_routes = permute(after(own_routes, got[-2]), exp=PAIR)
    other, own_msg = attend(1, [after(got[0], other_routes), *got[1:]])
    theirs = permute(other, exp=PAIR)
    (mine,) = attend(0, [after(got[0], other), *got[1:-1], own_msg])
    cut = width - max(width // 4, 128)
    near = after(shards[1], theirs)[:, cut:]
    for d in range(2, C, 2):
        shards[d + 1] = (
            permute(after(shards[d], mine)[:, :cut], exp=1),
            permute(near, exp=spread(d)),
        )
    place, other_place, gate, *staged = call(
        functools.partial(route_kernel, E, cap),
        [sds((slots, rows), BF16)] * 2
        + [sds((rows, 128), F32)]
        + [sds((qw, width), BF16), sds((rows, width), BF16)],
        5,
        scratch=[pltpu.VMEM((8, rows), jnp.int32), pltpu.VMEM((128, rows), F32)],
        cost=(0, 2**14),
        limit=16,
    )(after(own_routes, mine, *step), other_routes, tokens_last(gates), out_weight, res)
    shards[0], res = staged

    def gather(x, before=lambda: ()):
        atts = {0: x, 1: permute(x, ctx=1)}
        for s in range(2, C, 2):
            atts[s] = permute(x, ctx=s)
        due = before()
        for s in range(2, C, 2):
            atts[s + 1] = permute(after(atts[s], *due), ctx=1)
        return [atts[s] for s in range(C)]

    def project(atts, *extra):
        operands = [*extra, *atts, shards[0], shards[1], *[w for d in range(2, C - 1) for w in (shards[d] if d % 2 else [shards[d]])]]
        return call(
            functools.partial(project_kernel, C, bool(extra)),
            [sds((rows, width), F32), sds((rows, qw), BF16)],
            len(operands),
            scratch=[
                pltpu.VMEM((C, rows, qw), BF16),
            ],
            cost=(0, 2**14),
        )(*operands)

    mine_all = gather(mine)
    acc, last = project(mine_all, res)
    quarter = [shards[d][1] for d in range(3, C, 2)]
    theirs_all = gather(after(theirs, place, shards[1]), lambda: quarter)
    acc_far, last_far = project(theirs_all)
    gain = norm_gain.reshape(1, width)
    few = rows * 13 // 16
    own, first, second, *outgoing = call(
        functools.partial(last_kernel, E, cap),
        [
            sds((rows, width), F32),
            sds((few, width), BF16),
            sds((rows - few, width), BF16),
        ]
        + [sds((2 * cap, width), BF16)] * E,
        8,
        cost=(0, 2**14),
    )(acc, acc_far, last, last_far, *shards[C - 1], place, other_place)
    incoming = [permute(x, exp=b) if b else x for x, b in zip(outgoing, all_hops(E))]
    first = permute(after(first, incoming[all_hops(E).index(1)]), exp=PAIR)
    second = permute(after(second, first), exp=PAIR)

    order = [0]
    bit = C // 2
    while bit:
        order = order + [r | bit for r in order]
        bit //= 2
    keep, *sends = call(
        functools.partial(gate_up_kernel, C, E, cap, order),
        [sds((slots // 2, wide + 128), F32)] + [sds((slots // 4, wide + 128), BF16)] * 2,
        E + 2,
        scratch=[pltpu.VMEM((slots, width), BF16), pltpu.VMEM((slots, wide + 128), F32)],
        cost=(0, 2**10),
    )(*incoming, gain, w_gate_up.reshape(width, wide))
    bit = 1
    while 2 * bit < C:
        count = keep.shape[0] // 2
        keep, *sends = call(
            functools.partial(halve_kernel, len(sends)),
            [sds((count, wide + 128), F32)] + [sds((count // 2, wide + 128), BF16)] * 2,
            1 + len(sends),
            cost=(0, 2**10),
        )(keep, *[permute(x, ctx=bit) for x in sends])
        bit *= 2
    activated = call(
        functools.partial(activate_kernel, hidden),
        sds((own_rows, hidden), BF16),
        1 + len(sends),
        cost=(0, 2**10),
    )(keep, *[permute(x, ctx=bit) for x in sends])
    acts = {0: activated}
    acts[bit] = after(permute(activated, ctx=bit), first)
    bit //= 2
    while bit:
        for r in list(acts):
            acts[r ^ bit] = permute(acts[r], ctx=bit)
        bit //= 2
    expert_out = call(
        functools.partial(down_kernel, C, E, cap),
        [sds((2 * cap, width), BF16)] * (E // 2),
        C + 1,
        scratch=[pltpu.VMEM((slots, hidden), BF16), pltpu.VMEM((slots, width), BF16)],
        cost=(2 * slots * width * hidden, 2 * width * hidden),
    )(acts[0], *[acts[s] for s in range(1, C)], w_down.reshape(hidden, width))
    returned = [permute(expert_out[d], exp=spread(d)) for d in hops(E)[:-1]]
    returned.append(after(expert_out[0], second))
    far = call(
        functools.partial(forward_kernel, E, cap), sds((slots // 2, width), BF16), E // 2, cost=(0, 2**19)
    )(*returned)
    mixed = call(mix_kernel, sds((rows, width), F32), 3, cost=(0, 2**14))(own, first, second)
    columns = min(4, width // 128)
    result = call(
        functools.partial(combine_kernel, E, cap),
        sds((rows, width), BF16),
        4 + E // 2,
        scratch=[
            pltpu.VMEM((slots, width), BF16),
            pltpu.VMEM((columns, rows, width // columns), BF16),
            pltpu.SemaphoreType.DMA((columns,)),
        ],
        out_specs=HBM,
        cost=(0, 2 * 2**20),
    )(mixed, place, gate, *returned, permute(far, exp=PAIR))
    return result.reshape(C, 1, tok, width)


def solution(mesh):
    in_specs = (
        P("ctx", "exp", None, None),
        P("ctx", "exp", None, None),
        P("ctx", "exp", None, None),
        P(None, "exp", None, "ctx"),
        P("exp", "ctx"),
        P("ctx"),
        P(None, "exp", None, None),
        P(None, "exp", None, None),
        P("exp", "ctx", None),
        P("exp", None, "ctx"),
    )
    out_specs = P(None, "exp", None, "ctx")
    return jax.shard_map(body, mesh=mesh, in_specs=in_specs, out_specs=out_specs, check_vma=False)
```

```python
import functools
import math

import jax
import jax.numpy as jnp
from jax import lax
from jax.experimental import pallas as pl
from jax.experimental.pallas import tpu as pltpu
from jax.sharding import PartitionSpec as P

D = 4096
QUERY_HEADS = 32
KEY_VALUE_HEADS = 2
HEAD_SIZE = 128
GROUP_EXTENT = QUERY_HEADS // KEY_VALUE_HEADS
NEG_FILL = -1e30
EXPONENT = HEAD_SIZE ** (-0.5) * math.log2(math.e)
BF16 = jnp.bfloat16
F32 = jnp.float32
VMEM = pl.BlockSpec(memory_space=pltpu.VMEM)
HBM = pl.BlockSpec(memory_space=pltpu.HBM)
ANY = pl.BlockSpec(memory_space=pl.ANY)


def call(kernel, out_shape, n_in, scratch=(), cost=(0, 0), limit=32, **kw):
    kw.setdefault("in_specs", [VMEM] * n_in)
    kw.setdefault("out_specs", jax.tree.map(lambda _: VMEM, out_shape))
    return pl.pallas_call(
        kernel,
        out_shape=out_shape,
        scratch_shapes=list(scratch),
        cost_estimate=pl.CostEstimate(flops=cost[0], bytes_accessed=cost[1], transcendentals=0),
        compiler_params=pltpu.CompilerParams(vmem_limit_bytes=limit * 2**20),
        **kw,
    )


def in_hbm(x):
    return pltpu.with_memory_space_constraint(x, pltpu.HBM)


def sds(shape, dtype):
    return jax.ShapeDtypeStruct(shape, dtype)


def dot(a, b):
    return jnp.dot(a, b, preferred_element_type=F32)


PAIR = 4
PACK_LIMIT = 16


def spread(d):
    return (d // PAIR) * 2 * PAIR + d % PAIR


def own_hi_lo():
    e = lax.axis_index("exp")
    return lax.div(e, 2 * PAIR) * PAIR + lax.rem(e, PAIR), lax.rem(lax.div(e, PAIR), 2)


def aligned(x, n):
    return pl.multiple_of(x, n)


def run_copies(pairs, sems):
    copies = [pltpu.make_async_copy(src, dst, sems.at[i]) for i, (src, dst) in enumerate(pairs)]
    for c in copies:
        c.start()
    for c in copies:
        c.wait()


def far_first(C):
    return [*range(2, C), 1, 0]


def hops(E):
    return [*reversed(range(E // 2))]


def all_hops(E):
    far = [b for b in range(E) if b & PAIR]
    near = [b for b in reversed(range(1, E)) if not b & PAIR]
    order = []
    for i, b in enumerate(far):
        order += [b, *near[i : i + 1]]
    return [*order, 0]


def pack_kernel(C, qw, q_ref, new_ref, past_ref, *refs):
    outs, sems = refs[:C], refs[C]
    c = lax.axis_index("ctx")
    _, lo = own_hi_lo()
    kv = new_ref.shape[1]
    pairs = []
    for i, s in enumerate(far_first(C)):
        target = jnp.bitwise_xor(c, s)
        out = outs[i]
        for t in range(2):
            shard = lax.div(target, PAIR) * 2 * PAIR + lax.rem(target, PAIR)
            shard = shard + PAIR * jnp.bitwise_xor(lo, t)
            at = pl.ds(aligned(shard * qw, 128), qw)
            pairs.append((q_ref.at[:, at], out.at[:, t * qw : (t + 1) * qw]))
        pairs.append((new_ref, out.at[:, 2 * qw : 2 * qw + kv]))
        pairs.append((past_ref, out.at[:, 2 * qw + kv :]))
    run_copies(pairs, sems)


def attend_kernel(C, t, *refs):
    msgs, out, kv_s, q_s = refs[:C], refs[C], refs[-2], refs[-1]
    if t == 1:
        refs[C + 1][...] = msgs[-1][...]
    c = lax.axis_index("ctx")
    tok, qw = msgs[0].shape[0], out.shape[1]
    rows = C * tok
    _, lo = own_hi_lo()
    shard = lax.div(c, PAIR) * 2 * PAIR + lax.rem(c, PAIR) + PAIR * jnp.bitwise_xor(lo, t)
    head = lax.div(shard * (qw // HEAD_SIZE), GROUP_EXTENT)
    for msg, s in zip(msgs, far_first(C)):
        at = aligned(jnp.bitwise_xor(c, s) * tok, tok)
        q_s[pl.ds(at, tok), :] = msg[:, t * qw : (t + 1) * qw]
        for i, to in ((0, rows + at), (1, at)):
            for part in range(2):
                first = 2 * qw + (i * 2 + part) * KEY_VALUE_HEADS * HEAD_SIZE
                cols = pl.ds(aligned(first + head * HEAD_SIZE, 128), HEAD_SIZE)
                kv_s[pl.ds(to, tok), part * HEAD_SIZE : (part + 1) * HEAD_SIZE] = msg[:, cols]
    block = 128
    visible = lax.broadcasted_iota(jnp.int32, (block, block), 1) <= lax.broadcasted_iota(
        jnp.int32, (block, block), 0
    )
    for b in range(rows // block):
        seen = rows + (b + 1) * block
        k = kv_s[:seen, :HEAD_SIZE]
        v = kv_s[:seen, HEAD_SIZE:]
        at = slice(b * block, (b + 1) * block)
        for h in range(qw // HEAD_SIZE):
            q = q_s[at, h * HEAD_SIZE : (h + 1) * HEAD_SIZE]
            scores = lax.dot_general(q, k, (((1,), (1,)), ((), ())), preferred_element_type=F32)
            parts = (scores[:, : seen - block], jnp.where(visible, scores[:, seen - block :], NEG_FILL))
            top = jnp.maximum(*[jnp.max(x, axis=1, keepdims=True) for x in parts])
            parts = [jnp.exp2((x - top) * EXPONENT) for x in parts]
            total = sum(jnp.sum(x, axis=1, keepdims=True) for x in parts)
            numerator = dot(jnp.concatenate([x.astype(BF16) for x in parts], axis=1), v)
            out[at, h * HEAD_SIZE : (h + 1) * HEAD_SIZE] = (numerator / total).astype(BF16)


def route_kernel(E, cap, routes_ref, other_ref, gates_ref, *refs):
    line_s, gate_s = refs[-2:]
    for src, dst in zip(refs[:2], refs[5:7]):
        dst[...] = src[...]
    blocks, _, tok = routes_ref.shape
    rows = blocks * tok
    earlier = jnp.where(
        lax.broadcasted_iota(jnp.int32, (rows, rows), 0)
        < lax.broadcasted_iota(jnp.int32, (rows, rows), 1),
        1.0,
        0.0,
    ).astype(BF16)
    for t, ref in enumerate((routes_ref, other_ref)):
        for i in range(blocks):
            routes = ref[i]
            resident = routes < E
            target = jnp.sum(jnp.where(resident, routes + 1, 0), axis=0, keepdims=True) - 1
            line_s[:, i * tok : (i + 1) * tok] = jnp.broadcast_to(target, (8, tok))
            if t == 0:
                gate = jnp.sum(jnp.where(resident, gates_ref[i], 0.0), axis=0, keepdims=True)
                gate_s[:, i * tok : (i + 1) * tok] = jnp.broadcast_to(gate, (128, tok))
        target = line_s[:1, :]
        experts = lax.broadcasted_iota(jnp.int32, (E, rows), 0)
        one_hot = jnp.where(target == experts, 1.0, 0.0)
        rank = jnp.sum(dot(one_hot.astype(BF16), earlier) * one_hot, axis=0, keepdims=True)
        own = jnp.bitwise_xor(lax.axis_index("exp"), PAIR * t)
        slot = jnp.bitwise_xor(target, own) * cap + rank.astype(jnp.int32)
        slot = jnp.where(target >= 0, slot, -1)
        places = lax.broadcasted_iota(jnp.int32, (E * cap, rows), 0)
        refs[2 + t][...] = jnp.where(slot == places, 1.0, 0.0).astype(BF16)
    refs[4][...] = gate_s[...].T


def project_kernel(C, with_residual, *refs):
    refs, (acc, last, stacked) = list(refs[:-3]), refs[-3:]
    res = refs.pop(0) if with_residual else None
    atts, ws = refs[:C], refs[C:]
    hi, _ = own_hi_lo()
    turn = jnp.bitwise_xor(lax.axis_index("ctx"), hi)
    for s in range(C):
        stacked[jnp.bitwise_xor(turn, s)] = atts[s][...]
    last[...] = stacked[C - 1]
    half = acc.shape[1] // 2
    pieces = list(ws)
    shards = [pieces.pop(0) if d < 2 or d % 2 == 0 else (pieces.pop(0), pieces.pop(0)) for d in range(C - 1)]
    for j in range(2):
        at = slice(j * half, (j + 1) * half)
        total = res[:, at].astype(F32) if with_residual else None
        for d, w in enumerate(shards):
            if not isinstance(w, tuple):
                term = dot(stacked[d], w[:, at])
                total = term if total is None else total + term
        acc[:, at] = total
    for d, w in enumerate(shards):
        if isinstance(w, tuple):
            cut = w[0].shape[1]
            acc[:, :cut] += dot(stacked[d], w[0][...])
            acc[:, cut:] += dot(stacked[d], w[1][...])


def last_kernel(E, cap, *refs):
    accs, lasts, ws, places = refs[:2], refs[2:4], refs[4:6], refs[6:8]
    own_ref, first_ref, second_ref, *outs = refs[8:]
    few = first_ref.shape[0]
    cut = ws[0].shape[1]
    for j, cols in enumerate((slice(0, cut), slice(cut, own_ref.shape[1]))):
        for t in (1, 0):
            total = accs[t][:, cols] + dot(lasts[t][...], ws[j][...])
            rounded = total.astype(BF16)
            if t == 0:
                own_ref[:, cols] = total
            else:
                first_ref[:, cols] = rounded[:few]
                second_ref[:, cols] = rounded[few:]
            picked = dot(places[t][...], rounded).astype(BF16)
            for out, b in zip(outs, all_hops(E)):
                at = (b ^ (PAIR * t)) * cap
                out[t * cap : (t + 1) * cap, cols] = picked[at : at + cap]


def gate_up_kernel(C, E, cap, order, *refs):
    xs, gain_ref, w_ref, keep_ref, *sends, x_s, part_s = refs[:E], *refs[E:]
    c = lax.axis_index("ctx")
    e = lax.axis_index("exp")
    own_rows = E * cap // C
    wide = w_ref.shape[1]
    came = dict(zip(all_hops(E), xs))
    for b in range(E):
        at = aligned(jnp.bitwise_xor(e, b) * cap, cap)
        total = came[b][:cap, :].astype(F32) + came[b ^ PAIR][cap:, :].astype(F32)
        x_s[pl.ds(at, cap), :] = (total * gain_ref[...]).astype(BF16)
        square = jnp.sum(total * total, axis=1, keepdims=True)
        lane = lax.broadcasted_iota(jnp.int32, (cap, 128), 1)
        part_s[pl.ds(at, cap), wide:] = jnp.where(lane == 0, square, 0.0)
    step = 512
    for j in range(wide // step):
        at = slice(j * step, (j + 1) * step)
        part_s[:, at] = dot(x_s[...], w_ref[:, at])
    piece = min(own_rows, sends[0].shape[0])
    for k in range(C * own_rows // piece):
        i, rest = divmod(k * piece, own_rows)
        at = aligned(jnp.bitwise_xor(c, order[i]) * own_rows + rest, piece)
        block = part_s[pl.ds(at, piece), :]
        first = k * piece - C // 2 * own_rows
        if first < 0:
            keep_ref[k * piece : (k + 1) * piece, :] = block
        else:
            send_ref = sends[first // sends[0].shape[0]]
            to = first % sends[0].shape[0]
            send_ref[to : to + piece, :wide] = block[:, :wide].astype(BF16)
            square = block[:, wide:]
            high = square.astype(BF16).astype(F32)
            lane = lax.broadcasted_iota(jnp.int32, square.shape, 1)
            low = pltpu.roll(square - high, 1, 1)
            pair = jnp.where(lane == 1, low, high)
            send_ref[to : to + piece, wide:] = pair.astype(BF16)


def halve_kernel(pieces, keep_in, *refs):
    gots, keep_ref, sends = refs[:pieces], refs[pieces], refs[pieces + 1 :]
    rows = keep_ref.shape[0]
    wide = keep_ref.shape[1] - 128
    count = gots[0].shape[0]
    step = min(count, sends[0].shape[0])
    for at in range(0, 2 * rows, step):
        got = gots[at // count][at % count : at % count + step, :]
        total = keep_in[at : at + step, :] + got.astype(F32)
        if at < rows:
            keep_ref[at : at + step, :] = total
            continue
        send_ref = sends[(at - rows) // sends[0].shape[0]]
        to = (at - rows) % sends[0].shape[0]
        send_ref[to : to + step, :wide] = total[:, :wide].astype(BF16)
        square = jnp.sum(total[:, wide:], axis=1, keepdims=True)
        high = square.astype(BF16).astype(F32)
        lane = lax.broadcasted_iota(jnp.int32, (step, 128), 1)
        pair = jnp.where(lane == 0, high, jnp.where(lane == 1, square - high, 0.0))
        send_ref[to : to + step, wide:] = pair.astype(BF16)


def activate_kernel(hidden, keep_ref, *refs):
    gots, out = refs[:-1], refs[-1]
    count = gots[0].shape[0]
    for i, got in enumerate(gots):
        rows = slice(i * count, (i + 1) * count)

        def summed(at):
            return keep_ref[rows, at] + got[:, at].astype(F32)

        square = jnp.sum(summed(slice(2 * hidden, 2 * hidden + 128)), axis=1, keepdims=True)
        scale = lax.rsqrt(square / D + 1e-6)
        gate = summed(slice(0, hidden)) * scale
        up = summed(slice(hidden, 2 * hidden)) * scale
        out[rows, :] = (gate / (1.0 + jnp.exp(-gate)) * up).astype(BF16)


def down_kernel(C, E, cap, *refs):
    acts, w_ref, outs, x_s, part_s = refs[:C], refs[C], refs[C + 1 : C + 1 + E // 2], refs[-2], refs[-1]
    c = lax.axis_index("ctx")
    e = lax.axis_index("exp")
    own_rows = E * cap // C
    for s in range(C):
        at = aligned(jnp.bitwise_xor(c, s) * own_rows, own_rows)
        x_s[pl.ds(at, own_rows), :] = acts[s][...]
    part_s[...] = dot(x_s[...], w_ref[...]).astype(BF16)
    for d in range(E // 2):
        for t in range(2):
            at = aligned(jnp.bitwise_xor(e, spread(d) ^ (PAIR * t)) * cap, cap)
            outs[d][t * cap : (t + 1) * cap, :] = part_s[pl.ds(at, cap), :]


def forward_kernel(E, cap, *refs):
    for x, d in zip(refs[:-1], hops(E)):
        refs[-1][d * cap : (d + 1) * cap, :] = x[cap:, :]


def mix_kernel(own, first, second, out):
    few = first.shape[0]
    out[:few, :] = own[:few, :] + first[...].astype(F32)
    out[few:, :] = own[few:, :] + second[...].astype(F32)


def combine_kernel(E, cap, mixed, place_ref, gate_ref, *refs):
    xs, (far, out, x_s, out_s, sems) = refs[: E // 2], refs[E // 2 :]
    for x, d in zip(xs, hops(E)):
        at = spread(d) * cap
        x_s[at : at + cap, :] = x[:cap, :]
        at = (spread(d) ^ PAIR) * cap
        x_s[at : at + cap, :] = far[d * cap : (d + 1) * cap, :]
    count, _, width = out_s.shape
    copies = []
    for j in range(count):
        cols = slice(j * width, (j + 1) * width)
        collected = lax.dot_general(
            place_ref[...], x_s[:, cols], (((0,), (0,)), ((), ())), preferred_element_type=F32
        )
        out_s[j] = (mixed[:, cols] + gate_ref[:, :1] * collected).astype(BF16)
        copies.append(pltpu.make_async_copy(out_s.at[j], out.at[:, cols], sems.at[j]))
        copies[-1].start()
    for c in copies:
        c.wait()


def body(
    queries,
    new_keys_values,
    cached_keys_values,
    residual,
    out_weight,
    norm_gain,
    routes,
    gates,
    w_gate_up,
    w_down,
):
    C = lax.axis_size("ctx")
    E = lax.axis_size("exp")
    tok = queries.shape[2]
    rows = C * tok
    width = residual.shape[3]
    hidden = w_down.shape[1]
    wide = 2 * hidden
    cap = rows // (2 * E)
    slots = E * cap
    own_rows = slots // C
    qw = QUERY_HEADS // E * HEAD_SIZE

    def permute(x, ctx=0, exp=0):
        pairs = [(c * E + e, (c ^ ctx) * E + (e ^ exp)) for c in range(C) for e in range(E)]
        return lax.ppermute(x, ("ctx", "exp"), pairs)

    def after(x, *others):
        return lax.optimization_barrier((x, *others))[0]

    kv = new_keys_values.shape[3]
    msgs = call(
        functools.partial(pack_kernel, C, qw),
        [sds((tok, 2 * qw + 2 * kv), BF16)] * C,
        3,
        scratch=[pltpu.SemaphoreType.DMA((4 * C,))],
        in_specs=[HBM] * 3,
        cost=(0, 2**20),
        limit=PACK_LIMIT,
    )(
        in_hbm(queries.reshape(tok, queries.shape[3])),
        in_hbm(new_keys_values.reshape(tok, kv)),
        in_hbm(cached_keys_values.reshape(tok, kv)),
    )
    res = residual.reshape(rows, width)
    got = [permute(x, ctx=s) if s else x for s, x in zip(far_first(C), msgs)]
    shards = {0: out_weight, 1: permute(out_weight, exp=1)}
    for d in range(2, C, 2):
        shards[d] = permute(out_weight, exp=spread(d))
    step = [shards[d] for d in range(2, C, 2)]

    def attend(t, msgs):
        return call(
            functools.partial(attend_kernel, C, t),
            [sds((rows, qw), BF16)] + [sds(msgs[0].shape, BF16)] * t,
            C,
            scratch=[pltpu.VMEM((2 * rows, 2 * HEAD_SIZE), BF16), pltpu.VMEM((rows, qw), BF16)],
            cost=(0, 2**14),
            limit=16,
        )(*msgs)

    tokens_last = lambda x: jnp.transpose(x.reshape(C, tok, x.shape[3]), (0, 2, 1))
    own_routes = tokens_last(routes)
    other_routes = permute(after(own_routes, *got), exp=PAIR)
    other, own_msg = attend(1, got)
    theirs = permute(other, exp=PAIR)
    (mine,) = attend(0, [after(got[0], other), *got[1:-1], own_msg])
    cut = width - max(width // 4, 128)
    near = after(shards[1], theirs)[:, cut:]
    for d in range(2, C, 2):
        shards[d + 1] = (
            permute(after(shards[d], mine)[:, :cut], exp=1),
            permute(near, exp=spread(d)),
        )
    place, other_place, gate, *staged = call(
        functools.partial(route_kernel, E, cap),
        [sds((slots, rows), BF16)] * 2
        + [sds((rows, 128), F32)]
        + [sds((qw, width), BF16), sds((rows, width), BF16)],
        5,
        scratch=[pltpu.VMEM((8, rows), jnp.int32), pltpu.VMEM((128, rows), F32)],
        cost=(0, 2**14),
        limit=16,
    )(after(own_routes, mine, *step), other_routes, tokens_last(gates), out_weight, res)
    shards[0], res = staged

    def gather(x, before=lambda: ()):
        atts = {0: x, 1: permute(x, ctx=1)}
        for s in range(2, C, 2):
            atts[s] = permute(x, ctx=s)
        due = before()
        for s in range(2, C, 2):
            atts[s + 1] = permute(after(atts[s], *due), ctx=1)
        return [atts[s] for s in range(C)]

    def project(atts, *extra):
        operands = [*extra, *atts, shards[0], shards[1], *[w for d in range(2, C - 1) for w in (shards[d] if d % 2 else [shards[d]])]]
        return call(
            functools.partial(project_kernel, C, bool(extra)),
            [sds((rows, width), F32), sds((rows, qw), BF16)],
            len(operands),
            scratch=[
                pltpu.VMEM((C, rows, qw), BF16),
            ],
            cost=(0, 2**14),
        )(*operands)

    mine_all = gather(mine)
    acc, last = project(mine_all, res)
    quarter = [shards[d][1] for d in range(3, C, 2)]
    theirs_all = gather(after(theirs, place, shards[1]), lambda: quarter)
    acc_far, last_far = project(theirs_all)
    gain = norm_gain.reshape(1, width)
    few = rows * 5 // 8
    own, first, second, *outgoing = call(
        functools.partial(last_kernel, E, cap),
        [
            sds((rows, width), F32),
            sds((few, width), BF16),
            sds((rows - few, width), BF16),
        ]
        + [sds((2 * cap, width), BF16)] * E,
        8,
        cost=(0, 2**14),
    )(acc, acc_far, last, last_far, *shards[C - 1], place, other_place)
    incoming = [permute(x, exp=b) if b else x for x, b in zip(outgoing, all_hops(E))]
    first = permute(after(first, *incoming), exp=PAIR)
    second = permute(after(second, first), exp=PAIR)

    order = [0]
    bit = C // 2
    while bit:
        order = order + [r | bit for r in order]
        bit //= 2
    keep, *sends = call(
        functools.partial(gate_up_kernel, C, E, cap, order),
        [sds((slots // 2, wide + 128), F32)] + [sds((slots // 4, wide + 128), BF16)] * 2,
        E + 2,
        scratch=[pltpu.VMEM((slots, width), BF16), pltpu.VMEM((slots, wide + 128), F32)],
        cost=(0, 2**10),
    )(*incoming, gain, w_gate_up.reshape(width, wide))
    bit = 1
    while 2 * bit < C:
        count = keep.shape[0] // 2
        keep, *sends = call(
            functools.partial(halve_kernel, len(sends)),
            [sds((count, wide + 128), F32)] + [sds((count // 2, wide + 128), BF16)] * 2,
            1 + len(sends),
            cost=(0, 2**10),
        )(keep, *[permute(x, ctx=bit) for x in sends])
        bit *= 2
    activated = call(
        functools.partial(activate_kernel, hidden),
        sds((own_rows, hidden), BF16),
        1 + len(sends),
        cost=(0, 2**10),
    )(keep, *[permute(x, ctx=bit) for x in sends])
    acts = {0: activated}
    acts[bit] = after(permute(activated, ctx=bit), first)
    bit //= 2
    while bit:
        for r in list(acts):
            acts[r ^ bit] = permute(acts[r], ctx=bit)
        bit //= 2
    expert_out = call(
        functools.partial(down_kernel, C, E, cap),
        [sds((2 * cap, width), BF16)] * (E // 2),
        C + 1,
        scratch=[pltpu.VMEM((slots, hidden), BF16), pltpu.VMEM((slots, width), BF16)],
        cost=(2 * slots * width * hidden, 2 * width * hidden),
    )(acts[0], *[acts[s] for s in range(1, C)], w_down.reshape(hidden, width))
    returned = [permute(expert_out[d], exp=spread(d)) for d in hops(E)[:-1]]
    returned.append(after(expert_out[0], second))
    far = call(
        functools.partial(forward_kernel, E, cap), sds((slots // 2, width), BF16), E // 2, cost=(0, 2**19)
    )(*returned)
    mixed = call(mix_kernel, sds((rows, width), F32), 3, cost=(0, 2**14))(own, first, second)
    columns = min(4, width // 128)
    result = call(
        functools.partial(combine_kernel, E, cap),
        sds((rows, width), BF16),
        4 + E // 2,
        scratch=[
            pltpu.VMEM((slots, width), BF16),
            pltpu.VMEM((columns, rows, width // columns), BF16),
            pltpu.SemaphoreType.DMA((columns,)),
        ],
        out_specs=HBM,
        cost=(0, 2 * 2**20),
    )(mixed, place, gate, *returned, permute(far, exp=PAIR))
    return result.reshape(C, 1, tok, width)


def solution(mesh):
    in_specs = (
        P("ctx", "exp", None, None),
        P("ctx", "exp", None, None),
        P("ctx", "exp", None, None),
        P(None, "exp", None, "ctx"),
        P("exp", "ctx"),
        P("ctx"),
        P(None, "exp", None, None),
        P(None, "exp", None, None),
        P("exp", "ctx", None),
        P("exp", None, "ctx"),
    )
    out_specs = P(None, "exp", None, "ctx")
    return jax.shard_map(body, mesh=mesh, in_specs=in_specs, out_specs=out_specs, check_vma=False)
```

```python
import functools
import math

import jax
import jax.numpy as jnp
from jax import lax
from jax.experimental import pallas as pl
from jax.experimental.pallas import tpu as pltpu
from jax.sharding import PartitionSpec as P

D = 4096
QUERY_HEADS = 32
KEY_VALUE_HEADS = 2
HEAD_SIZE = 128
GROUP_EXTENT = QUERY_HEADS // KEY_VALUE_HEADS
NEG_FILL = -1e30
EXPONENT = HEAD_SIZE ** (-0.5) * math.log2(math.e)
BF16 = jnp.bfloat16
F32 = jnp.float32
VMEM = pl.BlockSpec(memory_space=pltpu.VMEM)
HBM = pl.BlockSpec(memory_space=pltpu.HBM)
ANY = pl.BlockSpec(memory_space=pl.ANY)


def call(kernel, out_shape, n_in, scratch=(), cost=(0, 0), limit=32, **kw):
    kw.setdefault("in_specs", [VMEM] * n_in)
    kw.setdefault("out_specs", jax.tree.map(lambda _: VMEM, out_shape))
    return pl.pallas_call(
        kernel,
        out_shape=out_shape,
        scratch_shapes=list(scratch),
        cost_estimate=pl.CostEstimate(flops=cost[0], bytes_accessed=cost[1], transcendentals=0),
        compiler_params=pltpu.CompilerParams(vmem_limit_bytes=limit * 2**20),
        **kw,
    )


def in_hbm(x):
    return pltpu.with_memory_space_constraint(x, pltpu.HBM)


def sds(shape, dtype):
    return jax.ShapeDtypeStruct(shape, dtype)


def dot(a, b):
    return jnp.dot(a, b, preferred_element_type=F32)


PAIR = 4
PACK_LIMIT = 16


def spread(d):
    return (d // PAIR) * 2 * PAIR + d % PAIR


def own_hi_lo():
    e = lax.axis_index("exp")
    return lax.div(e, 2 * PAIR) * PAIR + lax.rem(e, PAIR), lax.rem(lax.div(e, PAIR), 2)


def aligned(x, n):
    return pl.multiple_of(x, n)


def run_copies(pairs, sems):
    copies = [pltpu.make_async_copy(src, dst, sems.at[i]) for i, (src, dst) in enumerate(pairs)]
    for c in copies:
        c.start()
    for c in copies:
        c.wait()


def far_first(C):
    return [*range(2, C), 1, 0]


def all_hops(E):
    far = [b for b in range(E) if b & PAIR]
    near = [b for b in reversed(range(1, E)) if not b & PAIR]
    order = []
    for i, b in enumerate(far):
        order += [b, *near[i : i + 1]]
    return [*order, 0]


def pack_kernel(C, qw, q_ref, new_ref, past_ref, *refs):
    outs, sems = refs[:C], refs[C]
    c = lax.axis_index("ctx")
    _, lo = own_hi_lo()
    kv = new_ref.shape[1]
    pairs = []
    for i, s in enumerate(far_first(C)):
        target = jnp.bitwise_xor(c, s)
        out = outs[i]
        for t in range(2):
            shard = lax.div(target, PAIR) * 2 * PAIR + lax.rem(target, PAIR)
            shard = shard + PAIR * jnp.bitwise_xor(lo, t)
            at = pl.ds(aligned(shard * qw, 128), qw)
            pairs.append((q_ref.at[:, at], out.at[:, t * qw : (t + 1) * qw]))
        pairs.append((new_ref, out.at[:, 2 * qw : 2 * qw + kv]))
        pairs.append((past_ref, out.at[:, 2 * qw + kv :]))
    run_copies(pairs, sems)


def attend_kernel(C, t, *refs):
    msgs, out, kv_s, q_s = refs[:C], refs[C], refs[-2], refs[-1]
    if t == 1:
        refs[C + 1][...] = msgs[-1][...]
    c = lax.axis_index("ctx")
    tok, qw = msgs[0].shape[0], out.shape[1]
    rows = C * tok
    _, lo = own_hi_lo()
    shard = lax.div(c, PAIR) * 2 * PAIR + lax.rem(c, PAIR) + PAIR * jnp.bitwise_xor(lo, t)
    head = lax.div(shard * (qw // HEAD_SIZE), GROUP_EXTENT)
    for msg, s in zip(msgs, far_first(C)):
        at = aligned(jnp.bitwise_xor(c, s) * tok, tok)
        q_s[pl.ds(at, tok), :] = msg[:, t * qw : (t + 1) * qw]
        for i, to in ((0, rows + at), (1, at)):
            for part in range(2):
                first = 2 * qw + (i * 2 + part) * KEY_VALUE_HEADS * HEAD_SIZE
                cols = pl.ds(aligned(first + head * HEAD_SIZE, 128), HEAD_SIZE)
                kv_s[pl.ds(to, tok), part * HEAD_SIZE : (part + 1) * HEAD_SIZE] = msg[:, cols]
    block = 128
    visible = lax.broadcasted_iota(jnp.int32, (block, block), 1) <= lax.broadcasted_iota(
        jnp.int32, (block, block), 0
    )
    for b in range(rows // block):
        seen = rows + (b + 1) * block
        k = kv_s[:seen, :HEAD_SIZE]
        v = kv_s[:seen, HEAD_SIZE:]
        at = slice(b * block, (b + 1) * block)
        for h in range(qw // HEAD_SIZE):
            q = q_s[at, h * HEAD_SIZE : (h + 1) * HEAD_SIZE]
            scores = lax.dot_general(q, k, (((1,), (1,)), ((), ())), preferred_element_type=F32)
            parts = (scores[:, : seen - block], jnp.where(visible, scores[:, seen - block :], NEG_FILL))
            top = jnp.maximum(*[jnp.max(x, axis=1, keepdims=True) for x in parts])
            parts = [jnp.exp2((x - top) * EXPONENT) for x in parts]
            total = sum(jnp.sum(x, axis=1, keepdims=True) for x in parts)
            numerator = dot(jnp.concatenate([x.astype(BF16) for x in parts], axis=1), v)
            out[at, h * HEAD_SIZE : (h + 1) * HEAD_SIZE] = (numerator / total).astype(BF16)


def place_tokens(E, cap, t, routes_ref, place_ref, line_s):
    blocks, _, tok = routes_ref.shape
    rows = blocks * tok
    earlier = jnp.where(
        lax.broadcasted_iota(jnp.int32, (rows, rows), 0)
        < lax.broadcasted_iota(jnp.int32, (rows, rows), 1),
        1.0,
        0.0,
    ).astype(BF16)
    for i in range(blocks):
        routes = routes_ref[i]
        target = jnp.sum(jnp.where(routes < E, routes + 1, 0), axis=0, keepdims=True) - 1
        line_s[:, i * tok : (i + 1) * tok] = jnp.broadcast_to(target, (8, tok))
    target = line_s[:1, :]
    experts = lax.broadcasted_iota(jnp.int32, (E, rows), 0)
    one_hot = jnp.where(target == experts, 1.0, 0.0)
    rank = jnp.sum(dot(one_hot.astype(BF16), earlier) * one_hot, axis=0, keepdims=True)
    own = jnp.bitwise_xor(lax.axis_index("exp"), PAIR * t)
    slot = jnp.bitwise_xor(target, own) * cap + rank.astype(jnp.int32)
    slot = jnp.where(target >= 0, slot, -1)
    places = lax.broadcasted_iota(jnp.int32, (E * cap, rows), 0)
    place_ref[...] = jnp.where(slot == places, 1.0, 0.0).astype(BF16)


def route_kernel(E, cap, routes_ref, gates_ref, *refs):
    place_ref, gate_ref, line_s, gate_s = refs[2], refs[3], refs[-2], refs[-1]
    for src, dst in zip(refs[:2], refs[4:6]):
        dst[...] = src[...]
    place_tokens(E, cap, 0, routes_ref, place_ref, line_s)
    blocks, _, tok = routes_ref.shape
    for i in range(blocks):
        gate = jnp.sum(jnp.where(routes_ref[i] < E, gates_ref[i], 0.0), axis=0, keepdims=True)
        gate_s[:, i * tok : (i + 1) * tok] = jnp.broadcast_to(gate, (128, tok))
    gate_ref[...] = gate_s[...].T


def project_kernel(C, with_residual, *refs):
    refs, (acc, last, stacked) = list(refs[:-3]), refs[-3:]
    res = refs.pop(0) if with_residual else None
    atts, ws = refs[:C], refs[C:]
    hi, _ = own_hi_lo()
    turn = jnp.bitwise_xor(lax.axis_index("ctx"), hi)
    for s in range(C):
        stacked[jnp.bitwise_xor(turn, s)] = atts[s][...]
    last[...] = stacked[C - 1]
    half = acc.shape[1] // 2
    pieces = list(ws)
    shards = [pieces.pop(0) if d < 2 or d % 2 == 0 else (pieces.pop(0), pieces.pop(0)) for d in range(C - 1)]
    for j in range(2):
        at = slice(j * half, (j + 1) * half)
        total = res[:, at].astype(F32) if with_residual else None
        for d, w in enumerate(shards):
            if not isinstance(w, tuple):
                term = dot(stacked[d], w[:, at])
                total = term if total is None else total + term
        acc[:, at] = total
    for d, w in enumerate(shards):
        if isinstance(w, tuple):
            cut = w[0].shape[1]
            acc[:, :cut] += dot(stacked[d], w[0][...])
            acc[:, cut:] += dot(stacked[d], w[1][...])


def last_kernel(E, cap, *refs):
    accs, lasts, ws, places = refs[:2], refs[2:4], refs[4:6], refs[6:8]
    own_ref, first_ref, second_ref, *outs = refs[8:]
    few = first_ref.shape[0]
    cut = ws[0].shape[1]
    for j, cols in enumerate((slice(0, cut), slice(cut, own_ref.shape[1]))):
        for t in (1, 0):
            total = accs[t][:, cols] + dot(lasts[t][...], ws[j][...])
            rounded = total.astype(BF16)
            if t == 0:
                own_ref[:, cols] = total
            else:
                first_ref[:, cols] = rounded[:few]
                second_ref[:, cols] = rounded[few:]
            picked = dot(places[t][...], rounded).astype(BF16)
            for out, b in zip(outs, all_hops(E)):
                at = (b ^ (PAIR * t)) * cap
                out[t * cap : (t + 1) * cap, cols] = picked[at : at + cap]


def gate_up_kernel(C, E, cap, order, *refs):
    xs, gain_ref, w_ref, keep_ref, *sends, x_s, part_s = refs[:E], *refs[E:]
    c = lax.axis_index("ctx")
    e = lax.axis_index("exp")
    own_rows = E * cap // C
    wide = w_ref.shape[1]
    came = dict(zip(all_hops(E), xs))
    for b in range(E):
        at = aligned(jnp.bitwise_xor(e, b) * cap, cap)
        total = came[b][:cap, :].astype(F32) + came[b ^ PAIR][cap:, :].astype(F32)
        x_s[pl.ds(at, cap), :] = (total * gain_ref[...]).astype(BF16)
        square = jnp.sum(total * total, axis=1, keepdims=True)
        lane = lax.broadcasted_iota(jnp.int32, (cap, 128), 1)
        part_s[pl.ds(at, cap), wide:] = jnp.where(lane == 0, square, 0.0)
    step = 512
    for j in range(wide // step):
        at = slice(j * step, (j + 1) * step)
        part_s[:, at] = dot(x_s[...], w_ref[:, at])
    piece = min(own_rows, sends[0].shape[0])
    for k in range(C * own_rows // piece):
        i, rest = divmod(k * piece, own_rows)
        at = aligned(jnp.bitwise_xor(c, order[i]) * own_rows + rest, piece)
        block = part_s[pl.ds(at, piece), :]
        first = k * piece - C // 2 * own_rows
        if first < 0:
            keep_ref[k * piece : (k + 1) * piece, :] = block
        else:
            send_ref = sends[first // sends[0].shape[0]]
            to = first % sends[0].shape[0]
            send_ref[to : to + piece, :wide] = block[:, :wide].astype(BF16)
            square = block[:, wide:]
            high = square.astype(BF16).astype(F32)
            lane = lax.broadcasted_iota(jnp.int32, square.shape, 1)
            low = pltpu.roll(square - high, 1, 1)
            pair = jnp.where(lane == 1, low, high)
            send_ref[to : to + piece, wide:] = pair.astype(BF16)


def halve_kernel(pieces, keep_in, *refs):
    gots, keep_ref, sends = refs[:pieces], refs[pieces], refs[pieces + 1 :]
    rows = keep_ref.shape[0]
    wide = keep_ref.shape[1] - 128
    count = gots[0].shape[0]
    step = min(count, sends[0].shape[0])
    for at in range(0, 2 * rows, step):
        got = gots[at // count][at % count : at % count + step, :]
        total = keep_in[at : at + step, :] + got.astype(F32)
        if at < rows:
            keep_ref[at : at + step, :] = total
            continue
        send_ref = sends[(at - rows) // sends[0].shape[0]]
        to = (at - rows) % sends[0].shape[0]
        send_ref[to : to + step, :wide] = total[:, :wide].astype(BF16)
        square = jnp.sum(total[:, wide:], axis=1, keepdims=True)
        high = square.astype(BF16).astype(F32)
        lane = lax.broadcasted_iota(jnp.int32, (step, 128), 1)
        pair = jnp.where(lane == 0, high, jnp.where(lane == 1, square - high, 0.0))
        send_ref[to : to + step, wide:] = pair.astype(BF16)


def activate_kernel(hidden, keep_ref, *refs):
    gots, out = refs[:-1], refs[-1]
    count = gots[0].shape[0]
    for i, got in enumerate(gots):
        rows = slice(i * count, (i + 1) * count)

        def summed(at):
            return keep_ref[rows, at] + got[:, at].astype(F32)

        square = jnp.sum(summed(slice(2 * hidden, 2 * hidden + 128)), axis=1, keepdims=True)
        scale = lax.rsqrt(square / D + 1e-6)
        gate = summed(slice(0, hidden)) * scale
        up = summed(slice(hidden, 2 * hidden)) * scale
        out[rows, :] = (gate / (1.0 + jnp.exp(-gate)) * up).astype(BF16)


def down_kernel(C, E, cap, *refs):
    acts, w_ref, outs, x_s, part_s = refs[:C], refs[C], refs[C + 1 : C + 1 + E], refs[-2], refs[-1]
    c = lax.axis_index("ctx")
    e = lax.axis_index("exp")
    own_rows = E * cap // C
    for s in range(C):
        at = aligned(jnp.bitwise_xor(c, s) * own_rows, own_rows)
        x_s[pl.ds(at, own_rows), :] = acts[s][...]
    part_s[...] = dot(x_s[...], w_ref[...]).astype(BF16)
    for out, b in zip(outs, all_hops(E)):
        at = aligned(jnp.bitwise_xor(e, b) * cap, cap)
        out[...] = part_s[pl.ds(at, cap), :]


def mix_kernel(own, first, second, out):
    few = first.shape[0]
    out[:few, :] = own[:few, :] + first[...].astype(F32)
    out[few:, :] = own[few:, :] + second[...].astype(F32)


def combine_kernel(E, cap, mixed, place_ref, gate_ref, *refs):
    xs, (out, x_s, out_s, sems) = refs[:E], refs[E:]
    for x, b in zip(xs, all_hops(E)):
        x_s[b * cap : (b + 1) * cap, :] = x[...]
    count, _, width = out_s.shape
    copies = []
    for j in range(count):
        cols = slice(j * width, (j + 1) * width)
        collected = lax.dot_general(
            place_ref[...], x_s[:, cols], (((0,), (0,)), ((), ())), preferred_element_type=F32
        )
        out_s[j] = (mixed[:, cols] + gate_ref[:, :1] * collected).astype(BF16)
        copies.append(pltpu.make_async_copy(out_s.at[j], out.at[:, cols], sems.at[j]))
        copies[-1].start()
    for c in copies:
        c.wait()


def body(
    queries,
    new_keys_values,
    cached_keys_values,
    residual,
    out_weight,
    norm_gain,
    routes,
    gates,
    w_gate_up,
    w_down,
):
    C = lax.axis_size("ctx")
    E = lax.axis_size("exp")
    tok = queries.shape[2]
    rows = C * tok
    width = residual.shape[3]
    hidden = w_down.shape[1]
    wide = 2 * hidden
    cap = rows // (2 * E)
    slots = E * cap
    own_rows = slots // C
    qw = QUERY_HEADS // E * HEAD_SIZE

    def permute(x, ctx=0, exp=0):
        pairs = [(c * E + e, (c ^ ctx) * E + (e ^ exp)) for c in range(C) for e in range(E)]
        return lax.ppermute(x, ("ctx", "exp"), pairs)

    def after(x, *others):
        return lax.optimization_barrier((x, *others))[0]

    kv = new_keys_values.shape[3]
    msgs = call(
        functools.partial(pack_kernel, C, qw),
        [sds((tok, 2 * qw + 2 * kv), BF16)] * C,
        3,
        scratch=[pltpu.SemaphoreType.DMA((4 * C,))],
        in_specs=[HBM] * 3,
        cost=(0, 2**20),
        limit=PACK_LIMIT,
    )(
        in_hbm(queries.reshape(tok, queries.shape[3])),
        in_hbm(new_keys_values.reshape(tok, kv)),
        in_hbm(cached_keys_values.reshape(tok, kv)),
    )
    res = residual.reshape(rows, width)
    got = [permute(x, ctx=s) if s else x for s, x in zip(far_first(C), msgs)]
    shards = {0: out_weight, 1: permute(out_weight, exp=1)}
    for d in range(2, C, 2):
        shards[d] = permute(out_weight, exp=spread(d))
    step = [shards[d] for d in range(2, C, 2)]

    def attend(t, msgs):
        return call(
            functools.partial(attend_kernel, C, t),
            [sds((rows, qw), BF16)] + [sds(msgs[0].shape, BF16)] * t,
            C,
            scratch=[pltpu.VMEM((2 * rows, 2 * HEAD_SIZE), BF16), pltpu.VMEM((rows, qw), BF16)],
            cost=(0, 2**14),
            limit=16,
        )(*msgs)

    tokens_last = lambda x: jnp.transpose(x.reshape(C, tok, x.shape[3]), (0, 2, 1))
    own_routes = tokens_last(routes)
    other_routes = permute(after(own_routes, *got), exp=PAIR)
    other, own_msg = attend(1, got)
    theirs = permute(other, exp=PAIR)
    (mine,) = attend(0, [after(got[0], other), *got[1:-1], own_msg])
    place, gate, *staged = call(
        functools.partial(route_kernel, E, cap),
        [sds((slots, rows), BF16), sds((rows, 128), F32)]
        + [sds((qw, width), BF16), sds((rows, width), BF16)],
        4,
        scratch=[pltpu.VMEM((8, rows), jnp.int32), pltpu.VMEM((128, rows), F32)],
        cost=(0, 2**14),
        limit=16,
    )(after(own_routes, mine), tokens_last(gates), out_weight, res)
    other_place = call(
        functools.partial(place_tokens, E, cap, 1),
        sds((slots, rows), BF16),
        1,
        scratch=[pltpu.VMEM((8, rows), jnp.int32)],
        cost=(0, 2**14),
        limit=16,
    )(other_routes)
    shards[0], res = staged

    def gather(x, before=lambda: ()):
        atts = {0: x, 1: permute(x, ctx=1)}
        for s in range(2, C, 2):
            atts[s] = permute(x, ctx=s)
        due = before()
        for s in range(2, C, 2):
            atts[s + 1] = permute(after(atts[s], *due), ctx=1)
        return [atts[s] for s in range(C)]

    def project(atts, *extra):
        operands = [*extra, *atts, shards[0], shards[1], *[w for d in range(2, C - 1) for w in (shards[d] if d % 2 else [shards[d]])]]
        return call(
            functools.partial(project_kernel, C, bool(extra)),
            [sds((rows, width), F32), sds((rows, qw), BF16)],
            len(operands),
            scratch=[
                pltpu.VMEM((C, rows, qw), BF16),
            ],
            cost=(0, 2**14),
        )(*operands)

    mine_all = gather(mine)
    cut = width - max(width * 3 // 8, 128)
    near = after(shards[1], place)[:, cut:]
    for d in range(2, C, 2):
        shards[d + 1] = (
            permute(after(shards[d], place, *mine_all[2::2])[:, :cut], exp=1),
            permute(near, exp=spread(d)),
        )
    acc, last = project(mine_all, res)
    quarter = [shards[d][1] for d in range(3, C, 2)]
    theirs_all = gather(after(theirs, place, shards[1]), lambda: quarter)
    acc_far, last_far = project(theirs_all)
    gain = norm_gain.reshape(1, width)
    few = rows // 2
    own, first, second, *outgoing = call(
        functools.partial(last_kernel, E, cap),
        [
            sds((rows, width), F32),
            sds((few, width), BF16),
            sds((rows - few, width), BF16),
        ]
        + [sds((2 * cap, width), BF16)] * E,
        8,
        cost=(0, 2**14),
    )(acc, acc_far, last, last_far, *shards[C - 1], place, other_place)
    incoming = [permute(x, exp=b) if b else x for x, b in zip(outgoing, all_hops(E))]
    first = permute(after(first, *incoming), exp=PAIR)
    second = permute(after(second, first), exp=PAIR)

    order = [0]
    bit = C // 2
    while bit:
        order = order + [r | bit for r in order]
        bit //= 2
    keep, *sends = call(
        functools.partial(gate_up_kernel, C, E, cap, order),
        [sds((slots // 2, wide + 128), F32)] + [sds((slots // 4, wide + 128), BF16)] * 2,
        E + 2,
        scratch=[pltpu.VMEM((slots, width), BF16), pltpu.VMEM((slots, wide + 128), F32)],
        cost=(0, 2**10),
    )(*incoming, gain, w_gate_up.reshape(width, wide))
    bit = 1
    while 2 * bit < C:
        count = keep.shape[0] // 2
        keep, *sends = call(
            functools.partial(halve_kernel, len(sends)),
            [sds((count, wide + 128), F32)] + [sds((count // 2, wide + 128), BF16)] * 2,
            1 + len(sends),
            cost=(0, 2**10),
        )(keep, *[permute(x, ctx=bit) for x in sends])
        bit *= 2
    activated = call(
        functools.partial(activate_kernel, hidden),
        sds((own_rows, hidden), BF16),
        1 + len(sends),
        cost=(0, 2**10),
    )(keep, *[permute(x, ctx=bit) for x in sends])
    acts = {0: activated}
    acts[bit] = after(permute(activated, ctx=bit), first)
    bit //= 2
    while bit:
        for r in list(acts):
            acts[r ^ bit] = permute(acts[r], ctx=bit)
        bit //= 2
    expert_out = call(
        functools.partial(down_kernel, C, E, cap),
        [sds((cap, width), BF16)] * E,
        C + 1,
        scratch=[pltpu.VMEM((slots, hidden), BF16), pltpu.VMEM((slots, width), BF16)],
        cost=(2 * slots * width * hidden, 2 * width * hidden),
    )(acts[0], *[acts[s] for s in range(1, C)], w_down.reshape(hidden, width))
    returned = [permute(x, exp=b) if b else x for x, b in zip(expert_out, all_hops(E))]
    mixed = call(mix_kernel, sds((rows, width), F32), 3, cost=(0, 2**14))(own, first, second)
    columns = min(4, width // 128)
    result = call(
        functools.partial(combine_kernel, E, cap),
        sds((rows, width), BF16),
        3 + E,
        scratch=[
            pltpu.VMEM((slots, width), BF16),
            pltpu.VMEM((columns, rows, width // columns), BF16),
            pltpu.SemaphoreType.DMA((columns,)),
        ],
        out_specs=HBM,
        cost=(0, 2 * 2**20),
    )(mixed, place, gate, *returned)
    return result.reshape(C, 1, tok, width)


def solution(mesh):
    in_specs = (
        P("ctx", "exp", None, None),
        P("ctx", "exp", None, None),
        P("ctx", "exp", None, None),
        P(None, "exp", None, "ctx"),
        P("exp", "ctx"),
        P("ctx"),
        P(None, "exp", None, None),
        P(None, "exp", None, None),
        P("exp", "ctx", None),
        P("exp", None, "ctx"),
    )
    out_specs = P(None, "exp", None, "ctx")
    return jax.shard_map(body, mesh=mesh, in_specs=in_specs, out_specs=out_specs, check_vma=False)
```

```python
import functools
import math

import jax
import jax.numpy as jnp
from jax import lax
from jax.experimental import pallas as pl
from jax.experimental.pallas import tpu as pltpu
from jax.sharding import PartitionSpec as P

D = 4096
QUERY_HEADS = 32
KEY_VALUE_HEADS = 2
HEAD_SIZE = 128
GROUP_EXTENT = QUERY_HEADS // KEY_VALUE_HEADS
NEG_FILL = -1e30
EXPONENT = HEAD_SIZE ** (-0.5) * math.log2(math.e)
BF16 = jnp.bfloat16
F32 = jnp.float32
VMEM = pl.BlockSpec(memory_space=pltpu.VMEM)
HBM = pl.BlockSpec(memory_space=pltpu.HBM)
ANY = pl.BlockSpec(memory_space=pl.ANY)


def call(kernel, out_shape, n_in, scratch=(), cost=(0, 0), limit=32, **kw):
    kw.setdefault("in_specs", [VMEM] * n_in)
    kw.setdefault("out_specs", jax.tree.map(lambda _: VMEM, out_shape))
    return pl.pallas_call(
        kernel,
        out_shape=out_shape,
        scratch_shapes=list(scratch),
        cost_estimate=pl.CostEstimate(flops=cost[0], bytes_accessed=cost[1], transcendentals=0),
        compiler_params=pltpu.CompilerParams(vmem_limit_bytes=limit * 2**20),
        **kw,
    )


def in_hbm(x):
    return pltpu.with_memory_space_constraint(x, pltpu.HBM)


def sds(shape, dtype):
    return jax.ShapeDtypeStruct(shape, dtype)


def dot(a, b):
    return jnp.dot(a, b, preferred_element_type=F32)


PAIR = 4
PACK_LIMIT = 16


def spread(d):
    return (d // PAIR) * 2 * PAIR + d % PAIR


def own_hi_lo():
    e = lax.axis_index("exp")
    return lax.div(e, 2 * PAIR) * PAIR + lax.rem(e, PAIR), lax.rem(lax.div(e, PAIR), 2)


def aligned(x, n):
    return pl.multiple_of(x, n)


def run_copies(pairs, sems):
    copies = [pltpu.make_async_copy(src, dst, sems.at[i]) for i, (src, dst) in enumerate(pairs)]
    for c in copies:
        c.start()
    for c in copies:
        c.wait()


def far_first(C):
    return [*range(2, C), 1, 0]


def all_hops(E):
    return [b for b in range(E) if b & PAIR] + [b for b in reversed(range(E)) if not b & PAIR]


def pack_kernel(C, qw, q_ref, new_ref, past_ref, *refs):
    outs, sems = refs[:C], refs[C]
    c = lax.axis_index("ctx")
    _, lo = own_hi_lo()
    kv = new_ref.shape[1]
    pairs = []
    for i, s in enumerate(far_first(C)):
        target = jnp.bitwise_xor(c, s)
        out = outs[i]
        for t in range(2):
            shard = lax.div(target, PAIR) * 2 * PAIR + lax.rem(target, PAIR)
            shard = shard + PAIR * jnp.bitwise_xor(lo, t)
            at = pl.ds(aligned(shard * qw, 128), qw)
            pairs.append((q_ref.at[:, at], out.at[:, t * qw : (t + 1) * qw]))
        pairs.append((new_ref, out.at[:, 2 * qw : 2 * qw + kv]))
        pairs.append((past_ref, out.at[:, 2 * qw + kv :]))
    run_copies(pairs, sems)


def attend_kernel(C, t, *refs):
    msgs, out, kv_s, q_s = refs[:C], refs[C], refs[-2], refs[-1]
    if t == 1:
        refs[C + 1][...] = msgs[-1][...]
    c = lax.axis_index("ctx")
    tok, qw = msgs[0].shape[0], out.shape[1]
    rows = C * tok
    _, lo = own_hi_lo()
    shard = lax.div(c, PAIR) * 2 * PAIR + lax.rem(c, PAIR) + PAIR * jnp.bitwise_xor(lo, t)
    head = lax.div(shard * (qw // HEAD_SIZE), GROUP_EXTENT)
    for msg, s in zip(msgs, far_first(C)):
        at = aligned(jnp.bitwise_xor(c, s) * tok, tok)
        q_s[pl.ds(at, tok), :] = msg[:, t * qw : (t + 1) * qw]
        for i, to in ((0, rows + at), (1, at)):
            for part in range(2):
                first = 2 * qw + (i * 2 + part) * KEY_VALUE_HEADS * HEAD_SIZE
                cols = pl.ds(aligned(first + head * HEAD_SIZE, 128), HEAD_SIZE)
                kv_s[pl.ds(to, tok), part * HEAD_SIZE : (part + 1) * HEAD_SIZE] = msg[:, cols]
    block = 128
    visible = lax.broadcasted_iota(jnp.int32, (block, block), 1) <= lax.broadcasted_iota(
        jnp.int32, (block, block), 0
    )
    for b in range(rows // block):
        seen = rows + (b + 1) * block
        k = kv_s[:seen, :HEAD_SIZE]
        v = kv_s[:seen, HEAD_SIZE:]
        at = slice(b * block, (b + 1) * block)
        for h in range(qw // HEAD_SIZE):
            q = q_s[at, h * HEAD_SIZE : (h + 1) * HEAD_SIZE]
            scores = lax.dot_general(q, k, (((1,), (1,)), ((), ())), preferred_element_type=F32)
            parts = (scores[:, : seen - block], jnp.where(visible, scores[:, seen - block :], NEG_FILL))
            top = jnp.maximum(*[jnp.max(x, axis=1, keepdims=True) for x in parts])
            parts = [jnp.exp2((x - top) * EXPONENT) for x in parts]
            total = sum(jnp.sum(x, axis=1, keepdims=True) for x in parts)
            numerator = dot(jnp.concatenate([x.astype(BF16) for x in parts], axis=1), v)
            out[at, h * HEAD_SIZE : (h + 1) * HEAD_SIZE] = (numerator / total).astype(BF16)


def place_tokens(E, cap, t, routes_ref, place_ref, line_s):
    blocks, _, tok = routes_ref.shape
    rows = blocks * tok
    earlier = jnp.where(
        lax.broadcasted_iota(jnp.int32, (rows, rows), 0)
        < lax.broadcasted_iota(jnp.int32, (rows, rows), 1),
        1.0,
        0.0,
    ).astype(BF16)
    for i in range(blocks):
        routes = routes_ref[i]
        target = jnp.sum(jnp.where(routes < E, routes + 1, 0), axis=0, keepdims=True) - 1
        line_s[:, i * tok : (i + 1) * tok] = jnp.broadcast_to(target, (8, tok))
    target = line_s[:1, :]
    experts = lax.broadcasted_iota(jnp.int32, (E, rows), 0)
    one_hot = jnp.where(target == experts, 1.0, 0.0)
    rank = jnp.sum(dot(one_hot.astype(BF16), earlier) * one_hot, axis=0, keepdims=True)
    own = jnp.bitwise_xor(lax.axis_index("exp"), PAIR * t)
    slot = jnp.bitwise_xor(target, own) * cap + rank.astype(jnp.int32)
    slot = jnp.where(target >= 0, slot, -1)
    places = lax.broadcasted_iota(jnp.int32, (E * cap, rows), 0)
    place_ref[...] = jnp.where(slot == places, 1.0, 0.0).astype(BF16)


def route_kernel(E, cap, routes_ref, gates_ref, *refs):
    place_ref, gate_ref, line_s, gate_s = refs[2], refs[3], refs[-2], refs[-1]
    for src, dst in zip(refs[:2], refs[4:6]):
        dst[...] = src[...]
    place_tokens(E, cap, 0, routes_ref, place_ref, line_s)
    blocks, _, tok = routes_ref.shape
    for i in range(blocks):
        gate = jnp.sum(jnp.where(routes_ref[i] < E, gates_ref[i], 0.0), axis=0, keepdims=True)
        gate_s[:, i * tok : (i + 1) * tok] = jnp.broadcast_to(gate, (128, tok))
    gate_ref[...] = gate_s[...].T


def project_kernel(C, with_residual, *refs):
    refs, (acc, last, stacked) = list(refs[:-3]), refs[-3:]
    res = refs.pop(0) if with_residual else None
    atts, ws = refs[:C], refs[C:]
    hi, _ = own_hi_lo()
    turn = jnp.bitwise_xor(lax.axis_index("ctx"), hi)
    for s in range(C):
        stacked[jnp.bitwise_xor(turn, s)] = atts[s][...]
    last[...] = stacked[C - 1]
    half = acc.shape[1] // 2
    pieces = list(ws)
    shards = [pieces.pop(0) if d < 2 or d % 2 == 0 else (pieces.pop(0), pieces.pop(0)) for d in range(C - 1)]
    for j in range(2):
        at = slice(j * half, (j + 1) * half)
        total = res[:, at].astype(F32) if with_residual else None
        for d, w in enumerate(shards):
            if not isinstance(w, tuple):
                term = dot(stacked[d], w[:, at])
                total = term if total is None else total + term
        acc[:, at] = total
    for d, w in enumerate(shards):
        if isinstance(w, tuple):
            cut = w[0].shape[1]
            acc[:, :cut] += dot(stacked[d], w[0][...])
            acc[:, cut:] += dot(stacked[d], w[1][...])


def last_kernel(E, cap, *refs):
    accs, lasts, ws, places = refs[:2], refs[2:4], refs[4:6], refs[6:8]
    own_ref, full_ref, *outs = refs[8:]
    cut = ws[0].shape[1]
    for j, cols in enumerate((slice(0, cut), slice(cut, own_ref.shape[1]))):
        for t in (1, 0):
            total = accs[t][:, cols] + dot(lasts[t][...], ws[j][...])
            rounded = total.astype(BF16)
            if t == 0:
                own_ref[:, cols] = total
            else:
                full_ref[:, cols] = rounded
            picked = dot(places[t][...], rounded).astype(BF16)
            for out, b in zip(outs, all_hops(E)):
                at = (b ^ (PAIR * t)) * cap
                out[t * cap : (t + 1) * cap, cols] = picked[at : at + cap]


def gate_up_kernel(C, E, cap, order, *refs):
    xs, gain_ref, w_ref, keep_ref, *sends, x_s, part_s = refs[:E], *refs[E:]
    c = lax.axis_index("ctx")
    e = lax.axis_index("exp")
    own_rows = E * cap // C
    wide = w_ref.shape[1]
    came = dict(zip(all_hops(E), xs))
    for b in range(E):
        at = aligned(jnp.bitwise_xor(e, b) * cap, cap)
        total = came[b][:cap, :].astype(F32) + came[b ^ PAIR][cap:, :].astype(F32)
        x_s[pl.ds(at, cap), :] = (total * gain_ref[...]).astype(BF16)
        square = jnp.sum(total * total, axis=1, keepdims=True)
        lane = lax.broadcasted_iota(jnp.int32, (cap, 128), 1)
        part_s[pl.ds(at, cap), wide:] = jnp.where(lane == 0, square, 0.0)
    step = 512
    for j in range(wide // step):
        at = slice(j * step, (j + 1) * step)
        part_s[:, at] = dot(x_s[...], w_ref[:, at])
    piece = min(own_rows, sends[0].shape[0])
    for k in range(C * own_rows // piece):
        i, rest = divmod(k * piece, own_rows)
        at = aligned(jnp.bitwise_xor(c, order[i]) * own_rows + rest, piece)
        block = part_s[pl.ds(at, piece), :]
        first = k * piece - C // 2 * own_rows
        if first < 0:
            keep_ref[k * piece : (k + 1) * piece, :] = block
        else:
            send_ref = sends[first // sends[0].shape[0]]
            to = first % sends[0].shape[0]
            send_ref[to : to + piece, :wide] = block[:, :wide].astype(BF16)
            square = block[:, wide:]
            high = square.astype(BF16).astype(F32)
            lane = lax.broadcasted_iota(jnp.int32, square.shape, 1)
            low = pltpu.roll(square - high, 1, 1)
            pair = jnp.where(lane == 1, low, high)
            send_ref[to : to + piece, wide:] = pair.astype(BF16)


def halve_kernel(pieces, keep_in, *refs):
    gots, keep_ref, sends = refs[:pieces], refs[pieces], refs[pieces + 1 :]
    rows = keep_ref.shape[0]
    wide = keep_ref.shape[1] - 128
    count = gots[0].shape[0]
    step = min(count, sends[0].shape[0])
    for at in range(0, 2 * rows, step):
        got = gots[at // count][at % count : at % count + step, :]
        total = keep_in[at : at + step, :] + got.astype(F32)
        if at < rows:
            keep_ref[at : at + step, :] = total
            continue
        send_ref = sends[(at - rows) // sends[0].shape[0]]
        to = (at - rows) % sends[0].shape[0]
        send_ref[to : to + step, :wide] = total[:, :wide].astype(BF16)
        square = jnp.sum(total[:, wide:], axis=1, keepdims=True)
        high = square.astype(BF16).astype(F32)
        lane = lax.broadcasted_iota(jnp.int32, (step, 128), 1)
        pair = jnp.where(lane == 0, high, jnp.where(lane == 1, square - high, 0.0))
        send_ref[to : to + step, wide:] = pair.astype(BF16)


def activate_kernel(hidden, keep_ref, *refs):
    gots, out = refs[:-1], refs[-1]
    count = gots[0].shape[0]
    for i, got in enumerate(gots):
        rows = slice(i * count, (i + 1) * count)

        def summed(at):
            return keep_ref[rows, at] + got[:, at].astype(F32)

        square = jnp.sum(summed(slice(2 * hidden, 2 * hidden + 128)), axis=1, keepdims=True)
        scale = lax.rsqrt(square / D + 1e-6)
        gate = summed(slice(0, hidden)) * scale
        up = summed(slice(hidden, 2 * hidden)) * scale
        out[rows, :] = (gate / (1.0 + jnp.exp(-gate)) * up).astype(BF16)


def down_kernel(C, E, cap, *refs):
    acts, w_ref, outs, x_s, part_s = refs[:C], refs[C], refs[C + 1 : C + 1 + E], refs[-2], refs[-1]
    c = lax.axis_index("ctx")
    e = lax.axis_index("exp")
    own_rows = E * cap // C
    for s in range(C):
        at = aligned(jnp.bitwise_xor(c, s) * own_rows, own_rows)
        x_s[pl.ds(at, own_rows), :] = acts[s][...]
    part_s[...] = dot(x_s[...], w_ref[...]).astype(BF16)
    for out, b in zip(outs, all_hops(E)):
        at = aligned(jnp.bitwise_xor(e, b) * cap, cap)
        out[...] = part_s[pl.ds(at, cap), :]


def mix_kernel(own, got, out):
    out[...] = own[...] + got[...].astype(F32)


def combine_kernel(E, cap, mixed, place_ref, gate_ref, *refs):
    xs, (out, x_s, out_s, sems) = refs[:E], refs[E:]
    for x, b in zip(xs, all_hops(E)):
        x_s[b * cap : (b + 1) * cap, :] = x[...]
    count, _, width = out_s.shape
    copies = []
    for j in range(count):
        cols = slice(j * width, (j + 1) * width)
        collected = lax.dot_general(
            place_ref[...], x_s[:, cols], (((0,), (0,)), ((), ())), preferred_element_type=F32
        )
        out_s[j] = (mixed[:, cols] + gate_ref[:, :1] * collected).astype(BF16)
        copies.append(pltpu.make_async_copy(out_s.at[j], out.at[:, cols], sems.at[j]))
        copies[-1].start()
    for c in copies:
        c.wait()


def body(
    queries,
    new_keys_values,
    cached_keys_values,
    residual,
    out_weight,
    norm_gain,
    routes,
    gates,
    w_gate_up,
    w_down,
):
    C = lax.axis_size("ctx")
    E = lax.axis_size("exp")
    tok = queries.shape[2]
    rows = C * tok
    width = residual.shape[3]
    hidden = w_down.shape[1]
    wide = 2 * hidden
    cap = rows // (2 * E)
    slots = E * cap
    own_rows = slots // C
    qw = QUERY_HEADS // E * HEAD_SIZE

    def permute(x, ctx=0, exp=0):
        pairs = [(c * E + e, (c ^ ctx) * E + (e ^ exp)) for c in range(C) for e in range(E)]
        return lax.ppermute(x, ("ctx", "exp"), pairs)

    def after(x, *others):
        return lax.optimization_barrier((x, *others))[0]

    kv = new_keys_values.shape[3]
    msgs = call(
        functools.partial(pack_kernel, C, qw),
        [sds((tok, 2 * qw + 2 * kv), BF16)] * C,
        3,
        scratch=[pltpu.SemaphoreType.DMA((4 * C,))],
        in_specs=[HBM] * 3,
        cost=(0, 2**20),
        limit=PACK_LIMIT,
    )(
        in_hbm(queries.reshape(tok, queries.shape[3])),
        in_hbm(new_keys_values.reshape(tok, kv)),
        in_hbm(cached_keys_values.reshape(tok, kv)),
    )
    res = residual.reshape(rows, width)
    got = [permute(x, ctx=s) if s else x for s, x in zip(far_first(C), msgs)]
    shards = {0: out_weight, 1: permute(out_weight, exp=1)}
    for d in range(2, C, 2):
        shards[d] = permute(out_weight, exp=spread(d))
    step = [shards[d] for d in range(2, C, 2)]

    def attend(t, msgs):
        return call(
            functools.partial(attend_kernel, C, t),
            [sds((rows, qw), BF16)] + [sds(msgs[0].shape, BF16)] * t,
            C,
            scratch=[pltpu.VMEM((2 * rows, 2 * HEAD_SIZE), BF16), pltpu.VMEM((rows, qw), BF16)],
            cost=(0, 2**14),
            limit=16,
        )(*msgs)

    tokens_last = lambda x: jnp.transpose(x.reshape(C, tok, x.shape[3]), (0, 2, 1))
    own_routes = tokens_last(routes)
    other_routes = permute(after(own_routes, *got), exp=PAIR)
    other, own_msg = attend(1, got)
    theirs = permute(other, exp=PAIR)
    (mine,) = attend(0, [after(got[0], other), *got[1:-1], own_msg])
    place, gate, *staged = call(
        functools.partial(route_kernel, E, cap),
        [sds((slots, rows), BF16), sds((rows, 128), F32)]
        + [sds((qw, width), BF16), sds((rows, width), BF16)],
        4,
        scratch=[pltpu.VMEM((8, rows), jnp.int32), pltpu.VMEM((128, rows), F32)],
        cost=(0, 2**14),
        limit=16,
    )(after(own_routes, mine), tokens_last(gates), out_weight, res)
    other_place = call(
        functools.partial(place_tokens, E, cap, 1),
        sds((slots, rows), BF16),
        1,
        scratch=[pltpu.VMEM((8, rows), jnp.int32)],
        cost=(0, 2**14),
        limit=16,
    )(other_routes)
    shards[0], res = staged

    def gather(x, before=lambda: ()):
        atts = {0: x, 1: permute(x, ctx=1)}
        for s in range(2, C, 2):
            atts[s] = permute(x, ctx=s)
        due = before()
        for s in range(2, C, 2):
            atts[s + 1] = permute(after(atts[s], *due), ctx=1)
        return [atts[s] for s in range(C)]

    def project(atts, *extra):
        operands = [*extra, *atts, shards[0], shards[1], *[w for d in range(2, C - 1) for w in (shards[d] if d % 2 else [shards[d]])]]
        return call(
            functools.partial(project_kernel, C, bool(extra)),
            [sds((rows, width), F32), sds((rows, qw), BF16)],
            len(operands),
            scratch=[
                pltpu.VMEM((C, rows, qw), BF16),
            ],
            cost=(0, 2**14),
        )(*operands)

    mine_all = gather(mine)
    cut = width - max(width * 3 // 8, 128)
    near = after(shards[1], place)[:, cut:]
    for d in range(2, C, 2):
        shards[d + 1] = (
            permute(after(shards[d], place, *mine_all[2::2])[:, :cut], exp=1),
            permute(near, exp=spread(d)),
        )
    acc, last = project(mine_all, res)
    quarter = [shards[d][1] for d in range(3, C, 2)]
    theirs_all = gather(after(theirs, place, shards[1]), lambda: quarter)
    acc_far, last_far = project(theirs_all)
    gain = norm_gain.reshape(1, width)
    own, full, *outgoing = call(
        functools.partial(last_kernel, E, cap),
        [
            sds((rows, width), F32),
            sds((rows, width), BF16),
        ]
        + [sds((2 * cap, width), BF16)] * E,
        8,
        cost=(0, 2**14),
    )(acc, acc_far, last, last_far, *shards[C - 1], place, other_place)
    incoming = [permute(x, exp=b) if b else x for x, b in zip(outgoing, all_hops(E))]
    arrived = permute(after(full, *incoming), exp=PAIR)

    order = [0]
    bit = C // 2
    while bit:
        order = order + [r | bit for r in order]
        bit //= 2
    keep, *sends = call(
        functools.partial(gate_up_kernel, C, E, cap, order),
        [sds((slots // 2, wide + 128), F32)] + [sds((slots // 4, wide + 128), BF16)] * 2,
        E + 2,
        scratch=[pltpu.VMEM((slots, width), BF16), pltpu.VMEM((slots, wide + 128), F32)],
        cost=(0, 2**10),
    )(*incoming, gain, w_gate_up.reshape(width, wide))
    bit = 1
    while 2 * bit < C:
        count = keep.shape[0] // 2
        keep, *sends = call(
            functools.partial(halve_kernel, len(sends)),
            [sds((count, wide + 128), F32)] + [sds((count // 2, wide + 128), BF16)] * 2,
            1 + len(sends),
            cost=(0, 2**10),
        )(keep, *[permute(x, ctx=bit) for x in sends])
        bit *= 2
    activated = call(
        functools.partial(activate_kernel, hidden),
        sds((own_rows, hidden), BF16),
        1 + len(sends),
        cost=(0, 2**10),
    )(keep, *[permute(x, ctx=bit) for x in sends])
    acts = {0: activated}
    acts[bit] = permute(activated, ctx=bit)
    bit //= 2
    while bit:
        for r in list(acts):
            acts[r ^ bit] = permute(acts[r], ctx=bit)
        bit //= 2
    expert_out = call(
        functools.partial(down_kernel, C, E, cap),
        [sds((cap, width), BF16)] * E,
        C + 1,
        scratch=[pltpu.VMEM((slots, hidden), BF16), pltpu.VMEM((slots, width), BF16)],
        cost=(2 * slots * width * hidden, 2 * width * hidden),
    )(acts[0], *[acts[s] for s in range(1, C)], w_down.reshape(hidden, width))
    returned = [permute(x, exp=b) if b else x for x, b in zip(expert_out, all_hops(E))]
    mixed = call(mix_kernel, sds((rows, width), F32), 2, cost=(0, 2**14))(own, arrived)
    columns = min(4, width // 128)
    result = call(
        functools.partial(combine_kernel, E, cap),
        sds((rows, width), BF16),
        3 + E,
        scratch=[
            pltpu.VMEM((slots, width), BF16),
            pltpu.VMEM((columns, rows, width // columns), BF16),
            pltpu.SemaphoreType.DMA((columns,)),
        ],
        out_specs=HBM,
        cost=(0, 2 * 2**20),
    )(mixed, place, gate, *returned)
    return result.reshape(C, 1, tok, width)


def solution(mesh):
    in_specs = (
        P("ctx", "exp", None, None),
        P("ctx", "exp", None, None),
        P("ctx", "exp", None, None),
        P(None, "exp", None, "ctx"),
        P("exp", "ctx"),
        P("ctx"),
        P(None, "exp", None, None),
        P(None, "exp", None, None),
        P("exp", "ctx", None),
        P("exp", None, "ctx"),
    )
    out_specs = P(None, "exp", None, "ctx")
    return jax.shard_map(body, mesh=mesh, in_specs=in_specs, out_specs=out_specs, check_vma=False)
```

```python
import functools
import math

import jax
import jax.numpy as jnp
from jax import lax
from jax.experimental import pallas as pl
from jax.experimental.pallas import tpu as pltpu
from jax.sharding import PartitionSpec as P

D = 4096
QUERY_HEADS = 32
KEY_VALUE_HEADS = 2
HEAD_SIZE = 128
GROUP_EXTENT = QUERY_HEADS // KEY_VALUE_HEADS
NEG_FILL = -1e30
EXPONENT = HEAD_SIZE ** (-0.5) * math.log2(math.e)
BF16 = jnp.bfloat16
F32 = jnp.float32
VMEM = pl.BlockSpec(memory_space=pltpu.VMEM)
HBM = pl.BlockSpec(memory_space=pltpu.HBM)
ANY = pl.BlockSpec(memory_space=pl.ANY)


def call(kernel, out_shape, n_in, scratch=(), cost=(0, 0), limit=32, **kw):
    kw.setdefault("in_specs", [VMEM] * n_in)
    kw.setdefault("out_specs", jax.tree.map(lambda _: VMEM, out_shape))
    return pl.pallas_call(
        kernel,
        out_shape=out_shape,
        scratch_shapes=list(scratch),
        cost_estimate=pl.CostEstimate(flops=cost[0], bytes_accessed=cost[1], transcendentals=0),
        compiler_params=pltpu.CompilerParams(vmem_limit_bytes=limit * 2**20),
        **kw,
    )


def in_hbm(x):
    return pltpu.with_memory_space_constraint(x, pltpu.HBM)


def sds(shape, dtype):
    return jax.ShapeDtypeStruct(shape, dtype)


def dot(a, b):
    return jnp.dot(a, b, preferred_element_type=F32)


PAIR = 4
PACK_LIMIT = 16


def spread(d):
    return (d // PAIR) * 2 * PAIR + d % PAIR


def own_hi_lo():
    e = lax.axis_index("exp")
    return lax.div(e, 2 * PAIR) * PAIR + lax.rem(e, PAIR), lax.rem(lax.div(e, PAIR), 2)


def aligned(x, n):
    return pl.multiple_of(x, n)


def run_copies(pairs, sems):
    copies = [pltpu.make_async_copy(src, dst, sems.at[i]) for i, (src, dst) in enumerate(pairs)]
    for c in copies:
        c.start()
    for c in copies:
        c.wait()


def far_first(C):
    return [*range(2, C), 1, 0]


def all_hops(E):
    return [b for b in range(E) if b & PAIR] + [b for b in reversed(range(E)) if not b & PAIR]


def pack_kernel(C, qw, q_ref, new_ref, past_ref, *refs):
    outs, sems = refs[:C], refs[C]
    c = lax.axis_index("ctx")
    _, lo = own_hi_lo()
    kv = new_ref.shape[1]
    pairs = []
    for i, s in enumerate(far_first(C)):
        target = jnp.bitwise_xor(c, s)
        out = outs[i]
        for t in range(2):
            shard = lax.div(target, PAIR) * 2 * PAIR + lax.rem(target, PAIR)
            shard = shard + PAIR * jnp.bitwise_xor(lo, t)
            at = pl.ds(aligned(shard * qw, 128), qw)
            pairs.append((q_ref.at[:, at], out.at[:, t * qw : (t + 1) * qw]))
        pairs.append((new_ref, out.at[:, 2 * qw : 2 * qw + kv]))
        pairs.append((past_ref, out.at[:, 2 * qw + kv :]))
    run_copies(pairs, sems)


def attend_kernel(C, t, *refs):
    msgs, out, kv_s, q_s = refs[:C], refs[C], refs[-2], refs[-1]
    if t == 1:
        refs[C + 1][...] = msgs[-1][...]
    c = lax.axis_index("ctx")
    tok, qw = msgs[0].shape[0], out.shape[1]
    rows = C * tok
    _, lo = own_hi_lo()
    shard = lax.div(c, PAIR) * 2 * PAIR + lax.rem(c, PAIR) + PAIR * jnp.bitwise_xor(lo, t)
    head = lax.div(shard * (qw // HEAD_SIZE), GROUP_EXTENT)
    for msg, s in zip(msgs, far_first(C)):
        at = aligned(jnp.bitwise_xor(c, s) * tok, tok)
        q_s[pl.ds(at, tok), :] = msg[:, t * qw : (t + 1) * qw]
        for i, to in ((0, rows + at), (1, at)):
            for part in range(2):
                first = 2 * qw + (i * 2 + part) * KEY_VALUE_HEADS * HEAD_SIZE
                cols = pl.ds(aligned(first + head * HEAD_SIZE, 128), HEAD_SIZE)
                kv_s[pl.ds(to, tok), part * HEAD_SIZE : (part + 1) * HEAD_SIZE] = msg[:, cols]
    block = 128
    visible = lax.broadcasted_iota(jnp.int32, (block, block), 1) <= lax.broadcasted_iota(
        jnp.int32, (block, block), 0
    )
    for b in range(rows // block):
        seen = rows + (b + 1) * block
        k = kv_s[:seen, :HEAD_SIZE]
        v = kv_s[:seen, HEAD_SIZE:]
        at = slice(b * block, (b + 1) * block)
        for h in range(qw // HEAD_SIZE):
            q = q_s[at, h * HEAD_SIZE : (h + 1) * HEAD_SIZE]
            scores = lax.dot_general(q, k, (((1,), (1,)), ((), ())), preferred_element_type=F32)
            parts = (scores[:, : seen - block], jnp.where(visible, scores[:, seen - block :], NEG_FILL))
            top = jnp.maximum(*[jnp.max(x, axis=1, keepdims=True) for x in parts])
            parts = [jnp.exp2((x - top) * EXPONENT) for x in parts]
            total = sum(jnp.sum(x, axis=1, keepdims=True) for x in parts)
            numerator = dot(jnp.concatenate([x.astype(BF16) for x in parts], axis=1), v)
            out[at, h * HEAD_SIZE : (h + 1) * HEAD_SIZE] = (numerator / total).astype(BF16)


def place_tokens(E, cap, t, routes_ref, place_ref, line_s):
    blocks, _, tok = routes_ref.shape
    rows = blocks * tok
    earlier = jnp.where(
        lax.broadcasted_iota(jnp.int32, (rows, rows), 0)
        < lax.broadcasted_iota(jnp.int32, (rows, rows), 1),
        1.0,
        0.0,
    ).astype(BF16)
    for i in range(blocks):
        routes = routes_ref[i]
        target = jnp.sum(jnp.where(routes < E, routes + 1, 0), axis=0, keepdims=True) - 1
        line_s[:, i * tok : (i + 1) * tok] = jnp.broadcast_to(target, (8, tok))
    target = line_s[:1, :]
    experts = lax.broadcasted_iota(jnp.int32, (E, rows), 0)
    one_hot = jnp.where(target == experts, 1.0, 0.0)
    rank = jnp.sum(dot(one_hot.astype(BF16), earlier) * one_hot, axis=0, keepdims=True)
    own = jnp.bitwise_xor(lax.axis_index("exp"), PAIR * t)
    slot = jnp.bitwise_xor(target, own) * cap + rank.astype(jnp.int32)
    slot = jnp.where(target >= 0, slot, -1)
    places = lax.broadcasted_iota(jnp.int32, (E * cap, rows), 0)
    place_ref[...] = jnp.where(slot == places, 1.0, 0.0).astype(BF16)


def route_kernel(E, cap, routes_ref, gates_ref, *refs):
    place_ref, gate_ref, line_s, gate_s = refs[2], refs[3], refs[-2], refs[-1]
    for src, dst in zip(refs[:2], refs[4:6]):
        dst[...] = src[...]
    place_tokens(E, cap, 0, routes_ref, place_ref, line_s)
    blocks, _, tok = routes_ref.shape
    for i in range(blocks):
        gate = jnp.sum(jnp.where(routes_ref[i] < E, gates_ref[i], 0.0), axis=0, keepdims=True)
        gate_s[:, i * tok : (i + 1) * tok] = jnp.broadcast_to(gate, (128, tok))
    gate_ref[...] = gate_s[...].T


def project_kernel(C, with_residual, *refs):
    refs, (acc, last, stacked) = list(refs[:-3]), refs[-3:]
    res = refs.pop(0) if with_residual else None
    atts, ws = refs[:C], refs[C:]
    hi, _ = own_hi_lo()
    turn = jnp.bitwise_xor(lax.axis_index("ctx"), hi)
    for s in range(C):
        stacked[jnp.bitwise_xor(turn, s)] = atts[s][...]
    last[...] = stacked[C - 1]
    half = acc.shape[1] // 2
    pieces = list(ws)
    shards = [pieces.pop(0) if d < 2 or d % 2 == 0 else (pieces.pop(0), pieces.pop(0)) for d in range(C - 1)]
    for j in range(2):
        at = slice(j * half, (j + 1) * half)
        total = res[:, at].astype(F32) if with_residual else None
        for d, w in enumerate(shards):
            if not isinstance(w, tuple):
                term = dot(stacked[d], w[:, at])
                total = term if total is None else total + term
        acc[:, at] = total
    for d, w in enumerate(shards):
        if isinstance(w, tuple):
            cut = w[0].shape[1]
            acc[:, :cut] += dot(stacked[d], w[0][...])
            acc[:, cut:] += dot(stacked[d], w[1][...])


def last_kernel(E, cap, *refs):
    accs, lasts, ws, places = refs[:2], refs[2:4], refs[4:6], refs[6:8]
    own_ref, full_ref, *outs = refs[8:]
    cut = ws[0].shape[1]
    for j, cols in enumerate((slice(0, cut), slice(cut, own_ref.shape[1]))):
        for t in (1, 0):
            total = accs[t][:, cols] + dot(lasts[t][...], ws[j][...])
            rounded = total.astype(BF16)
            if t == 0:
                own_ref[:, cols] = total
            else:
                full_ref[:, cols] = rounded
            picked = dot(places[t][...], rounded).astype(BF16)
            for out, b in zip(outs, all_hops(E)):
                at = (b ^ (PAIR * t)) * cap
                out[t * cap : (t + 1) * cap, cols] = picked[at : at + cap]


def gate_up_kernel(C, E, cap, order, *refs):
    xs, gain_ref, w_ref, keep_ref, *sends, x_s, part_s = refs[:E], *refs[E:]
    c = lax.axis_index("ctx")
    e = lax.axis_index("exp")
    own_rows = E * cap // C
    wide = w_ref.shape[1]
    came = dict(zip(all_hops(E), xs))
    for b in range(E):
        at = aligned(jnp.bitwise_xor(e, b) * cap, cap)
        total = came[b][:cap, :].astype(F32) + came[b ^ PAIR][cap:, :].astype(F32)
        x_s[pl.ds(at, cap), :] = (total * gain_ref[...]).astype(BF16)
        square = jnp.sum(total * total, axis=1, keepdims=True)
        lane = lax.broadcasted_iota(jnp.int32, (cap, 128), 1)
        part_s[pl.ds(at, cap), wide:] = jnp.where(lane == 0, square, 0.0)
    step = 512
    for j in range(wide // step):
        at = slice(j * step, (j + 1) * step)
        part_s[:, at] = dot(x_s[...], w_ref[:, at])
    piece = min(own_rows, sends[0].shape[0])
    for k in range(C * own_rows // piece):
        i, rest = divmod(k * piece, own_rows)
        at = aligned(jnp.bitwise_xor(c, order[i]) * own_rows + rest, piece)
        block = part_s[pl.ds(at, piece), :]
        first = k * piece - C // 2 * own_rows
        if first < 0:
            keep_ref[k * piece : (k + 1) * piece, :] = block
        else:
            send_ref = sends[first // sends[0].shape[0]]
            to = first % sends[0].shape[0]
            send_ref[to : to + piece, :wide] = block[:, :wide].astype(BF16)
            square = block[:, wide:]
            high = square.astype(BF16).astype(F32)
            lane = lax.broadcasted_iota(jnp.int32, square.shape, 1)
            low = pltpu.roll(square - high, 1, 1)
            pair = jnp.where(lane == 1, low, high)
            send_ref[to : to + piece, wide:] = pair.astype(BF16)


def halve_kernel(pieces, keep_in, *refs):
    gots, keep_ref, sends = refs[:pieces], refs[pieces], refs[pieces + 1 :]
    rows = keep_ref.shape[0]
    wide = keep_ref.shape[1] - 128
    count = gots[0].shape[0]
    step = min(count, sends[0].shape[0])
    for at in range(0, 2 * rows, step):
        got = gots[at // count][at % count : at % count + step, :]
        total = keep_in[at : at + step, :] + got.astype(F32)
        if at < rows:
            keep_ref[at : at + step, :] = total
            continue
        send_ref = sends[(at - rows) // sends[0].shape[0]]
        to = (at - rows) % sends[0].shape[0]
        send_ref[to : to + step, :wide] = total[:, :wide].astype(BF16)
        square = jnp.sum(total[:, wide:], axis=1, keepdims=True)
        high = square.astype(BF16).astype(F32)
        lane = lax.broadcasted_iota(jnp.int32, (step, 128), 1)
        pair = jnp.where(lane == 0, high, jnp.where(lane == 1, square - high, 0.0))
        send_ref[to : to + step, wide:] = pair.astype(BF16)


def activate_kernel(hidden, keep_ref, *refs):
    gots, out = refs[:-1], refs[-1]
    count = gots[0].shape[0]
    for i, got in enumerate(gots):
        rows = slice(i * count, (i + 1) * count)

        def summed(at):
            return keep_ref[rows, at] + got[:, at].astype(F32)

        square = jnp.sum(summed(slice(2 * hidden, 2 * hidden + 128)), axis=1, keepdims=True)
        scale = lax.rsqrt(square / D + 1e-6)
        gate = summed(slice(0, hidden)) * scale
        up = summed(slice(hidden, 2 * hidden)) * scale
        out[rows, :] = (gate / (1.0 + jnp.exp(-gate)) * up).astype(BF16)


def down_kernel(C, E, cap, *refs):
    acts, w_ref, outs, x_s, part_s = refs[:C], refs[C], refs[C + 1 : C + 1 + E], refs[-2], refs[-1]
    c = lax.axis_index("ctx")
    e = lax.axis_index("exp")
    own_rows = E * cap // C
    for s in range(C):
        at = aligned(jnp.bitwise_xor(c, s) * own_rows, own_rows)
        x_s[pl.ds(at, own_rows), :] = acts[s][...]
    part_s[...] = dot(x_s[...], w_ref[...]).astype(BF16)
    for out, b in zip(outs, all_hops(E)):
        at = aligned(jnp.bitwise_xor(e, b) * cap, cap)
        out[...] = part_s[pl.ds(at, cap), :]


def mix_kernel(own, got, out):
    out[...] = own[...] + got[...].astype(F32)


def combine_kernel(E, cap, mixed, place_ref, gate_ref, *refs):
    xs, (out, x_s, out_s, sems) = refs[:E], refs[E:]
    for x, b in zip(xs, all_hops(E)):
        x_s[b * cap : (b + 1) * cap, :] = x[...]
    count, _, width = out_s.shape
    copies = []
    for j in range(count):
        cols = slice(j * width, (j + 1) * width)
        collected = lax.dot_general(
            place_ref[...], x_s[:, cols], (((0,), (0,)), ((), ())), preferred_element_type=F32
        )
        out_s[j] = (mixed[:, cols] + gate_ref[:, :1] * collected).astype(BF16)
        copies.append(pltpu.make_async_copy(out_s.at[j], out.at[:, cols], sems.at[j]))
        copies[-1].start()
    for c in copies:
        c.wait()


def body(
    queries,
    new_keys_values,
    cached_keys_values,
    residual,
    out_weight,
    norm_gain,
    routes,
    gates,
    w_gate_up,
    w_down,
):
    C = lax.axis_size("ctx")
    E = lax.axis_size("exp")
    tok = queries.shape[2]
    rows = C * tok
    width = residual.shape[3]
    hidden = w_down.shape[1]
    wide = 2 * hidden
    cap = rows // (2 * E)
    slots = E * cap
    own_rows = slots // C
    qw = QUERY_HEADS // E * HEAD_SIZE

    def permute(x, ctx=0, exp=0):
        pairs = [(c * E + e, (c ^ ctx) * E + (e ^ exp)) for c in range(C) for e in range(E)]
        return lax.ppermute(x, ("ctx", "exp"), pairs)

    def after(x, *others):
        return lax.optimization_barrier((x, *others))[0]

    kv = new_keys_values.shape[3]
    msgs = call(
        functools.partial(pack_kernel, C, qw),
        [sds((tok, 2 * qw + 2 * kv), BF16)] * C,
        3,
        scratch=[pltpu.SemaphoreType.DMA((4 * C,))],
        in_specs=[HBM] * 3,
        cost=(0, 2**20),
        limit=PACK_LIMIT,
    )(
        in_hbm(queries.reshape(tok, queries.shape[3])),
        in_hbm(new_keys_values.reshape(tok, kv)),
        in_hbm(cached_keys_values.reshape(tok, kv)),
    )
    res = residual.reshape(rows, width)
    got = [permute(x, ctx=s) if s else x for s, x in zip(far_first(C), msgs)]
    shards = {0: out_weight, 1: permute(out_weight, exp=1)}
    for d in range(2, C, 2):
        shards[d] = permute(out_weight, exp=spread(d))
    step = [shards[d] for d in range(2, C, 2)]

    def attend(t, msgs):
        return call(
            functools.partial(attend_kernel, C, t),
            [sds((rows, qw), BF16)] + [sds(msgs[0].shape, BF16)] * t,
            C,
            scratch=[pltpu.VMEM((2 * rows, 2 * HEAD_SIZE), BF16), pltpu.VMEM((rows, qw), BF16)],
            cost=(0, 2**14),
            limit=16,
        )(*msgs)

    tokens_last = lambda x: jnp.transpose(x.reshape(C, tok, x.shape[3]), (0, 2, 1))
    own_routes = tokens_last(routes)
    other_routes = permute(after(own_routes, *got), exp=PAIR)
    other, own_msg = attend(1, got)
    theirs = permute(other, exp=PAIR)
    (mine,) = attend(0, [after(got[0], other), *got[1:-1], own_msg])
    place, gate, *staged = call(
        functools.partial(route_kernel, E, cap),
        [sds((slots, rows), BF16), sds((rows, 128), F32)]
        + [sds((qw, width), BF16), sds((rows, width), BF16)],
        4,
        scratch=[pltpu.VMEM((8, rows), jnp.int32), pltpu.VMEM((128, rows), F32)],
        cost=(0, 2**14),
        limit=16,
    )(after(own_routes, mine), tokens_last(gates), out_weight, res)
    other_place = call(
        functools.partial(place_tokens, E, cap, 1),
        sds((slots, rows), BF16),
        1,
        scratch=[pltpu.VMEM((8, rows), jnp.int32)],
        cost=(0, 2**14),
        limit=16,
    )(other_routes)
    shards[0], res = staged

    def gather(x, before=lambda: ()):
        atts = {0: x, 1: permute(x, ctx=1)}
        for s in range(2, C, 2):
            atts[s] = permute(x, ctx=s)
        due = before()
        for s in range(2, C, 2):
            atts[s + 1] = permute(after(atts[s], *due), ctx=1)
        return [atts[s] for s in range(C)]

    def project(atts, *extra):
        operands = [*extra, *atts, shards[0], shards[1], *[w for d in range(2, C - 1) for w in (shards[d] if d % 2 else [shards[d]])]]
        return call(
            functools.partial(project_kernel, C, bool(extra)),
            [sds((rows, width), F32), sds((rows, qw), BF16)],
            len(operands),
            scratch=[
                pltpu.VMEM((C, rows, qw), BF16),
            ],
            cost=(0, 2**14),
        )(*operands)

    mine_all = gather(mine)
    cut = width - max(width * 3 // 8, 128)
    near = after(shards[1], place)[:, cut:]
    for d in range(2, C, 2):
        shards[d + 1] = (
            permute(after(shards[d], place, *mine_all[2::2])[:, :cut], exp=1),
            permute(near, exp=spread(d)),
        )
    acc, last = project(mine_all, res)
    quarter = [shards[d][1] for d in range(3, C, 2)]
    theirs_all = gather(after(theirs, place, shards[1]), lambda: (acc, other_place, *quarter))
    acc_far, last_far = project(theirs_all)
    gain = norm_gain.reshape(1, width)
    own, full, *outgoing = call(
        functools.partial(last_kernel, E, cap),
        [
            sds((rows, width), F32),
            sds((rows, width), BF16),
        ]
        + [sds((2 * cap, width), BF16)] * E,
        8,
        cost=(0, 2**14),
    )(acc, acc_far, last, last_far, *shards[C - 1], place, other_place)
    incoming = [permute(x, exp=b) if b else x for x, b in zip(outgoing, all_hops(E))]
    arrived = permute(after(full, *incoming), exp=PAIR)

    order = [0]
    bit = C // 2
    while bit:
        order = order + [r | bit for r in order]
        bit //= 2
    keep, *sends = call(
        functools.partial(gate_up_kernel, C, E, cap, order),
        [sds((slots // 2, wide + 128), F32)] + [sds((slots // 4, wide + 128), BF16)] * 2,
        E + 2,
        scratch=[pltpu.VMEM((slots, width), BF16), pltpu.VMEM((slots, wide + 128), F32)],
        cost=(0, 2**10),
    )(*incoming, gain, w_gate_up.reshape(width, wide))
    bit = 1
    while 2 * bit < C:
        count = keep.shape[0] // 2
        keep, *sends = call(
            functools.partial(halve_kernel, len(sends)),
            [sds((count, wide + 128), F32)] + [sds((count // 2, wide + 128), BF16)] * 2,
            1 + len(sends),
            cost=(0, 2**10),
        )(keep, *[permute(x, ctx=bit) for x in sends])
        bit *= 2
    activated = call(
        functools.partial(activate_kernel, hidden),
        sds((own_rows, hidden), BF16),
        1 + len(sends),
        cost=(0, 2**10),
    )(keep, *[permute(x, ctx=bit) for x in sends])
    acts = {0: activated}
    acts[bit] = permute(activated, ctx=bit)
    bit //= 2
    while bit:
        for r in list(acts):
            acts[r ^ bit] = permute(acts[r], ctx=bit)
        bit //= 2
    expert_out = call(
        functools.partial(down_kernel, C, E, cap),
        [sds((cap, width), BF16)] * E,
        C + 1,
        scratch=[pltpu.VMEM((slots, hidden), BF16), pltpu.VMEM((slots, width), BF16)],
        cost=(2 * slots * width * hidden, 2 * width * hidden),
    )(acts[0], *[acts[s] for s in range(1, C)], w_down.reshape(hidden, width))
    returned = [permute(x, exp=b) if b else x for x, b in zip(expert_out, all_hops(E))]
    mixed = call(mix_kernel, sds((rows, width), F32), 2, cost=(0, 2**14))(own, arrived)
    columns = min(4, width // 128)
    result = call(
        functools.partial(combine_kernel, E, cap),
        sds((rows, width), BF16),
        3 + E,
        scratch=[
            pltpu.VMEM((slots, width), BF16),
            pltpu.VMEM((columns, rows, width // columns), BF16),
            pltpu.SemaphoreType.DMA((columns,)),
        ],
        out_specs=HBM,
        cost=(0, 2 * 2**20),
    )(mixed, place, gate, *returned)
    return result.reshape(C, 1, tok, width)


def solution(mesh):
    in_specs = (
        P("ctx", "exp", None, None),
        P("ctx", "exp", None, None),
        P("ctx", "exp", None, None),
        P(None, "exp", None, "ctx"),
        P("exp", "ctx"),
        P("ctx"),
        P(None, "exp", None, None),
        P(None, "exp", None, None),
        P("exp", "ctx", None),
        P("exp", None, "ctx"),
    )
    out_specs = P(None, "exp", None, "ctx")
    return jax.shard_map(body, mesh=mesh, in_specs=in_specs, out_specs=out_specs, check_vma=False)
```

```python
import functools
import math

import jax
import jax.numpy as jnp
from jax import lax
from jax.experimental import pallas as pl
from jax.experimental.pallas import tpu as pltpu
from jax.sharding import PartitionSpec as P

D = 4096
QUERY_HEADS = 32
KEY_VALUE_HEADS = 2
HEAD_SIZE = 128
GROUP_EXTENT = QUERY_HEADS // KEY_VALUE_HEADS
NEG_FILL = -1e30
EXPONENT = HEAD_SIZE ** (-0.5) * math.log2(math.e)
BF16 = jnp.bfloat16
F32 = jnp.float32
VMEM = pl.BlockSpec(memory_space=pltpu.VMEM)
HBM = pl.BlockSpec(memory_space=pltpu.HBM)
ANY = pl.BlockSpec(memory_space=pl.ANY)


def call(kernel, out_shape, n_in, scratch=(), cost=(0, 0), limit=32, **kw):
    kw.setdefault("in_specs", [VMEM] * n_in)
    kw.setdefault("out_specs", jax.tree.map(lambda _: VMEM, out_shape))
    return pl.pallas_call(
        kernel,
        out_shape=out_shape,
        scratch_shapes=list(scratch),
        cost_estimate=pl.CostEstimate(flops=cost[0], bytes_accessed=cost[1], transcendentals=0),
        compiler_params=pltpu.CompilerParams(vmem_limit_bytes=limit * 2**20),
        **kw,
    )


def in_hbm(x):
    return pltpu.with_memory_space_constraint(x, pltpu.HBM)


def sds(shape, dtype):
    return jax.ShapeDtypeStruct(shape, dtype)


def dot(a, b):
    return jnp.dot(a, b, preferred_element_type=F32)


PAIR = 4
PACK_LIMIT = 16


def spread(d):
    return (d // PAIR) * 2 * PAIR + d % PAIR


def own_hi_lo():
    e = lax.axis_index("exp")
    return lax.div(e, 2 * PAIR) * PAIR + lax.rem(e, PAIR), lax.rem(lax.div(e, PAIR), 2)


def aligned(x, n):
    return pl.multiple_of(x, n)


def run_copies(pairs, sems):
    copies = [pltpu.make_async_copy(src, dst, sems.at[i]) for i, (src, dst) in enumerate(pairs)]
    for c in copies:
        c.start()
    for c in copies:
        c.wait()


def far_first(C):
    return [*range(2, C), 1, 0]


def all_hops(E):
    return [b for b in range(E) if b & PAIR] + [b for b in reversed(range(E)) if not b & PAIR]


def pack_kernel(C, qw, q_ref, new_ref, past_ref, *refs):
    outs, sems = refs[:C], refs[C]
    c = lax.axis_index("ctx")
    _, lo = own_hi_lo()
    kv = new_ref.shape[1]
    pairs = []
    for i, s in enumerate(far_first(C)):
        target = jnp.bitwise_xor(c, s)
        out = outs[i]
        for t in range(2):
            shard = lax.div(target, PAIR) * 2 * PAIR + lax.rem(target, PAIR)
            shard = shard + PAIR * jnp.bitwise_xor(lo, t)
            at = pl.ds(aligned(shard * qw, 128), qw)
            pairs.append((q_ref.at[:, at], out.at[:, t * qw : (t + 1) * qw]))
        pairs.append((new_ref, out.at[:, 2 * qw : 2 * qw + kv]))
        pairs.append((past_ref, out.at[:, 2 * qw + kv :]))
    run_copies(pairs, sems)


def attend_kernel(C, t, *refs):
    msgs, out, kv_s, q_s = refs[:C], refs[C], refs[-2], refs[-1]
    if t == 1:
        refs[C + 1][...] = msgs[-1][...]
    c = lax.axis_index("ctx")
    tok, qw = msgs[0].shape[0], out.shape[1]
    rows = C * tok
    _, lo = own_hi_lo()
    shard = lax.div(c, PAIR) * 2 * PAIR + lax.rem(c, PAIR) + PAIR * jnp.bitwise_xor(lo, t)
    head = lax.div(shard * (qw // HEAD_SIZE), GROUP_EXTENT)
    for msg, s in zip(msgs, far_first(C)):
        at = aligned(jnp.bitwise_xor(c, s) * tok, tok)
        q_s[pl.ds(at, tok), :] = msg[:, t * qw : (t + 1) * qw]
        for i, to in ((0, rows + at), (1, at)):
            for part in range(2):
                first = 2 * qw + (i * 2 + part) * KEY_VALUE_HEADS * HEAD_SIZE
                cols = pl.ds(aligned(first + head * HEAD_SIZE, 128), HEAD_SIZE)
                kv_s[pl.ds(to, tok), part * HEAD_SIZE : (part + 1) * HEAD_SIZE] = msg[:, cols]
    block = 128
    visible = lax.broadcasted_iota(jnp.int32, (block, block), 1) <= lax.broadcasted_iota(
        jnp.int32, (block, block), 0
    )
    for b in range(rows // block):
        seen = rows + (b + 1) * block
        k = kv_s[:seen, :HEAD_SIZE]
        v = kv_s[:seen, HEAD_SIZE:]
        at = slice(b * block, (b + 1) * block)
        for h in range(qw // HEAD_SIZE):
            q = q_s[at, h * HEAD_SIZE : (h + 1) * HEAD_SIZE]
            scores = lax.dot_general(q, k, (((1,), (1,)), ((), ())), preferred_element_type=F32)
            parts = (scores[:, : seen - block], jnp.where(visible, scores[:, seen - block :], NEG_FILL))
            top = jnp.maximum(*[jnp.max(x, axis=1, keepdims=True) for x in parts])
            parts = [jnp.exp2((x - top) * EXPONENT) for x in parts]
            total = sum(jnp.sum(x, axis=1, keepdims=True) for x in parts)
            numerator = dot(jnp.concatenate([x.astype(BF16) for x in parts], axis=1), v)
            out[at, h * HEAD_SIZE : (h + 1) * HEAD_SIZE] = (numerator / total).astype(BF16)


def place_tokens(E, cap, t, routes_ref, place_ref, line_s):
    blocks, _, tok = routes_ref.shape
    rows = blocks * tok
    earlier = jnp.where(
        lax.broadcasted_iota(jnp.int32, (rows, rows), 0)
        < lax.broadcasted_iota(jnp.int32, (rows, rows), 1),
        1.0,
        0.0,
    ).astype(BF16)
    for i in range(blocks):
        routes = routes_ref[i]
        target = jnp.sum(jnp.where(routes < E, routes + 1, 0), axis=0, keepdims=True) - 1
        line_s[:, i * tok : (i + 1) * tok] = jnp.broadcast_to(target, (8, tok))
    target = line_s[:1, :]
    experts = lax.broadcasted_iota(jnp.int32, (E, rows), 0)
    one_hot = jnp.where(target == experts, 1.0, 0.0)
    rank = jnp.sum(dot(one_hot.astype(BF16), earlier) * one_hot, axis=0, keepdims=True)
    own = jnp.bitwise_xor(lax.axis_index("exp"), PAIR * t)
    slot = jnp.bitwise_xor(target, own) * cap + rank.astype(jnp.int32)
    slot = jnp.where(target >= 0, slot, -1)
    places = lax.broadcasted_iota(jnp.int32, (E * cap, rows), 0)
    place_ref[...] = jnp.where(slot == places, 1.0, 0.0).astype(BF16)


def route_kernel(E, cap, routes_ref, gates_ref, *refs):
    place_ref, gate_ref, line_s, gate_s = refs[2], refs[3], refs[-2], refs[-1]
    for src, dst in zip(refs[:2], refs[4:6]):
        dst[...] = src[...]
    place_tokens(E, cap, 0, routes_ref, place_ref, line_s)
    blocks, _, tok = routes_ref.shape
    for i in range(blocks):
        gate = jnp.sum(jnp.where(routes_ref[i] < E, gates_ref[i], 0.0), axis=0, keepdims=True)
        gate_s[:, i * tok : (i + 1) * tok] = jnp.broadcast_to(gate, (128, tok))
    gate_ref[...] = gate_s[...].T


def project_kernel(C, with_residual, *refs):
    refs, (acc, last, stacked) = list(refs[:-3]), refs[-3:]
    res = refs.pop(0) if with_residual else None
    atts, ws = refs[:C], refs[C:]
    hi, _ = own_hi_lo()
    turn = jnp.bitwise_xor(lax.axis_index("ctx"), hi)
    for s in range(C):
        stacked[jnp.bitwise_xor(turn, s)] = atts[s][...]
    last[...] = stacked[C - 1]
    half = acc.shape[1] // 2
    pieces = list(ws)
    shards = [pieces.pop(0) if d < 2 or d % 2 == 0 else (pieces.pop(0), pieces.pop(0)) for d in range(C - 1)]
    for j in range(2):
        at = slice(j * half, (j + 1) * half)
        total = res[:, at].astype(F32) if with_residual else None
        for d, w in enumerate(shards):
            if not isinstance(w, tuple):
                term = dot(stacked[d], w[:, at])
                total = term if total is None else total + term
        acc[:, at] = total
    for d, w in enumerate(shards):
        if isinstance(w, tuple):
            cut = w[0].shape[1]
            acc[:, :cut] += dot(stacked[d], w[0][...])
            acc[:, cut:] += dot(stacked[d], w[1][...])


def last_kernel(E, cap, *refs):
    accs, lasts, ws, places = refs[:2], refs[2:4], refs[4:6], refs[6:8]
    own_ref, full_ref, *outs = refs[8:]
    cut = ws[0].shape[1]
    for j, cols in enumerate((slice(0, cut), slice(cut, own_ref.shape[1]))):
        for t in (1, 0):
            total = accs[t][:, cols] + dot(lasts[t][...], ws[j][...])
            rounded = total.astype(BF16)
            if t == 0:
                own_ref[:, cols] = total
            else:
                full_ref[:, cols] = rounded
            picked = dot(places[t][...], rounded).astype(BF16)
            for out, b in zip(outs, all_hops(E)):
                at = (b ^ (PAIR * t)) * cap
                out[t * cap : (t + 1) * cap, cols] = picked[at : at + cap]


def gate_up_kernel(C, E, cap, order, *refs):
    xs, gain_ref, w_ref, keep_ref, *sends, x_s, part_s = refs[:E], *refs[E:]
    c = lax.axis_index("ctx")
    e = lax.axis_index("exp")
    own_rows = E * cap // C
    wide = w_ref.shape[1]
    came = dict(zip(all_hops(E), xs))
    for b in range(E):
        at = aligned(jnp.bitwise_xor(e, b) * cap, cap)
        total = came[b][:cap, :].astype(F32) + came[b ^ PAIR][cap:, :].astype(F32)
        x_s[pl.ds(at, cap), :] = (total * gain_ref[...]).astype(BF16)
        square = jnp.sum(total * total, axis=1, keepdims=True)
        lane = lax.broadcasted_iota(jnp.int32, (cap, 128), 1)
        part_s[pl.ds(at, cap), wide:] = jnp.where(lane == 0, square, 0.0)
    step = 512
    for j in range(wide // step):
        at = slice(j * step, (j + 1) * step)
        part_s[:, at] = dot(x_s[...], w_ref[:, at])
    piece = min(own_rows, sends[0].shape[0])
    for k in range(C * own_rows // piece):
        i, rest = divmod(k * piece, own_rows)
        at = aligned(jnp.bitwise_xor(c, order[i]) * own_rows + rest, piece)
        block = part_s[pl.ds(at, piece), :]
        first = k * piece - C // 2 * own_rows
        if first < 0:
            keep_ref[k * piece : (k + 1) * piece, :] = block
        else:
            send_ref = sends[first // sends[0].shape[0]]
            to = first % sends[0].shape[0]
            send_ref[to : to + piece, :wide] = block[:, :wide].astype(BF16)
            square = block[:, wide:]
            high = square.astype(BF16).astype(F32)
            lane = lax.broadcasted_iota(jnp.int32, square.shape, 1)
            low = pltpu.roll(square - high, 1, 1)
            pair = jnp.where(lane == 1, low, high)
            send_ref[to : to + piece, wide:] = pair.astype(BF16)


def halve_kernel(pieces, keep_in, *refs):
    gots, keep_ref, sends = refs[:pieces], refs[pieces], refs[pieces + 1 :]
    rows = keep_ref.shape[0]
    wide = keep_ref.shape[1] - 128
    count = gots[0].shape[0]
    step = min(count, sends[0].shape[0])
    for at in range(0, 2 * rows, step):
        got = gots[at // count][at % count : at % count + step, :]
        total = keep_in[at : at + step, :] + got.astype(F32)
        if at < rows:
            keep_ref[at : at + step, :] = total
            continue
        send_ref = sends[(at - rows) // sends[0].shape[0]]
        to = (at - rows) % sends[0].shape[0]
        send_ref[to : to + step, :wide] = total[:, :wide].astype(BF16)
        square = jnp.sum(total[:, wide:], axis=1, keepdims=True)
        high = square.astype(BF16).astype(F32)
        lane = lax.broadcasted_iota(jnp.int32, (step, 128), 1)
        pair = jnp.where(lane == 0, high, jnp.where(lane == 1, square - high, 0.0))
        send_ref[to : to + step, wide:] = pair.astype(BF16)


def activate_kernel(hidden, keep_ref, *refs):
    gots, out = refs[:-1], refs[-1]
    count = gots[0].shape[0]
    for i, got in enumerate(gots):
        rows = slice(i * count, (i + 1) * count)

        def summed(at):
            return keep_ref[rows, at] + got[:, at].astype(F32)

        square = jnp.sum(summed(slice(2 * hidden, 2 * hidden + 128)), axis=1, keepdims=True)
        scale = lax.rsqrt(square / D + 1e-6)
        gate = summed(slice(0, hidden)) * scale
        up = summed(slice(hidden, 2 * hidden)) * scale
        out[rows, :] = (gate / (1.0 + jnp.exp(-gate)) * up).astype(BF16)


def down_kernel(C, E, cap, *refs):
    acts, w_ref, outs, x_s, part_s = refs[:C], refs[C], refs[C + 1 : C + 1 + E], refs[-2], refs[-1]
    c = lax.axis_index("ctx")
    e = lax.axis_index("exp")
    own_rows = E * cap // C
    for s in range(C):
        at = aligned(jnp.bitwise_xor(c, s) * own_rows, own_rows)
        x_s[pl.ds(at, own_rows), :] = acts[s][...]
    part_s[...] = dot(x_s[...], w_ref[...]).astype(BF16)
    for out, b in zip(outs, all_hops(E)):
        at = aligned(jnp.bitwise_xor(e, b) * cap, cap)
        out[...] = part_s[pl.ds(at, cap), :]


def mix_kernel(own, got, out):
    out[...] = own[...] + got[...].astype(F32)


def combine_kernel(E, cap, mixed, place_ref, gate_ref, *refs):
    xs, (out, x_s, out_s, sems) = refs[:E], refs[E:]
    for x, b in zip(xs, all_hops(E)):
        x_s[b * cap : (b + 1) * cap, :] = x[...]
    count, _, width = out_s.shape
    copies = []
    for j in range(count):
        cols = slice(j * width, (j + 1) * width)
        collected = lax.dot_general(
            place_ref[...], x_s[:, cols], (((0,), (0,)), ((), ())), preferred_element_type=F32
        )
        out_s[j] = (mixed[:, cols] + gate_ref[:, :1] * collected).astype(BF16)
        copies.append(pltpu.make_async_copy(out_s.at[j], out.at[:, cols], sems.at[j]))
        copies[-1].start()
    for c in copies:
        c.wait()


def body(
    queries,
    new_keys_values,
    cached_keys_values,
    residual,
    out_weight,
    norm_gain,
    routes,
    gates,
    w_gate_up,
    w_down,
):
    C = lax.axis_size("ctx")
    E = lax.axis_size("exp")
    tok = queries.shape[2]
    rows = C * tok
    width = residual.shape[3]
    hidden = w_down.shape[1]
    wide = 2 * hidden
    cap = rows // (2 * E)
    slots = E * cap
    own_rows = slots // C
    qw = QUERY_HEADS // E * HEAD_SIZE

    def permute(x, ctx=0, exp=0):
        pairs = [(c * E + e, (c ^ ctx) * E + (e ^ exp)) for c in range(C) for e in range(E)]
        return lax.ppermute(x, ("ctx", "exp"), pairs)

    def after(x, *others):
        return lax.optimization_barrier((x, *others))[0]

    kv = new_keys_values.shape[3]
    msgs = call(
        functools.partial(pack_kernel, C, qw),
        [sds((tok, 2 * qw + 2 * kv), BF16)] * C,
        3,
        scratch=[pltpu.SemaphoreType.DMA((4 * C,))],
        in_specs=[HBM] * 3,
        cost=(0, 2**20),
        limit=PACK_LIMIT,
    )(
        in_hbm(queries.reshape(tok, queries.shape[3])),
        in_hbm(new_keys_values.reshape(tok, kv)),
        in_hbm(cached_keys_values.reshape(tok, kv)),
    )
    res = residual.reshape(rows, width)
    got = [permute(x, ctx=s) if s else x for s, x in zip(far_first(C), msgs)]
    shards = {0: out_weight, 1: permute(out_weight, exp=1)}
    for d in range(2, C, 2):
        shards[d] = permute(out_weight, exp=spread(d))
    step = [shards[d] for d in range(2, C, 2)]

    def attend(t, msgs):
        return call(
            functools.partial(attend_kernel, C, t),
            [sds((rows, qw), BF16)] + [sds(msgs[0].shape, BF16)] * t,
            C,
            scratch=[pltpu.VMEM((2 * rows, 2 * HEAD_SIZE), BF16), pltpu.VMEM((rows, qw), BF16)],
            cost=(0, 2**14),
            limit=16,
        )(*msgs)

    tokens_last = lambda x: jnp.transpose(x.reshape(C, tok, x.shape[3]), (0, 2, 1))
    own_routes = tokens_last(routes)
    other_routes = permute(after(own_routes, *got), exp=PAIR)
    other, own_msg = attend(1, got)
    theirs = permute(other, exp=PAIR)
    (mine,) = attend(0, [after(got[0], other), *got[1:-1], own_msg])
    place, gate, *staged = call(
        functools.partial(route_kernel, E, cap),
        [sds((slots, rows), BF16), sds((rows, 128), F32)]
        + [sds((qw, width), BF16), sds((rows, width), BF16)],
        4,
        scratch=[pltpu.VMEM((8, rows), jnp.int32), pltpu.VMEM((128, rows), F32)],
        cost=(0, 2**14),
        limit=16,
    )(after(own_routes, mine), tokens_last(gates), out_weight, res)
    other_place = call(
        functools.partial(place_tokens, E, cap, 1),
        sds((slots, rows), BF16),
        1,
        scratch=[pltpu.VMEM((8, rows), jnp.int32)],
        cost=(0, 2**14),
        limit=16,
    )(other_routes)
    shards[0], res = staged

    def gather(x, before=lambda: ()):
        atts = {0: x, 1: permute(x, ctx=1)}
        for s in range(2, C, 2):
            atts[s] = permute(x, ctx=s)
        due = before()
        for s in range(2, C, 2):
            atts[s + 1] = permute(after(atts[s], *due), ctx=1)
        return [atts[s] for s in range(C)]

    def project(atts, *extra):
        operands = [*extra, *atts, shards[0], shards[1], *[w for d in range(2, C - 1) for w in (shards[d] if d % 2 else [shards[d]])]]
        return call(
            functools.partial(project_kernel, C, bool(extra)),
            [sds((rows, width), F32), sds((rows, qw), BF16)],
            len(operands),
            scratch=[
                pltpu.VMEM((C, rows, qw), BF16),
            ],
            cost=(0, 2**14),
        )(*operands)

    mine_all = gather(mine)
    cut = width - max(width * 3 // 8, 128)
    near = after(shards[1], place)[:, cut:]
    for d in range(2, C, 2):
        shards[d + 1] = (
            permute(after(shards[d], place, *mine_all[2::2])[:, :cut], exp=1),
            permute(near, exp=spread(d)),
        )
    acc, last = project(mine_all, res)
    quarter = [shards[d][1] for d in range(3, C, 2)]
    theirs_all = gather(after(theirs, place, shards[1]), lambda: quarter)
    acc_far, last_far = project(theirs_all)
    gain = norm_gain.reshape(1, width)
    own, full, *outgoing = call(
        functools.partial(last_kernel, E, cap),
        [
            sds((rows, width), F32),
            sds((rows, width), BF16),
        ]
        + [sds((2 * cap, width), BF16)] * E,
        8,
        cost=(0, 2**14),
    )(acc, acc_far, last, last_far, *shards[C - 1], place, other_place)
    incoming = [permute(x, exp=b) if b else x for x, b in zip(outgoing, all_hops(E))]
    arrived = permute(after(full, *incoming), exp=PAIR)

    order = [0]
    bit = C // 2
    while bit:
        order = order + [r | bit for r in order]
        bit //= 2
    keep, *sends = call(
        functools.partial(gate_up_kernel, C, E, cap, order),
        [sds((slots // 2, wide + 128), F32)] + [sds((slots // 8, wide + 128), BF16)] * 4,
        E + 2,
        scratch=[pltpu.VMEM((slots, width), BF16), pltpu.VMEM((slots, wide + 128), F32)],
        cost=(0, 2**10),
    )(*incoming, gain, w_gate_up.reshape(width, wide))
    bit = 1
    while 2 * bit < C:
        count = keep.shape[0] // 2
        keep, *sends = call(
            functools.partial(halve_kernel, len(sends)),
            [sds((count, wide + 128), F32)] + [sds((count // 2, wide + 128), BF16)] * 2,
            1 + len(sends),
            cost=(0, 2**10),
        )(keep, *[permute(x, ctx=bit) for x in sends])
        bit *= 2
    activated = call(
        functools.partial(activate_kernel, hidden),
        sds((own_rows, hidden), BF16),
        1 + len(sends),
        cost=(0, 2**10),
    )(keep, *[permute(x, ctx=bit) for x in sends])
    acts = {0: activated}
    acts[bit] = permute(activated, ctx=bit)
    bit //= 2
    while bit:
        for r in list(acts):
            acts[r ^ bit] = permute(acts[r], ctx=bit)
        bit //= 2
    expert_out = call(
        functools.partial(down_kernel, C, E, cap),
        [sds((cap, width), BF16)] * E,
        C + 1,
        scratch=[pltpu.VMEM((slots, hidden), BF16), pltpu.VMEM((slots, width), BF16)],
        cost=(2 * slots * width * hidden, 2 * width * hidden),
    )(acts[0], *[acts[s] for s in range(1, C)], w_down.reshape(hidden, width))
    returned = [permute(x, exp=b) if b else x for x, b in zip(expert_out, all_hops(E))]
    mixed = call(mix_kernel, sds((rows, width), F32), 2, cost=(0, 2**14))(own, arrived)
    columns = min(4, width // 128)
    result = call(
        functools.partial(combine_kernel, E, cap),
        sds((rows, width), BF16),
        3 + E,
        scratch=[
            pltpu.VMEM((slots, width), BF16),
            pltpu.VMEM((columns, rows, width // columns), BF16),
            pltpu.SemaphoreType.DMA((columns,)),
        ],
        out_specs=HBM,
        cost=(0, 2 * 2**20),
    )(mixed, place, gate, *returned)
    return result.reshape(C, 1, tok, width)


def solution(mesh):
    in_specs = (
        P("ctx", "exp", None, None),
        P("ctx", "exp", None, None),
        P("ctx", "exp", None, None),
        P(None, "exp", None, "ctx"),
        P("exp", "ctx"),
        P("ctx"),
        P(None, "exp", None, None),
        P(None, "exp", None, None),
        P("exp", "ctx", None),
        P("exp", None, "ctx"),
    )
    out_specs = P(None, "exp", None, "ctx")
    return jax.shard_map(body, mesh=mesh, in_specs=in_specs, out_specs=out_specs, check_vma=False)
```

```python
import functools
import math

import jax
import jax.numpy as jnp
from jax import lax
from jax.experimental import pallas as pl
from jax.experimental.pallas import tpu as pltpu
from jax.sharding import PartitionSpec as P

D = 4096
QUERY_HEADS = 32
KEY_VALUE_HEADS = 2
HEAD_SIZE = 128
GROUP_EXTENT = QUERY_HEADS // KEY_VALUE_HEADS
NEG_FILL = -1e30
EXPONENT = HEAD_SIZE ** (-0.5) * math.log2(math.e)
BF16 = jnp.bfloat16
F32 = jnp.float32
VMEM = pl.BlockSpec(memory_space=pltpu.VMEM)
HBM = pl.BlockSpec(memory_space=pltpu.HBM)
ANY = pl.BlockSpec(memory_space=pl.ANY)


def call(kernel, out_shape, n_in, scratch=(), cost=(0, 0), limit=32, **kw):
    kw.setdefault("in_specs", [VMEM] * n_in)
    kw.setdefault("out_specs", jax.tree.map(lambda _: VMEM, out_shape))
    return pl.pallas_call(
        kernel,
        out_shape=out_shape,
        scratch_shapes=list(scratch),
        cost_estimate=pl.CostEstimate(flops=cost[0], bytes_accessed=cost[1], transcendentals=0),
        compiler_params=pltpu.CompilerParams(vmem_limit_bytes=limit * 2**20),
        **kw,
    )


def in_hbm(x):
    return pltpu.with_memory_space_constraint(x, pltpu.HBM)


def sds(shape, dtype):
    return jax.ShapeDtypeStruct(shape, dtype)


def dot(a, b):
    return jnp.dot(a, b, preferred_element_type=F32)


PAIR = 4
PACK_LIMIT = 16


def spread(d):
    return (d // PAIR) * 2 * PAIR + d % PAIR


def own_hi_lo():
    e = lax.axis_index("exp")
    return lax.div(e, 2 * PAIR) * PAIR + lax.rem(e, PAIR), lax.rem(lax.div(e, PAIR), 2)


def aligned(x, n):
    return pl.multiple_of(x, n)


def run_copies(pairs, sems):
    copies = [pltpu.make_async_copy(src, dst, sems.at[i]) for i, (src, dst) in enumerate(pairs)]
    for c in copies:
        c.start()
    for c in copies:
        c.wait()


def far_first(C):
    return [*range(2, C), 1, 0]


def all_hops(E):
    return [b for b in range(E) if b & PAIR] + [b for b in reversed(range(E)) if not b & PAIR]


def pack_kernel(C, qw, q_ref, new_ref, past_ref, *refs):
    outs, sems = refs[:C], refs[C]
    c = lax.axis_index("ctx")
    _, lo = own_hi_lo()
    kv = new_ref.shape[1]
    pairs = []
    for i, s in enumerate(far_first(C)):
        target = jnp.bitwise_xor(c, s)
        out = outs[i]
        for t in range(2):
            shard = lax.div(target, PAIR) * 2 * PAIR + lax.rem(target, PAIR)
            shard = shard + PAIR * jnp.bitwise_xor(lo, t)
            at = pl.ds(aligned(shard * qw, 128), qw)
            pairs.append((q_ref.at[:, at], out.at[:, t * qw : (t + 1) * qw]))
        pairs.append((new_ref, out.at[:, 2 * qw : 2 * qw + kv]))
        pairs.append((past_ref, out.at[:, 2 * qw + kv :]))
    run_copies(pairs, sems)


def attend_kernel(C, t, *refs):
    msgs, out, kv_s, q_s = refs[:C], refs[C], refs[-2], refs[-1]
    if t == 1:
        refs[C + 1][...] = msgs[-1][...]
    c = lax.axis_index("ctx")
    tok, qw = msgs[0].shape[0], out.shape[1]
    rows = C * tok
    _, lo = own_hi_lo()
    shard = lax.div(c, PAIR) * 2 * PAIR + lax.rem(c, PAIR) + PAIR * jnp.bitwise_xor(lo, t)
    head = lax.div(shard * (qw // HEAD_SIZE), GROUP_EXTENT)
    for msg, s in zip(msgs, far_first(C)):
        at = aligned(jnp.bitwise_xor(c, s) * tok, tok)
        q_s[pl.ds(at, tok), :] = msg[:, t * qw : (t + 1) * qw]
        for i, to in ((0, rows + at), (1, at)):
            for part in range(2):
                first = 2 * qw + (i * 2 + part) * KEY_VALUE_HEADS * HEAD_SIZE
                cols = pl.ds(aligned(first + head * HEAD_SIZE, 128), HEAD_SIZE)
                kv_s[pl.ds(to, tok), part * HEAD_SIZE : (part + 1) * HEAD_SIZE] = msg[:, cols]
    block = 128
    visible = lax.broadcasted_iota(jnp.int32, (block, block), 1) <= lax.broadcasted_iota(
        jnp.int32, (block, block), 0
    )
    for b in range(rows // block):
        seen = rows + (b + 1) * block
        k = kv_s[:seen, :HEAD_SIZE]
        v = kv_s[:seen, HEAD_SIZE:]
        at = slice(b * block, (b + 1) * block)
        for h in range(qw // HEAD_SIZE):
            q = q_s[at, h * HEAD_SIZE : (h + 1) * HEAD_SIZE]
            scores = lax.dot_general(q, k, (((1,), (1,)), ((), ())), preferred_element_type=F32)
            parts = (scores[:, : seen - block], jnp.where(visible, scores[:, seen - block :], NEG_FILL))
            top = jnp.maximum(*[jnp.max(x, axis=1, keepdims=True) for x in parts])
            parts = [jnp.exp2((x - top) * EXPONENT) for x in parts]
            total = sum(jnp.sum(x, axis=1, keepdims=True) for x in parts)
            numerator = dot(jnp.concatenate([x.astype(BF16) for x in parts], axis=1), v)
            out[at, h * HEAD_SIZE : (h + 1) * HEAD_SIZE] = (numerator / total).astype(BF16)


def place_tokens(E, cap, t, routes_ref, place_ref, line_s):
    blocks, _, tok = routes_ref.shape
    rows = blocks * tok
    earlier = jnp.where(
        lax.broadcasted_iota(jnp.int32, (rows, rows), 0)
        < lax.broadcasted_iota(jnp.int32, (rows, rows), 1),
        1.0,
        0.0,
    ).astype(BF16)
    for i in range(blocks):
        routes = routes_ref[i]
        target = jnp.sum(jnp.where(routes < E, routes + 1, 0), axis=0, keepdims=True) - 1
        line_s[:, i * tok : (i + 1) * tok] = jnp.broadcast_to(target, (8, tok))
    target = line_s[:1, :]
    experts = lax.broadcasted_iota(jnp.int32, (E, rows), 0)
    one_hot = jnp.where(target == experts, 1.0, 0.0)
    rank = jnp.sum(dot(one_hot.astype(BF16), earlier) * one_hot, axis=0, keepdims=True)
    own = jnp.bitwise_xor(lax.axis_index("exp"), PAIR * t)
    slot = jnp.bitwise_xor(target, own) * cap + rank.astype(jnp.int32)
    slot = jnp.where(target >= 0, slot, -1)
    places = lax.broadcasted_iota(jnp.int32, (E * cap, rows), 0)
    place_ref[...] = jnp.where(slot == places, 1.0, 0.0).astype(BF16)


def route_kernel(E, cap, routes_ref, gates_ref, *refs):
    place_ref, gate_ref, line_s, gate_s = refs[2], refs[3], refs[-2], refs[-1]
    for src, dst in zip(refs[:2], refs[4:6]):
        dst[...] = src[...]
    place_tokens(E, cap, 0, routes_ref, place_ref, line_s)
    blocks, _, tok = routes_ref.shape
    for i in range(blocks):
        gate = jnp.sum(jnp.where(routes_ref[i] < E, gates_ref[i], 0.0), axis=0, keepdims=True)
        gate_s[:, i * tok : (i + 1) * tok] = jnp.broadcast_to(gate, (128, tok))
    gate_ref[...] = gate_s[...].T


def project_kernel(C, with_residual, *refs):
    refs, (acc, last, stacked) = list(refs[:-3]), refs[-3:]
    res = refs.pop(0) if with_residual else None
    atts, ws = refs[:C], refs[C:]
    hi, _ = own_hi_lo()
    turn = jnp.bitwise_xor(lax.axis_index("ctx"), hi)
    for s in range(C):
        stacked[jnp.bitwise_xor(turn, s)] = atts[s][...]
    last[...] = stacked[C - 1]
    half = acc.shape[1] // 2
    pieces = list(ws)
    shards = [pieces.pop(0) if d < 2 or d % 2 == 0 else (pieces.pop(0), pieces.pop(0)) for d in range(C - 1)]
    for j in range(2):
        at = slice(j * half, (j + 1) * half)
        total = res[:, at].astype(F32) if with_residual else None
        for d, w in enumerate(shards):
            if not isinstance(w, tuple):
                term = dot(stacked[d], w[:, at])
                total = term if total is None else total + term
        acc[:, at] = total
    for d, w in enumerate(shards):
        if isinstance(w, tuple):
            cut = w[0].shape[1]
            acc[:, :cut] += dot(stacked[d], w[0][...])
            acc[:, cut:] += dot(stacked[d], w[1][...])


def last_kernel(E, cap, *refs):
    accs, lasts, ws, places = refs[:2], refs[2:4], refs[4:6], refs[6:8]
    own_ref, full_ref, *outs = refs[8:]
    cut = ws[0].shape[1]
    for j, cols in enumerate((slice(0, cut), slice(cut, own_ref.shape[1]))):
        for t in (1, 0):
            total = accs[t][:, cols] + dot(lasts[t][...], ws[j][...])
            rounded = total.astype(BF16)
            if t == 0:
                own_ref[:, cols] = total
            else:
                full_ref[:, cols] = rounded
            picked = dot(places[t][...], rounded).astype(BF16)
            for out, b in zip(outs, all_hops(E)):
                at = (b ^ (PAIR * t)) * cap
                out[t * cap : (t + 1) * cap, cols] = picked[at : at + cap]


def gate_up_kernel(C, E, cap, order, *refs):
    xs, gain_ref, w_ref, keep_ref, *sends, x_s, part_s = refs[:E], *refs[E:]
    c = lax.axis_index("ctx")
    e = lax.axis_index("exp")
    own_rows = E * cap // C
    wide = w_ref.shape[1]
    came = dict(zip(all_hops(E), xs))
    for b in range(E):
        at = aligned(jnp.bitwise_xor(e, b) * cap, cap)
        total = came[b][:cap, :].astype(F32) + came[b ^ PAIR][cap:, :].astype(F32)
        x_s[pl.ds(at, cap), :] = (total * gain_ref[...]).astype(BF16)
        square = jnp.sum(total * total, axis=1, keepdims=True)
        lane = lax.broadcasted_iota(jnp.int32, (cap, 128), 1)
        part_s[pl.ds(at, cap), wide:] = jnp.where(lane == 0, square, 0.0)
    step = 512
    for j in range(wide // step):
        at = slice(j * step, (j + 1) * step)
        part_s[:, at] = dot(x_s[...], w_ref[:, at])
    piece = min(own_rows, sends[0].shape[0])
    for k in range(C * own_rows // piece):
        i, rest = divmod(k * piece, own_rows)
        at = aligned(jnp.bitwise_xor(c, order[i]) * own_rows + rest, piece)
        block = part_s[pl.ds(at, piece), :]
        first = k * piece - C // 2 * own_rows
        if first < 0:
            keep_ref[k * piece : (k + 1) * piece, :] = block
        else:
            send_ref = sends[first // sends[0].shape[0]]
            to = first % sends[0].shape[0]
            send_ref[to : to + piece, :wide] = block[:, :wide].astype(BF16)
            square = block[:, wide:]
            high = square.astype(BF16).astype(F32)
            lane = lax.broadcasted_iota(jnp.int32, square.shape, 1)
            low = pltpu.roll(square - high, 1, 1)
            pair = jnp.where(lane == 1, low, high)
            send_ref[to : to + piece, wide:] = pair.astype(BF16)


def halve_kernel(pieces, keep_in, *refs):
    gots, keep_ref, sends = refs[:pieces], refs[pieces], refs[pieces + 1 :]
    rows = keep_ref.shape[0]
    wide = keep_ref.shape[1] - 128
    count = gots[0].shape[0]
    step = min(count, sends[0].shape[0])
    for at in range(0, 2 * rows, step):
        got = gots[at // count][at % count : at % count + step, :]
        total = keep_in[at : at + step, :] + got.astype(F32)
        if at < rows:
            keep_ref[at : at + step, :] = total
            continue
        send_ref = sends[(at - rows) // sends[0].shape[0]]
        to = (at - rows) % sends[0].shape[0]
        send_ref[to : to + step, :wide] = total[:, :wide].astype(BF16)
        square = jnp.sum(total[:, wide:], axis=1, keepdims=True)
        high = square.astype(BF16).astype(F32)
        lane = lax.broadcasted_iota(jnp.int32, (step, 128), 1)
        pair = jnp.where(lane == 0, high, jnp.where(lane == 1, square - high, 0.0))
        send_ref[to : to + step, wide:] = pair.astype(BF16)


def activate_kernel(hidden, keep_ref, *refs):
    gots, out = refs[:-1], refs[-1]
    count = gots[0].shape[0]
    for i, got in enumerate(gots):
        rows = slice(i * count, (i + 1) * count)

        def summed(at):
            return keep_ref[rows, at] + got[:, at].astype(F32)

        square = jnp.sum(summed(slice(2 * hidden, 2 * hidden + 128)), axis=1, keepdims=True)
        scale = lax.rsqrt(square / D + 1e-6)
        gate = summed(slice(0, hidden)) * scale
        up = summed(slice(hidden, 2 * hidden)) * scale
        out[rows, :] = (gate / (1.0 + jnp.exp(-gate)) * up).astype(BF16)


def down_kernel(C, E, cap, *refs):
    acts, w_ref, outs, x_s, part_s = refs[:C], refs[C], refs[C + 1 : C + 1 + E], refs[-2], refs[-1]
    c = lax.axis_index("ctx")
    e = lax.axis_index("exp")
    own_rows = E * cap // C
    for s in range(C):
        at = aligned(jnp.bitwise_xor(c, s) * own_rows, own_rows)
        x_s[pl.ds(at, own_rows), :] = acts[s][...]
    part_s[...] = dot(x_s[...], w_ref[...]).astype(BF16)
    for out, b in zip(outs, all_hops(E)):
        at = aligned(jnp.bitwise_xor(e, b) * cap, cap)
        out[...] = part_s[pl.ds(at, cap), :]


def mix_kernel(own, got, out):
    out[...] = own[...] + got[...].astype(F32)


def combine_kernel(E, cap, mixed, place_ref, gate_ref, *refs):
    xs, (out, x_s, out_s, sems) = refs[:E], refs[E:]
    for x, b in zip(xs, all_hops(E)):
        x_s[b * cap : (b + 1) * cap, :] = x[...]
    count, _, width = out_s.shape
    copies = []
    for j in range(count):
        cols = slice(j * width, (j + 1) * width)
        collected = lax.dot_general(
            place_ref[...], x_s[:, cols], (((0,), (0,)), ((), ())), preferred_element_type=F32
        )
        out_s[j] = (mixed[:, cols] + gate_ref[:, :1] * collected).astype(BF16)
        copies.append(pltpu.make_async_copy(out_s.at[j], out.at[:, cols], sems.at[j]))
        copies[-1].start()
    for c in copies:
        c.wait()


def body(
    queries,
    new_keys_values,
    cached_keys_values,
    residual,
    out_weight,
    norm_gain,
    routes,
    gates,
    w_gate_up,
    w_down,
):
    C = lax.axis_size("ctx")
    E = lax.axis_size("exp")
    tok = queries.shape[2]
    rows = C * tok
    width = residual.shape[3]
    hidden = w_down.shape[1]
    wide = 2 * hidden
    cap = rows // (2 * E)
    slots = E * cap
    own_rows = slots // C
    qw = QUERY_HEADS // E * HEAD_SIZE

    def permute(x, ctx=0, exp=0):
        pairs = [(c * E + e, (c ^ ctx) * E + (e ^ exp)) for c in range(C) for e in range(E)]
        return lax.ppermute(x, ("ctx", "exp"), pairs)

    def after(x, *others):
        return lax.optimization_barrier((x, *others))[0]

    kv = new_keys_values.shape[3]
    msgs = call(
        functools.partial(pack_kernel, C, qw),
        [sds((tok, 2 * qw + 2 * kv), BF16)] * C,
        3,
        scratch=[pltpu.SemaphoreType.DMA((4 * C,))],
        in_specs=[HBM] * 3,
        cost=(0, 2**20),
        limit=PACK_LIMIT,
    )(
        in_hbm(queries.reshape(tok, queries.shape[3])),
        in_hbm(new_keys_values.reshape(tok, kv)),
        in_hbm(cached_keys_values.reshape(tok, kv)),
    )
    res = residual.reshape(rows, width)
    got = [permute(x, ctx=s) if s else x for s, x in zip(far_first(C), msgs)]
    shards = {0: out_weight, 1: permute(out_weight, exp=1)}
    for d in range(2, C, 2):
        shards[d] = permute(out_weight, exp=spread(d))
    step = [shards[d] for d in range(2, C, 2)]

    def attend(t, msgs):
        return call(
            functools.partial(attend_kernel, C, t),
            [sds((rows, qw), BF16)] + [sds(msgs[0].shape, BF16)] * t,
            C,
            scratch=[pltpu.VMEM((2 * rows, 2 * HEAD_SIZE), BF16), pltpu.VMEM((rows, qw), BF16)],
            cost=(0, 2**14),
            limit=16,
        )(*msgs)

    tokens_last = lambda x: jnp.transpose(x.reshape(C, tok, x.shape[3]), (0, 2, 1))
    own_routes = tokens_last(routes)
    other_routes = permute(after(own_routes, *got), exp=PAIR)
    other, own_msg = attend(1, got)
    theirs = permute(other, exp=PAIR)
    (mine,) = attend(0, [after(got[0], other), *got[1:-1], own_msg])
    place, gate, *staged = call(
        functools.partial(route_kernel, E, cap),
        [sds((slots, rows), BF16), sds((rows, 128), F32)]
        + [sds((qw, width), BF16), sds((rows, width), BF16)],
        4,
        scratch=[pltpu.VMEM((8, rows), jnp.int32), pltpu.VMEM((128, rows), F32)],
        cost=(0, 2**14),
        limit=16,
    )(after(own_routes, mine), tokens_last(gates), out_weight, res)
    other_place = call(
        functools.partial(place_tokens, E, cap, 1),
        sds((slots, rows), BF16),
        1,
        scratch=[pltpu.VMEM((8, rows), jnp.int32)],
        cost=(0, 2**14),
        limit=16,
    )(other_routes)
    shards[0], res = staged

    def gather(x, before=lambda: ()):
        atts = {0: x, 1: permute(x, ctx=1)}
        for s in range(2, C, 2):
            atts[s] = permute(x, ctx=s)
        due = before()
        for s in range(2, C, 2):
            atts[s + 1] = permute(after(atts[s], *due), ctx=1)
        return [atts[s] for s in range(C)]

    def project(atts, *extra):
        operands = [*extra, *atts, shards[0], shards[1], *[w for d in range(2, C - 1) for w in (shards[d] if d % 2 else [shards[d]])]]
        return call(
            functools.partial(project_kernel, C, bool(extra)),
            [sds((rows, width), F32), sds((rows, qw), BF16)],
            len(operands),
            scratch=[
                pltpu.VMEM((C, rows, qw), BF16),
            ],
            cost=(0, 2**14),
        )(*operands)

    mine_all = gather(mine)
    cut = width - max(width * 3 // 8, 128)
    near = after(shards[1], place)[:, cut:]
    for d in range(2, C, 2):
        shards[d + 1] = (
            permute(after(shards[d], place)[:, :cut], exp=1),
            permute(near, exp=spread(d)),
        )
    acc, last = project(mine_all, res)
    quarter = [shards[d][1] for d in range(3, C, 2)]
    theirs_all = gather(after(theirs, place, shards[1]), lambda: quarter)
    acc_far, last_far = project(theirs_all)
    gain = norm_gain.reshape(1, width)
    own, full, *outgoing = call(
        functools.partial(last_kernel, E, cap),
        [
            sds((rows, width), F32),
            sds((rows, width), BF16),
        ]
        + [sds((2 * cap, width), BF16)] * E,
        8,
        cost=(0, 2**14),
    )(acc, acc_far, last, last_far, *shards[C - 1], place, other_place)
    incoming = [permute(x, exp=b) if b else x for x, b in zip(outgoing, all_hops(E))]
    arrived = permute(after(full, *incoming[: E // 2]), exp=PAIR)

    order = [0]
    bit = C // 2
    while bit:
        order = order + [r | bit for r in order]
        bit //= 2
    keep, *sends = call(
        functools.partial(gate_up_kernel, C, E, cap, order),
        [sds((slots // 2, wide + 128), F32)] + [sds((slots // 8, wide + 128), BF16)] * 4,
        E + 2,
        scratch=[pltpu.VMEM((slots, width), BF16), pltpu.VMEM((slots, wide + 128), F32)],
        cost=(0, 2**10),
    )(*incoming, gain, w_gate_up.reshape(width, wide))
    bit = 1
    while 2 * bit < C:
        count = keep.shape[0] // 2
        keep, *sends = call(
            functools.partial(halve_kernel, len(sends)),
            [sds((count, wide + 128), F32)] + [sds((count // 2, wide + 128), BF16)] * 2,
            1 + len(sends),
            cost=(0, 2**10),
        )(keep, *[permute(x, ctx=bit) for x in sends])
        bit *= 2
    activated = call(
        functools.partial(activate_kernel, hidden),
        sds((own_rows, hidden), BF16),
        1 + len(sends),
        cost=(0, 2**10),
    )(keep, *[permute(x, ctx=bit) for x in sends])
    acts = {0: activated}
    acts[bit] = permute(activated, ctx=bit)
    bit //= 2
    while bit:
        for r in list(acts):
            acts[r ^ bit] = permute(acts[r], ctx=bit)
        bit //= 2
    expert_out = call(
        functools.partial(down_kernel, C, E, cap),
        [sds((cap, width), BF16)] * E,
        C + 1,
        scratch=[pltpu.VMEM((slots, hidden), BF16), pltpu.VMEM((slots, width), BF16)],
        cost=(2 * slots * width * hidden, 2 * width * hidden),
    )(acts[0], *[acts[s] for s in range(1, C)], w_down.reshape(hidden, width))
    returned = [permute(x, exp=b) if b else x for x, b in zip(expert_out, all_hops(E))]
    mixed = call(mix_kernel, sds((rows, width), F32), 2, cost=(0, 2**14))(own, arrived)
    columns = min(4, width // 128)
    result = call(
        functools.partial(combine_kernel, E, cap),
        sds((rows, width), BF16),
        3 + E,
        scratch=[
            pltpu.VMEM((slots, width), BF16),
            pltpu.VMEM((columns, rows, width // columns), BF16),
            pltpu.SemaphoreType.DMA((columns,)),
        ],
        out_specs=HBM,
        cost=(0, 2 * 2**20),
    )(mixed, place, gate, *returned)
    return result.reshape(C, 1, tok, width)


def solution(mesh):
    in_specs = (
        P("ctx", "exp", None, None),
        P("ctx", "exp", None, None),
        P("ctx", "exp", None, None),
        P(None, "exp", None, "ctx"),
        P("exp", "ctx"),
        P("ctx"),
        P(None, "exp", None, None),
        P(None, "exp", None, None),
        P("exp", "ctx", None),
        P("exp", None, "ctx"),
    )
    out_specs = P(None, "exp", None, "ctx")
    return jax.shard_map(body, mesh=mesh, in_specs=in_specs, out_specs=out_specs, check_vma=False)
```

```python
import functools
import math

import jax
import jax.numpy as jnp
from jax import lax
from jax.experimental import pallas as pl
from jax.experimental.pallas import tpu as pltpu
from jax.sharding import PartitionSpec as P

D = 4096
QUERY_HEADS = 32
KEY_VALUE_HEADS = 2
HEAD_SIZE = 128
GROUP_EXTENT = QUERY_HEADS // KEY_VALUE_HEADS
NEG_FILL = -1e30
EXPONENT = HEAD_SIZE ** (-0.5) * math.log2(math.e)
BF16 = jnp.bfloat16
F32 = jnp.float32
VMEM = pl.BlockSpec(memory_space=pltpu.VMEM)
HBM = pl.BlockSpec(memory_space=pltpu.HBM)
ANY = pl.BlockSpec(memory_space=pl.ANY)


def call(kernel, out_shape, n_in, scratch=(), cost=(0, 0), limit=32, **kw):
    kw.setdefault("in_specs", [VMEM] * n_in)
    kw.setdefault("out_specs", jax.tree.map(lambda _: VMEM, out_shape))
    return pl.pallas_call(
        kernel,
        out_shape=out_shape,
        scratch_shapes=list(scratch),
        cost_estimate=pl.CostEstimate(flops=cost[0], bytes_accessed=cost[1], transcendentals=0),
        compiler_params=pltpu.CompilerParams(vmem_limit_bytes=limit * 2**20),
        **kw,
    )


def in_hbm(x):
    return pltpu.with_memory_space_constraint(x, pltpu.HBM)


def sds(shape, dtype):
    return jax.ShapeDtypeStruct(shape, dtype)


def dot(a, b):
    return jnp.dot(a, b, preferred_element_type=F32)


PAIR = 4
PACK_LIMIT = 16


def spread(d):
    return (d // PAIR) * 2 * PAIR + d % PAIR


def own_hi_lo():
    e = lax.axis_index("exp")
    return lax.div(e, 2 * PAIR) * PAIR + lax.rem(e, PAIR), lax.rem(lax.div(e, PAIR), 2)


def aligned(x, n):
    return pl.multiple_of(x, n)


def run_copies(pairs, sems):
    copies = [pltpu.make_async_copy(src, dst, sems.at[i]) for i, (src, dst) in enumerate(pairs)]
    for c in copies:
        c.start()
    for c in copies:
        c.wait()


def far_first(C):
    return [*range(2, C), 1, 0]


def all_hops(E):
    return [b for b in range(E) if b & PAIR] + [b for b in reversed(range(E)) if not b & PAIR]


def pack_kernel(C, qw, q_ref, new_ref, past_ref, *refs):
    outs, sems = refs[:C], refs[C]
    c = lax.axis_index("ctx")
    _, lo = own_hi_lo()
    kv = new_ref.shape[1]
    pairs = []
    for i, s in enumerate(far_first(C)):
        target = jnp.bitwise_xor(c, s)
        out = outs[i]
        for t in range(2):
            shard = lax.div(target, PAIR) * 2 * PAIR + lax.rem(target, PAIR)
            shard = shard + PAIR * jnp.bitwise_xor(lo, t)
            at = pl.ds(aligned(shard * qw, 128), qw)
            pairs.append((q_ref.at[:, at], out.at[:, t * qw : (t + 1) * qw]))
        pairs.append((new_ref, out.at[:, 2 * qw : 2 * qw + kv]))
        pairs.append((past_ref, out.at[:, 2 * qw + kv :]))
    run_copies(pairs, sems)


def attend_kernel(C, t, *refs):
    msgs, out, kv_s, q_s = refs[:C], refs[C], refs[-2], refs[-1]
    if t == 1:
        refs[C + 1][...] = msgs[-1][...]
    c = lax.axis_index("ctx")
    tok, qw = msgs[0].shape[0], out.shape[1]
    rows = C * tok
    _, lo = own_hi_lo()
    shard = lax.div(c, PAIR) * 2 * PAIR + lax.rem(c, PAIR) + PAIR * jnp.bitwise_xor(lo, t)
    head = lax.div(shard * (qw // HEAD_SIZE), GROUP_EXTENT)
    for msg, s in zip(msgs, far_first(C)):
        at = aligned(jnp.bitwise_xor(c, s) * tok, tok)
        q_s[pl.ds(at, tok), :] = msg[:, t * qw : (t + 1) * qw]
        for i, to in ((0, rows + at), (1, at)):
            for part in range(2):
                first = 2 * qw + (i * 2 + part) * KEY_VALUE_HEADS * HEAD_SIZE
                cols = pl.ds(aligned(first + head * HEAD_SIZE, 128), HEAD_SIZE)
                kv_s[pl.ds(to, tok), part * HEAD_SIZE : (part + 1) * HEAD_SIZE] = msg[:, cols]
    block = 128
    visible = lax.broadcasted_iota(jnp.int32, (block, block), 1) <= lax.broadcasted_iota(
        jnp.int32, (block, block), 0
    )
    for b in range(rows // block):
        seen = rows + (b + 1) * block
        k = kv_s[:seen, :HEAD_SIZE]
        v = kv_s[:seen, HEAD_SIZE:]
        at = slice(b * block, (b + 1) * block)
        for h in range(qw // HEAD_SIZE):
            q = q_s[at, h * HEAD_SIZE : (h + 1) * HEAD_SIZE]
            scores = lax.dot_general(q, k, (((1,), (1,)), ((), ())), preferred_element_type=F32)
            parts = (scores[:, : seen - block], jnp.where(visible, scores[:, seen - block :], NEG_FILL))
            top = jnp.maximum(*[jnp.max(x, axis=1, keepdims=True) for x in parts])
            parts = [jnp.exp2((x - top) * EXPONENT) for x in parts]
            total = sum(jnp.sum(x, axis=1, keepdims=True) for x in parts)
            numerator = dot(jnp.concatenate([x.astype(BF16) for x in parts], axis=1), v)
            out[at, h * HEAD_SIZE : (h + 1) * HEAD_SIZE] = (numerator / total).astype(BF16)


def place_tokens(E, cap, t, routes_ref, place_ref, line_s):
    blocks, _, tok = routes_ref.shape
    rows = blocks * tok
    earlier = jnp.where(
        lax.broadcasted_iota(jnp.int32, (rows, rows), 0)
        < lax.broadcasted_iota(jnp.int32, (rows, rows), 1),
        1.0,
        0.0,
    ).astype(BF16)
    for i in range(blocks):
        routes = routes_ref[i]
        target = jnp.sum(jnp.where(routes < E, routes + 1, 0), axis=0, keepdims=True) - 1
        line_s[:, i * tok : (i + 1) * tok] = jnp.broadcast_to(target, (8, tok))
    target = line_s[:1, :]
    experts = lax.broadcasted_iota(jnp.int32, (E, rows), 0)
    one_hot = jnp.where(target == experts, 1.0, 0.0)
    rank = jnp.sum(dot(one_hot.astype(BF16), earlier) * one_hot, axis=0, keepdims=True)
    own = jnp.bitwise_xor(lax.axis_index("exp"), PAIR * t)
    slot = jnp.bitwise_xor(target, own) * cap + rank.astype(jnp.int32)
    slot = jnp.where(target >= 0, slot, -1)
    places = lax.broadcasted_iota(jnp.int32, (E * cap, rows), 0)
    place_ref[...] = jnp.where(slot == places, 1.0, 0.0).astype(BF16)


def route_kernel(E, cap, routes_ref, gates_ref, *refs):
    place_ref, gate_ref, line_s, gate_s = refs[2], refs[3], refs[-2], refs[-1]
    for src, dst in zip(refs[:2], refs[4:6]):
        dst[...] = src[...]
    place_tokens(E, cap, 0, routes_ref, place_ref, line_s)
    blocks, _, tok = routes_ref.shape
    for i in range(blocks):
        gate = jnp.sum(jnp.where(routes_ref[i] < E, gates_ref[i], 0.0), axis=0, keepdims=True)
        gate_s[:, i * tok : (i + 1) * tok] = jnp.broadcast_to(gate, (128, tok))
    gate_ref[...] = gate_s[...].T


def project_kernel(C, with_residual, *refs):
    refs, (acc, last, stacked) = list(refs[:-3]), refs[-3:]
    res = refs.pop(0) if with_residual else None
    atts, ws = refs[:C], refs[C:]
    hi, _ = own_hi_lo()
    turn = jnp.bitwise_xor(lax.axis_index("ctx"), hi)
    for s in range(C):
        stacked[jnp.bitwise_xor(turn, s)] = atts[s][...]
    last[...] = stacked[C - 1]
    half = acc.shape[1] // 2
    pieces = list(ws)
    shards = [pieces.pop(0) if d < 2 or d % 2 == 0 else (pieces.pop(0), pieces.pop(0)) for d in range(C - 1)]
    for j in range(2):
        at = slice(j * half, (j + 1) * half)
        total = res[:, at].astype(F32) if with_residual else None
        for d, w in enumerate(shards):
            if not isinstance(w, tuple):
                term = dot(stacked[d], w[:, at])
                total = term if total is None else total + term
        acc[:, at] = total
    for d, w in enumerate(shards):
        if isinstance(w, tuple):
            cut = w[0].shape[1]
            acc[:, :cut] += dot(stacked[d], w[0][...])
            acc[:, cut:] += dot(stacked[d], w[1][...])


def last_kernel(E, cap, *refs):
    accs, lasts, ws, places = refs[:2], refs[2:4], refs[4:6], refs[6:8]
    own_ref, full_ref, *outs = refs[8:]
    cut = ws[0].shape[1]
    for j, cols in enumerate((slice(0, cut), slice(cut, own_ref.shape[1]))):
        for t in (1, 0):
            total = accs[t][:, cols] + dot(lasts[t][...], ws[j][...])
            rounded = total.astype(BF16)
            if t == 0:
                own_ref[:, cols] = total
            else:
                full_ref[:, cols] = rounded
            picked = dot(places[t][...], rounded).astype(BF16)
            for out, b in zip(outs, all_hops(E)):
                at = (b ^ (PAIR * t)) * cap
                out[t * cap : (t + 1) * cap, cols] = picked[at : at + cap]


def gate_up_kernel(C, E, cap, order, *refs):
    xs, gain_ref, w_ref, keep_ref, *sends, x_s, part_s = refs[:E], *refs[E:]
    c = lax.axis_index("ctx")
    e = lax.axis_index("exp")
    own_rows = E * cap // C
    wide = w_ref.shape[1]
    came = dict(zip(all_hops(E), xs))
    for b in range(E):
        at = aligned(jnp.bitwise_xor(e, b) * cap, cap)
        total = came[b][:cap, :].astype(F32) + came[b ^ PAIR][cap:, :].astype(F32)
        x_s[pl.ds(at, cap), :] = (total * gain_ref[...]).astype(BF16)
        square = jnp.sum(total * total, axis=1, keepdims=True)
        lane = lax.broadcasted_iota(jnp.int32, (cap, 128), 1)
        part_s[pl.ds(at, cap), wide:] = jnp.where(lane == 0, square, 0.0)
    step = 512
    for j in range(wide // step):
        at = slice(j * step, (j + 1) * step)
        part_s[:, at] = dot(x_s[...], w_ref[:, at])
    piece = min(own_rows, sends[0].shape[0])
    for k in range(C * own_rows // piece):
        i, rest = divmod(k * piece, own_rows)
        at = aligned(jnp.bitwise_xor(c, order[i]) * own_rows + rest, piece)
        block = part_s[pl.ds(at, piece), :]
        first = k * piece - C // 2 * own_rows
        if first < 0:
            keep_ref[k * piece : (k + 1) * piece, :] = block
        else:
            send_ref = sends[first // sends[0].shape[0]]
            to = first % sends[0].shape[0]
            send_ref[to : to + piece, :wide] = block[:, :wide].astype(BF16)
            square = block[:, wide:]
            high = square.astype(BF16).astype(F32)
            lane = lax.broadcasted_iota(jnp.int32, square.shape, 1)
            low = pltpu.roll(square - high, 1, 1)
            pair = jnp.where(lane == 1, low, high)
            send_ref[to : to + piece, wide:] = pair.astype(BF16)


def halve_kernel(pieces, keep_in, *refs):
    gots, keep_ref, sends = refs[:pieces], refs[pieces], refs[pieces + 1 :]
    rows = keep_ref.shape[0]
    wide = keep_ref.shape[1] - 128
    count = gots[0].shape[0]
    step = min(count, sends[0].shape[0])
    for at in range(0, 2 * rows, step):
        got = gots[at // count][at % count : at % count + step, :]
        total = keep_in[at : at + step, :] + got.astype(F32)
        if at < rows:
            keep_ref[at : at + step, :] = total
            continue
        send_ref = sends[(at - rows) // sends[0].shape[0]]
        to = (at - rows) % sends[0].shape[0]
        send_ref[to : to + step, :wide] = total[:, :wide].astype(BF16)
        square = jnp.sum(total[:, wide:], axis=1, keepdims=True)
        high = square.astype(BF16).astype(F32)
        lane = lax.broadcasted_iota(jnp.int32, (step, 128), 1)
        pair = jnp.where(lane == 0, high, jnp.where(lane == 1, square - high, 0.0))
        send_ref[to : to + step, wide:] = pair.astype(BF16)


def activate_kernel(hidden, keep_ref, *refs):
    gots, out = refs[:-1], refs[-1]
    count = gots[0].shape[0]
    for i, got in enumerate(gots):
        rows = slice(i * count, (i + 1) * count)

        def summed(at):
            return keep_ref[rows, at] + got[:, at].astype(F32)

        square = jnp.sum(summed(slice(2 * hidden, 2 * hidden + 128)), axis=1, keepdims=True)
        scale = lax.rsqrt(square / D + 1e-6)
        gate = summed(slice(0, hidden)) * scale
        up = summed(slice(hidden, 2 * hidden)) * scale
        out[rows, :] = (gate / (1.0 + jnp.exp(-gate)) * up).astype(BF16)


def down_kernel(C, E, cap, *refs):
    acts, w_ref, outs, x_s, part_s = refs[:C], refs[C], refs[C + 1 : C + 1 + E], refs[-2], refs[-1]
    c = lax.axis_index("ctx")
    e = lax.axis_index("exp")
    own_rows = E * cap // C
    for s in range(C):
        at = aligned(jnp.bitwise_xor(c, s) * own_rows, own_rows)
        x_s[pl.ds(at, own_rows), :] = acts[s][...]
    part_s[...] = dot(x_s[...], w_ref[...]).astype(BF16)
    for out, b in zip(outs, all_hops(E)):
        at = aligned(jnp.bitwise_xor(e, b) * cap, cap)
        out[...] = part_s[pl.ds(at, cap), :]


def mix_kernel(own, got, out):
    out[...] = own[...] + got[...].astype(F32)


def combine_kernel(E, cap, mixed, place_ref, gate_ref, *refs):
    xs, (out, x_s, out_s, sems) = refs[:E], refs[E:]
    for x, b in zip(xs, all_hops(E)):
        x_s[b * cap : (b + 1) * cap, :] = x[...]
    count, _, width = out_s.shape
    copies = []
    for j in range(count):
        cols = slice(j * width, (j + 1) * width)
        collected = lax.dot_general(
            place_ref[...], x_s[:, cols], (((0,), (0,)), ((), ())), preferred_element_type=F32
        )
        out_s[j] = (mixed[:, cols] + gate_ref[:, :1] * collected).astype(BF16)
        copies.append(pltpu.make_async_copy(out_s.at[j], out.at[:, cols], sems.at[j]))
        copies[-1].start()
    for c in copies:
        c.wait()


def body(
    queries,
    new_keys_values,
    cached_keys_values,
    residual,
    out_weight,
    norm_gain,
    routes,
    gates,
    w_gate_up,
    w_down,
):
    C = lax.axis_size("ctx")
    E = lax.axis_size("exp")
    tok = queries.shape[2]
    rows = C * tok
    width = residual.shape[3]
    hidden = w_down.shape[1]
    wide = 2 * hidden
    cap = rows // (2 * E)
    slots = E * cap
    own_rows = slots // C
    qw = QUERY_HEADS // E * HEAD_SIZE

    def permute(x, ctx=0, exp=0):
        pairs = [(c * E + e, (c ^ ctx) * E + (e ^ exp)) for c in range(C) for e in range(E)]
        return lax.ppermute(x, ("ctx", "exp"), pairs)

    def after(x, *others):
        return lax.optimization_barrier((x, *others))[0]

    kv = new_keys_values.shape[3]
    msgs = call(
        functools.partial(pack_kernel, C, qw),
        [sds((tok, 2 * qw + 2 * kv), BF16)] * C,
        3,
        scratch=[pltpu.SemaphoreType.DMA((4 * C,))],
        in_specs=[HBM] * 3,
        cost=(0, 2**20),
        limit=PACK_LIMIT,
    )(
        in_hbm(queries.reshape(tok, queries.shape[3])),
        in_hbm(new_keys_values.reshape(tok, kv)),
        in_hbm(cached_keys_values.reshape(tok, kv)),
    )
    res = residual.reshape(rows, width)
    got = [permute(x, ctx=s) if s else x for s, x in zip(far_first(C), msgs)]
    shards = {0: out_weight, 1: permute(out_weight, exp=1)}
    for d in range(2, C, 2):
        shards[d] = permute(out_weight, exp=spread(d))
    step = [shards[d] for d in range(2, C, 2)]

    def attend(t, msgs):
        return call(
            functools.partial(attend_kernel, C, t),
            [sds((rows, qw), BF16)] + [sds(msgs[0].shape, BF16)] * t,
            C,
            scratch=[pltpu.VMEM((2 * rows, 2 * HEAD_SIZE), BF16), pltpu.VMEM((rows, qw), BF16)],
            cost=(0, 2**14),
            limit=16,
        )(*msgs)

    tokens_last = lambda x: jnp.transpose(x.reshape(C, tok, x.shape[3]), (0, 2, 1))
    own_routes = tokens_last(routes)
    other_routes = permute(after(own_routes, *got), exp=PAIR)
    other, own_msg = attend(1, got)
    theirs = permute(other, exp=PAIR)
    (mine,) = attend(0, [after(got[0], other), *got[1:-1], own_msg])
    place, gate, *staged = call(
        functools.partial(route_kernel, E, cap),
        [sds((slots, rows), BF16), sds((rows, 128), F32)]
        + [sds((qw, width), BF16), sds((rows, width), BF16)],
        4,
        scratch=[pltpu.VMEM((8, rows), jnp.int32), pltpu.VMEM((128, rows), F32)],
        cost=(0, 2**14),
        limit=16,
    )(after(own_routes, other), tokens_last(gates), out_weight, res)
    other_place = call(
        functools.partial(place_tokens, E, cap, 1),
        sds((slots, rows), BF16),
        1,
        scratch=[pltpu.VMEM((8, rows), jnp.int32)],
        cost=(0, 2**14),
        limit=16,
    )(other_routes)
    shards[0], res = staged

    def gather(x, before=lambda: ()):
        atts = {0: x, 1: permute(x, ctx=1)}
        for s in range(2, C, 2):
            atts[s] = permute(x, ctx=s)
        due = before()
        for s in range(2, C, 2):
            atts[s + 1] = permute(after(atts[s], *due), ctx=1)
        return [atts[s] for s in range(C)]

    def project(atts, *extra):
        operands = [*extra, *atts, shards[0], shards[1], *[w for d in range(2, C - 1) for w in (shards[d] if d % 2 else [shards[d]])]]
        return call(
            functools.partial(project_kernel, C, bool(extra)),
            [sds((rows, width), F32), sds((rows, qw), BF16)],
            len(operands),
            scratch=[
                pltpu.VMEM((C, rows, qw), BF16),
            ],
            cost=(0, 2**14),
        )(*operands)

    mine_all = gather(mine)
    cut = width - max(width * 3 // 8, 128)
    near = after(shards[1], place)[:, cut:]
    for d in range(2, C, 2):
        shards[d + 1] = (
            permute(after(shards[d], place, mine)[:, :cut], exp=1),
            permute(near, exp=spread(d)),
        )
    acc, last = project(mine_all, res)
    quarter = [shards[d][1] for d in range(3, C, 2)]
    theirs_all = gather(after(theirs, place, shards[1]), lambda: quarter)
    acc_far, last_far = project(theirs_all)
    gain = norm_gain.reshape(1, width)
    own, full, *outgoing = call(
        functools.partial(last_kernel, E, cap),
        [
            sds((rows, width), F32),
            sds((rows, width), BF16),
        ]
        + [sds((2 * cap, width), BF16)] * E,
        8,
        cost=(0, 2**14),
    )(acc, acc_far, last, last_far, *shards[C - 1], place, other_place)
    incoming = [permute(x, exp=b) if b else x for x, b in zip(outgoing, all_hops(E))]
    arrived = permute(after(full, *incoming[: E // 2]), exp=PAIR)

    order = [0]
    bit = C // 2
    while bit:
        order = order + [r | bit for r in order]
        bit //= 2
    keep, *sends = call(
        functools.partial(gate_up_kernel, C, E, cap, order),
        [sds((slots // 2, wide + 128), F32)] + [sds((slots // 8, wide + 128), BF16)] * 4,
        E + 2,
        scratch=[pltpu.VMEM((slots, width), BF16), pltpu.VMEM((slots, wide + 128), F32)],
        cost=(0, 2**10),
    )(*incoming, gain, w_gate_up.reshape(width, wide))
    bit = 1
    while 2 * bit < C:
        count = keep.shape[0] // 2
        keep, *sends = call(
            functools.partial(halve_kernel, len(sends)),
            [sds((count, wide + 128), F32)] + [sds((count // 2, wide + 128), BF16)] * 2,
            1 + len(sends),
            cost=(0, 2**10),
        )(keep, *[permute(x, ctx=bit) for x in sends])
        bit *= 2
    activated = call(
        functools.partial(activate_kernel, hidden),
        sds((own_rows, hidden), BF16),
        1 + len(sends),
        cost=(0, 2**10),
    )(keep, *[permute(x, ctx=bit) for x in sends])
    acts = {0: activated}
    acts[bit] = permute(activated, ctx=bit)
    bit //= 2
    while bit:
        for r in list(acts):
            acts[r ^ bit] = permute(acts[r], ctx=bit)
        bit //= 2
    expert_out = call(
        functools.partial(down_kernel, C, E, cap),
        [sds((cap, width), BF16)] * E,
        C + 1,
        scratch=[pltpu.VMEM((slots, hidden), BF16), pltpu.VMEM((slots, width), BF16)],
        cost=(2 * slots * width * hidden, 2 * width * hidden),
    )(acts[0], *[acts[s] for s in range(1, C)], w_down.reshape(hidden, width))
    returned = [permute(x, exp=b) if b else x for x, b in zip(expert_out, all_hops(E))]
    mixed = call(mix_kernel, sds((rows, width), F32), 2, cost=(0, 2**14))(own, arrived)
    columns = min(4, width // 128)
    result = call(
        functools.partial(combine_kernel, E, cap),
        sds((rows, width), BF16),
        3 + E,
        scratch=[
            pltpu.VMEM((slots, width), BF16),
            pltpu.VMEM((columns, rows, width // columns), BF16),
            pltpu.SemaphoreType.DMA((columns,)),
        ],
        out_specs=HBM,
        cost=(0, 2 * 2**20),
    )(mixed, place, gate, *returned)
    return result.reshape(C, 1, tok, width)


def solution(mesh):
    in_specs = (
        P("ctx", "exp", None, None),
        P("ctx", "exp", None, None),
        P("ctx", "exp", None, None),
        P(None, "exp", None, "ctx"),
        P("exp", "ctx"),
        P("ctx"),
        P(None, "exp", None, None),
        P(None, "exp", None, None),
        P("exp", "ctx", None),
        P("exp", None, "ctx"),
    )
    out_specs = P(None, "exp", None, "ctx")
    return jax.shard_map(body, mesh=mesh, in_specs=in_specs, out_specs=out_specs, check_vma=False)
```

```python
import functools
import math

import jax
import jax.numpy as jnp
from jax import lax
from jax.experimental import pallas as pl
from jax.experimental.pallas import tpu as pltpu
from jax.sharding import PartitionSpec as P

D = 4096
QUERY_HEADS = 32
KEY_VALUE_HEADS = 2
HEAD_SIZE = 128
GROUP_EXTENT = QUERY_HEADS // KEY_VALUE_HEADS
NEG_FILL = -1e30
EXPONENT = HEAD_SIZE ** (-0.5) * math.log2(math.e)
BF16 = jnp.bfloat16
F32 = jnp.float32
VMEM = pl.BlockSpec(memory_space=pltpu.VMEM)
HBM = pl.BlockSpec(memory_space=pltpu.HBM)
ANY = pl.BlockSpec(memory_space=pl.ANY)


def call(kernel, out_shape, n_in, scratch=(), cost=(0, 0), limit=32, **kw):
    kw.setdefault("in_specs", [VMEM] * n_in)
    kw.setdefault("out_specs", jax.tree.map(lambda _: VMEM, out_shape))
    return pl.pallas_call(
        kernel,
        out_shape=out_shape,
        scratch_shapes=list(scratch),
        cost_estimate=pl.CostEstimate(flops=cost[0], bytes_accessed=cost[1], transcendentals=0),
        compiler_params=pltpu.CompilerParams(vmem_limit_bytes=limit * 2**20),
        **kw,
    )


def in_hbm(x):
    return pltpu.with_memory_space_constraint(x, pltpu.HBM)


def sds(shape, dtype):
    return jax.ShapeDtypeStruct(shape, dtype)


def dot(a, b):
    return jnp.dot(a, b, preferred_element_type=F32)


PAIR = 4
PACK_LIMIT = 16


def spread(d):
    return (d // PAIR) * 2 * PAIR + d % PAIR


def own_hi_lo():
    e = lax.axis_index("exp")
    return lax.div(e, 2 * PAIR) * PAIR + lax.rem(e, PAIR), lax.rem(lax.div(e, PAIR), 2)


def aligned(x, n):
    return pl.multiple_of(x, n)


def run_copies(pairs, sems):
    copies = [pltpu.make_async_copy(src, dst, sems.at[i]) for i, (src, dst) in enumerate(pairs)]
    for c in copies:
        c.start()
    for c in copies:
        c.wait()


def far_first(C):
    return [*range(2, C), 1, 0]


def all_hops(E):
    return [b for b in range(E) if b & PAIR] + [b for b in reversed(range(E)) if not b & PAIR]


def pack_kernel(C, qw, q_ref, new_ref, past_ref, *refs):
    outs, sems = refs[:C], refs[C]
    c = lax.axis_index("ctx")
    _, lo = own_hi_lo()
    kv = new_ref.shape[1]
    pairs = []
    for i, s in enumerate(far_first(C)):
        target = jnp.bitwise_xor(c, s)
        out = outs[i]
        for t in range(2):
            shard = lax.div(target, PAIR) * 2 * PAIR + lax.rem(target, PAIR)
            shard = shard + PAIR * jnp.bitwise_xor(lo, t)
            at = pl.ds(aligned(shard * qw, 128), qw)
            pairs.append((q_ref.at[:, at], out.at[:, t * qw : (t + 1) * qw]))
        pairs.append((new_ref, out.at[:, 2 * qw : 2 * qw + kv]))
        pairs.append((past_ref, out.at[:, 2 * qw + kv :]))
    run_copies(pairs, sems)


def attend_kernel(C, t, *refs):
    msgs, out, kv_s, q_s = refs[:C], refs[C], refs[-2], refs[-1]
    if t == 1:
        refs[C + 1][...] = msgs[-1][...]
    c = lax.axis_index("ctx")
    tok, qw = msgs[0].shape[0], out.shape[1]
    rows = C * tok
    _, lo = own_hi_lo()
    shard = lax.div(c, PAIR) * 2 * PAIR + lax.rem(c, PAIR) + PAIR * jnp.bitwise_xor(lo, t)
    head = lax.div(shard * (qw // HEAD_SIZE), GROUP_EXTENT)
    for msg, s in zip(msgs, far_first(C)):
        at = aligned(jnp.bitwise_xor(c, s) * tok, tok)
        q_s[pl.ds(at, tok), :] = msg[:, t * qw : (t + 1) * qw]
        for i, to in ((0, rows + at), (1, at)):
            for part in range(2):
                first = 2 * qw + (i * 2 + part) * KEY_VALUE_HEADS * HEAD_SIZE
                cols = pl.ds(aligned(first + head * HEAD_SIZE, 128), HEAD_SIZE)
                kv_s[pl.ds(to, tok), part * HEAD_SIZE : (part + 1) * HEAD_SIZE] = msg[:, cols]
    block = 128
    visible = lax.broadcasted_iota(jnp.int32, (block, block), 1) <= lax.broadcasted_iota(
        jnp.int32, (block, block), 0
    )
    for b in range(rows // block):
        seen = rows + (b + 1) * block
        k = kv_s[:seen, :HEAD_SIZE]
        v = kv_s[:seen, HEAD_SIZE:]
        at = slice(b * block, (b + 1) * block)
        for h in range(qw // HEAD_SIZE):
            q = q_s[at, h * HEAD_SIZE : (h + 1) * HEAD_SIZE]
            scores = lax.dot_general(q, k, (((1,), (1,)), ((), ())), preferred_element_type=F32)
            parts = (scores[:, : seen - block], jnp.where(visible, scores[:, seen - block :], NEG_FILL))
            top = jnp.maximum(*[jnp.max(x, axis=1, keepdims=True) for x in parts])
            parts = [jnp.exp2((x - top) * EXPONENT) for x in parts]
            total = sum(jnp.sum(x, axis=1, keepdims=True) for x in parts)
            numerator = dot(jnp.concatenate([x.astype(BF16) for x in parts], axis=1), v)
            out[at, h * HEAD_SIZE : (h + 1) * HEAD_SIZE] = (numerator / total).astype(BF16)


def place_tokens(E, cap, t, routes_ref, place_ref, line_s):
    blocks, _, tok = routes_ref.shape
    rows = blocks * tok
    earlier = jnp.where(
        lax.broadcasted_iota(jnp.int32, (rows, rows), 0)
        < lax.broadcasted_iota(jnp.int32, (rows, rows), 1),
        1.0,
        0.0,
    ).astype(BF16)
    for i in range(blocks):
        routes = routes_ref[i]
        target = jnp.sum(jnp.where(routes < E, routes + 1, 0), axis=0, keepdims=True) - 1
        line_s[:, i * tok : (i + 1) * tok] = jnp.broadcast_to(target, (8, tok))
    target = line_s[:1, :]
    experts = lax.broadcasted_iota(jnp.int32, (E, rows), 0)
    one_hot = jnp.where(target == experts, 1.0, 0.0)
    rank = jnp.sum(dot(one_hot.astype(BF16), earlier) * one_hot, axis=0, keepdims=True)
    own = jnp.bitwise_xor(lax.axis_index("exp"), PAIR * t)
    slot = jnp.bitwise_xor(target, own) * cap + rank.astype(jnp.int32)
    slot = jnp.where(target >= 0, slot, -1)
    places = lax.broadcasted_iota(jnp.int32, (E * cap, rows), 0)
    place_ref[...] = jnp.where(slot == places, 1.0, 0.0).astype(BF16)


def route_kernel(E, cap, routes_ref, gates_ref, *refs):
    place_ref, gate_ref, line_s, gate_s = refs[2], refs[3], refs[-2], refs[-1]
    for src, dst in zip(refs[:2], refs[4:6]):
        dst[...] = src[...]
    place_tokens(E, cap, 0, routes_ref, place_ref, line_s)
    blocks, _, tok = routes_ref.shape
    for i in range(blocks):
        gate = jnp.sum(jnp.where(routes_ref[i] < E, gates_ref[i], 0.0), axis=0, keepdims=True)
        gate_s[:, i * tok : (i + 1) * tok] = jnp.broadcast_to(gate, (128, tok))
    gate_ref[...] = gate_s[...].T


def project_kernel(C, with_residual, *refs):
    refs, (acc, last, stacked) = list(refs[:-3]), refs[-3:]
    res = refs.pop(0) if with_residual else None
    atts, ws = refs[:C], refs[C:]
    hi, _ = own_hi_lo()
    turn = jnp.bitwise_xor(lax.axis_index("ctx"), hi)
    for s in range(C):
        stacked[jnp.bitwise_xor(turn, s)] = atts[s][...]
    last[...] = stacked[C - 1]
    half = acc.shape[1] // 2
    pieces = list(ws)
    shards = [pieces.pop(0) if d < 2 or d % 2 == 0 else (pieces.pop(0), pieces.pop(0)) for d in range(C - 1)]
    for j in range(2):
        at = slice(j * half, (j + 1) * half)
        total = res[:, at].astype(F32) if with_residual else None
        for d, w in enumerate(shards):
            if not isinstance(w, tuple):
                term = dot(stacked[d], w[:, at])
                total = term if total is None else total + term
        acc[:, at] = total
    for d, w in enumerate(shards):
        if isinstance(w, tuple):
            cut = w[0].shape[1]
            acc[:, :cut] += dot(stacked[d], w[0][...])
            acc[:, cut:] += dot(stacked[d], w[1][...])


def last_kernel(E, cap, *refs):
    accs, lasts, ws, places = refs[:2], refs[2:4], refs[4:6], refs[6:8]
    own_ref, full_ref, *outs = refs[8:]
    cut = ws[0].shape[1]
    for j, cols in enumerate((slice(0, cut), slice(cut, own_ref.shape[1]))):
        for t in (1, 0):
            total = accs[t][:, cols] + dot(lasts[t][...], ws[j][...])
            rounded = total.astype(BF16)
            if t == 0:
                own_ref[:, cols] = total
            else:
                full_ref[:, cols] = rounded
            picked = dot(places[t][...], rounded).astype(BF16)
            for out, b in zip(outs, all_hops(E)):
                at = (b ^ (PAIR * t)) * cap
                out[t * cap : (t + 1) * cap, cols] = picked[at : at + cap]


def gate_up_kernel(C, E, cap, order, *refs):
    xs, gain_ref, w_ref, keep_ref, *sends, x_s, part_s = refs[:E], *refs[E:]
    c = lax.axis_index("ctx")
    e = lax.axis_index("exp")
    own_rows = E * cap // C
    wide = w_ref.shape[1]
    came = dict(zip(all_hops(E), xs))
    for b in range(E):
        at = aligned(jnp.bitwise_xor(e, b) * cap, cap)
        total = came[b][:cap, :].astype(F32) + came[b ^ PAIR][cap:, :].astype(F32)
        x_s[pl.ds(at, cap), :] = (total * gain_ref[...]).astype(BF16)
        square = jnp.sum(total * total, axis=1, keepdims=True)
        lane = lax.broadcasted_iota(jnp.int32, (cap, 128), 1)
        part_s[pl.ds(at, cap), wide:] = jnp.where(lane == 0, square, 0.0)
    step = 512
    for j in range(wide // step):
        at = slice(j * step, (j + 1) * step)
        part_s[:, at] = dot(x_s[...], w_ref[:, at])
    piece = min(own_rows, sends[0].shape[0])
    for k in range(C * own_rows // piece):
        i, rest = divmod(k * piece, own_rows)
        at = aligned(jnp.bitwise_xor(c, order[i]) * own_rows + rest, piece)
        block = part_s[pl.ds(at, piece), :]
        first = k * piece - C // 2 * own_rows
        if first < 0:
            keep_ref[k * piece : (k + 1) * piece, :] = block
        else:
            send_ref = sends[first // sends[0].shape[0]]
            to = first % sends[0].shape[0]
            send_ref[to : to + piece, :wide] = block[:, :wide].astype(BF16)
            square = block[:, wide:]
            high = square.astype(BF16).astype(F32)
            lane = lax.broadcasted_iota(jnp.int32, square.shape, 1)
            low = pltpu.roll(square - high, 1, 1)
            pair = jnp.where(lane == 1, low, high)
            send_ref[to : to + piece, wide:] = pair.astype(BF16)


def halve_kernel(pieces, keep_in, *refs):
    gots, keep_ref, sends = refs[:pieces], refs[pieces], refs[pieces + 1 :]
    rows = keep_ref.shape[0]
    wide = keep_ref.shape[1] - 128
    count = gots[0].shape[0]
    step = min(count, sends[0].shape[0])
    for at in range(0, 2 * rows, step):
        got = gots[at // count][at % count : at % count + step, :]
        total = keep_in[at : at + step, :] + got.astype(F32)
        if at < rows:
            keep_ref[at : at + step, :] = total
            continue
        send_ref = sends[(at - rows) // sends[0].shape[0]]
        to = (at - rows) % sends[0].shape[0]
        send_ref[to : to + step, :wide] = total[:, :wide].astype(BF16)
        square = jnp.sum(total[:, wide:], axis=1, keepdims=True)
        high = square.astype(BF16).astype(F32)
        lane = lax.broadcasted_iota(jnp.int32, (step, 128), 1)
        pair = jnp.where(lane == 0, high, jnp.where(lane == 1, square - high, 0.0))
        send_ref[to : to + step, wide:] = pair.astype(BF16)


def activate_kernel(hidden, keep_ref, *refs):
    gots, out = refs[:-1], refs[-1]
    count = gots[0].shape[0]
    for i, got in enumerate(gots):
        rows = slice(i * count, (i + 1) * count)

        def summed(at):
            return keep_ref[rows, at] + got[:, at].astype(F32)

        square = jnp.sum(summed(slice(2 * hidden, 2 * hidden + 128)), axis=1, keepdims=True)
        scale = lax.rsqrt(square / D + 1e-6)
        gate = summed(slice(0, hidden)) * scale
        up = summed(slice(hidden, 2 * hidden)) * scale
        out[rows, :] = (gate / (1.0 + jnp.exp(-gate)) * up).astype(BF16)


def down_kernel(C, E, cap, *refs):
    acts, w_ref, outs, x_s, part_s = refs[:C], refs[C], refs[C + 1 : C + 1 + E], refs[-2], refs[-1]
    c = lax.axis_index("ctx")
    e = lax.axis_index("exp")
    own_rows = E * cap // C
    for s in range(C):
        at = aligned(jnp.bitwise_xor(c, s) * own_rows, own_rows)
        x_s[pl.ds(at, own_rows), :] = acts[s][...]
    part_s[...] = dot(x_s[...], w_ref[...]).astype(BF16)
    for out, b in zip(outs, all_hops(E)):
        at = aligned(jnp.bitwise_xor(e, b) * cap, cap)
        out[...] = part_s[pl.ds(at, cap), :]


def mix_kernel(own, got, out):
    out[...] = own[...] + got[...].astype(F32)


def combine_kernel(E, cap, mixed, place_ref, gate_ref, *refs):
    xs, (out, x_s, out_s, sems) = refs[:E], refs[E:]
    for x, b in zip(xs, all_hops(E)):
        x_s[b * cap : (b + 1) * cap, :] = x[...]
    count, _, width = out_s.shape
    copies = []
    for j in range(count):
        cols = slice(j * width, (j + 1) * width)
        collected = lax.dot_general(
            place_ref[...], x_s[:, cols], (((0,), (0,)), ((), ())), preferred_element_type=F32
        )
        out_s[j] = (mixed[:, cols] + gate_ref[:, :1] * collected).astype(BF16)
        copies.append(pltpu.make_async_copy(out_s.at[j], out.at[:, cols], sems.at[j]))
        copies[-1].start()
    for c in copies:
        c.wait()


def body(
    queries,
    new_keys_values,
    cached_keys_values,
    residual,
    out_weight,
    norm_gain,
    routes,
    gates,
    w_gate_up,
    w_down,
):
    C = lax.axis_size("ctx")
    E = lax.axis_size("exp")
    tok = queries.shape[2]
    rows = C * tok
    width = residual.shape[3]
    hidden = w_down.shape[1]
    wide = 2 * hidden
    cap = rows // (2 * E)
    slots = E * cap
    own_rows = slots // C
    qw = QUERY_HEADS // E * HEAD_SIZE

    def permute(x, ctx=0, exp=0):
        pairs = [(c * E + e, (c ^ ctx) * E + (e ^ exp)) for c in range(C) for e in range(E)]
        return lax.ppermute(x, ("ctx", "exp"), pairs)

    def after(x, *others):
        return lax.optimization_barrier((x, *others))[0]

    kv = new_keys_values.shape[3]
    msgs = call(
        functools.partial(pack_kernel, C, qw),
        [sds((tok, 2 * qw + 2 * kv), BF16)] * C,
        3,
        scratch=[pltpu.SemaphoreType.DMA((4 * C,))],
        in_specs=[HBM] * 3,
        cost=(0, 2**20),
        limit=PACK_LIMIT,
    )(
        in_hbm(queries.reshape(tok, queries.shape[3])),
        in_hbm(new_keys_values.reshape(tok, kv)),
        in_hbm(cached_keys_values.reshape(tok, kv)),
    )
    res = residual.reshape(rows, width)
    got = [permute(x, ctx=s) if s else x for s, x in zip(far_first(C), msgs)]
    shards = {0: out_weight, 1: permute(out_weight, exp=1)}
    for d in range(2, C, 2):
        shards[d] = permute(out_weight, exp=spread(d))
    step = [shards[d] for d in range(2, C, 2)]

    def attend(t, msgs):
        return call(
            functools.partial(attend_kernel, C, t),
            [sds((rows, qw), BF16)] + [sds(msgs[0].shape, BF16)] * t,
            C,
            scratch=[pltpu.VMEM((2 * rows, 2 * HEAD_SIZE), BF16), pltpu.VMEM((rows, qw), BF16)],
            cost=(0, 2**14),
            limit=16,
        )(*msgs)

    tokens_last = lambda x: jnp.transpose(x.reshape(C, tok, x.shape[3]), (0, 2, 1))
    own_routes = tokens_last(routes)
    other_routes = permute(after(own_routes, *got), exp=PAIR)
    other, own_msg = attend(1, got)
    theirs = permute(other, exp=PAIR)
    (mine,) = attend(0, [after(got[0], other), *got[1:-1], own_msg])
    place, gate, *staged = call(
        functools.partial(route_kernel, E, cap),
        [sds((slots, rows), BF16), sds((rows, 128), F32)]
        + [sds((qw, width), BF16), sds((rows, width), BF16)],
        4,
        scratch=[pltpu.VMEM((8, rows), jnp.int32), pltpu.VMEM((128, rows), F32)],
        cost=(0, 2**14),
        limit=16,
    )(after(own_routes, mine), tokens_last(gates), out_weight, res)
    other_place = call(
        functools.partial(place_tokens, E, cap, 1),
        sds((slots, rows), BF16),
        1,
        scratch=[pltpu.VMEM((8, rows), jnp.int32)],
        cost=(0, 2**14),
        limit=16,
    )(other_routes)
    shards[0], res = staged

    def gather(x, before=lambda: ()):
        atts = {0: x, 1: permute(x, ctx=1)}
        for s in range(2, C, 2):
            atts[s] = permute(x, ctx=s)
        due = before()
        for s in range(2, C, 2):
            atts[s + 1] = permute(after(atts[s], *due), ctx=1)
        return [atts[s] for s in range(C)]

    def project(atts, *extra):
        operands = [*extra, *atts, shards[0], shards[1], *[w for d in range(2, C - 1) for w in (shards[d] if d % 2 else [shards[d]])]]
        return call(
            functools.partial(project_kernel, C, bool(extra)),
            [sds((rows, width), F32), sds((rows, qw), BF16)],
            len(operands),
            scratch=[
                pltpu.VMEM((C, rows, qw), BF16),
            ],
            cost=(0, 2**14),
        )(*operands)

    mine_all = gather(mine)
    cut = width - max(width // 4, 128)
    near = after(shards[1], place)[:, cut:]
    for d in range(2, C, 2):
        shards[d + 1] = (
            permute(after(shards[d], place)[:, :cut], exp=1),
            permute(near, exp=spread(d)),
        )
    acc, last = project(mine_all, res)
    quarter = [shards[d][1] for d in range(3, C, 2)]
    theirs_all = gather(after(theirs, place, shards[1]), lambda: quarter)
    acc_far, last_far = project(theirs_all)
    gain = norm_gain.reshape(1, width)
    own, full, *outgoing = call(
        functools.partial(last_kernel, E, cap),
        [
            sds((rows, width), F32),
            sds((rows, width), BF16),
        ]
        + [sds((2 * cap, width), BF16)] * E,
        8,
        cost=(0, 2**14),
    )(acc, acc_far, last, last_far, *shards[C - 1], place, other_place)
    incoming = [permute(x, exp=b) if b else x for x, b in zip(outgoing, all_hops(E))]
    arrived = permute(after(full, *incoming[: E // 2]), exp=PAIR)

    order = [0]
    bit = C // 2
    while bit:
        order = order + [r | bit for r in order]
        bit //= 2
    keep, *sends = call(
        functools.partial(gate_up_kernel, C, E, cap, order),
        [sds((slots // 2, wide + 128), F32)] + [sds((slots // 8, wide + 128), BF16)] * 4,
        E + 2,
        scratch=[pltpu.VMEM((slots, width), BF16), pltpu.VMEM((slots, wide + 128), F32)],
        cost=(0, 2**10),
    )(*incoming, gain, w_gate_up.reshape(width, wide))
    bit = 1
    while 2 * bit < C:
        count = keep.shape[0] // 2
        keep, *sends = call(
            functools.partial(halve_kernel, len(sends)),
            [sds((count, wide + 128), F32)] + [sds((count // 2, wide + 128), BF16)] * 2,
            1 + len(sends),
            cost=(0, 2**10),
        )(keep, *[permute(x, ctx=bit) for x in sends])
        bit *= 2
    activated = call(
        functools.partial(activate_kernel, hidden),
        sds((own_rows, hidden), BF16),
        1 + len(sends),
        cost=(0, 2**10),
    )(keep, *[permute(x, ctx=bit) for x in sends])
    acts = {0: activated}
    acts[bit] = permute(activated, ctx=bit)
    bit //= 2
    while bit:
        for r in list(acts):
            acts[r ^ bit] = permute(acts[r], ctx=bit)
        bit //= 2
    expert_out = call(
        functools.partial(down_kernel, C, E, cap),
        [sds((cap, width), BF16)] * E,
        C + 1,
        scratch=[pltpu.VMEM((slots, hidden), BF16), pltpu.VMEM((slots, width), BF16)],
        cost=(2 * slots * width * hidden, 2 * width * hidden),
    )(acts[0], *[acts[s] for s in range(1, C)], w_down.reshape(hidden, width))
    returned = [permute(x, exp=b) if b else x for x, b in zip(expert_out, all_hops(E))]
    mixed = call(mix_kernel, sds((rows, width), F32), 2, cost=(0, 2**14))(own, arrived)
    columns = min(4, width // 128)
    result = call(
        functools.partial(combine_kernel, E, cap),
        sds((rows, width), BF16),
        3 + E,
        scratch=[
            pltpu.VMEM((slots, width), BF16),
            pltpu.VMEM((columns, rows, width // columns), BF16),
            pltpu.SemaphoreType.DMA((columns,)),
        ],
        out_specs=HBM,
        cost=(0, 2 * 2**20),
    )(mixed, place, gate, *returned)
    return result.reshape(C, 1, tok, width)


def solution(mesh):
    in_specs = (
        P("ctx", "exp", None, None),
        P("ctx", "exp", None, None),
        P("ctx", "exp", None, None),
        P(None, "exp", None, "ctx"),
        P("exp", "ctx"),
        P("ctx"),
        P(None, "exp", None, None),
        P(None, "exp", None, None),
        P("exp", "ctx", None),
        P("exp", None, "ctx"),
    )
    out_specs = P(None, "exp", None, "ctx")
    return jax.shard_map(body, mesh=mesh, in_specs=in_specs, out_specs=out_specs, check_vma=False)
```

```python
import functools
import math

import jax
import jax.numpy as jnp
from jax import lax
from jax.experimental import pallas as pl
from jax.experimental.pallas import tpu as pltpu
from jax.sharding import PartitionSpec as P

D = 4096
QUERY_HEADS = 32
KEY_VALUE_HEADS = 2
HEAD_SIZE = 128
GROUP_EXTENT = QUERY_HEADS // KEY_VALUE_HEADS
NEG_FILL = -1e30
EXPONENT = HEAD_SIZE ** (-0.5) * math.log2(math.e)
BF16 = jnp.bfloat16
F32 = jnp.float32
VMEM = pl.BlockSpec(memory_space=pltpu.VMEM)
HBM = pl.BlockSpec(memory_space=pltpu.HBM)
ANY = pl.BlockSpec(memory_space=pl.ANY)


def call(kernel, out_shape, n_in, scratch=(), cost=(0, 0), limit=32, **kw):
    kw.setdefault("in_specs", [VMEM] * n_in)
    kw.setdefault("out_specs", jax.tree.map(lambda _: VMEM, out_shape))
    return pl.pallas_call(
        kernel,
        out_shape=out_shape,
        scratch_shapes=list(scratch),
        cost_estimate=pl.CostEstimate(flops=cost[0], bytes_accessed=cost[1], transcendentals=0),
        compiler_params=pltpu.CompilerParams(vmem_limit_bytes=limit * 2**20),
        **kw,
    )


def in_hbm(x):
    return pltpu.with_memory_space_constraint(x, pltpu.HBM)


def sds(shape, dtype):
    return jax.ShapeDtypeStruct(shape, dtype)


def dot(a, b):
    return jnp.dot(a, b, preferred_element_type=F32)


PAIR = 4
PACK_LIMIT = 16


def spread(d):
    return (d // PAIR) * 2 * PAIR + d % PAIR


def own_hi_lo():
    e = lax.axis_index("exp")
    return lax.div(e, 2 * PAIR) * PAIR + lax.rem(e, PAIR), lax.rem(lax.div(e, PAIR), 2)


def aligned(x, n):
    return pl.multiple_of(x, n)


def run_copies(pairs, sems):
    copies = [pltpu.make_async_copy(src, dst, sems.at[i]) for i, (src, dst) in enumerate(pairs)]
    for c in copies:
        c.start()
    for c in copies:
        c.wait()


def far_first(C):
    return [*range(2, C), 1, 0]


def all_hops(E):
    return [b for b in range(E) if b & PAIR] + [b for b in reversed(range(E)) if not b & PAIR]


def pack_kernel(C, qw, q_ref, new_ref, past_ref, *refs):
    outs, sems = refs[:C], refs[C]
    c = lax.axis_index("ctx")
    _, lo = own_hi_lo()
    kv = new_ref.shape[1]
    pairs = []
    for i, s in enumerate(far_first(C)):
        target = jnp.bitwise_xor(c, s)
        out = outs[i]
        for t in range(2):
            shard = lax.div(target, PAIR) * 2 * PAIR + lax.rem(target, PAIR)
            shard = shard + PAIR * jnp.bitwise_xor(lo, t)
            at = pl.ds(aligned(shard * qw, 128), qw)
            pairs.append((q_ref.at[:, at], out.at[:, t * qw : (t + 1) * qw]))
        pairs.append((new_ref, out.at[:, 2 * qw : 2 * qw + kv]))
        pairs.append((past_ref, out.at[:, 2 * qw + kv :]))
    run_copies(pairs, sems)


def attend_kernel(C, t, *refs):
    msgs, out, kv_s, q_s = refs[:C], refs[C], refs[-2], refs[-1]
    if t == 1:
        refs[C + 1][...] = msgs[-1][...]
    c = lax.axis_index("ctx")
    tok, qw = msgs[0].shape[0], out.shape[1]
    rows = C * tok
    _, lo = own_hi_lo()
    shard = lax.div(c, PAIR) * 2 * PAIR + lax.rem(c, PAIR) + PAIR * jnp.bitwise_xor(lo, t)
    head = lax.div(shard * (qw // HEAD_SIZE), GROUP_EXTENT)
    for msg, s in zip(msgs, far_first(C)):
        at = aligned(jnp.bitwise_xor(c, s) * tok, tok)
        q_s[pl.ds(at, tok), :] = msg[:, t * qw : (t + 1) * qw]
        for i, to in ((0, rows + at), (1, at)):
            for part in range(2):
                first = 2 * qw + (i * 2 + part) * KEY_VALUE_HEADS * HEAD_SIZE
                cols = pl.ds(aligned(first + head * HEAD_SIZE, 128), HEAD_SIZE)
                kv_s[pl.ds(to, tok), part * HEAD_SIZE : (part + 1) * HEAD_SIZE] = msg[:, cols]
    block = 128
    visible = lax.broadcasted_iota(jnp.int32, (block, block), 1) <= lax.broadcasted_iota(
        jnp.int32, (block, block), 0
    )
    for b in range(rows // block):
        seen = rows + (b + 1) * block
        k = kv_s[:seen, :HEAD_SIZE]
        v = kv_s[:seen, HEAD_SIZE:]
        at = slice(b * block, (b + 1) * block)
        for h in range(qw // HEAD_SIZE):
            q = q_s[at, h * HEAD_SIZE : (h + 1) * HEAD_SIZE]
            scores = lax.dot_general(q, k, (((1,), (1,)), ((), ())), preferred_element_type=F32)
            parts = (scores[:, : seen - block], jnp.where(visible, scores[:, seen - block :], NEG_FILL))
            top = jnp.maximum(*[jnp.max(x, axis=1, keepdims=True) for x in parts])
            parts = [jnp.exp2((x - top) * EXPONENT) for x in parts]
            total = sum(jnp.sum(x, axis=1, keepdims=True) for x in parts)
            numerator = dot(jnp.concatenate([x.astype(BF16) for x in parts], axis=1), v)
            out[at, h * HEAD_SIZE : (h + 1) * HEAD_SIZE] = (numerator / total).astype(BF16)


def place_tokens(E, cap, t, routes_ref, place_ref, line_s):
    blocks, _, tok = routes_ref.shape
    rows = blocks * tok
    earlier = jnp.where(
        lax.broadcasted_iota(jnp.int32, (rows, rows), 0)
        < lax.broadcasted_iota(jnp.int32, (rows, rows), 1),
        1.0,
        0.0,
    ).astype(BF16)
    for i in range(blocks):
        routes = routes_ref[i]
        target = jnp.sum(jnp.where(routes < E, routes + 1, 0), axis=0, keepdims=True) - 1
        line_s[:, i * tok : (i + 1) * tok] = jnp.broadcast_to(target, (8, tok))
    target = line_s[:1, :]
    experts = lax.broadcasted_iota(jnp.int32, (E, rows), 0)
    one_hot = jnp.where(target == experts, 1.0, 0.0)
    rank = jnp.sum(dot(one_hot.astype(BF16), earlier) * one_hot, axis=0, keepdims=True)
    own = jnp.bitwise_xor(lax.axis_index("exp"), PAIR * t)
    slot = jnp.bitwise_xor(target, own) * cap + rank.astype(jnp.int32)
    slot = jnp.where(target >= 0, slot, -1)
    places = lax.broadcasted_iota(jnp.int32, (E * cap, rows), 0)
    place_ref[...] = jnp.where(slot == places, 1.0, 0.0).astype(BF16)


def route_kernel(E, cap, routes_ref, gates_ref, *refs):
    place_ref, gate_ref, line_s, gate_s = refs[2], refs[3], refs[-2], refs[-1]
    for src, dst in zip(refs[:2], refs[4:6]):
        dst[...] = src[...]
    place_tokens(E, cap, 0, routes_ref, place_ref, line_s)
    blocks, _, tok = routes_ref.shape
    for i in range(blocks):
        gate = jnp.sum(jnp.where(routes_ref[i] < E, gates_ref[i], 0.0), axis=0, keepdims=True)
        gate_s[:, i * tok : (i + 1) * tok] = jnp.broadcast_to(gate, (128, tok))
    gate_ref[...] = gate_s[...].T


def project_kernel(C, with_residual, *refs):
    refs, (acc, last, stacked) = list(refs[:-3]), refs[-3:]
    res = refs.pop(0) if with_residual else None
    atts, ws = refs[:C], refs[C:]
    hi, _ = own_hi_lo()
    turn = jnp.bitwise_xor(lax.axis_index("ctx"), hi)
    for s in range(C):
        stacked[jnp.bitwise_xor(turn, s)] = atts[s][...]
    last[...] = stacked[C - 1]
    half = acc.shape[1] // 2
    pieces = list(ws)
    shards = [pieces.pop(0) if d < 2 or d % 2 == 0 else (pieces.pop(0), pieces.pop(0)) for d in range(C - 1)]
    for j in range(2):
        at = slice(j * half, (j + 1) * half)
        total = res[:, at].astype(F32) if with_residual else None
        for d, w in enumerate(shards):
            if not isinstance(w, tuple):
                term = dot(stacked[d], w[:, at])
                total = term if total is None else total + term
        acc[:, at] = total
    for d, w in enumerate(shards):
        if isinstance(w, tuple):
            cut = w[0].shape[1]
            acc[:, :cut] += dot(stacked[d], w[0][...])
            acc[:, cut:] += dot(stacked[d], w[1][...])


def last_kernel(E, cap, *refs):
    accs, lasts, ws, places = refs[:2], refs[2:4], refs[4:6], refs[6:8]
    own_ref, full_ref, *outs = refs[8:]
    cut = ws[0].shape[1]
    for j, cols in enumerate((slice(0, cut), slice(cut, own_ref.shape[1]))):
        for t in (1, 0):
            total = accs[t][:, cols] + dot(lasts[t][...], ws[j][...])
            rounded = total.astype(BF16)
            if t == 0:
                own_ref[:, cols] = total
            else:
                full_ref[:, cols] = rounded
            picked = dot(places[t][...], rounded).astype(BF16)
            for out, b in zip(outs, all_hops(E)):
                at = (b ^ (PAIR * t)) * cap
                out[t * cap : (t + 1) * cap, cols] = picked[at : at + cap]


def gate_up_kernel(C, E, cap, order, *refs):
    xs, gain_ref, w_ref, keep_ref, *sends, x_s, part_s = refs[:E], *refs[E:]
    c = lax.axis_index("ctx")
    e = lax.axis_index("exp")
    own_rows = E * cap // C
    wide = w_ref.shape[1]
    came = dict(zip(all_hops(E), xs))
    for b in range(E):
        at = aligned(jnp.bitwise_xor(e, b) * cap, cap)
        total = came[b][:cap, :].astype(F32) + came[b ^ PAIR][cap:, :].astype(F32)
        x_s[pl.ds(at, cap), :] = (total * gain_ref[...]).astype(BF16)
        square = jnp.sum(total * total, axis=1, keepdims=True)
        lane = lax.broadcasted_iota(jnp.int32, (cap, 128), 1)
        part_s[pl.ds(at, cap), wide:] = jnp.where(lane == 0, square, 0.0)
    step = 512
    for j in range(wide // step):
        at = slice(j * step, (j + 1) * step)
        part_s[:, at] = dot(x_s[...], w_ref[:, at])
    piece = min(own_rows, sends[0].shape[0])
    for k in range(C * own_rows // piece):
        i, rest = divmod(k * piece, own_rows)
        at = aligned(jnp.bitwise_xor(c, order[i]) * own_rows + rest, piece)
        block = part_s[pl.ds(at, piece), :]
        first = k * piece - C // 2 * own_rows
        if first < 0:
            keep_ref[k * piece : (k + 1) * piece, :] = block
        else:
            send_ref = sends[first // sends[0].shape[0]]
            to = first % sends[0].shape[0]
            send_ref[to : to + piece, :wide] = block[:, :wide].astype(BF16)
            square = block[:, wide:]
            high = square.astype(BF16).astype(F32)
            lane = lax.broadcasted_iota(jnp.int32, square.shape, 1)
            low = pltpu.roll(square - high, 1, 1)
            pair = jnp.where(lane == 1, low, high)
            send_ref[to : to + piece, wide:] = pair.astype(BF16)


def halve_kernel(pieces, keep_in, *refs):
    gots, keep_ref, sends = refs[:pieces], refs[pieces], refs[pieces + 1 :]
    rows = keep_ref.shape[0]
    wide = keep_ref.shape[1] - 128
    count = gots[0].shape[0]
    step = min(count, sends[0].shape[0])
    for at in range(0, 2 * rows, step):
        got = gots[at // count][at % count : at % count + step, :]
        total = keep_in[at : at + step, :] + got.astype(F32)
        if at < rows:
            keep_ref[at : at + step, :] = total
            continue
        send_ref = sends[(at - rows) // sends[0].shape[0]]
        to = (at - rows) % sends[0].shape[0]
        send_ref[to : to + step, :wide] = total[:, :wide].astype(BF16)
        square = jnp.sum(total[:, wide:], axis=1, keepdims=True)
        high = square.astype(BF16).astype(F32)
        lane = lax.broadcasted_iota(jnp.int32, (step, 128), 1)
        pair = jnp.where(lane == 0, high, jnp.where(lane == 1, square - high, 0.0))
        send_ref[to : to + step, wide:] = pair.astype(BF16)


def activate_kernel(hidden, keep_ref, *refs):
    gots, out = refs[:-1], refs[-1]
    count = gots[0].shape[0]
    for i, got in enumerate(gots):
        rows = slice(i * count, (i + 1) * count)

        def summed(at):
            return keep_ref[rows, at] + got[:, at].astype(F32)

        square = jnp.sum(summed(slice(2 * hidden, 2 * hidden + 128)), axis=1, keepdims=True)
        scale = lax.rsqrt(square / D + 1e-6)
        gate = summed(slice(0, hidden)) * scale
        up = summed(slice(hidden, 2 * hidden)) * scale
        out[rows, :] = (gate / (1.0 + jnp.exp(-gate)) * up).astype(BF16)


def down_kernel(C, E, cap, *refs):
    acts, w_ref, outs, x_s, part_s = refs[:C], refs[C], refs[C + 1 : C + 1 + E], refs[-2], refs[-1]
    c = lax.axis_index("ctx")
    e = lax.axis_index("exp")
    own_rows = E * cap // C
    for s in range(C):
        at = aligned(jnp.bitwise_xor(c, s) * own_rows, own_rows)
        x_s[pl.ds(at, own_rows), :] = acts[s][...]
    part_s[...] = dot(x_s[...], w_ref[...]).astype(BF16)
    for out, b in zip(outs, all_hops(E)):
        at = aligned(jnp.bitwise_xor(e, b) * cap, cap)
        out[...] = part_s[pl.ds(at, cap), :]


def mix_kernel(own, got, out):
    out[...] = own[...] + got[...].astype(F32)


def combine_kernel(E, cap, mixed, place_ref, gate_ref, *refs):
    xs, (out, x_s, out_s, sems) = refs[:E], refs[E:]
    for x, b in zip(xs, all_hops(E)):
        x_s[b * cap : (b + 1) * cap, :] = x[...]
    count, _, width = out_s.shape
    copies = []
    for j in range(count):
        cols = slice(j * width, (j + 1) * width)
        collected = lax.dot_general(
            place_ref[...], x_s[:, cols], (((0,), (0,)), ((), ())), preferred_element_type=F32
        )
        out_s[j] = (mixed[:, cols] + gate_ref[:, :1] * collected).astype(BF16)
        copies.append(pltpu.make_async_copy(out_s.at[j], out.at[:, cols], sems.at[j]))
        copies[-1].start()
    for c in copies:
        c.wait()


def body(
    queries,
    new_keys_values,
    cached_keys_values,
    residual,
    out_weight,
    norm_gain,
    routes,
    gates,
    w_gate_up,
    w_down,
):
    C = lax.axis_size("ctx")
    E = lax.axis_size("exp")
    tok = queries.shape[2]
    rows = C * tok
    width = residual.shape[3]
    hidden = w_down.shape[1]
    wide = 2 * hidden
    cap = rows // (2 * E)
    slots = E * cap
    own_rows = slots // C
    qw = QUERY_HEADS // E * HEAD_SIZE

    def permute(x, ctx=0, exp=0):
        pairs = [(c * E + e, (c ^ ctx) * E + (e ^ exp)) for c in range(C) for e in range(E)]
        return lax.ppermute(x, ("ctx", "exp"), pairs)

    def after(x, *others):
        return lax.optimization_barrier((x, *others))[0]

    kv = new_keys_values.shape[3]
    msgs = call(
        functools.partial(pack_kernel, C, qw),
        [sds((tok, 2 * qw + 2 * kv), BF16)] * C,
        3,
        scratch=[pltpu.SemaphoreType.DMA((4 * C,))],
        in_specs=[HBM] * 3,
        cost=(0, 2**20),
        limit=PACK_LIMIT,
    )(
        in_hbm(queries.reshape(tok, queries.shape[3])),
        in_hbm(new_keys_values.reshape(tok, kv)),
        in_hbm(cached_keys_values.reshape(tok, kv)),
    )
    res = residual.reshape(rows, width)
    got = [permute(x, ctx=s) if s else x for s, x in zip(far_first(C), msgs)]
    shards = {0: out_weight, 1: permute(out_weight, exp=1)}
    for d in range(2, C, 2):
        shards[d] = permute(out_weight, exp=spread(d))
    step = [shards[d] for d in range(2, C, 2)]

    def attend(t, msgs):
        return call(
            functools.partial(attend_kernel, C, t),
            [sds((rows, qw), BF16)] + [sds(msgs[0].shape, BF16)] * t,
            C,
            scratch=[pltpu.VMEM((2 * rows, 2 * HEAD_SIZE), BF16), pltpu.VMEM((rows, qw), BF16)],
            cost=(0, 2**14),
            limit=16,
        )(*msgs)

    tokens_last = lambda x: jnp.transpose(x.reshape(C, tok, x.shape[3]), (0, 2, 1))
    own_routes = tokens_last(routes)
    other_routes = permute(after(own_routes, *got), exp=PAIR)
    other, own_msg = attend(1, got)
    theirs = permute(other, exp=PAIR)
    (mine,) = attend(0, [after(got[0], other), *got[1:-1], own_msg])
    place, gate, *staged = call(
        functools.partial(route_kernel, E, cap),
        [sds((slots, rows), BF16), sds((rows, 128), F32)]
        + [sds((qw, width), BF16), sds((rows, width), BF16)],
        4,
        scratch=[pltpu.VMEM((8, rows), jnp.int32), pltpu.VMEM((128, rows), F32)],
        cost=(0, 2**14),
        limit=16,
    )(after(own_routes, mine), tokens_last(gates), out_weight, res)
    other_place = call(
        functools.partial(place_tokens, E, cap, 1),
        sds((slots, rows), BF16),
        1,
        scratch=[pltpu.VMEM((8, rows), jnp.int32)],
        cost=(0, 2**14),
        limit=16,
    )(other_routes)
    shards[0], res = staged

    def gather(x, before=lambda: ()):
        atts = {0: x, 1: permute(x, ctx=1)}
        for s in range(2, C, 2):
            atts[s] = permute(x, ctx=s)
        due = before()
        for s in range(2, C, 2):
            atts[s + 1] = permute(after(atts[s], *due), ctx=1)
        return [atts[s] for s in range(C)]

    def project(atts, *extra):
        operands = [*extra, *atts, shards[0], shards[1], *[w for d in range(2, C - 1) for w in (shards[d] if d % 2 else [shards[d]])]]
        return call(
            functools.partial(project_kernel, C, bool(extra)),
            [sds((rows, width), F32), sds((rows, qw), BF16)],
            len(operands),
            scratch=[
                pltpu.VMEM((C, rows, qw), BF16),
            ],
            cost=(0, 2**14),
        )(*operands)

    mine_all = gather(mine)
    cut = width - max(width // 4, 128)
    near = after(shards[1], place)[:, cut:]
    for d in range(2, C, 2):
        shards[d + 1] = (
            permute(after(shards[d], place)[:, :cut], exp=1),
            permute(near, exp=spread(d)),
        )
    acc, last = project(mine_all, res)
    quarter = [shards[d][1] for d in range(3, C, 2)]
    theirs_all = gather(after(theirs, place, shards[1]), lambda: quarter)
    acc_far, last_far = project(theirs_all)
    gain = norm_gain.reshape(1, width)
    own, full, *outgoing = call(
        functools.partial(last_kernel, E, cap),
        [
            sds((rows, width), F32),
            sds((rows, width), BF16),
        ]
        + [sds((2 * cap, width), BF16)] * E,
        8,
        cost=(0, 2**14),
    )(acc, acc_far, last, last_far, *shards[C - 1], place, other_place)
    incoming = [permute(x, exp=b) if b else x for x, b in zip(outgoing, all_hops(E))]
    arrived = permute(after(full, *incoming[: E // 2 - 1]), exp=PAIR)

    order = [0]
    bit = C // 2
    while bit:
        order = order + [r | bit for r in order]
        bit //= 2
    keep, *sends = call(
        functools.partial(gate_up_kernel, C, E, cap, order),
        [sds((slots // 2, wide + 128), F32)] + [sds((slots // 8, wide + 128), BF16)] * 4,
        E + 2,
        scratch=[pltpu.VMEM((slots, width), BF16), pltpu.VMEM((slots, wide + 128), F32)],
        cost=(0, 2**10),
    )(*incoming, gain, w_gate_up.reshape(width, wide))
    bit = 1
    while 2 * bit < C:
        count = keep.shape[0] // 2
        keep, *sends = call(
            functools.partial(halve_kernel, len(sends)),
            [sds((count, wide + 128), F32)] + [sds((count // 2, wide + 128), BF16)] * 2,
            1 + len(sends),
            cost=(0, 2**10),
        )(keep, *[permute(x, ctx=bit) for x in sends])
        bit *= 2
    activated = call(
        functools.partial(activate_kernel, hidden),
        sds((own_rows, hidden), BF16),
        1 + len(sends),
        cost=(0, 2**10),
    )(keep, *[permute(x, ctx=bit) for x in sends])
    acts = {0: activated}
    acts[bit] = permute(activated, ctx=bit)
    bit //= 2
    while bit:
        for r in list(acts):
            acts[r ^ bit] = permute(acts[r], ctx=bit)
        bit //= 2
    expert_out = call(
        functools.partial(down_kernel, C, E, cap),
        [sds((cap, width), BF16)] * E,
        C + 1,
        scratch=[pltpu.VMEM((slots, hidden), BF16), pltpu.VMEM((slots, width), BF16)],
        cost=(2 * slots * width * hidden, 2 * width * hidden),
    )(acts[0], *[acts[s] for s in range(1, C)], w_down.reshape(hidden, width))
    returned = [permute(x, exp=b) if b else x for x, b in zip(expert_out, all_hops(E))]
    mixed = call(mix_kernel, sds((rows, width), F32), 2, cost=(0, 2**14))(own, arrived)
    columns = min(4, width // 128)
    result = call(
        functools.partial(combine_kernel, E, cap),
        sds((rows, width), BF16),
        3 + E,
        scratch=[
            pltpu.VMEM((slots, width), BF16),
            pltpu.VMEM((columns, rows, width // columns), BF16),
            pltpu.SemaphoreType.DMA((columns,)),
        ],
        out_specs=HBM,
        cost=(0, 2 * 2**20),
    )(mixed, place, gate, *returned)
    return result.reshape(C, 1, tok, width)


def solution(mesh):
    in_specs = (
        P("ctx", "exp", None, None),
        P("ctx", "exp", None, None),
        P("ctx", "exp", None, None),
        P(None, "exp", None, "ctx"),
        P("exp", "ctx"),
        P("ctx"),
        P(None, "exp", None, None),
        P(None, "exp", None, None),
        P("exp", "ctx", None),
        P("exp", None, "ctx"),
    )
    out_specs = P(None, "exp", None, "ctx")
    return jax.shard_map(body, mesh=mesh, in_specs=in_specs, out_specs=out_specs, check_vma=False)
```
